32 devices in a mesh: fsdp: 32 (over z, y, x, core).
Axes of the slice: x: 2, y: 2, z: 4, core: 2. Of those that a mesh axis runs over, the one named last changes fastest.
Arguments:
- images: float32 [64, 32, 32, 3], P('fsdp'), may hold values from -1 to 1
- noise_draws: float32 [64, 32, 32, 3], P('fsdp'), may hold values from -5 to 5
- labels: int32 [64], P('fsdp'), may hold values from 0 to 999
- step_index: int32 [64], P('fsdp'), may hold values from 0 to 38
- valid_rows: int32 [64], P('fsdp'), may hold values from 16 to 32
- counts: int32 [32], P('fsdp'), may hold values from 1 to 2, as said below
- master_weights: float32 [9273344], P('fsdp'), as said below
- momentum: float32 [9273344], P('fsdp'), may hold values from -0.00048828125 to 0.00048828125
- ema_weights: float32 [9273344], P('fsdp'), as said below
Outputs:
- loss: float32 [], replicated
- new_momentum: float32 [9273344], P('fsdp')
- new_master: float32 [9273344], P('fsdp')
- new_ema: float32 [9273344], P('fsdp')
- bias_gradient: float32 [3], replicated
The draws below stay inside these ranges and needn't reach their ends.
Inputs may be any that keep to these rules, and one draw needn't show every extreme that they name: `counts`: some device holds 2 images. `master_weights`: weights of the layout above: matrices of spread one over the root of their rows (attn_out four times that), gains near one, shifts and biases small, zeros past 9272451. `ema_weights`: weights of the same kind as master_weights, drawn apart.
All inputs are finite; a program needn't handle non-finite values.
Results may differ from the reference program's by a relative error of at most 0.0095.
Values may be sent and summed in bfloat16 or wider, within the bound.
No kernel may reach another device: no remote copies, remote signals or barrier semaphores. Data moves between devices by JAX's collectives and lax.ppermute only.
A program may use at most 256 MiB of HBM per device.

```python
import math
import jax
import jax.numpy as jnp
from jax import lax

CH_BASE = 192
CH_MID = 384
EMB_DIM = 768
HEADS = 6
HEAD_DIM = 64
CLASSES = 1000
GROUPS = 32
RES = 32
MB_DEV = 2
DISCRETE = 40
IMAGES = 64
PARAMS = 9272451
P_ALL = 9273344
N_FSDP = 32


def draw_layout():
    shapes = [('conv_in', (27, CH_BASE), 'matrix'), ('bias_in', (CH_BASE,), 'bias'), ('conv_down', (9 * CH_BASE, CH_MID), 'matrix'), ('bias_down', (CH_MID,), 'bias'), ('time_one', (CH_BASE, EMB_DIM), 'matrix'), ('time_bias_one', (EMB_DIM,), 'bias'), ('time_two', (EMB_DIM, EMB_DIM), 'matrix'), ('time_bias_two', (EMB_DIM,), 'bias'), ('class_table', (CLASSES, EMB_DIM), 'table')]
    for parameter_prefix in ('first', 'second'):
        shapes += [(parameter_prefix + '_gains', (4, CH_MID), 'gains'), (parameter_prefix + '_conv_one', (9 * CH_MID, CH_MID), 'matrix'), (parameter_prefix + '_bias_one', (CH_MID,), 'bias'), (parameter_prefix + '_embed', (EMB_DIM, 2 * CH_MID), 'matrix'), (parameter_prefix + '_embed_bias', (2 * CH_MID,), 'bias'), (parameter_prefix + '_conv_two', (9 * CH_MID, CH_MID), 'matrix'), (parameter_prefix + '_bias_two', (CH_MID,), 'bias')]
    shapes += [('attn_gains', (2, CH_MID), 'gains'), ('attn_qkv', (CH_MID, 3 * CH_MID), 'matrix'), ('attn_out', (CH_MID, CH_MID), 'wide'), ('attn_bias', (CH_MID,), 'bias'), ('final_gains', (2, CH_MID), 'gains'), ('conv_out', (9 * CH_MID, 3), 'matrix'), ('bias_out', (3,), 'bias')]
    return shapes


def draw_flat(base_key):
    pieces = []
    for seg_index, seg_entry in enumerate(draw_layout()):
        seg_shape = seg_entry[1]
        seg_kind = seg_entry[2]
        normal_draw = jax.random.normal(jax.random.fold_in(base_key, seg_index), seg_shape, jnp.float32)
        if seg_kind == 'matrix':
            piece = normal_draw * seg_shape[0] ** (-0.5)
        elif seg_kind == 'wide':
            piece = normal_draw * 4.0 * seg_shape[0] ** (-0.5)
        elif seg_kind == 'gains':
            centers = jnp.tile(jnp.array([1.0, 0.0], jnp.float32), seg_shape[0] // 2)[:, None]
            spreads = jnp.tile(jnp.array([0.2, 0.3], jnp.float32), seg_shape[0] // 2)[:, None]
            piece = centers + spreads * normal_draw
        elif seg_kind == 'bias':
            piece = 0.3 * normal_draw
        else:
            piece = normal_draw
        pieces.append(piece.reshape(-1))
    flat_vec = jnp.concatenate(pieces)
    return jnp.pad(flat_vec, (0, P_ALL - flat_vec.shape[0]))


def draw_master_weights(key, part):
    return draw_flat(jax.random.fold_in(key, 11))


def draw_ema_weights(key, part):
    return draw_flat(jax.random.fold_in(key, 23))


def draw_counts(key, part):
    base_counts = jax.random.randint(jax.random.fold_in(key, 5), (N_FSDP,), 1, MB_DEV + 1)
    chosen = jax.random.randint(jax.random.fold_in(key, 6), (), 0, N_FSDP)
    return jnp.where(jnp.arange(N_FSDP) == chosen, MB_DEV, base_counts).astype(jnp.int32)


def plant(values, key, smallest, top_value):
    index_at = [jax.random.randint(jax.random.fold_in(key, axis), (), 0, length) for axis, length in enumerate(values.shape)]
    main_axis = values.shape.index(max(values.shape))
    beside = index_at[:main_axis] + [(index_at[main_axis] + 1) % values.shape[main_axis]] + index_at[main_axis + 1:]
    return values.at[tuple(index_at)].set(smallest).at[tuple(beside)].set(top_value)


def block_scale(rng, shape, split, smallest, largest):
    factor_of, own = 1.0, jax.random.fold_in(rng, 6)
    for position, parts in split:
        heights = jnp.exp(jax.random.uniform(jax.random.fold_in(own, position), (parts,), jnp.float32, smallest / len(split), largest / len(split)))
        factor_of = factor_of * jnp.repeat(heights, shape[position] // parts).reshape([-1 if axis == position else 1 for axis in range(len(shape))])
    return factor_of


def noise(key, dims, scale, bound, shards=(), held_as=jnp.bfloat16):
    values = scale * jax.random.normal(key, dims, jnp.float32)
    if shards:
        values = values * block_scale(key, dims, shards, -0.22, 0.18)
    return jnp.clip(values, -bound, bound).astype(held_as)


def setup_inputs(seed: int = 0) -> dict:
    arg_keys = jax.random.split(jax.random.key(seed), 10)
    return {
        "images": jnp.clip(jax.random.uniform(arg_keys[0], (IMAGES, RES, RES, 3), jnp.float32, -1.0, 1.0) * block_scale(arg_keys[0], (IMAGES, RES, RES, 3), ((0, 32),), -0.4, 0.0), -1.0, 1.0),
        "noise_draws": noise(arg_keys[1], (IMAGES, RES, RES, 3), 1.0, 5.0, ((0, 32),), jnp.float32),
        "labels": plant(jax.random.randint(arg_keys[2], (IMAGES,), 0, CLASSES), jax.random.fold_in(arg_keys[2], 1), 0, CLASSES - 1).astype(jnp.int32),
        "step_index": plant(jax.random.randint(arg_keys[3], (IMAGES,), 0, DISCRETE - 1), jax.random.fold_in(arg_keys[3], 1), 0, (DISCRETE - 1) - 1).astype(jnp.int32),
        "valid_rows": plant(jax.random.randint(arg_keys[4], (IMAGES,), RES // 2, RES + 1), jax.random.fold_in(arg_keys[4], 1), RES // 2, RES).astype(jnp.int32),
        "counts": draw_counts(jax.random.fold_in(arg_keys[9], 71), 0),
        "master_weights": draw_master_weights(jax.random.fold_in(arg_keys[9], 71), 0),
        "momentum": noise(arg_keys[7], (P_ALL,), (0.0003 * IMAGES ** -0.5), 0.00048828125, ((0, 32),), jnp.float32),
        "ema_weights": draw_ema_weights(jax.random.fold_in(arg_keys[9], 71), 0),
    }


EPSILON = 1e-05
SIGMA_DATA = 0.5
SIGMA_LOW = 0.002
SIGMA_HIGH = 80.0
RHO_POWER = 7.0
MOMENTUM = 0.9
EMA_DECAY = 0.9
LEARN_RATE = 2000.0
HIGHEST = lax.Precision.HIGHEST

@jax.custom_vjp
def low(v):
    return lax.optimization_barrier(v.astype(jnp.bfloat16)).astype(jnp.float32)

@jax.custom_vjp
def low_back(v):
    return v

def low_keep(v):
    return (low(v), None)

def low_pass(kept, grad):
    return (grad,)

def back_keep(v):
    return (v, None)

def back_low(kept, grad):
    return (low(grad),)
low.defvjp(low_keep, low_pass)
low_back.defvjp(back_keep, back_low)

def layout():
    shapes = [('conv_in', (27, CH_BASE)), ('bias_in', (CH_BASE,)), ('conv_down', (9 * CH_BASE, CH_MID)), ('bias_down', (CH_MID,)), ('time_one', (CH_BASE, EMB_DIM)), ('time_bias_one', (EMB_DIM,)), ('time_two', (EMB_DIM, EMB_DIM)), ('time_bias_two', (EMB_DIM,)), ('class_table', (CLASSES, EMB_DIM))]
    for parameter_prefix in ('first', 'second'):
        shapes += [(parameter_prefix + '_gains', (4, CH_MID)), (parameter_prefix + '_conv_one', (9 * CH_MID, CH_MID)), (parameter_prefix + '_bias_one', (CH_MID,)), (parameter_prefix + '_embed', (EMB_DIM, 2 * CH_MID)), (parameter_prefix + '_embed_bias', (2 * CH_MID,)), (parameter_prefix + '_conv_two', (9 * CH_MID, CH_MID)), (parameter_prefix + '_bias_two', (CH_MID,))]
    shapes += [('attn_gains', (2, CH_MID)), ('attn_qkv', (CH_MID, 3 * CH_MID)), ('attn_out', (CH_MID, CH_MID)), ('attn_bias', (CH_MID,)), ('final_gains', (2, CH_MID)), ('conv_out', (9 * CH_MID, 3)), ('bias_out', (3,))]
    return shapes

def unflatten(flat_vec):
    network_parameters = {}
    offset = 0
    for key_name, seg_shape in layout():
        length = math.prod(seg_shape)
        network_parameters[key_name] = flat_vec[offset:offset + length].reshape(seg_shape)
        offset += length
    return network_parameters

def karras(index):
    ramp_frac = index.astype(jnp.float32) / (DISCRETE - 1)
    low_root = SIGMA_LOW ** (1.0 / RHO_POWER)
    high_root = SIGMA_HIGH ** (1.0 / RHO_POWER)
    return (low_root + ramp_frac * (high_root - low_root)) ** RHO_POWER

def preconditioning_factors(noise_sigma_level):
    variance_sum = noise_sigma_level * noise_sigma_level + SIGMA_DATA ** 2
    skip_scaling_factor = SIGMA_DATA ** 2 / ((noise_sigma_level - SIGMA_LOW) ** 2 + SIGMA_DATA ** 2)
    output_scaling_factor = (noise_sigma_level - SIGMA_LOW) * SIGMA_DATA * lax.rsqrt(variance_sum)
    return (skip_scaling_factor, output_scaling_factor, lax.rsqrt(variance_sum))

def noise_features(noise_sigma_level):
    half_width = CH_BASE // 2
    frequency = jnp.exp(-math.log(10000.0) * jnp.arange(half_width, dtype=jnp.float32) / half_width)
    phases = 250.0 * jnp.log(noise_sigma_level) * frequency
    return jnp.concatenate([jnp.cos(phases), jnp.sin(phases)])

def group_norm(values, gain_row, shift_row):
    grouped = values.reshape(-1, GROUPS, values.shape[-1] // GROUPS)
    center = lax.optimization_barrier(jnp.mean(grouped, axis=(0, 2), keepdims=True))
    spread = lax.optimization_barrier(jnp.mean(jnp.square(grouped - center), axis=(0, 2), keepdims=True))
    normed = ((grouped - center) * lax.rsqrt(spread + EPSILON)).reshape(values.shape)
    return normed * gain_row + shift_row

def convolve(image_val, weight, stride):
    kernel = weight.reshape(3, 3, image_val.shape[-1], weight.shape[1])
    result = lax.conv_general_dilated(image_val[None], kernel, (stride, stride), ((1, 1), (1, 1)), dimension_numbers=('NHWC', 'HWIO', 'NHWC'), precision=HIGHEST)
    return result[0]

def embedding_of(network_parameters, noise_sigma_level, onehot):
    hidden_activation = jax.nn.silu(jnp.dot(noise_features(noise_sigma_level), network_parameters['time_one'], precision=HIGHEST) + network_parameters['time_bias_one'])
    second_activation = jnp.dot(hidden_activation, network_parameters['time_two'], precision=HIGHEST) + network_parameters['time_bias_two']
    return second_activation + jnp.dot(onehot, network_parameters['class_table'], precision=HIGHEST)

def residual_unit(network_parameters, parameter_prefix, hidden_activation, condition_embedding):
    gain_rows = network_parameters[parameter_prefix + '_gains']
    act_one = low(jax.nn.silu(group_norm(hidden_activation, gain_rows[0], gain_rows[1])))
    inner_out = low_back(convolve(act_one, network_parameters[parameter_prefix + '_conv_one'], 1)) + network_parameters[parameter_prefix + '_bias_one']
    modulation = jnp.dot(jax.nn.silu(condition_embedding), network_parameters[parameter_prefix + '_embed'], precision=HIGHEST) + network_parameters[parameter_prefix + '_embed_bias']
    normed = group_norm(inner_out, gain_rows[2], gain_rows[3])
    act_two = low(jax.nn.silu(normed * (1.0 + modulation[:CH_MID]) + modulation[CH_MID:]))
    return hidden_activation + low_back(convolve(act_two, network_parameters[parameter_prefix + '_conv_two'], 1)) + network_parameters[parameter_prefix + '_bias_two']

def attention(network_parameters, hidden_activation):
    tokens = hidden_activation.reshape(-1, CH_MID)
    gain_rows = network_parameters['attn_gains']
    normed = low(group_norm(tokens, gain_rows[0], gain_rows[1]))
    triple = low(low_back(jnp.dot(normed, network_parameters['attn_qkv'], precision=HIGHEST)))
    queries = triple[:, :CH_MID].reshape(-1, HEADS, HEAD_DIM)
    key_vals = triple[:, CH_MID:2 * CH_MID].reshape(-1, HEADS, HEAD_DIM)
    values_v = triple[:, 2 * CH_MID:].reshape(-1, HEADS, HEAD_DIM)
    scores = low_back(jnp.einsum('qhd,khd->hqk', queries, key_vals, precision=HIGHEST) * HEAD_DIM ** (-0.5))
    prob_vals = low(jax.nn.softmax(scores, axis=-1))
    mixed_out = low(low_back(jnp.einsum('hqk,khd->qhd', prob_vals, values_v, precision=HIGHEST))).reshape(-1, CH_MID)
    output = low_back(jnp.dot(mixed_out, network_parameters['attn_out'], precision=HIGHEST)) + network_parameters['attn_bias']
    return hidden_activation + output.reshape(hidden_activation.shape)

def denoise(network_parameters, noisy, noise_sigma_level, onehot):
    skip_scaling_factor, output_scaling_factor, input_scaling_factor = preconditioning_factors(noise_sigma_level)
    first_map = low_back(convolve(low(input_scaling_factor * noisy), network_parameters['conv_in'], 1)) + network_parameters['bias_in']
    hidden_activation = low_back(convolve(low(first_map), network_parameters['conv_down'], 2)) + network_parameters['bias_down']
    condition_embedding = embedding_of(network_parameters, noise_sigma_level, onehot)
    hidden_activation = residual_unit(network_parameters, 'first', hidden_activation, condition_embedding)
    hidden_activation = attention(network_parameters, hidden_activation)
    hidden_activation = residual_unit(network_parameters, 'second', hidden_activation, condition_embedding)
    gain_rows = network_parameters['final_gains']
    act_low = low(jax.nn.silu(group_norm(hidden_activation, gain_rows[0], gain_rows[1])))
    upsampled = jnp.repeat(jnp.repeat(act_low, 2, axis=0), 2, axis=1)
    model_out = low_back(convolve(upsampled, network_parameters['conv_out'], 1)) + network_parameters['bias_out']
    return skip_scaling_factor * noisy + output_scaling_factor * model_out

def reference(images, noise_draws, labels, step_index, valid_rows, counts, master_weights, momentum, ema_weights):
    online = low(master_weights)
    target = unflatten(low(ema_weights))
    slot_live = (jnp.arange(MB_DEV)[None, :] < counts[:, None]).reshape(-1)
    row_live = jnp.arange(RES)[None, :] < valid_rows[:, None]
    pixel_mask = (slot_live[:, None] & row_live).astype(jnp.float32)
    pixel_total = 3.0 * RES * jnp.sum(pixel_mask)

    def per_image(clean_img, noise_img, label_one, index, mask_row):
        sigma_lo = karras(index)
        sigma_hi = karras(index + 1)
        onehot = (jnp.arange(CLASSES) == label_one).astype(jnp.float32)
        target_out = denoise(target, clean_img + sigma_lo * noise_img, sigma_lo, onehot)

        def loss_fn(flat_vec):
            online_out = denoise(unflatten(flat_vec), clean_img + sigma_hi * noise_img, sigma_hi, onehot)
            return jnp.sum(mask_row[:, None, None] * jnp.square(online_out - target_out)) / pixel_total
        loss_value, pullback = jax.vjp(loss_fn, online)
        grad_flat, = pullback(jnp.ones_like(loss_value))
        return (loss_value, grad_flat)

    def per_device(running, scan_item):
        device_loss = jnp.zeros((), jnp.float32)
        device_grad = jnp.zeros_like(master_weights)
        for slot_index in range(MB_DEV):
            slot_item = tuple((member[slot_index] for member in scan_item))
            loss_value, grad_flat = per_image(*slot_item)
            device_loss = device_loss + loss_value
            device_grad = device_grad + grad_flat
        return ((running[0] + device_loss, running[1] + device_grad), None)

    def grouped(array_in):
        return array_in.reshape((N_FSDP, MB_DEV) + array_in.shape[1:])
    start = (jnp.zeros((), jnp.float32), jnp.zeros_like(master_weights))
    scan_items = (grouped(images), grouped(noise_draws), grouped(labels), grouped(step_index), grouped(pixel_mask))
    (loss, grad_sum), _ = lax.scan(per_device, start, scan_items)
    bias_gradient = grad_sum[PARAMS - 3:PARAMS]
    new_momentum = MOMENTUM * momentum + grad_sum
    new_master = master_weights - LEARN_RATE * (grad_sum + MOMENTUM * new_momentum)
    new_ema = EMA_DECAY * ema_weights + (1.0 - EMA_DECAY) * new_master
    return (loss, new_momentum, new_master, new_ema, bias_gradient)
```

```python
import math

import jax
import jax.numpy as jnp
import numpy as np
from jax import lax
from jax.experimental import pallas as pl
from jax.experimental.pallas import tpu as pltpu
from jax.sharding import PartitionSpec as P

CH_BASE = 192
CH_MID = 384
EMB_DIM = 768
HEADS = 6
HEAD_DIM = 64
CLASSES = 1000
GROUPS = 32
RES = 32
MB_DEV = 2
DISCRETE = 40

EPSILON = 1e-05
SIGMA_DATA = 0.5
SIGMA_LOW = 0.002
SIGMA_HIGH = 80.0
RHO_POWER = 7.0
MOMENTUM = 0.9
EMA_DECAY = 0.9
LEARN_RATE = 2000.0

F32 = jnp.float32
BF16 = jnp.bfloat16
LINE = 128
HALF = RES // 2
PIX = HALF * HALF
ROWS = MB_DEV * PIX
GROUP_SIZE = PIX * (CH_MID // GROUPS)
CHUNK = 64
PADDED = 16 + MB_DEV * (PIX + 16)
NN = (((1,), (0,)), ((), ()))
NT = (((1,), (1,)), ((), ()))
TN = (((0,), (0,)), ((), ()))


class Place:
    pass


class Cut:
    def __init__(self):
        self.offset = 0

    def take(self, *shape):
        at = self.offset
        self.offset += math.prod(shape)
        return at // LINE


def block_place(cut):
    at = Place()
    at.gains = cut.take(4, CH_MID)
    at.conv_one = cut.take(9 * CH_MID, CH_MID)
    at.bias_one = cut.take(CH_MID)
    at.embed = cut.take(EMB_DIM, 2 * CH_MID)
    at.embed_bias = cut.take(2 * CH_MID)
    at.conv_two = cut.take(9 * CH_MID, CH_MID)
    at.bias_two = cut.take(CH_MID)
    return at


def places():
    cut, at = Cut(), Place()
    at.conv_in = cut.take(27, CH_BASE)
    at.bias_in = cut.take(CH_BASE)
    at.conv_down = cut.take(9 * CH_BASE, CH_MID)
    at.bias_down = cut.take(CH_MID)
    at.time_one = cut.take(CH_BASE, EMB_DIM)
    at.time_bias_one = cut.take(EMB_DIM)
    at.time_two = cut.take(EMB_DIM, EMB_DIM)
    at.time_bias_two = cut.take(EMB_DIM)
    at.class_table = cut.take(CLASSES, EMB_DIM)
    at.first = block_place(cut)
    at.second = block_place(cut)
    at.attn_gains = cut.take(2, CH_MID)
    at.attn_qkv = cut.take(CH_MID, 3 * CH_MID)
    at.attn_out = cut.take(CH_MID, CH_MID)
    at.attn_bias = cut.take(CH_MID)
    at.final_gains = cut.take(2, CH_MID)
    at.conv_out = cut.take(9 * CH_MID, 3)
    at.bias_out = cut.take(3)
    return at


AT = places()
TAIL = AT.conv_out
SHARDS, PLANE = 32, 8
SHARD = 2264
ROOM = 2272
ALL_LINES = SHARDS * SHARD
MIDDLE = ALL_LINES // 2
SPLIT = AT.first.conv_two // 16 * 16

V_DOWN, V_G1, V_B11, V_B12, V_AG, V_AB, V_FG, V_G2, V_B21, V_B22 = 0, 1, 5, 6, 7, 9, 10, 12, 16, 17
VEC_ROWS = 24


def group_table():
    at = np.arange(CH_MID) // (CH_MID // GROUPS)
    return (at[:, None] == at[None, :]).astype(np.float32)


def spread_tables():
    select = np.zeros((LINE, LINE), np.float32)
    gather = np.zeros((LINE, LINE), np.float32)
    for ky in range(3):
        for kx in range(3):
            for a in range(2):
                for b in range(2):
                    dy, dx = (a + ky - 1) // 2, (b + kx - 1) // 2
                    shift = (dy + 1) * 3 + dx + 1
                    for c in range(3):
                        out = (a * 2 + b) * 3 + c
                        select[(ky * 3 + kx) * 3 + c, shift * 12 + out] = 1.0
                        gather[shift * 12 + out, out] = 1.0
    return select, gather


def split3(v):
    hi = v.astype(BF16)
    rest = v - hi.astype(F32)
    mid = rest.astype(BF16)
    low = (rest - mid.astype(F32)).astype(BF16)
    return hi, mid, low


def dot(a, b, dims=NN):
    return lax.dot_general(a, b, dims, preferred_element_type=F32)


def dot3(a, b, dims=NN):
    rows = a.shape[0]
    hi, mid, low = split3(a)
    if rows % 16:
        out = dot(jnp.concatenate([p.astype(F32) for p in (hi, mid, low)], 0).astype(BF16), b, dims)
    else:
        out = dot(jnp.concatenate([hi, mid, low], 0), b, dims)
    return out[:rows] + out[rows : 2 * rows] + out[2 * rows :]


def outer(a, b):
    pa, pb = split3(a), split3(b)
    pairs = [(0, 0), (0, 1), (1, 0), (1, 1), (0, 2), (2, 0)]
    left = jnp.concatenate([pa[i].astype(F32) for i, _ in pairs], 0).astype(BF16)
    right = jnp.concatenate([pb[j].astype(F32) for _, j in pairs], 0).astype(BF16)
    return dot(left, right, TN)


def sigmoid(z):
    return 1.0 / (1.0 + jnp.exp(-z))


def silu(z):
    return z * sigmoid(z)


def silu_slope(z):
    s = sigmoid(z)
    return s * (1.0 + z * (1.0 - s))


def colsum(ref, base, count=PIX):
    def body(c, acc):
        return acc + jnp.sum(ref[pl.ds(pl.multiple_of(base + c * CHUNK, 8), CHUNK), :], 0, keepdims=True)

    return lax.fori_loop(0, count // CHUNK, body, jnp.zeros((1, ref.shape[1]), F32))


def eight(v):
    return jnp.broadcast_to(v, (8, v.shape[1]))


def group_mean(v, gm_ref):
    return dot3(eight(v), gm_ref[...])[:1] * (1.0 / GROUP_SIZE)


def group_stats(x_ref, img, gm_ref):
    mean = group_mean(colsum(x_ref, img * PIX), gm_ref)

    def body(c, acc):
        gap = x_ref[pl.ds(pl.multiple_of(img * PIX + c * CHUNK, 8), CHUNK), :] - mean
        return acc + jnp.sum(gap * gap, 0, keepdims=True)

    square = lax.fori_loop(0, PIX // CHUNK, body, jnp.zeros((1, CH_MID), F32))
    return mean, lax.rsqrt(group_mean(square, gm_ref) + EPSILON)


def norm_to(pbuf, x_ref, stats, scales, act):
    for img in range(MB_DEV):
        (mean, rstd), (k, o) = stats[img], scales[img]

        def body(c, carry):
            r = pl.multiple_of(img * PIX + c * CHUNK, 8)
            z = (x_ref[pl.ds(r, CHUNK), :] - mean) * rstd * k + o
            pbuf[pl.ds(r + 8, CHUNK), :] = silu(z) if act else z
            return carry

        lax.fori_loop(0, PIX // CHUNK, body, 0)


def norm_back(x_ref, d_ref, stats, scales, act, gm_ref, emit):
    sums = []
    for img in range(MB_DEV):
        (mean, rstd), (k, o) = stats[img], scales[img]

        def one(c, carry):
            r = pl.multiple_of(img * PIX + c * CHUNK, 8)
            xhat = (x_ref[pl.ds(r, CHUNK), :] - mean) * rstd
            dz = d_ref[pl.ds(r, CHUNK), :]
            if act:
                dz = dz * silu_slope(xhat * k + o)
                d_ref[pl.ds(r, CHUNK), :] = dz
            return (carry[0] + jnp.sum(dz, 0, keepdims=True), carry[1] + jnp.sum(dz * xhat, 0, keepdims=True))

        zero = jnp.zeros((1, CH_MID), F32)
        a, b = lax.fori_loop(0, PIX // CHUNK, one, (zero, zero))
        m1, m2 = group_mean(a * k, gm_ref), group_mean(b * k, gm_ref)

        def two(c, carry):
            r = pl.multiple_of(img * PIX + c * CHUNK, 8)
            xhat = (x_ref[pl.ds(r, CHUNK), :] - mean) * rstd
            emit(r, rstd * (d_ref[pl.ds(r, CHUNK), :] * k - m1 - xhat * m2))
            return carry

        lax.fori_loop(0, PIX // CHUNK, two, 0)
        sums.append((a, b))
    return sums


def clear_pads(sbuf):
    for k in range(3):
        for r in range(0, PADDED, PIX + 16):
            sbuf[k, pl.ds(r, 16), :] = jnp.zeros((16, sbuf.shape[2]), BF16)


def shift_to(sbuf, pbuf):
    column = lax.rem(lax.broadcasted_iota(jnp.int32, (CHUNK, CH_MID), 0), HALF)
    for r in range(0, ROWS, CHUNK):
        for k in range(3):
            v = pbuf[r + 7 + k : r + 7 + k + CHUNK, :]
            if k == 0:
                v = jnp.where(column == 0, 0.0, v)
            if k == 2:
                v = jnp.where(column == HALF - 1, 0.0, v)
            start = r + 16 * (r // PIX + 1)
            sbuf[k, start : start + CHUNK, :] = v.astype(BF16)


def shifted(sbuf, k, row):
    first = sbuf[k, pl.ds(pl.multiple_of(row, 16), PIX), :]
    second = sbuf[k, pl.ds(pl.multiple_of(row + PIX + 16, 16), PIX), :]
    return jnp.concatenate([first, second], 0)


def conv_forward(sbuf, w_ref, out_ref):
    def body(t, carry):
        lhs = shifted(sbuf, lax.rem(t, 3), lax.div(t, 3) * 16)
        out_ref[...] += dot(lhs, w_ref[pl.ds(pl.multiple_of(t * CH_MID, CH_MID), CH_MID), :])
        return carry

    lax.fori_loop(0, 9, body, 0)


def put_lines(g_ref, at, value, step, more=None):
    n = value.shape[0]
    low = at // 8 * 8
    start = low if more is None else pl.multiple_of(low + more, 8)
    view = g_ref.at[pl.ds(start, min(n * step + 8, g_ref.shape[0] - low)), :] if more is None else g_ref.at[pl.ds(start, n * step + 8), :]
    for j in range(step):
        view[pl.ds(at - low + j, n, stride=step), :] = value[:, j * LINE : (j + 1) * LINE]


def put_row(g_ref, at, row):
    for j in range(row.shape[1] // LINE):
        g_ref[pl.ds(at + j, 1), :] = row[:, j * LINE : (j + 1) * LINE]


def conv_back(sbuf, at_ref, w_ref, dx_ref, g_ref, at):
    dx_ref[...] = jnp.zeros_like(dx_ref)

    def body(s, carry):
        t = 8 - s
        d = shifted(sbuf, lax.rem(s, 3), lax.div(s, 3) * 16)
        w = w_ref[pl.ds(pl.multiple_of(t * CH_MID, CH_MID), CH_MID), :]
        dx_ref[...] += dot(d, w, NT)
        put_lines(g_ref, at, dot(at_ref[...], d), 3, t * (3 * CH_MID))
        return carry

    lax.fori_loop(0, 9, body, 0)


def transpose_to(at_ref, pbuf):
    for c in range(ROWS // LINE):
        at_ref[:, c * LINE : (c + 1) * LINE] = pbuf[8 + c * LINE : 8 + (c + 1) * LINE, :].T.astype(BF16)


class Lines:
    def __init__(self, lines, stage, wide, sem):
        self.lines, self.stage, self.wide, self.sem = lines, stage, wide, sem

    def copy(self, l0, l1):
        low, top = l0 // 16 * 16, -(-l1 // 16) * 16
        return pltpu.make_async_copy(
            self.lines.at[pl.ds(low, top - low), :], self.stage.at[pl.ds(0, top - low), :], self.sem
        )

    def start(self, span):
        self.copy(*span).start()

    def take(self, span, then=None):
        l0, l1 = span
        self.copy(l0, l1).wait()
        self.low = l0 // 16 * 16
        count = -(-l1 // 16) * 16 - self.low
        whole, rest = divmod(count, 256)

        def body(c, carry):
            r = pl.multiple_of(c * 256, 256)
            self.wide[pl.ds(r, 256), :] = self.stage[pl.ds(r, 256), :].astype(F32)
            return carry

        lax.fori_loop(0, whole, body, 0)
        if rest:
            self.wide[whole * 256 : count, :] = self.stage[whole * 256 : count, :].astype(F32)
        if then is not None:
            self.start(then)

    def matrix(self, w_ref, at, rows, step):
        block = 128 if rows % 192 else 192
        base = at - self.low
        low = base // 8 * 8

        def body(c, carry):
            r = pl.multiple_of(c * block, block)
            view = self.wide.at[pl.ds(pl.multiple_of(low + r * step, 8), block * step + 8), :]
            for j in range(step):
                v = view[pl.ds(base - low + j, block, stride=step), :]
                w_ref[pl.ds(r, block), j * LINE : (j + 1) * LINE] = v.astype(BF16)
            return carry

        lax.fori_loop(0, rows // block, body, 0)

    def row(self, at, step):
        base = at - self.low
        return jnp.concatenate([self.wide[pl.ds(base + j, 1), :] for j in range(step)], 1)


def attention_pair(qkv_ref, img, pair):
    rows = pl.ds(pl.multiple_of(img * PIX, PIX), PIX)
    return [qkv_ref[rows, part * CH_MID + pair * LINE : part * CH_MID + (pair + 1) * LINE] for part in range(3)]


def lane_half():
    return lax.broadcasted_iota(jnp.int32, (1, LINE), 1) < HEAD_DIM


def keep_half(v, half, side):
    mine = half if side == 0 else jnp.logical_not(half)
    return jnp.where(mine, v.astype(F32), 0.0).astype(BF16)


SPAN_TIME = (AT.time_one, AT.class_table)
SPAN_EMB1 = (AT.first.embed, AT.first.conv_two)
SPAN_EMB2 = (AT.second.embed, AT.second.conv_two)
SPAN_DOWN = (AT.conv_down, AT.time_one)
SPAN_ONE1 = (AT.first.gains, AT.first.embed)
SPAN_TWO1 = (AT.first.conv_two, AT.second.gains)
SPAN_ATTN = (AT.attn_gains, AT.conv_out)
SPAN_ONE2 = (AT.second.gains, AT.second.embed)
SPAN_TWO2 = (AT.second.conv_two, AT.attn_gains)


def block_scales(vec, row, mod_ref=None, mod_row=0):
    gain, shift = vec[row : row + 1, :], vec[row + 1 : row + 2, :]
    if mod_ref is None:
        return [(gain, shift)] * MB_DEV
    out = []
    for img in range(MB_DEV):
        scale = 1.0 + mod_ref[mod_row + img : mod_row + img + 1, :CH_MID]
        out.append((gain * scale, shift * scale + mod_ref[mod_row + img : mod_row + img + 1, CH_MID:]))
    return out


def upsample_masks(shift):
    dy, dx = shift // 3 - 1, shift % 3 - 1
    p = lax.broadcasted_iota(jnp.int32, (ROWS, 1), 0)
    i, j = lax.rem(lax.div(p, HALF), HALF), lax.rem(p, HALF)
    inside = (i + dy >= 0) & (i + dy < HALF) & (j + dx >= 0) & (j + dx < HALF)
    lane = lax.broadcasted_iota(jnp.int32, (1, LINE), 1)
    return inside & (lane >= shift * 12) & (lane < shift * 12 + 12), dy * HALF + dx


def forward_kernel(save, *refs):
    labels, lines, xp, win, bin_, wz, bz, phi, gm, sel, gat = refs[:11]
    f_out = refs[11]
    (h0s, h1, u1, h2, qkv, mixed, h3, u2, h4, vec, mod, emb, pre) = refs[12:25]
    if save:
        sw_time, sw_emb1, sw_emb2, sw_down, sw_11, sw_12, sw_attn, sw_21, sw_22 = refs[25:34]
    stage, wide, w_ref, w_sq, sbuf, pbuf, h0p, table, sem, save_sem, tab_sem = refs[34 if save else 25 :]
    src = Lines(lines, stage, wide, sem)
    pending = []

    def keep(source, target):
        if save:
            cp = pltpu.make_async_copy(source, target, save_sem)
            cp.start()
            pending.append(cp)

    def free():
        while pending:
            pending.pop().wait()

    tabs = []
    for n in range(MB_DEV):
        at = AT.class_table + labels[n] * (EMB_DIM // LINE)
        low = pl.multiple_of(lax.div(at, 16) * 16, 16)
        cp = pltpu.make_async_copy(lines.at[pl.ds(low, 32), :], table.at[pl.ds(n * 32, 32), :], tab_sem.at[n])
        cp.start()
        tabs.append((cp, at - low))
    src.start(SPAN_TIME)
    clear_pads(sbuf)
    pbuf[0:8, :] = jnp.zeros((8, CH_MID), F32)
    pbuf[ROWS + 8 : ROWS + 16, :] = jnp.zeros((8, CH_MID), F32)
    src.take(SPAN_TIME, SPAN_EMB1)
    src.matrix(w_sq.at[0], AT.time_one, CH_BASE, 6)
    src.matrix(w_sq.at[1], AT.time_two, EMB_DIM, 6)
    pre[...] = dot3(phi[...], w_sq[0, :CH_BASE, :]) + src.row(AT.time_bias_one, 6)
    emb[...] = dot3(silu(pre[...]), w_sq[1]) + src.row(AT.time_bias_two, 6)
    for n in range(MB_DEV):
        tabs[n][0].wait()
    wide[0 : 32 * MB_DEV, :] = table[...].astype(F32)
    for n in range(MB_DEV):
        for j in range(6):
            cols = slice(j * LINE, (j + 1) * LINE)
            emb[n : n + 1, cols] += wide[pl.ds(n * 32 + tabs[n][1] + j, 1), :]
    keep(w_sq.at[1], sw_time if save else None)
    se = silu(emb[...])
    src.take(SPAN_EMB1, SPAN_EMB2)
    src.matrix(w_sq.at[0], AT.first.embed, EMB_DIM, 6)
    m1 = dot3(se, w_sq[0]) + src.row(AT.first.embed_bias, 6)
    free()
    keep(w_sq.at[0], sw_emb1 if save else None)
    src.take(SPAN_EMB2, SPAN_DOWN)
    src.matrix(w_sq.at[1], AT.second.embed, EMB_DIM, 6)
    m2 = dot3(se, w_sq[1]) + src.row(AT.second.embed_bias, 6)
    free()
    keep(w_sq.at[1], sw_emb2 if save else None)
    mod[0:2, :] = m1[0:2]
    mod[2:4, :] = m2[0:2]
    mod[4:8, :] = jnp.zeros((4, EMB_DIM), F32)

    for ph in range(4):
        v = dot(xp[ph * ROWS : (ph + 1) * ROWS, :], win[...]) + bin_[...]
        h0s[ph * ROWS : (ph + 1) * ROWS, :] = v.astype(BF16)
    src.take(SPAN_DOWN, SPAN_ONE1)
    for j in range(3):
        vec[V_DOWN : V_DOWN + 1, j * LINE : (j + 1) * LINE] = src.row(AT.bias_down + j, 1)
    src.matrix(w_ref, AT.conv_down, 9 * CH_BASE, 3)
    free()
    keep(w_ref.at[pl.ds(0, 9 * CH_BASE), :], sw_down if save else None)
    h1[...] = jnp.broadcast_to(vec[V_DOWN : V_DOWN + 1, :], (ROWS, CH_MID))
    p = lax.broadcasted_iota(jnp.int32, (ROWS, 1), 0)
    has_left, has_up = lax.rem(p, HALF) > 0, lax.rem(lax.div(p, HALF), HALF) > 0
    for ph in range(4):
        h0p[0:32, :] = jnp.zeros((32, h0p.shape[1]), F32)
        h0p[32 : 32 + ROWS, :] = h0s[ph * ROWS : (ph + 1) * ROWS, :].astype(F32)
        for ky in ((0, 2) if ph // 2 else (1,)):
            for kx in ((0, 2) if ph % 2 else (1,)):
                back = (16 if ky == 0 else 0) + (1 if kx == 0 else 0)
                v = h0p[32 - back : 32 - back + ROWS, :]
                if ky == 0:
                    v = jnp.where(has_up, v, 0.0)
                if kx == 0:
                    v = jnp.where(has_left, v, 0.0)
                t = 3 * ky + kx
                h1[...] += dot(v[:, :CH_BASE].astype(BF16), w_ref[t * CH_BASE : (t + 1) * CH_BASE, :])

    def vectors(row, at, count):
        for n in range(count):
            for j in range(3):
                vec[row + n : row + n + 1, j * LINE : (j + 1) * LINE] = src.row(at + 3 * n + j, 1)

    def half_block(x_ref, scales, bias_row, add_ref, out_ref, at, target):
        src.matrix(w_ref, at, 9 * CH_MID, 3)
        keep(w_ref, target)
        stats = [group_stats(x_ref, img, gm) for img in range(MB_DEV)]
        norm_to(pbuf, x_ref, stats, scales, True)
        shift_to(sbuf, pbuf)
        bias = jnp.broadcast_to(vec[bias_row : bias_row + 1, :], (ROWS, CH_MID))
        out_ref[...] = bias if add_ref is None else add_ref[...] + bias
        conv_forward(sbuf, w_ref, out_ref)

    def block(h_in, u, h_out, prefix, g_row, b1_row, b2_row, mod_row, spans, nxt, targets):
        src.take(spans[0], spans[1])
        free()
        vectors(g_row, prefix.gains, 4)
        vectors(b1_row, prefix.bias_one, 1)
        half_block(h_in, block_scales(vec, g_row), b1_row, None, u, prefix.conv_one, targets[0])
        src.take(spans[1], nxt)
        free()
        vectors(b2_row, prefix.bias_two, 1)
        half_block(u, block_scales(vec, g_row + 2, mod, mod_row), b2_row, h_in, h_out, prefix.conv_two, targets[1])

    saved = (sw_11, sw_12, sw_21, sw_22) if save else (None,) * 4
    block(h1, u1, h2, AT.first, V_G1, V_B11, V_B12, 0, (SPAN_ONE1, SPAN_TWO1), SPAN_ATTN, saved[:2])

    src.take(SPAN_ATTN, SPAN_ONE2)
    free()
    vectors(V_AG, AT.attn_gains, 2)
    vectors(V_AB, AT.attn_bias, 1)
    vectors(V_FG, AT.final_gains, 2)
    for part in range(3):
        base = AT.attn_qkv - src.low
        for j in range(3):
            v = wide[pl.ds(base + part * 3 + j, CH_MID, stride=9), :]
            w_ref[part * CH_MID : (part + 1) * CH_MID, j * LINE : (j + 1) * LINE] = v.astype(BF16)
    src.matrix(w_ref.at[pl.ds(3 * CH_MID, CH_MID), :], AT.attn_out, CH_MID, 3)
    keep(w_ref.at[pl.ds(0, 4 * CH_MID), :], sw_attn if save else None)
    stats = [group_stats(h2, img, gm) for img in range(MB_DEV)]
    norm_to(pbuf, h2, stats, block_scales(vec, V_AG), False)
    n_low = pbuf[8 : 8 + ROWS, :].astype(BF16)
    for part in range(3):
        v = dot(n_low, w_ref[part * CH_MID : (part + 1) * CH_MID, :])
        qkv[:, part * CH_MID : (part + 1) * CH_MID] = v.astype(BF16)
    half = lane_half()

    def heads(img, carry):
        for pair in range(HEADS // 2):
            q, k, v = attention_pair(qkv, img, pair)
            outs = []
            for side in range(2):
                s = dot(keep_half(q, half, side), k, NT) * HEAD_DIM ** (-0.5)
                e = jnp.exp(s - jnp.max(s, 1, keepdims=True))
                prob = (e / jnp.sum(e, 1, keepdims=True)).astype(BF16)
                outs.append(dot(prob, v))
            mixed[pl.ds(pl.multiple_of(img * PIX, PIX), PIX), pair * LINE : (pair + 1) * LINE] = jnp.where(
                half, outs[0], outs[1]
            ).astype(BF16)
        return carry

    lax.fori_loop(0, MB_DEV, heads, 0)
    h3[...] = h2[...] + dot(mixed[...], w_ref[3 * CH_MID : 4 * CH_MID, :]) + vec[V_AB : V_AB + 1, :]

    block(h3, u2, h4, AT.second, V_G2, V_B21, V_B22, 2, (SPAN_ONE2, SPAN_TWO2), None, saved[2:])

    stats = [group_stats(h4, img, gm) for img in range(MB_DEV)]
    norm_to(pbuf, h4, stats, block_scales(vec, V_FG), True)
    z = dot(pbuf[8 : 8 + ROWS, :].astype(BF16), wz[...])
    t_all = dot3(z, sel[...])
    u_all = jnp.zeros((ROWS, LINE), F32)
    for shift in range(9):
        inside, by = upsample_masks(shift)
        moved = t_all if by == 0 else pltpu.roll(t_all, (-by) % ROWS, 0)
        u_all = u_all + jnp.where(inside, moved, 0.0)
    f_out[...] = dot3(u_all, gat[...]) + bz[...]
    free()


def vmem(*shape_dtype):
    return pltpu.VMEM(*shape_dtype)


VM = pl.BlockSpec(memory_space=pltpu.VMEM)
HB = pl.BlockSpec(memory_space=pl.ANY)
SM = pl.BlockSpec(memory_space=pltpu.SMEM)


def state_shapes():
    act = ((ROWS, CH_MID), F32)
    return [
        ((4 * ROWS, 256), BF16),
        act, act, act,
        ((ROWS, 3 * CH_MID), BF16),
        ((ROWS, CH_MID), BF16),
        act, act, act,
        ((VEC_ROWS, CH_MID), F32),
        ((8, EMB_DIM), F32),
        ((8, EMB_DIM), F32),
        ((8, EMB_DIM), F32),
    ]


def weight_shapes():
    sq = ((EMB_DIM, EMB_DIM), BF16)
    conv = ((9 * CH_MID, CH_MID), BF16)
    return [sq, sq, sq, ((9 * CH_BASE, CH_MID), BF16), conv, conv, ((4 * CH_MID, CH_MID), BF16), conv, conv]


def forward_call(save, labels, lines, xp, win, bin_, wz, bz, phi, tables):
    sds = lambda s: jax.ShapeDtypeStruct(*s)
    outs = [sds(((ROWS, LINE), F32))]
    out_specs = [VM]
    state = state_shapes()
    scratch = []
    if save:
        outs += [sds(s) for s in state] + [sds(s) for s in weight_shapes()]
        out_specs += [VM] * len(state) + [HB] * len(weight_shapes())
    else:
        scratch += [vmem(*s) for s in state]
    stage_rows = 10416
    scratch += [
        vmem((stage_rows, LINE), BF16),
        vmem((stage_rows, LINE), F32),
        vmem((9 * CH_MID, CH_MID), BF16),
        vmem((2, EMB_DIM, EMB_DIM), BF16),
        vmem((3, PADDED, CH_MID), BF16),
        vmem((ROWS + 16, CH_MID), F32),
        vmem((ROWS + 32, 256), F32),
        vmem((32 * MB_DEV, LINE), BF16),
        pltpu.SemaphoreType.DMA,
        pltpu.SemaphoreType.DMA,
        pltpu.SemaphoreType.DMA((MB_DEV,)),
    ]

    def body(*refs):
        forward_kernel(save, *refs)

    return pl.pallas_call(
        body,
        out_shape=outs,
        in_specs=[SM, HB] + [VM] * 9,
        out_specs=out_specs,
        scratch_shapes=scratch,
        compiler_params=pltpu.CompilerParams(vmem_limit_bytes=60 * 1024 * 1024),
        cost_estimate=pl.CostEstimate(flops=8 * 10**9, bytes_accessed=4 * 10**7, transcendentals=10**6),
        name="forward_save" if save else "forward_plain",
    )(labels, lines, xp, win, bin_, wz, bz, phi, *tables)


def column_sum(pbuf):
    def body(c, acc):
        return acc + jnp.sum(pbuf[pl.ds(pl.multiple_of(c * CHUNK + 8, 8), CHUNK), :], 0, keepdims=True)

    return lax.fori_loop(0, ROWS // CHUNK, body, jnp.zeros((1, CH_MID), F32))


def refill(pbuf, source):
    for c in range(0, ROWS, CHUNK):
        pbuf[8 + c : 8 + c + CHUNK, :] = source[c : c + CHUNK, :]


def block_back_two(dh, u_ref, at, base, rows, vec, mod, mod_row, weights, tools, g, dm):
    g_row, b1_row, b2_row = rows
    sbuf, pbuf, dx, at_ref, gm = tools
    put_row(g, at.bias_two - base, colsum(dh, 0, ROWS))
    u_stats = [group_stats(u_ref, img, gm) for img in range(MB_DEV)]
    scales = block_scales(vec, g_row + 2, mod, mod_row)
    norm_to(pbuf, u_ref, u_stats, scales, True)
    transpose_to(at_ref, pbuf)
    refill(pbuf, dh)
    shift_to(sbuf, pbuf)
    conv_back(sbuf, at_ref, weights.take(), dx, g, at.conv_two - base)
    weights.begin()

    def emit_inner(r, v):
        pbuf[pl.ds(r + 8, CHUNK), :] = v

    sums = norm_back(u_ref, dx, u_stats, scales, True, gm, emit_inner)
    gain, shift = vec[g_row + 2 : g_row + 3, :], vec[g_row + 3 : g_row + 4, :]
    d_gain = d_shift = 0.0
    dm[...] = jnp.zeros_like(dm)
    for img, (a, b) in enumerate(sums):
        scale = 1.0 + mod[mod_row + img : mod_row + img + 1, :CH_MID]
        d_gain, d_shift = d_gain + scale * b, d_shift + scale * a
        dm[img : img + 1, :CH_MID] = gain * b + shift * a
        dm[img : img + 1, CH_MID:] = a
    return d_gain, d_shift


def block_back_one(dh, x_ref, at, base, rows, vec, weights, tools, g):
    g_row, b1_row, b2_row = rows
    sbuf, pbuf, dx, at_ref, gm = tools
    put_row(g, at.bias_one - base, column_sum(pbuf))
    shift_to(sbuf, pbuf)
    stats = [group_stats(x_ref, img, gm) for img in range(MB_DEV)]
    scales = block_scales(vec, g_row)
    norm_to(pbuf, x_ref, stats, scales, True)
    transpose_to(at_ref, pbuf)
    conv_back(sbuf, at_ref, weights.take(), dx, g, at.conv_one - base)
    weights.begin()

    def emit_outer(r, v):
        dh[pl.ds(r, CHUNK), :] += v

    sums = norm_back(x_ref, dx, stats, scales, True, gm, emit_outer)
    put_row(g, at.gains - base, sums[0][1] + sums[1][1])
    put_row(g, at.gains + 3 - base, sums[0][0] + sums[1][0])


def rowsum(v):
    return jnp.sum(v, 0, keepdims=True)


def put_outer(g, at, left, right):
    for c in range(-(-left.shape[1] // LINE)):
        piece = outer(left[:, c * LINE : (c + 1) * LINE], right)
        put_lines(g, at + c * LINE * (EMB_DIM // LINE), piece, EMB_DIM // LINE)


class Weights:
    def __init__(self, sources, slots, sems):
        self.copies = []
        for n, source in enumerate(sources):
            target = slots.at[n % 2, pl.ds(0, source.shape[0]), :]
            self.copies.append((pltpu.make_async_copy(source, target, sems.at[n % 2]), target))
        self.begun = self.done = 0

    def begin(self):
        if self.begun < len(self.copies):
            self.copies[self.begun][0].start()
            self.begun += 1

    def take(self):
        copy, target = self.copies[self.done]
        copy.wait()
        self.done += 1
        return target


class Leave:
    def __init__(self, me, g, base, keep, send, stage, sems):
        self.core, self.place = lax.rem(me[0], 2), lax.div(me[0], 2)
        self.g, self.base, self.keep, self.send, self.stage, self.sems = g, base, keep, send, stage, sems
        self.copies = []

    def plane(self, plane, slot):
        pairs = PLANE // 2
        for q in range(pairs):
            at = q ^ self.place
            first = (plane * PLANE + 2 * q) * SHARD - self.base
            mine = pl.multiple_of(first + self.core * SHARD, 8)
            other = pl.multiple_of(first + (1 - self.core) * SHARD, 8)
            kept = pltpu.make_async_copy(self.g.at[pl.ds(mine, ROOM), :], self.keep.at[slot, at], self.sems.at[0])
            kept.start()
            stage = self.stage.at[slot * pairs + q]
            block = ROOM // 8

            def body(c, carry):
                stage[pl.ds(pl.multiple_of(c * 288, 16), 288), :] = self.g[
                    pl.ds(pl.multiple_of(other + c * 288, 8), 288), :
                ].astype(BF16)
                return carry

            whole = ROOM // 288
            lax.fori_loop(0, whole, body, 0)
            rest = ROOM - whole * 288
            stage[whole * 288 :, :] = self.g[pl.ds(pl.multiple_of(other + whole * 288, 8), rest), :].astype(BF16)
            sent = pltpu.make_async_copy(stage, self.send.at[slot, at], self.sems.at[1])
            sent.start()
            self.copies += [kept, sent]

    def wait(self):
        for copy in self.copies:
            copy.wait()


def clear_lines(g, first, count):
    if count:
        g[first : first + count, :] = jnp.zeros((count, LINE), F32)


def back_two_kernel(*refs):
    me, df, wz, gm, sel, gat, vec, mod, emb, h4, u2, h3, qkv, mixed, h2, u1, s22, s21, s_attn, s12, s_emb = refs[:21]
    keep, send, rest, dh, du, dm_first, extra, dse, dwz = refs[21:30]
    g, slots, w_sq, sbuf, pbuf, dx, at_ref, dqkv, dm, stage, sems, sq_sem, out_sems = refs[30:]
    weights = Weights([s22, s21, s_attn, s12], slots, sems)
    weights.begin()
    weights.begin()
    sq_copy = pltpu.make_async_copy(s_emb, w_sq, sq_sem)
    sq_copy.start()
    clear_pads(sbuf)
    clear_lines(g, TAIL - SPLIT, g.shape[0] - (TAIL - SPLIT))
    pbuf[0:8, :] = jnp.zeros((8, CH_MID), F32)
    pbuf[ROWS + 8 : ROWS + 16, :] = jnp.zeros((8, CH_MID), F32)
    tools = (sbuf, pbuf, dx, at_ref, gm)

    stats = [group_stats(h4, img, gm) for img in range(MB_DEV)]
    scales = block_scales(vec, V_FG)
    norm_to(pbuf, h4, stats, scales, True)
    transpose_to(at_ref, pbuf)
    spread = dot(df[...].astype(BF16), gat[...], NT)
    dt = jnp.zeros((ROWS, LINE), F32)
    for shift in range(9):
        inside, by = upsample_masks(shift)
        part = jnp.where(inside, spread, 0.0)
        dt = dt + (part if by == 0 else pltpu.roll(part, by % ROWS, 0))
    dz = dot(dt.astype(BF16), sel[...], NT)
    parts = split3(dz)
    dwz[...] = dot(at_ref[...], parts[0]) + dot(at_ref[...], parts[1]) + dot(at_ref[...], parts[2])
    dx[...] = dot(parts[0], wz[...], NT) + dot(parts[1], wz[...], NT) + dot(parts[2], wz[...], NT)

    def emit_first(r, v):
        dh[pl.ds(r, CHUNK), :] = v

    sums = norm_back(h4, dx, stats, scales, True, gm, emit_first)
    put_row(g, AT.final_gains - SPLIT, sums[0][1] + sums[1][1])
    put_row(g, AT.final_gains + 3 - SPLIT, sums[0][0] + sums[1][0])

    rows = (V_G2, V_B21, V_B22)
    d_gain, d_shift = block_back_two(dh, u2, AT.second, SPLIT, rows, vec, mod, 2, weights, tools, g, dm)
    put_row(g, AT.second.gains + 6 - SPLIT, d_gain)
    put_row(g, AT.second.gains + 9 - SPLIT, d_shift)
    block_back_one(dh, h3, AT.second, SPLIT, rows, vec, weights, tools, g)
    se = silu(emb[...])
    put_outer(g, AT.second.embed - SPLIT, se, dm[...])
    put_row(g, AT.second.embed_bias - SPLIT, rowsum(dm[...]))
    sq_copy.wait()
    dse[...] = dot3(dm[...], w_sq[...], NT)

    put_row(g, AT.attn_bias - SPLIT, colsum(dh, 0, ROWS))
    w = weights.take()
    d_low = dh[...].astype(BF16)
    for c in range(ROWS // LINE):
        at_ref[:, c * LINE : (c + 1) * LINE] = mixed[c * LINE : (c + 1) * LINE, :].astype(F32).T.astype(BF16)
    put_lines(g, AT.attn_out - SPLIT, dot(at_ref[...], d_low), 3)
    pbuf[8 : 8 + ROWS, :] = dot(d_low, w[3 * CH_MID : 4 * CH_MID, :], NT)
    half = lane_half()
    scale = HEAD_DIM ** (-0.5)

    def heads(img, carry):
        rows = pl.ds(pl.multiple_of(img * PIX, PIX), PIX)
        for pair in range(HEADS // 2):
            q, k, v = attention_pair(qkv, img, pair)
            cols = slice(pair * LINE, (pair + 1) * LINE)
            do = pbuf[pl.ds(pl.multiple_of(img * PIX + 8, 8), PIX), cols].astype(BF16)
            dqs, dks, dvs = [], [], []
            for side in range(2):
                s = dot(keep_half(k, half, side), q, NT) * scale
                e = jnp.exp(s - jnp.max(s, 0, keepdims=True))
                prob = e / jnp.sum(e, 0, keepdims=True)
                dvs.append(dot(prob.astype(BF16), do))
                dp = dot(keep_half(v, half, side), do, NT)
                ds = prob * (dp - jnp.sum(dp * prob, 0, keepdims=True))
                dks.append(dot(ds.astype(BF16), q))
                dqs.append(dot(ds.T.astype(BF16), k))
            for part, pieces in enumerate((dqs, dks, dvs)):
                value = jnp.where(half, pieces[0], pieces[1])
                if part < 2:
                    value = value * scale
                dqkv[rows, part * CH_MID + pair * LINE : part * CH_MID + (pair + 1) * LINE] = value.astype(BF16)
        return carry

    lax.fori_loop(0, MB_DEV, heads, 0)
    stats = [group_stats(h2, img, gm) for img in range(MB_DEV)]
    scales = block_scales(vec, V_AG)
    norm_to(pbuf, h2, stats, scales, False)
    transpose_to(at_ref, pbuf)
    dx[...] = jnp.zeros_like(dx)
    for part in range(3):
        d = dqkv[:, part * CH_MID : (part + 1) * CH_MID]
        dw = dot(at_ref[...], d)
        for j in range(3):
            g[pl.ds(AT.attn_qkv - SPLIT + part * 3 + j, CH_MID, stride=9), :] = dw[:, j * LINE : (j + 1) * LINE]
        dx[...] += dot(d, w[part * CH_MID : (part + 1) * CH_MID, :], NT)
    weights.begin()

    def emit(r, v):
        dh[pl.ds(r, CHUNK), :] += v

    sums = norm_back(h2, dx, stats, scales, False, gm, emit)
    put_row(g, AT.attn_gains - SPLIT, sums[0][1] + sums[1][1])
    put_row(g, AT.attn_gains + 3 - SPLIT, sums[0][0] + sums[1][0])

    leave = Leave(me, g, SPLIT, keep, send, stage, out_sems)
    leave.plane(3, 1)
    rows = (V_G1, V_B11, V_B12)
    d_gain, d_shift = block_back_two(dh, u1, AT.first, SPLIT, rows, vec, mod, 0, weights, tools, g, dm_first)
    extra[...] = jnp.zeros_like(extra)
    extra[0:1, :] = d_gain
    extra[1:2, :] = d_shift
    for c in range(0, ROWS, CHUNK):
        du[c : c + CHUNK, :] = pbuf[8 + c : 8 + c + CHUNK, :]
    leave.plane(2, 0)
    below = pltpu.make_async_copy(g.at[pl.ds(0, MIDDLE - SPLIT), :], rest, out_sems.at[2])
    below.start()
    below.wait()
    leave.wait()


def back_one_kernel(*refs):
    (me, labels, dh_in, du, dm, extra, dse_in, gm, vec, emb, pre, phi, h1, h0s, xpt) = refs[:15]
    s11, s_down, s_emb, s_time, rest = refs[15:20]
    keep, send, dwin, dbin = refs[20:24]
    g, slots, w_sq, sbuf, pbuf, dx, at_ref, dh, h0t, demb_ref, stage, sems, sq_sem, out_sems = refs[24:]
    above = pltpu.make_async_copy(rest, g.at[pl.ds(SPLIT, MIDDLE - SPLIT), :], out_sems.at[2])
    above.start()
    weights = Weights([s11, s_down], slots, sems)
    weights.begin()
    weights.begin()
    sq_copies = [pltpu.make_async_copy(s, w_sq.at[n], sq_sem.at[n]) for n, s in enumerate((s_emb, s_time))]
    for copy in sq_copies:
        copy.start()
    clear_pads(sbuf)
    clear_lines(g, 0, AT.conv_down)
    clear_lines(g, MIDDLE, g.shape[0] - MIDDLE)
    pbuf[0:8, :] = jnp.zeros((8, CH_MID), F32)
    pbuf[ROWS + 8 : ROWS + 16, :] = jnp.zeros((8, CH_MID), F32)
    refill(pbuf, du)
    for c in range(0, ROWS, CHUNK):
        dh[c : c + CHUNK, :] = dh_in[c : c + CHUNK, :]
    above.wait()
    tools = (sbuf, pbuf, dx, at_ref, gm)
    block_back_one(dh, h1, AT.first, 0, (V_G1, V_B11, V_B12), vec, weights, tools, g)
    put_row(g, AT.first.gains + 6, extra[0:1, :])
    put_row(g, AT.first.gains + 9, extra[1:2, :])
    se = silu(emb[...])
    put_outer(g, AT.first.embed, se, dm[...])
    put_row(g, AT.first.embed_bias, rowsum(dm[...]))
    leave = Leave(me, g, 0, keep, send, stage, out_sems)
    for copy in sq_copies:
        copy.wait()
    demb = (dse_in[...] + dot3(dm[...], w_sq[0], NT)) * silu_slope(emb[...])
    put_row(g, AT.time_bias_two, rowsum(demb))
    put_outer(g, AT.time_two, silu(pre[...]), demb)
    dpre = dot3(demb, w_sq[1], NT) * silu_slope(pre[...])
    put_row(g, AT.time_bias_one, rowsum(dpre))
    put_outer(g, AT.time_one, phi[...], dpre)
    clear = 240
    first, lines = AT.class_table, CLASSES * (EMB_DIM // LINE)

    def wipe(c, carry):
        g[pl.ds(first + c * clear, clear), :] = jnp.zeros((clear, LINE), F32)
        return carry

    lax.fori_loop(0, lines // clear, wipe, 0)
    demb_ref[...] = demb
    for n in range(MB_DEV):
        for j in range(EMB_DIM // LINE):
            at = first + labels[n] * (EMB_DIM // LINE) + j
            g[pl.ds(at, 1), :] += demb_ref[n : n + 1, j * LINE : (j + 1) * LINE]
    leave.plane(1, 1)

    put_row(g, AT.bias_down, colsum(dh, 0, ROWS))
    refill(pbuf, dh)
    shift_to(sbuf, pbuf)
    w = weights.take()
    dwin[...] = jnp.zeros_like(dwin)
    dbin[...] = jnp.zeros_like(dbin)
    for ph in range(4):
        for c in range(ROWS // LINE):
            rows = slice(ph * ROWS + c * LINE, ph * ROWS + (c + 1) * LINE)
            h0t[:, c * LINE : (c + 1) * LINE] = h0s[rows, :].astype(F32).T.astype(BF16)
        d0 = jnp.zeros((ROWS, CH_BASE), F32)
        for ky in ((0, 2) if ph // 2 else (1,)):
            for kx in ((0, 2) if ph % 2 else (1,)):
                d = shifted(sbuf, 2 if kx == 0 else 1, 32 if ky == 0 else 16)
                t = 3 * ky + kx
                d0 = d0 + dot(d, w[t * CH_BASE : (t + 1) * CH_BASE, :], NT)
                put_lines(g, AT.conv_down + t * CH_BASE * 3, dot(h0t[0:CH_BASE, :], d), 3)
        dbin[:, :CH_BASE] += rowsum(d0)
        dwin[:, :CH_BASE] += dot(xpt[:, ph * ROWS : (ph + 1) * ROWS], d0.astype(BF16))
    leave.plane(0, 0)
    leave.wait()


def kernel_params():
    return dict(
        compiler_params=pltpu.CompilerParams(vmem_limit_bytes=60 * 1024 * 1024),
        cost_estimate=pl.CostEstimate(flops=8 * 10**9, bytes_accessed=4 * 10**7, transcendentals=10**6),
    )


def back_scratch(lines):
    return [
        vmem((lines + 8, LINE), F32),
        vmem((2, 9 * CH_MID, CH_MID), BF16),
        vmem((2, EMB_DIM, EMB_DIM), BF16),
        vmem((3, PADDED, CH_MID), BF16),
        vmem((ROWS + 16, CH_MID), F32),
        vmem((ROWS, CH_MID), F32),
        vmem((CH_MID, ROWS), BF16),
    ]


def plane_shapes():
    pairs = PLANE // 2
    return [
        jax.ShapeDtypeStruct((2, pairs, ROOM, LINE), F32),
        jax.ShapeDtypeStruct((2, pairs, ROOM, LINE), BF16),
    ]


def back_two_call(args):
    sds = lambda *s: jax.ShapeDtypeStruct(*s)
    act = sds((ROWS, CH_MID), F32)
    scratch = back_scratch(ALL_LINES - SPLIT)
    scratch[2] = vmem((EMB_DIM, EMB_DIM), BF16)
    return pl.pallas_call(
        back_two_kernel,
        out_shape=plane_shapes()
        + [
            sds((MIDDLE - SPLIT, LINE), F32),
            act,
            act,
            sds((8, EMB_DIM), F32),
            sds((8, CH_MID), F32),
            sds((8, EMB_DIM), F32),
            sds((CH_MID, LINE), F32),
        ],
        in_specs=[SM] + [VM] * 15 + [HB] * 5,
        out_specs=[HB] * 3 + [VM] * 6,
        scratch_shapes=scratch
        + [
            vmem((ROWS, 3 * CH_MID), BF16),
            vmem((8, EMB_DIM), F32),
            vmem((PLANE, ROOM, LINE), BF16),
            pltpu.SemaphoreType.DMA((2,)),
            pltpu.SemaphoreType.DMA,
            pltpu.SemaphoreType.DMA((3,)),
        ],
        name="back_two",
        **kernel_params(),
    )(*args)


def back_one_call(args):
    sds = lambda *s: jax.ShapeDtypeStruct(*s)
    return pl.pallas_call(
        back_one_kernel,
        out_shape=plane_shapes() + [sds((32, 256), F32), sds((1, 256), F32)],
        in_specs=[SM] * 2 + [VM] * 13 + [HB] * 5,
        out_specs=[HB] * 2 + [VM] * 2,
        scratch_shapes=back_scratch(MIDDLE)
        + [
            vmem((ROWS, CH_MID), F32),
            vmem((256, ROWS), BF16),
            vmem((8, EMB_DIM), F32),
            vmem((PLANE, ROOM, LINE), BF16),
            pltpu.SemaphoreType.DMA((2,)),
            pltpu.SemaphoreType.DMA((2,)),
            pltpu.SemaphoreType.DMA((3,)),
        ],
        name="back_one",
        **kernel_params(),
    )(*args)


def karras(index):
    ramp_frac = index.astype(F32) / (DISCRETE - 1)
    low_root = SIGMA_LOW ** (1.0 / RHO_POWER)
    high_root = SIGMA_HIGH ** (1.0 / RHO_POWER)
    return (low_root + ramp_frac * (high_root - low_root)) ** RHO_POWER


def preconditioning_factors(sigma):
    variance_sum = sigma * sigma + SIGMA_DATA**2
    skip = SIGMA_DATA**2 / ((sigma - SIGMA_LOW) ** 2 + SIGMA_DATA**2)
    out = (sigma - SIGMA_LOW) * SIGMA_DATA * lax.rsqrt(variance_sum)
    return (skip, out, lax.rsqrt(variance_sum))


def noise_features(sigma):
    half_width = CH_BASE // 2
    frequency = jnp.exp(-math.log(10000.0) * jnp.arange(half_width, dtype=F32) / half_width)
    phases = 250.0 * jnp.log(sigma)[:, None] * frequency
    return jnp.pad(jnp.concatenate([jnp.cos(phases), jnp.sin(phases)], 1), ((0, 8 - MB_DEV), (0, 0)))


def by_parity(image):
    channels = image.shape[-1]
    split = image.reshape(MB_DEV, HALF, 2, HALF, 2, channels)
    return split.transpose(2, 4, 0, 1, 3, 5).reshape(4, ROWS, channels)


def pixels(image):
    return by_parity(image).transpose(1, 0, 2).reshape(ROWS, 12)


def input_patches(noisy, scale):
    low = (scale[:, None, None, None] * noisy).astype(BF16)
    padded = jnp.pad(low, ((0, 0), (1, 1), (1, 1), (0, 0)))
    taps = [padded[:, t // 3 : t // 3 + RES, t % 3 : t % 3 + RES] for t in range(9)]
    flat = by_parity(jnp.concatenate(taps, 3)).reshape(4 * ROWS, 27)
    return jnp.pad(flat, ((0, 0), (0, 5)))


def small_weights(lines):
    front = lines[: AT.conv_down].reshape(-1)
    size = 27 * CH_BASE
    win = jnp.pad(front[:size].reshape(27, CH_BASE), ((0, 5), (0, 64)))
    bin_ = jnp.pad(front[size : size + CH_BASE].astype(F32)[None], ((0, 0), (0, 64)))
    tail = lines[TAIL:].reshape(-1)
    size = 27 * CH_MID
    wz = tail[:size].reshape(9, CH_MID, 3).transpose(1, 0, 2).reshape(CH_MID, 27)
    bz = jnp.tile(tail[size : size + 3].astype(F32), 4)
    return win, bin_, jnp.pad(wz, ((0, 0), (0, LINE - 27))), jnp.pad(bz, (0, LINE - 12))[None]


def per_part(labels, lines, noisy, sigma, save, tables):
    skip, out_scale, in_scale = preconditioning_factors(sigma)
    xp = input_patches(noisy, in_scale)
    phi = noise_features(sigma)
    win, bin_, wz, bz = small_weights(lines)
    results = forward_call(save, labels, lines, xp, win, bin_, wz, bz, phi, tables)
    model = results[0][:, :12]
    per_row = lambda v: jnp.repeat(v, PIX)[:, None]
    denoised = per_row(skip) * pixels(noisy) + per_row(out_scale) * model
    return denoised, (xp, phi, wz, out_scale, results[1:])


AXIS = "fsdp"
CORE, EAST, SOUTH, UP = 1, 2, 4, 8
CUT_ROWS = ROOM // 2


def swap(values, hop):
    return lax.ppermute(values, AXIS, [(i, i ^ hop) for i in range(SHARDS)])


def total_of(values, n):
    hop = 1
    while hop < n:
        values = values + lax.ppermute(values, AXIS, [(i, i ^ hop) for i in range(n)])
        hop *= 2
    return values


def reduce_planes(keep, send):
    planes = keep.shape[0]
    got = swap(send, CORE)
    low = lambda v: v.astype(BF16)
    wide = lambda v: v.astype(F32)
    a, b = slice(0, CUT_ROWS), slice(CUT_ROWS, ROOM)
    quarter = lambda i, rows: keep[:, i, rows] + wide(got[:, i, rows])
    send_a = low(jnp.stack([quarter(1, a), quarter(3, a)], 1))
    send_b = low(jnp.stack([quarter(2, b), quarter(3, b)], 1))
    got_a, got_b = swap(send_a, EAST), swap(send_b, SOUTH)
    last_a = low(quarter(2, a) + wide(got_a[:, 1]))
    last_b = low(quarter(1, b) + wide(got_b[:, 1]))
    end_a, end_b = swap(last_a, SOUTH), swap(last_b, EAST)
    sum_a = quarter(0, a) + wide(got_a[:, 0]) + wide(end_a)
    sum_b = quarter(0, b) + wide(got_b[:, 0]) + wide(end_b)
    return jnp.concatenate([sum_a, sum_b], 1)


def reduce_column(part, z):
    planes = part.shape[0]
    pick = lambda p: lax.dynamic_index_in_dim(part, jnp.clip(p, 0, planes - 1), 0, keepdims=False)
    total = pick(z)
    for way in (1, -1):
        run = None
        for far in range(planes - 1, 0, -1):
            value = pick(z + way * far)
            if run is not None:
                value = value + run
            holders = [q for q in range(planes) if 0 <= q + way * far < planes]
            pairs = [(q * PLANE + i, (q + way) * PLANE + i) for q in holders for i in range(PLANE)]
            run = lax.ppermute(value.astype(BF16), AXIS, pairs).astype(F32)
        total = total + run
    return total


def per_device(n, images, noise_draws, labels, step_index, valid_rows, counts, master, momentum, ema):
    direct = n == SHARDS
    index = lax.axis_index(AXIS)
    me = jnp.where(direct, lax.rem(index, PLANE), 0).astype(jnp.int32)[None]
    gather = lambda v: lax.all_gather(v.astype(BF16).reshape(-1, LINE), AXIS, axis=0, tiled=True)
    online, target = gather(master), gather(ema)
    select, collect = spread_tables()
    tables = (jnp.asarray(group_table(), BF16), jnp.asarray(select, BF16), jnp.asarray(collect, BF16))
    slot_live = (jnp.arange(MB_DEV) < counts[0]).astype(F32)
    row_live = (jnp.arange(RES)[None, :] < valid_rows[:, None]).astype(F32)
    pixel_mask = slot_live[:, None] * row_live
    pixel_total = 3.0 * RES * total_of(jnp.sum(pixel_mask), n)
    mask = pixels(jnp.broadcast_to(pixel_mask[:, :, None, None], images.shape))
    sigma_lo, sigma_hi = karras(step_index), karras(step_index + 1)
    add_noise = lambda sigma: images + sigma[:, None, None, None] * noise_draws
    online_out, (xp, phi, wz, out_scale, saved) = per_part(labels, online, add_noise(sigma_hi), sigma_hi, True, tables)
    target_out, _ = per_part(labels, target, add_noise(sigma_lo), sigma_lo, False, tables)
    gap = online_out - target_out
    local_loss = jnp.sum(mask * jnp.square(gap))
    grad_model = jnp.repeat(out_scale, PIX)[:, None] * 2.0 * mask * gap / pixel_total
    bias_out = jnp.sum(grad_model.reshape(ROWS, 4, 3), axis=(0, 1))
    (h0s, h1, u1, h2, qkv, mixed, h3, u2, h4, vec, mod, emb, pre) = saved[:13]
    s_time, s_emb1, s_emb2, s_down, s11, s12, s_attn, s21, s22 = saved[13:]
    gm, sel, gat = tables
    df = jnp.pad(grad_model, ((0, 0), (0, LINE - 12)))
    keep_top, send_top, rest, dh, du, dm, extra, dse, dwz = back_two_call(
        (me, df, wz, gm, sel, gat, vec, mod, emb, h4, u2, h3, qkv, mixed, h2, u1, s22, s21, s_attn, s12, s_emb2)
    )
    keep_low, send_low, dwin, dbin = back_one_call(
        (me, labels, dh, du, dm, extra, dse, gm, vec, emb, pre, phi, h1, h0s, xp.T, s11, s_down, s_emb1, s_time, rest)
    )
    tail = dwz[:, :27].reshape(CH_MID, 9, 3).transpose(1, 0, 2).reshape(-1)
    small = jnp.concatenate([dwin[:27, :CH_BASE].reshape(-1), dbin[0, :CH_BASE], tail, bias_out, local_loss[None]])
    front_size, tail_size = AT.conv_down * LINE, tail.shape[0] + 3
    small = jnp.pad(small, (0, LINE * LINE - small.shape[0])).reshape(LINE, LINE)
    small = total_of(small, n).reshape(-1)
    if direct:
        part = jnp.concatenate([reduce_planes(keep_low, send_low), reduce_planes(keep_top, send_top)])
        reduced = reduce_column(part, lax.div(index, PLANE))[:SHARD].reshape(-1)
    else:
        both = [jnp.stack([k, s.astype(F32)], 2) for k, s in ((keep_low, send_low), (keep_top, send_top))]
        lines = jnp.concatenate(both).reshape(SHARDS, ROOM, LINE)[:, :SHARD].reshape(n, -1)
        reduced = lax.psum_scatter(lines, AXIS, scatter_dimension=0, tiled=True).reshape(-1)
    size = master.shape[0]
    start = TAIL * LINE - (n - 1) * size
    first = jnp.where(index == 0, small[:front_size], 0.0)
    last = jnp.where(index == n - 1, small[front_size : front_size + tail_size], 0.0)
    reduced = reduced + jnp.pad(first, (0, size - front_size)) + jnp.pad(last, (start, size - start - tail_size))
    new_momentum = MOMENTUM * momentum + reduced
    new_master = master - LEARN_RATE * (reduced + MOMENTUM * new_momentum)
    new_ema = EMA_DECAY * ema + (1.0 - EMA_DECAY) * new_master
    end = front_size + tail_size
    return (small[end] / pixel_total, new_momentum, new_master, new_ema, small[end - 3 : end])


def solution(mesh):
    n = mesh.shape[AXIS]

    def step(*args):
        return per_device(n, *args)

    return jax.shard_map(
        step,
        mesh=mesh,
        in_specs=(P(AXIS, None, None, None),) * 2 + (P(AXIS),) * 7,
        out_specs=(P(), P(AXIS), P(AXIS), P(AXIS), P()),
        check_vma=False,
    )
```

```python
import math

import jax
import jax.numpy as jnp
import numpy as np
from jax import lax
from jax.experimental import pallas as pl
from jax.experimental.pallas import tpu as pltpu
from jax.sharding import PartitionSpec as P

CH_BASE = 192
CH_MID = 384
EMB_DIM = 768
HEADS = 6
HEAD_DIM = 64
CLASSES = 1000
GROUPS = 32
RES = 32
MB_DEV = 2
DISCRETE = 40

EPSILON = 1e-05
SIGMA_DATA = 0.5
SIGMA_LOW = 0.002
SIGMA_HIGH = 80.0
RHO_POWER = 7.0
MOMENTUM = 0.9
EMA_DECAY = 0.9
LEARN_RATE = 2000.0

F32 = jnp.float32
BF16 = jnp.bfloat16
LINE = 128
HALF = RES // 2
PIX = HALF * HALF
ROWS = MB_DEV * PIX
GROUP_SIZE = PIX * (CH_MID // GROUPS)
CHUNK = 64
PADDED = 16 + MB_DEV * (PIX + 16)
NN = (((1,), (0,)), ((), ()))
NT = (((1,), (1,)), ((), ()))
TN = (((0,), (0,)), ((), ()))


class Place:
    pass


class Cut:
    def __init__(self):
        self.offset = 0

    def take(self, *shape):
        at = self.offset
        self.offset += math.prod(shape)
        return at // LINE


def block_place(cut):
    at = Place()
    at.gains = cut.take(4, CH_MID)
    at.conv_one = cut.take(9 * CH_MID, CH_MID)
    at.bias_one = cut.take(CH_MID)
    at.embed = cut.take(EMB_DIM, 2 * CH_MID)
    at.embed_bias = cut.take(2 * CH_MID)
    at.conv_two = cut.take(9 * CH_MID, CH_MID)
    at.bias_two = cut.take(CH_MID)
    return at


def places():
    cut, at = Cut(), Place()
    at.conv_in = cut.take(27, CH_BASE)
    at.bias_in = cut.take(CH_BASE)
    at.conv_down = cut.take(9 * CH_BASE, CH_MID)
    at.bias_down = cut.take(CH_MID)
    at.time_one = cut.take(CH_BASE, EMB_DIM)
    at.time_bias_one = cut.take(EMB_DIM)
    at.time_two = cut.take(EMB_DIM, EMB_DIM)
    at.time_bias_two = cut.take(EMB_DIM)
    at.class_table = cut.take(CLASSES, EMB_DIM)
    at.first = block_place(cut)
    at.second = block_place(cut)
    at.attn_gains = cut.take(2, CH_MID)
    at.attn_qkv = cut.take(CH_MID, 3 * CH_MID)
    at.attn_out = cut.take(CH_MID, CH_MID)
    at.attn_bias = cut.take(CH_MID)
    at.final_gains = cut.take(2, CH_MID)
    at.conv_out = cut.take(9 * CH_MID, 3)
    at.bias_out = cut.take(3)
    return at


AT = places()
TAIL = AT.conv_out
SHARDS, PLANE = 32, 8
SHARD = 2264
ROOM = 2272
ALL_LINES = SHARDS * SHARD
MIDDLE = ALL_LINES // 2
SPLIT = AT.first.conv_two // 16 * 16

V_DOWN, V_G1, V_B11, V_B12, V_AG, V_AB, V_FG, V_G2, V_B21, V_B22 = 0, 1, 5, 6, 7, 9, 10, 12, 16, 17
VEC_ROWS = 24


def group_table():
    at = np.arange(CH_MID) // (CH_MID // GROUPS)
    return (at[:, None] == at[None, :]).astype(np.float32)


TAPS = 16


def spread_tables():
    select = np.zeros((LINE, LINE), np.float32)
    gather = np.zeros((LINE, LINE), np.float32)
    tile = np.zeros((LINE, LINE), np.float32)
    for ky in range(3):
        for kx in range(3):
            for a in range(2):
                for b in range(2):
                    dy, dx = (a + ky - 1) // 2, (b + kx - 1) // 2
                    shift = (dy + 1) * 3 + dx + 1
                    for c in range(3):
                        out = (a * 2 + b) * 3 + c
                        select[c * TAPS + ky * 3 + kx, shift * 12 + out] = 1.0
                        gather[out::12, out][:9] = 1.0
                        tile[c, out] = 1.0
    return select, gather, tile


def patch_table():
    pick = np.zeros((4, LINE, 32), np.float32)
    for a in range(2):
        for b in range(2):
            for ky in range(3):
                for kx in range(3):
                    (dy, ya), (dx, xb) = divmod(a + ky - 1, 2), divmod(b + kx - 1, 2)
                    shift = (dy + 1) * 3 + dx + 1
                    for c in range(3):
                        k = (ky * 3 + kx) * 3 + c
                        pick[a * 2 + b, shift * 12 + (ya * 2 + xb) * 3 + c, k // 2 + 16 * (k % 2)] = 1.0
    return pick


def expand_table():
    return (np.arange(3 * CH_MID)[None, :] // 3 == np.arange(CH_MID)[:, None]).astype(np.float32)


def colour(c):
    lane = lax.broadcasted_iota(jnp.int32, (1, 3 * CH_MID), 1)
    return lax.rem(lane, 3) == c


def first_lanes():
    return lax.broadcasted_iota(jnp.int32, (1, LINE), 1) < LINE // 2


def split3(v):
    hi = v.astype(BF16)
    rest = v - hi.astype(F32)
    mid = rest.astype(BF16)
    low = (rest - mid.astype(F32)).astype(BF16)
    return hi, mid, low


def dot(a, b, dims=NN):
    return lax.dot_general(a, b, dims, preferred_element_type=F32)


def dot3(a, b, dims=NN):
    rows = a.shape[0]
    hi, mid, low = split3(a)
    if rows % 16:
        out = dot(jnp.concatenate([p.astype(F32) for p in (hi, mid, low)], 0).astype(BF16), b, dims)
    else:
        out = dot(jnp.concatenate([hi, mid, low], 0), b, dims)
    return out[:rows] + out[rows : 2 * rows] + out[2 * rows :]


def outer(a, b):
    pa, pb = split3(a), split3(b)
    pairs = [(0, 0), (0, 1), (1, 0), (1, 1), (0, 2), (2, 0)]
    left = jnp.concatenate([pa[i].astype(F32) for i, _ in pairs], 0).astype(BF16)
    right = jnp.concatenate([pb[j].astype(F32) for _, j in pairs], 0).astype(BF16)
    return dot(left, right, TN)


def sigmoid(z):
    return 1.0 / (1.0 + jnp.exp(-z))


def silu(z):
    return z * sigmoid(z)


def silu_slope(z):
    s = sigmoid(z)
    return s * (1.0 + z * (1.0 - s))


def colsum(ref, base, count=PIX):
    def body(c, acc):
        return acc + jnp.sum(ref[pl.ds(pl.multiple_of(base + c * CHUNK, 8), CHUNK), :], 0, keepdims=True)

    return lax.fori_loop(0, count // CHUNK, body, jnp.zeros((1, ref.shape[1]), F32))


def eight(v):
    return jnp.broadcast_to(v, (8, v.shape[1]))


def group_mean(v, gm_ref):
    return dot3(eight(v), gm_ref[...])[:1] * (1.0 / GROUP_SIZE)


def group_stats(x_ref, img, gm_ref):
    mean = group_mean(colsum(x_ref, img * PIX), gm_ref)

    def body(c, acc):
        gap = x_ref[pl.ds(pl.multiple_of(img * PIX + c * CHUNK, 8), CHUNK), :] - mean
        return acc + jnp.sum(gap * gap, 0, keepdims=True)

    square = lax.fori_loop(0, PIX // CHUNK, body, jnp.zeros((1, CH_MID), F32))
    return mean, lax.rsqrt(group_mean(square, gm_ref) + EPSILON)


def norm_to(pbuf, x_ref, stats, scales, act):
    for img in range(MB_DEV):
        (mean, rstd), (k, o) = stats[img], scales[img]

        def body(c, carry):
            r = pl.multiple_of(img * PIX + c * CHUNK, 8)
            z = (x_ref[pl.ds(r, CHUNK), :] - mean) * rstd * k + o
            pbuf[pl.ds(r + 8, CHUNK), :] = silu(z) if act else z
            return carry

        lax.fori_loop(0, PIX // CHUNK, body, 0)


def norm_back(x_ref, d_ref, stats, scales, act, gm_ref, emit):
    sums = []
    for img in range(MB_DEV):
        (mean, rstd), (k, o) = stats[img], scales[img]

        def one(c, carry):
            r = pl.multiple_of(img * PIX + c * CHUNK, 8)
            xhat = (x_ref[pl.ds(r, CHUNK), :] - mean) * rstd
            dz = d_ref[pl.ds(r, CHUNK), :]
            if act:
                dz = dz * silu_slope(xhat * k + o)
                d_ref[pl.ds(r, CHUNK), :] = dz
            return (carry[0] + jnp.sum(dz, 0, keepdims=True), carry[1] + jnp.sum(dz * xhat, 0, keepdims=True))

        zero = jnp.zeros((1, CH_MID), F32)
        a, b = lax.fori_loop(0, PIX // CHUNK, one, (zero, zero))
        m1, m2 = group_mean(a * k, gm_ref), group_mean(b * k, gm_ref)

        def two(c, carry):
            r = pl.multiple_of(img * PIX + c * CHUNK, 8)
            xhat = (x_ref[pl.ds(r, CHUNK), :] - mean) * rstd
            emit(r, rstd * (d_ref[pl.ds(r, CHUNK), :] * k - m1 - xhat * m2))
            return carry

        lax.fori_loop(0, PIX // CHUNK, two, 0)
        sums.append((a, b))
    return sums


def clear_pads(sbuf):
    for k in range(3):
        for r in range(0, PADDED, PIX + 16):
            sbuf[k, pl.ds(r, 16), :] = jnp.zeros((16, sbuf.shape[2]), BF16)


def shift_to(sbuf, pbuf):
    column = lax.rem(lax.broadcasted_iota(jnp.int32, (CHUNK, CH_MID), 0), HALF)
    for r in range(0, ROWS, CHUNK):
        for k in range(3):
            v = pbuf[r + 7 + k : r + 7 + k + CHUNK, :]
            if k == 0:
                v = jnp.where(column == 0, 0.0, v)
            if k == 2:
                v = jnp.where(column == HALF - 1, 0.0, v)
            start = r + 16 * (r // PIX + 1)
            sbuf[k, start : start + CHUNK, :] = v.astype(BF16)


def shifted(sbuf, k, row):
    first = sbuf[k, pl.ds(pl.multiple_of(row, 16), PIX), :]
    second = sbuf[k, pl.ds(pl.multiple_of(row + PIX + 16, 16), PIX), :]
    return jnp.concatenate([first, second], 0)


def conv_forward(sbuf, w_ref, out_ref):
    def body(t, carry):
        lhs = shifted(sbuf, lax.rem(t, 3), lax.div(t, 3) * 16)
        out_ref[...] += dot(lhs, w_ref[pl.ds(pl.multiple_of(t * CH_MID, CH_MID), CH_MID), :])
        return carry

    lax.fori_loop(0, 9, body, 0)


def put_lines(g_ref, at, value, step, more=None):
    n = value.shape[0]
    low = at // 8 * 8
    start = low if more is None else pl.multiple_of(low + more, 8)
    view = g_ref.at[pl.ds(start, min(n * step + 8, g_ref.shape[0] - low)), :] if more is None else g_ref.at[pl.ds(start, n * step + 8), :]
    for j in range(step):
        view[pl.ds(at - low + j, n, stride=step), :] = value[:, j * LINE : (j + 1) * LINE]


def put_row(g_ref, at, row):
    for j in range(row.shape[1] // LINE):
        g_ref[pl.ds(at + j, 1), :] = row[:, j * LINE : (j + 1) * LINE]


def conv_back(sbuf, at_ref, w_ref, dx_ref, g_ref, at):
    dx_ref[...] = jnp.zeros_like(dx_ref)

    def body(s, carry):
        t = 8 - s
        d = shifted(sbuf, lax.rem(s, 3), lax.div(s, 3) * 16)
        w = w_ref[pl.ds(pl.multiple_of(t * CH_MID, CH_MID), CH_MID), :]
        dx_ref[...] += dot(d, w, NT)
        put_lines(g_ref, at, dot(at_ref[...], d), 3, t * (3 * CH_MID))
        return carry

    lax.fori_loop(0, 9, body, 0)


def transpose_to(at_ref, pbuf):
    for c in range(ROWS // LINE):
        at_ref[:, c * LINE : (c + 1) * LINE] = pbuf[8 + c * LINE : 8 + (c + 1) * LINE, :].T.astype(BF16)


class Lines:
    def __init__(self, held, wide):
        self.held, self.wide = held, wide

    def take(self, span):
        l0, l1 = span
        first = l0 // SHARD
        self.low = first * SHARD + (l0 - first * SHARD) // 16 * 16
        for s in range(first, (l1 - 1) // SHARD + 1):
            start = max(l0 - s * SHARD, 0) // 16 * 16
            count = -(-min(l1 - s * SHARD, SHARD) // 16) * 16 - start
            to = s * SHARD + start - self.low
            block = self.held.at[s // PLANE, s % PLANE]
            whole, rest = divmod(count, 256)

            def body(c, carry):
                self.wide[pl.ds(pl.multiple_of(to + c * 256, 8), 256), :] = block[
                    pl.ds(pl.multiple_of(start + c * 256, 16), 256), :
                ].astype(F32)
                return carry

            lax.fori_loop(0, whole, body, 0)
            if rest:
                done = whole * 256
                self.wide[to + done : to + count, :] = block[start + done : start + count, :].astype(F32)

    def line(self, at, scratch):
        shard = lax.div(at, SHARD)
        row = at - shard * SHARD
        low = pl.multiple_of(lax.div(row, 16) * 16, 16)
        scratch[...] = self.held[lax.div(shard, PLANE), lax.rem(shard, PLANE), pl.ds(low, 16), :].astype(F32)
        return scratch[pl.ds(row - low, 1), :]

    def matrix(self, w_ref, at, rows, step):
        block = 128 if rows % 192 else 192
        base = at - self.low
        low = base // 8 * 8

        def body(c, carry):
            r = pl.multiple_of(c * block, block)
            view = self.wide.at[pl.ds(pl.multiple_of(low + r * step, 8), block * step + 8), :]
            for j in range(step):
                v = view[pl.ds(base - low + j, block, stride=step), :]
                w_ref[pl.ds(r, block), j * LINE : (j + 1) * LINE] = v.astype(BF16)
            return carry

        lax.fori_loop(0, rows // block, body, 0)

    def row(self, at, step):
        base = at - self.low
        return jnp.concatenate([self.wide[pl.ds(base + j, 1), :] for j in range(step)], 1)


def attention_pair(qkv_ref, img, pair):
    rows = pl.ds(pl.multiple_of(img * PIX, PIX), PIX)
    return [qkv_ref[rows, part * CH_MID + pair * LINE : part * CH_MID + (pair + 1) * LINE] for part in range(3)]


def lane_half():
    return lax.broadcasted_iota(jnp.int32, (1, LINE), 1) < HEAD_DIM


def keep_half(v, half, side):
    mine = half if side == 0 else jnp.logical_not(half)
    return jnp.where(mine, v.astype(F32), 0.0).astype(BF16)


SPAN_TIME = (AT.time_one, AT.class_table)
SPAN_EMB1 = (AT.first.embed, AT.first.conv_two)
SPAN_EMB2 = (AT.second.embed, AT.second.conv_two)
SPAN_DOWN = (AT.conv_in, AT.time_one)
SPAN_ONE1 = (AT.first.gains, AT.first.embed)
SPAN_TWO1 = (AT.first.conv_two, AT.second.gains)
SPAN_ATTN = (AT.attn_gains, ALL_LINES)
SPAN_ONE2 = (AT.second.gains, AT.second.embed)
SPAN_TWO2 = (AT.second.conv_two, AT.attn_gains)


def block_scales(vec, row, mod_ref=None, mod_row=0):
    gain, shift = vec[row : row + 1, :], vec[row + 1 : row + 2, :]
    if mod_ref is None:
        return [(gain, shift)] * MB_DEV
    out = []
    for img in range(MB_DEV):
        scale = 1.0 + mod_ref[mod_row + img : mod_row + img + 1, :CH_MID]
        out.append((gain * scale, shift * scale + mod_ref[mod_row + img : mod_row + img + 1, CH_MID:]))
    return out


def upsample_masks(shift):
    dy, dx = shift // 3 - 1, shift % 3 - 1
    p = lax.broadcasted_iota(jnp.int32, (ROWS, 1), 0)
    i, j = lax.rem(lax.div(p, HALF), HALF), lax.rem(p, HALF)
    inside = (i + dy >= 0) & (i + dy < HALF) & (j + dx >= 0) & (j + dx < HALF)
    lane = lax.broadcasted_iota(jnp.int32, (1, LINE), 1)
    return inside & (lane >= shift * 12) & (lane < shift * 12 + 12), dy * HALF + dx


def forward_kernel(save, moves, flip, *refs):
    me, labels, x_in, phi, gm, sel, gat, tile, expand, pick = refs[:10]
    sources = max(move[0] for move in moves) + 1
    pieces, refs = refs[10 : 10 + sources], refs[10 + sources :]
    f_out = refs[0]
    (h0s, h1, u1, h2, qkv, mixed, h3, u2, h4, vec, mod, emb, pre, wz, xp) = refs[1:16]
    if save:
        sw_time, sw_emb1, sw_emb2, sw_down, sw_11, sw_12, sw_attn, sw_21, sw_22 = refs[16:25]
    held, wide, w_ref, w_sq, sbuf, pbuf, h0p, table, w_in, b_out, sems, save_sem = refs[25 if save else 16 :]
    src = Lines(held, wide)
    arriving = []
    for plane in range(SHARDS // PLANE):
        copies = []
        for n, lead, r, row, rows in moves:
            target = held.at[plane, r ^ me[0], pl.ds(row, rows), :]
            source = pieces[n].at[plane, lead] if flip[n] else pieces[n].at[lead, plane]
            copies.append(pltpu.make_async_copy(source, target, sems.at[plane]))
        for copy in copies:
            copy.start()
        arriving.append(copies)

    def arrive(plane):
        for copy in arriving[plane]:
            copy.wait()

    pending = []

    def keep(source, target):
        if save:
            cp = pltpu.make_async_copy(source, target, save_sem)
            cp.start()
            pending.append(cp)

    def free():
        while pending:
            pending.pop().wait()

    clear_pads(sbuf)
    pbuf[0:8, :] = jnp.zeros((8, CH_MID), F32)
    pbuf[ROWS + 8 : ROWS + 16, :] = jnp.zeros((8, CH_MID), F32)
    arrive(0)
    src.take(SPAN_TIME)
    src.matrix(w_sq.at[0], AT.time_one, CH_BASE, 6)
    src.matrix(w_sq.at[1], AT.time_two, EMB_DIM, 6)
    pre[...] = dot3(phi[...], w_sq[0, :CH_BASE, :]) + src.row(AT.time_bias_one, 6)
    emb[...] = dot3(silu(pre[...]), w_sq[1]) + src.row(AT.time_bias_two, 6)
    for n in range(MB_DEV):
        for j in range(6):
            cols = slice(j * LINE, (j + 1) * LINE)
            emb[n : n + 1, cols] += src.line(AT.class_table + labels[n] * 6 + j, table)
    keep(w_sq.at[1], sw_time if save else None)
    se = silu(emb[...])
    arrive(1)
    src.take(SPAN_EMB1)
    src.matrix(w_sq.at[0], AT.first.embed, EMB_DIM, 6)
    m1 = dot3(se, w_sq[0]) + src.row(AT.first.embed_bias, 6)
    free()
    keep(w_sq.at[0], sw_emb1 if save else None)
    mod[0:2, :] = m1[0:2]
    mod[4:8, :] = jnp.zeros((4, EMB_DIM), F32)

    src.take(SPAN_DOWN)
    trio = [wide[pl.ds(j, 16, stride=3), :] for j in range(3)]
    turned = [pltpu.roll(v, LINE // 2, 1) for v in trio[1:]]
    w_in[0:16, 0:LINE] = trio[0]
    w_in[0:16, LINE : 2 * LINE] = trio[1]
    w_in[16:32, 0:LINE] = jnp.where(first_lanes(), turned[0], turned[1])
    w_in[16:32, LINE : 2 * LINE] = turned[1]
    w_low = w_in[...].astype(BF16)
    spread = dot(x_in[...], gat[...], NT)
    around = jnp.zeros((ROWS, LINE), F32)
    for shift in range(9):
        inside, by = upsample_masks(shift)
        around = around + jnp.where(inside, spread if by == 0 else pltpu.roll(spread, (-by) % ROWS, 0), 0.0)
    around = around.astype(BF16)
    one = (lax.broadcasted_iota(jnp.int32, (1, 32), 1) == 29).astype(F32)
    for ph in range(4):
        patch = (dot(around, pick[ph]) + one).astype(BF16)
        xp[ph * ROWS : (ph + 1) * ROWS, :] = patch
        h0s[ph * ROWS : (ph + 1) * ROWS, :] = dot(patch, w_low).astype(BF16)
    for j in range(3):
        vec[V_DOWN : V_DOWN + 1, j * LINE : (j + 1) * LINE] = src.row(AT.bias_down + j, 1)
    src.matrix(w_ref, AT.conv_down, 9 * CH_BASE, 3)
    free()
    keep(w_ref.at[pl.ds(0, 9 * CH_BASE), :], sw_down if save else None)
    h1[...] = jnp.broadcast_to(vec[V_DOWN : V_DOWN + 1, :], (ROWS, CH_MID))
    p = lax.broadcasted_iota(jnp.int32, (ROWS, 1), 0)
    has_left, has_up = lax.rem(p, HALF) > 0, lax.rem(lax.div(p, HALF), HALF) > 0
    for ph in range(4):
        h0p[0:32, :] = jnp.zeros((32, h0p.shape[1]), F32)
        h0p[32 : 32 + ROWS, :] = h0s[ph * ROWS : (ph + 1) * ROWS, :].astype(F32)
        for ky in ((0, 2) if ph // 2 else (1,)):
            for kx in ((0, 2) if ph % 2 else (1,)):
                back = (16 if ky == 0 else 0) + (1 if kx == 0 else 0)
                v = h0p[32 - back : 32 - back + ROWS, :]
                if ky == 0:
                    v = jnp.where(has_up, v, 0.0)
                if kx == 0:
                    v = jnp.where(has_left, v, 0.0)
                t = 3 * ky + kx
                h1[...] += dot(v[:, :CH_BASE].astype(BF16), w_ref[t * CH_BASE : (t + 1) * CH_BASE, :])

    def vectors(row, at, count):
        for n in range(count):
            for j in range(3):
                vec[row + n : row + n + 1, j * LINE : (j + 1) * LINE] = src.row(at + 3 * n + j, 1)

    def half_block(x_ref, scales, bias_row, add_ref, out_ref, at, target):
        src.matrix(w_ref, at, 9 * CH_MID, 3)
        keep(w_ref, target)
        stats = [group_stats(x_ref, img, gm) for img in range(MB_DEV)]
        norm_to(pbuf, x_ref, stats, scales, True)
        shift_to(sbuf, pbuf)
        bias = jnp.broadcast_to(vec[bias_row : bias_row + 1, :], (ROWS, CH_MID))
        out_ref[...] = bias if add_ref is None else add_ref[...] + bias
        conv_forward(sbuf, w_ref, out_ref)

    def block(h_in, u, h_out, prefix, g_row, b1_row, b2_row, mod_row, spans, targets):
        src.take(spans[0])
        free()
        vectors(g_row, prefix.gains, 4)
        vectors(b1_row, prefix.bias_one, 1)
        half_block(h_in, block_scales(vec, g_row), b1_row, None, u, prefix.conv_one, targets[0])
        src.take(spans[1])
        free()
        vectors(b2_row, prefix.bias_two, 1)
        half_block(u, block_scales(vec, g_row + 2, mod, mod_row), b2_row, h_in, h_out, prefix.conv_two, targets[1])

    saved = (sw_11, sw_12, sw_21, sw_22) if save else (None,) * 4
    arrive(2)
    block(h1, u1, h2, AT.first, V_G1, V_B11, V_B12, 0, (SPAN_ONE1, SPAN_TWO1), saved[:2])

    arrive(3)
    src.take(SPAN_ATTN)
    free()
    vectors(V_AG, AT.attn_gains, 2)
    vectors(V_AB, AT.attn_bias, 1)
    vectors(V_FG, AT.final_gains, 2)
    base = AT.conv_out - src.low
    tap_row = lax.broadcasted_iota(jnp.int32, (TAPS, 1), 0) < 9
    taps = [jnp.where(tap_row, wide[pl.ds(base + j, TAPS, stride=9), :], 0.0) for j in range(9)]
    taps = jnp.concatenate(taps, 1)
    rows_out = jnp.concatenate([jnp.where(colour(c), taps, 0.0) for c in range(3)], 0).astype(BF16)
    wz[...] = jnp.zeros_like(wz)
    wz[0 : 3 * TAPS, :] = dot(rows_out, expand[...], NT).astype(BF16)
    last = AT.bias_out - src.low
    b_out[...] = dot(eight(wide[last : last + 1, :]).astype(BF16), tile[...])
    for part in range(3):
        base = AT.attn_qkv - src.low
        for j in range(3):
            v = wide[pl.ds(base + part * 3 + j, CH_MID, stride=9), :]
            w_ref[part * CH_MID : (part + 1) * CH_MID, j * LINE : (j + 1) * LINE] = v.astype(BF16)
    src.matrix(w_ref.at[pl.ds(3 * CH_MID, CH_MID), :], AT.attn_out, CH_MID, 3)
    keep(w_ref.at[pl.ds(0, 4 * CH_MID), :], sw_attn if save else None)
    stats = [group_stats(h2, img, gm) for img in range(MB_DEV)]
    norm_to(pbuf, h2, stats, block_scales(vec, V_AG), False)
    n_low = pbuf[8 : 8 + ROWS, :].astype(BF16)
    for part in range(3):
        v = dot(n_low, w_ref[part * CH_MID : (part + 1) * CH_MID, :])
        qkv[:, part * CH_MID : (part + 1) * CH_MID] = v.astype(BF16)
    half = lane_half()

    def heads(img, carry):
        for pair in range(HEADS // 2):
            q, k, v = attention_pair(qkv, img, pair)
            outs = []
            for side in range(2):
                s = dot(keep_half(q, half, side), k, NT) * HEAD_DIM ** (-0.5)
                e = jnp.exp(s - jnp.max(s, 1, keepdims=True))
                prob = (e / jnp.sum(e, 1, keepdims=True)).astype(BF16)
                outs.append(dot(prob, v))
            mixed[pl.ds(pl.multiple_of(img * PIX, PIX), PIX), pair * LINE : (pair + 1) * LINE] = jnp.where(
                half, outs[0], outs[1]
            ).astype(BF16)
        return carry

    lax.fori_loop(0, MB_DEV, heads, 0)
    h3[...] = h2[...] + dot(mixed[...], w_ref[3 * CH_MID : 4 * CH_MID, :]) + vec[V_AB : V_AB + 1, :]

    src.take(SPAN_EMB2)
    src.matrix(w_sq.at[1], AT.second.embed, EMB_DIM, 6)
    m2 = dot3(silu(emb[...]), w_sq[1]) + src.row(AT.second.embed_bias, 6)
    mod[2:4, :] = m2[0:2]
    free()
    keep(w_sq.at[1], sw_emb2 if save else None)
    block(h3, u2, h4, AT.second, V_G2, V_B21, V_B22, 2, (SPAN_ONE2, SPAN_TWO2), saved[2:])

    stats = [group_stats(h4, img, gm) for img in range(MB_DEV)]
    norm_to(pbuf, h4, stats, block_scales(vec, V_FG), True)
    z = dot(pbuf[8 : 8 + ROWS, :].astype(BF16), wz[...], NT)
    t_all = dot3(z, sel[...])
    u_all = jnp.zeros((ROWS, LINE), F32)
    for shift in range(9):
        inside, by = upsample_masks(shift)
        moved = t_all if by == 0 else pltpu.roll(t_all, (-by) % ROWS, 0)
        u_all = u_all + jnp.where(inside, moved, 0.0)
    f_out[...] = dot3(u_all, gat[...]) + b_out[0:1, :]
    free()


def vmem(*shape_dtype):
    return pltpu.VMEM(*shape_dtype)


VM = pl.BlockSpec(memory_space=pltpu.VMEM)
HB = pl.BlockSpec(memory_space=pl.ANY)
SM = pl.BlockSpec(memory_space=pltpu.SMEM)


def state_shapes():
    act = ((ROWS, CH_MID), F32)
    return [
        ((4 * ROWS, 256), BF16),
        act, act, act,
        ((ROWS, 3 * CH_MID), BF16),
        ((ROWS, CH_MID), BF16),
        act, act, act,
        ((VEC_ROWS, CH_MID), F32),
        ((8, EMB_DIM), F32),
        ((8, EMB_DIM), F32),
        ((8, EMB_DIM), F32),
        ((LINE, CH_MID), BF16),
        ((4 * ROWS, 32), BF16),
    ]


def weight_shapes():
    sq = ((EMB_DIM, EMB_DIM), BF16)
    conv = ((9 * CH_MID, CH_MID), BF16)
    return [sq, sq, sq, ((9 * CH_BASE, CH_MID), BF16), conv, conv, ((4 * CH_MID, CH_MID), BF16), conv, conv]


def forward_call(save, me, labels, lines, x_in, phi, tables):
    pieces, moves, flip = lines
    sds = lambda s: jax.ShapeDtypeStruct(*s)
    outs = [sds(((ROWS, LINE), F32))]
    out_specs = [VM]
    state = state_shapes()
    scratch = []
    if save:
        outs += [sds(s) for s in state] + [sds(s) for s in weight_shapes()]
        out_specs += [VM] * len(state) + [HB] * len(weight_shapes())
    else:
        scratch += [vmem(*s) for s in state]
    scratch += [
        vmem((SHARDS // PLANE, PLANE, ROOM, LINE), BF16),
        vmem((10432, LINE), F32),
        vmem((9 * CH_MID, CH_MID), BF16),
        vmem((2, EMB_DIM, EMB_DIM), BF16),
        vmem((3, PADDED, CH_MID), BF16),
        vmem((ROWS + 16, CH_MID), F32),
        vmem((ROWS + 48, 256), F32),
        vmem((16, LINE), F32),
        vmem((32, 2 * LINE), F32),
        vmem((8, LINE), F32),
        pltpu.SemaphoreType.DMA((SHARDS // PLANE,)),
        pltpu.SemaphoreType.DMA,
    ]

    def body(*refs):
        forward_kernel(save, moves, flip, *refs)

    return pl.pallas_call(
        body,
        out_shape=outs,
        in_specs=[SM] * 2 + [VM] * 8 + [HB] * len(pieces),
        out_specs=out_specs,
        scratch_shapes=scratch,
        name="forward_save" if save else "forward_plain",
        **kernel_params(),
    )(me, labels, x_in, phi, *tables, *pieces)


def column_sum(pbuf):
    def body(c, acc):
        return acc + jnp.sum(pbuf[pl.ds(pl.multiple_of(c * CHUNK + 8, 8), CHUNK), :], 0, keepdims=True)

    return lax.fori_loop(0, ROWS // CHUNK, body, jnp.zeros((1, CH_MID), F32))


def refill(pbuf, source):
    for c in range(0, ROWS, CHUNK):
        pbuf[8 + c : 8 + c + CHUNK, :] = source[c : c + CHUNK, :]


def block_back_two(dh, u_ref, at, base, rows, vec, mod, mod_row, weights, tools, g, dm):
    g_row, b1_row, b2_row = rows
    sbuf, pbuf, dx, at_ref, gm = tools
    put_row(g, at.bias_two - base, colsum(dh, 0, ROWS))
    u_stats = [group_stats(u_ref, img, gm) for img in range(MB_DEV)]
    scales = block_scales(vec, g_row + 2, mod, mod_row)
    norm_to(pbuf, u_ref, u_stats, scales, True)
    transpose_to(at_ref, pbuf)
    refill(pbuf, dh)
    shift_to(sbuf, pbuf)
    conv_back(sbuf, at_ref, weights.take(), dx, g, at.conv_two - base)
    weights.begin()

    def emit_inner(r, v):
        pbuf[pl.ds(r + 8, CHUNK), :] = v

    sums = norm_back(u_ref, dx, u_stats, scales, True, gm, emit_inner)
    gain, shift = vec[g_row + 2 : g_row + 3, :], vec[g_row + 3 : g_row + 4, :]
    d_gain = d_shift = 0.0
    dm[...] = jnp.zeros_like(dm)
    for img, (a, b) in enumerate(sums):
        scale = 1.0 + mod[mod_row + img : mod_row + img + 1, :CH_MID]
        d_gain, d_shift = d_gain + scale * b, d_shift + scale * a
        dm[img : img + 1, :CH_MID] = gain * b + shift * a
        dm[img : img + 1, CH_MID:] = a
    return d_gain, d_shift


def block_back_one(dh, x_ref, at, base, rows, vec, weights, tools, g):
    g_row, b1_row, b2_row = rows
    sbuf, pbuf, dx, at_ref, gm = tools
    put_row(g, at.bias_one - base, column_sum(pbuf))
    shift_to(sbuf, pbuf)
    stats = [group_stats(x_ref, img, gm) for img in range(MB_DEV)]
    scales = block_scales(vec, g_row)
    norm_to(pbuf, x_ref, stats, scales, True)
    transpose_to(at_ref, pbuf)
    conv_back(sbuf, at_ref, weights.take(), dx, g, at.conv_one - base)
    weights.begin()

    def emit_outer(r, v):
        dh[pl.ds(r, CHUNK), :] += v

    sums = norm_back(x_ref, dx, stats, scales, True, gm, emit_outer)
    put_row(g, at.gains - base, sums[0][1] + sums[1][1])
    put_row(g, at.gains + 3 - base, sums[0][0] + sums[1][0])


def rowsum(v):
    return jnp.sum(v, 0, keepdims=True)


def put_outer(g, at, left, right):
    for c in range(-(-left.shape[1] // LINE)):
        piece = outer(left[:, c * LINE : (c + 1) * LINE], right)
        put_lines(g, at + c * LINE * (EMB_DIM // LINE), piece, EMB_DIM // LINE)


class Weights:
    def __init__(self, sources, slots, sems):
        self.copies = []
        for n, source in enumerate(sources):
            target = slots.at[n % 2, pl.ds(0, source.shape[0]), :]
            self.copies.append((pltpu.make_async_copy(source, target, sems.at[n % 2]), target))
        self.begun = self.done = 0

    def begin(self):
        if self.begun < len(self.copies):
            self.copies[self.begun][0].start()
            self.begun += 1

    def take(self):
        copy, target = self.copies[self.done]
        copy.wait()
        self.done += 1
        return target


class Leave:
    def __init__(self, me, g, base, keep, send, stage, sems):
        self.core, self.place = lax.rem(me[0], 2), lax.div(me[0], 2)
        self.g, self.base, self.keep, self.send, self.stage, self.sems = g, base, keep, send, stage, sems
        self.copies = []

    def plane(self, plane, slot):
        pairs = PLANE // 2
        for q in range(pairs):
            at = q ^ self.place
            first = (plane * PLANE + 2 * q) * SHARD - self.base
            mine = pl.multiple_of(first + self.core * SHARD, 8)
            other = pl.multiple_of(first + (1 - self.core) * SHARD, 8)
            kept = pltpu.make_async_copy(self.g.at[pl.ds(mine, ROOM), :], self.keep.at[slot, at], self.sems.at[0])
            kept.start()
            stage = self.stage.at[slot * pairs + q]
            block = ROOM // 8

            def body(c, carry):
                stage[pl.ds(pl.multiple_of(c * 288, 16), 288), :] = self.g[
                    pl.ds(pl.multiple_of(other + c * 288, 8), 288), :
                ].astype(BF16)
                return carry

            whole = ROOM // 288
            lax.fori_loop(0, whole, body, 0)
            rest = ROOM - whole * 288
            stage[whole * 288 :, :] = self.g[pl.ds(pl.multiple_of(other + whole * 288, 8), rest), :].astype(BF16)
            sent = pltpu.make_async_copy(stage, self.send.at[slot, at], self.sems.at[1])
            sent.start()
            self.copies += [kept, sent]

    def wait(self):
        for copy in self.copies:
            copy.wait()


def clear_lines(g, first, count):
    if count:
        g[first : first + count, :] = jnp.zeros((count, LINE), F32)


def back_two_kernel(*refs):
    me, df, wz, gm, sel, gat, tile, expand, vec, mod, emb, h4, u2, h3, qkv, mixed, h2, u1, s22, s21, s_attn, s12, s_emb = refs[:23]
    keep, send, rest, dh, du, dm_first, extra, dse = refs[23:31]
    g, slots, w_sq, sbuf, pbuf, dx, at_ref, dqkv, dm, stage, sems, sq_sem, out_sems = refs[31:]
    weights = Weights([s22, s21, s_attn, s12], slots, sems)
    weights.begin()
    weights.begin()
    sq_copy = pltpu.make_async_copy(s_emb, w_sq, sq_sem)
    sq_copy.start()
    clear_pads(sbuf)
    clear_lines(g, TAIL - SPLIT, g.shape[0] - (TAIL - SPLIT))
    pbuf[0:8, :] = jnp.zeros((8, CH_MID), F32)
    pbuf[ROWS + 8 : ROWS + 16, :] = jnp.zeros((8, CH_MID), F32)
    tools = (sbuf, pbuf, dx, at_ref, gm)

    stats = [group_stats(h4, img, gm) for img in range(MB_DEV)]
    scales = block_scales(vec, V_FG)
    norm_to(pbuf, h4, stats, scales, True)
    transpose_to(at_ref, pbuf)
    spread = dot(df[...].astype(BF16), gat[...], NT)
    dt = jnp.zeros((ROWS, LINE), F32)
    for shift in range(9):
        inside, by = upsample_masks(shift)
        part = jnp.where(inside, spread, 0.0)
        dt = dt + (part if by == 0 else pltpu.roll(part, by % ROWS, 0))
    dz = dot(dt.astype(BF16), sel[...], NT)
    parts = split3(dz)
    dwz = dot(at_ref[...], parts[0]) + dot(at_ref[...], parts[1]) + dot(at_ref[...], parts[2])
    dx[...] = dot(parts[0], wz[...]) + dot(parts[1], wz[...]) + dot(parts[2], wz[...])
    d_rows = dot3(dwz.T[0 : 3 * TAPS, :], expand[...])
    d_taps = jnp.zeros((TAPS, 3 * CH_MID), F32)
    for c in range(3):
        d_taps = d_taps + jnp.where(colour(c), d_rows[c * TAPS : (c + 1) * TAPS, :], 0.0)
    for j in range(9):
        g[pl.ds(TAIL - SPLIT + j, 9, stride=9), :] = d_taps[0:9, j * LINE : (j + 1) * LINE]
    b_row = AT.bias_out - SPLIT
    g[b_row : b_row + 1, :] = dot3(eight(colsum(df, 0, ROWS)), tile[...], NT)[0:1]

    def emit_first(r, v):
        dh[pl.ds(r, CHUNK), :] = v

    sums = norm_back(h4, dx, stats, scales, True, gm, emit_first)
    put_row(g, AT.final_gains - SPLIT, sums[0][1] + sums[1][1])
    put_row(g, AT.final_gains + 3 - SPLIT, sums[0][0] + sums[1][0])

    rows = (V_G2, V_B21, V_B22)
    d_gain, d_shift = block_back_two(dh, u2, AT.second, SPLIT, rows, vec, mod, 2, weights, tools, g, dm)
    put_row(g, AT.second.gains + 6 - SPLIT, d_gain)
    put_row(g, AT.second.gains + 9 - SPLIT, d_shift)
    block_back_one(dh, h3, AT.second, SPLIT, rows, vec, weights, tools, g)
    se = silu(emb[...])
    put_outer(g, AT.second.embed - SPLIT, se, dm[...])
    put_row(g, AT.second.embed_bias - SPLIT, rowsum(dm[...]))
    sq_copy.wait()
    dse[...] = dot3(dm[...], w_sq[...], NT)

    put_row(g, AT.attn_bias - SPLIT, colsum(dh, 0, ROWS))
    w = weights.take()
    d_low = dh[...].astype(BF16)
    for c in range(ROWS // LINE):
        at_ref[:, c * LINE : (c + 1) * LINE] = mixed[c * LINE : (c + 1) * LINE, :].astype(F32).T.astype(BF16)
    put_lines(g, AT.attn_out - SPLIT, dot(at_ref[...], d_low), 3)
    pbuf[8 : 8 + ROWS, :] = dot(d_low, w[3 * CH_MID : 4 * CH_MID, :], NT)
    half = lane_half()
    scale = HEAD_DIM ** (-0.5)

    def heads(img, carry):
        rows = pl.ds(pl.multiple_of(img * PIX, PIX), PIX)
        for pair in range(HEADS // 2):
            q, k, v = attention_pair(qkv, img, pair)
            cols = slice(pair * LINE, (pair + 1) * LINE)
            do = pbuf[pl.ds(pl.multiple_of(img * PIX + 8, 8), PIX), cols].astype(BF16)
            dqs, dks, dvs = [], [], []
            for side in range(2):
                s = dot(keep_half(k, half, side), q, NT) * scale
                e = jnp.exp(s - jnp.max(s, 0, keepdims=True))
                prob = e / jnp.sum(e, 0, keepdims=True)
                dvs.append(dot(prob.astype(BF16), do))
                dp = dot(keep_half(v, half, side), do, NT)
                ds = prob * (dp - jnp.sum(dp * prob, 0, keepdims=True))
                dks.append(dot(ds.astype(BF16), q))
                dqs.append(dot(ds.T.astype(BF16), k))
            for part, pieces in enumerate((dqs, dks, dvs)):
                value = jnp.where(half, pieces[0], pieces[1])
                if part < 2:
                    value = value * scale
                dqkv[rows, part * CH_MID + pair * LINE : part * CH_MID + (pair + 1) * LINE] = value.astype(BF16)
        return carry

    lax.fori_loop(0, MB_DEV, heads, 0)
    stats = [group_stats(h2, img, gm) for img in range(MB_DEV)]
    scales = block_scales(vec, V_AG)
    norm_to(pbuf, h2, stats, scales, False)
    transpose_to(at_ref, pbuf)
    dx[...] = jnp.zeros_like(dx)
    for part in range(3):
        d = dqkv[:, part * CH_MID : (part + 1) * CH_MID]
        dw = dot(at_ref[...], d)
        for j in range(3):
            g[pl.ds(AT.attn_qkv - SPLIT + part * 3 + j, CH_MID, stride=9), :] = dw[:, j * LINE : (j + 1) * LINE]
        dx[...] += dot(d, w[part * CH_MID : (part + 1) * CH_MID, :], NT)
    weights.begin()

    def emit(r, v):
        dh[pl.ds(r, CHUNK), :] += v

    sums = norm_back(h2, dx, stats, scales, False, gm, emit)
    put_row(g, AT.attn_gains - SPLIT, sums[0][1] + sums[1][1])
    put_row(g, AT.attn_gains + 3 - SPLIT, sums[0][0] + sums[1][0])

    leave = Leave(me, g, SPLIT, keep, send, stage, out_sems)
    leave.plane(3, 1)
    rows = (V_G1, V_B11, V_B12)
    d_gain, d_shift = block_back_two(dh, u1, AT.first, SPLIT, rows, vec, mod, 0, weights, tools, g, dm_first)
    extra[...] = jnp.zeros_like(extra)
    extra[0:1, :] = d_gain
    extra[1:2, :] = d_shift
    for c in range(0, ROWS, CHUNK):
        du[c : c + CHUNK, :] = pbuf[8 + c : 8 + c + CHUNK, :]
    leave.plane(2, 0)
    below = pltpu.make_async_copy(g.at[pl.ds(0, MIDDLE - SPLIT), :], rest, out_sems.at[2])
    below.start()
    below.wait()
    leave.wait()


def back_one_kernel(*refs):
    (me, labels, dh_in, du, dm, extra, dse_in, gm, vec, emb, pre, phi, h1, h0s, xp) = refs[:15]
    s11, s_down, s_emb, s_time, rest = refs[15:20]
    keep, send = refs[20:22]
    g, slots, w_sq, sbuf, pbuf, dx, at_ref, dh, h0t, demb_ref, stage, dwin, dbin, sems, sq_sem, out_sems = refs[22:]
    above = pltpu.make_async_copy(rest, g.at[pl.ds(SPLIT, MIDDLE - SPLIT), :], out_sems.at[2])
    above.start()
    weights = Weights([s11, s_down], slots, sems)
    weights.begin()
    weights.begin()
    sq_copies = [pltpu.make_async_copy(s, w_sq.at[n], sq_sem.at[n]) for n, s in enumerate((s_emb, s_time))]
    for copy in sq_copies:
        copy.start()
    clear_pads(sbuf)
    clear_lines(g, MIDDLE, g.shape[0] - MIDDLE)
    pbuf[0:8, :] = jnp.zeros((8, CH_MID), F32)
    pbuf[ROWS + 8 : ROWS + 16, :] = jnp.zeros((8, CH_MID), F32)
    refill(pbuf, du)
    for c in range(0, ROWS, CHUNK):
        dh[c : c + CHUNK, :] = dh_in[c : c + CHUNK, :]
    above.wait()
    tools = (sbuf, pbuf, dx, at_ref, gm)
    block_back_one(dh, h1, AT.first, 0, (V_G1, V_B11, V_B12), vec, weights, tools, g)
    put_row(g, AT.first.gains + 6, extra[0:1, :])
    put_row(g, AT.first.gains + 9, extra[1:2, :])
    se = silu(emb[...])
    put_outer(g, AT.first.embed, se, dm[...])
    put_row(g, AT.first.embed_bias, rowsum(dm[...]))
    leave = Leave(me, g, 0, keep, send, stage, out_sems)
    for copy in sq_copies:
        copy.wait()
    demb = (dse_in[...] + dot3(dm[...], w_sq[0], NT)) * silu_slope(emb[...])
    put_row(g, AT.time_bias_two, rowsum(demb))
    put_outer(g, AT.time_two, silu(pre[...]), demb)
    dpre = dot3(demb, w_sq[1], NT) * silu_slope(pre[...])
    put_row(g, AT.time_bias_one, rowsum(dpre))
    put_outer(g, AT.time_one, phi[...], dpre)
    clear = 240
    first, lines = AT.class_table, CLASSES * (EMB_DIM // LINE)

    def wipe(c, carry):
        g[pl.ds(first + c * clear, clear), :] = jnp.zeros((clear, LINE), F32)
        return carry

    lax.fori_loop(0, lines // clear, wipe, 0)
    demb_ref[...] = demb
    for n in range(MB_DEV):
        for j in range(EMB_DIM // LINE):
            at = first + labels[n] * (EMB_DIM // LINE) + j
            g[pl.ds(at, 1), :] += demb_ref[n : n + 1, j * LINE : (j + 1) * LINE]
    leave.plane(1, 1)

    put_row(g, AT.bias_down, colsum(dh, 0, ROWS))
    refill(pbuf, dh)
    shift_to(sbuf, pbuf)
    w = weights.take()
    dwin[...] = jnp.zeros_like(dwin)
    dbin[...] = jnp.zeros_like(dbin)
    for ph in range(4):
        for c in range(ROWS // LINE):
            rows = slice(ph * ROWS + c * LINE, ph * ROWS + (c + 1) * LINE)
            h0t[:, c * LINE : (c + 1) * LINE] = h0s[rows, :].astype(F32).T.astype(BF16)
        d0 = jnp.zeros((ROWS, CH_BASE), F32)
        for ky in ((0, 2) if ph // 2 else (1,)):
            for kx in ((0, 2) if ph % 2 else (1,)):
                d = shifted(sbuf, 2 if kx == 0 else 1, 32 if ky == 0 else 16)
                t = 3 * ky + kx
                d0 = d0 + dot(d, w[t * CH_BASE : (t + 1) * CH_BASE, :], NT)
                put_lines(g, AT.conv_down + t * CH_BASE * 3, dot(h0t[0:CH_BASE, :], d), 3)
        dbin[0:1, :CH_BASE] += rowsum(d0)
        dwin[:, :CH_BASE] += dot(xp[ph * ROWS : (ph + 1) * ROWS, :], d0.astype(BF16), TN)
    dwin[29:30, :] = dbin[0:1, :]
    even, odd = dwin[0:16, :], dwin[16:32, :]
    turned = pltpu.roll(odd[:, :LINE], LINE // 2, 1), pltpu.roll(odd[:, LINE:], LINE // 2, 1)
    g[pl.ds(0, 14, stride=3), :] = even[0:14, :LINE]
    g[pl.ds(1, 14, stride=3), :] = jnp.where(first_lanes(), even[:, LINE:], turned[0])[0:14]
    g[pl.ds(2, 14, stride=3), :] = jnp.where(first_lanes(), turned[0], turned[1])[0:14]
    leave.plane(0, 0)
    leave.wait()


def kernel_params():
    return dict(
        compiler_params=pltpu.CompilerParams(vmem_limit_bytes=60 * 1024 * 1024),
        cost_estimate=pl.CostEstimate(flops=8 * 10**9, bytes_accessed=4 * 10**7, transcendentals=10**6),
    )


def back_scratch(lines):
    return [
        vmem((lines + 8, LINE), F32),
        vmem((2, 9 * CH_MID, CH_MID), BF16),
        vmem((2, EMB_DIM, EMB_DIM), BF16),
        vmem((3, PADDED, CH_MID), BF16),
        vmem((ROWS + 16, CH_MID), F32),
        vmem((ROWS, CH_MID), F32),
        vmem((CH_MID, ROWS), BF16),
    ]


def plane_shapes():
    pairs = PLANE // 2
    return [
        jax.ShapeDtypeStruct((2, pairs, ROOM, LINE), F32),
        jax.ShapeDtypeStruct((2, pairs, ROOM, LINE), BF16),
    ]


def back_two_call(args):
    sds = lambda *s: jax.ShapeDtypeStruct(*s)
    act = sds((ROWS, CH_MID), F32)
    scratch = back_scratch(ALL_LINES - SPLIT)
    scratch[2] = vmem((EMB_DIM, EMB_DIM), BF16)
    return pl.pallas_call(
        back_two_kernel,
        out_shape=plane_shapes()
        + [
            sds((MIDDLE - SPLIT, LINE), F32),
            act,
            act,
            sds((8, EMB_DIM), F32),
            sds((8, CH_MID), F32),
            sds((8, EMB_DIM), F32),
        ],
        in_specs=[SM] + [VM] * 17 + [HB] * 5,
        out_specs=[HB] * 3 + [VM] * 5,
        scratch_shapes=scratch
        + [
            vmem((ROWS, 3 * CH_MID), BF16),
            vmem((8, EMB_DIM), F32),
            vmem((PLANE, ROOM, LINE), BF16),
            pltpu.SemaphoreType.DMA((2,)),
            pltpu.SemaphoreType.DMA,
            pltpu.SemaphoreType.DMA((3,)),
        ],
        name="back_two",
        **kernel_params(),
    )(*args)


def back_one_call(args):
    return pl.pallas_call(
        back_one_kernel,
        out_shape=plane_shapes(),
        in_specs=[SM] * 2 + [VM] * 13 + [HB] * 5,
        out_specs=[HB] * 2,
        scratch_shapes=back_scratch(MIDDLE)
        + [
            vmem((ROWS, CH_MID), F32),
            vmem((256, ROWS), BF16),
            vmem((8, EMB_DIM), F32),
            vmem((PLANE, ROOM, LINE), BF16),
            vmem((32, 2 * LINE), F32),
            vmem((8, 2 * LINE), F32),
            pltpu.SemaphoreType.DMA((2,)),
            pltpu.SemaphoreType.DMA((2,)),
            pltpu.SemaphoreType.DMA((3,)),
        ],
        name="back_one",
        **kernel_params(),
    )(*args)


def karras(index):
    ramp_frac = index.astype(F32) / (DISCRETE - 1)
    low_root = SIGMA_LOW ** (1.0 / RHO_POWER)
    high_root = SIGMA_HIGH ** (1.0 / RHO_POWER)
    return (low_root + ramp_frac * (high_root - low_root)) ** RHO_POWER


def preconditioning_factors(sigma):
    variance_sum = sigma * sigma + SIGMA_DATA**2
    skip = SIGMA_DATA**2 / ((sigma - SIGMA_LOW) ** 2 + SIGMA_DATA**2)
    out = (sigma - SIGMA_LOW) * SIGMA_DATA * lax.rsqrt(variance_sum)
    return (skip, out, lax.rsqrt(variance_sum))


def noise_features(sigma):
    half_width = CH_BASE // 2
    frequency = jnp.exp(-math.log(10000.0) * jnp.arange(half_width, dtype=F32) / half_width)
    phases = 250.0 * jnp.log(sigma)[:, None] * frequency
    return jnp.pad(jnp.concatenate([jnp.cos(phases), jnp.sin(phases)], 1), ((0, 8 - MB_DEV), (0, 0)))


def pixels(images):
    lead = images.shape[0]
    split = images.reshape(lead, MB_DEV, HALF, 2, HALF, 2, 3)
    return split.transpose(0, 1, 2, 4, 3, 5, 6).reshape(lead, ROWS, 12)


def pixel_live(counts, valid_rows):
    row = lax.broadcasted_iota(jnp.int32, (ROWS, 12), 0)
    lane = lax.broadcasted_iota(jnp.int32, (ROWS, 12), 1)
    slot = row // PIX
    line = 2 * ((row // HALF) % HALF) + lane // 6
    top = jnp.where(slot == 0, valid_rows[0], valid_rows[1])
    return ((slot < counts[0]) & (line < top)).astype(F32)


def per_part(me, labels, lines, inputs, save, tables):
    _, x_in, phi, _ = inputs
    results = forward_call(save, me, labels, lines, x_in, phi, tables)
    return results[0], results[1:]


AXIS = "fsdp"
CORE, EAST, SOUTH, UP = 1, 2, 4, 8
CUT_ROWS = ROOM // 2


def swap(values, hop):
    return lax.ppermute(values, AXIS, [(i, i ^ hop) for i in range(SHARDS)])


def total_of(values, n):
    hop = 1
    while hop < n:
        values = values + lax.ppermute(values, AXIS, [(i, i ^ hop) for i in range(n)])
        hop *= 2
    return values


CUTS = (0, 864, 1728, ROOM)
TALL = SHARDS // PLANE


def gate(values, after):
    count = len(values)

    def body(*refs):
        pass

    return pl.pallas_call(
        body,
        out_shape=[jax.ShapeDtypeStruct(v.shape, v.dtype) for v in values],
        in_specs=[HB] * (count + len(after)),
        out_specs=[HB] * count,
        input_output_aliases={i: i for i in range(count)},
        name="gate",
    )(*values, *after)


def climb(values, way, far, first=0):
    planes = range(first, TALL - far) if way == 1 else range(TALL - 1 - first, far - 1, -1)
    pairs = [(q * PLANE + i, (q + way * far) * PLANE + i) for q in planes for i in range(PLANE)]
    return lax.ppermute(values, AXIS, pairs)


def column_window(slots, z):
    rows = []
    for p in range(TALL):
        value = slots[TALL - 1 + p]
        for q in range(1, TALL):
            value = jnp.where(z == q, slots[TALL - 1 - q + p], value)
        rows.append(value)
    return jnp.stack(rows)


def column_one(own):
    return climb(own, 1, 1), climb(own, -1, 1)


def column_two(own, one):
    below, above = one
    return climb(below, 1, 1, 1), climb(above, -1, 1, 1), climb(own, 1, 3), climb(own, -1, 3)


def column_all(own, one, two, z):
    return column_window([two[2], two[0], one[0], own, one[1], two[1], two[3]], z)


def gather_both(online, target, z, early):
    ab_o, ab_t = online[: CUTS[2]], target[: CUTS[2]]
    c_own = jnp.stack([online[CUTS[2] :], target[CUTS[2] :]])
    one = column_one(ab_o)
    c_two = jnp.stack([c_own, swap(c_own, SOUTH)])
    c_four = jnp.concatenate([c_two, swap(c_two, EAST)])
    two = column_two(ab_o, one)
    column = column_all(ab_o, one, two, z)
    za, zb = column[:, : CUTS[1]], column[:, CUTS[1] :]
    done = early([two[0][:16], two[1][:16]])
    a_two, b_two = jnp.stack([za, swap(za, EAST)]), jnp.stack([zb, swap(zb, SOUTH)])
    a_far, b_far = swap(a_two, SOUTH), swap(b_two, EAST)
    (ab_t,) = gate([ab_t], two)
    one = column_one(ab_t)
    two = column_two(ab_t, one)
    column = column_all(ab_t, one, two, z)
    za, zb = column[:, : CUTS[1]], column[:, CUTS[1] :]
    co_four, ct_four = c_four[:, 0], c_four[:, 1]
    (co_four,) = gate([co_four], two)
    c_one = column_one(co_four)
    c_next = column_two(co_four, c_one)
    c_all = column_all(co_four, c_one, c_next, z)
    first = [a_two, a_far, b_two, b_far, c_all]
    first = first + [swap(v, CORE) for v in first]
    za, zb = gate([za, zb], [a_far, b_far])
    a_east, b_south = swap(za, EAST), swap(zb, SOUTH)
    at_two, bt_two = jnp.stack([za, a_east]), jnp.stack([zb, b_south])
    (ct_four,) = gate([ct_four], c_next)
    ct_one = column_one(ct_four)
    ct_next = column_two(ct_four, ct_one)
    at_far, bt_far = swap(at_two, SOUTH), swap(bt_two, EAST)
    at_core, bt_core = swap(at_two, CORE), swap(bt_two, CORE)

    def second(model):
        af, bf, c0, c1, c2, c3 = gate([at_far, bt_far, *ct_next], [model])
        ct_all = column_all(ct_four, ct_one, (c0, c1, c2, c3), z)
        rest = [swap(v, CORE) for v in (af, bf, ct_all)]
        return [at_two, af, bt_two, bf, ct_all, at_core, rest[0], bt_core, rest[1], rest[2]]

    return done, first, [a_east, b_south, *ct_one], second


def gather_moves():
    places = [(0, 1), (2, 3), (0, 2), (1, 3), (0, 2, 1, 3)]
    part = (0, 0, 1, 1, 2)
    moves = []
    for core in range(2):
        for n in range(5):
            row, end = CUTS[part[n]], CUTS[part[n] + 1]
            for lead, place in enumerate(places[n]):
                moves.append((core * 5 + n, lead, 2 * place + core, row, end - row))
    return moves


def gather_plain(shard):
    lines = lax.all_gather(shard, AXIS, axis=0, tiled=True).reshape(SHARDS // PLANE, PLANE, SHARD, LINE)
    lines = jnp.pad(lines, ((0, 0), (0, 0), (0, ROOM - SHARD), (0, 0)))
    return [lines], [(0, r, r, 0, ROOM) for r in range(PLANE)], (True,)


def reduce_planes(keep, send):
    planes = keep.shape[0]
    got = swap(send, CORE)
    low = lambda v: v.astype(BF16)
    wide = lambda v: v.astype(F32)
    a, b = slice(0, CUT_ROWS), slice(CUT_ROWS, ROOM)
    quarter = lambda i, rows: keep[:, i, rows] + wide(got[:, i, rows])
    send_a = low(jnp.stack([quarter(1, a), quarter(3, a)], 1))
    send_b = low(jnp.stack([quarter(2, b), quarter(3, b)], 1))
    got_a, got_b = swap(send_a, EAST), swap(send_b, SOUTH)
    last_a = low(quarter(2, a) + wide(got_a[:, 1]))
    last_b = low(quarter(1, b) + wide(got_b[:, 1]))
    end_a, end_b = swap(last_a, SOUTH), swap(last_b, EAST)
    sum_a = quarter(0, a) + wide(got_a[:, 0]) + wide(end_a)
    sum_b = quarter(0, b) + wide(got_b[:, 0]) + wide(end_b)
    return jnp.concatenate([sum_a, sum_b], 1)


def reduce_column(part, z):
    planes = part.shape[0]
    pick = lambda p: lax.dynamic_index_in_dim(part, jnp.clip(p, 0, planes - 1), 0, keepdims=False)
    total = pick(z)
    for way in (1, -1):
        run = None
        for far in range(planes - 1, 0, -1):
            value = pick(z + way * far)
            if run is not None:
                value = value + run
            holders = [q for q in range(planes) if 0 <= q + way * far < planes]
            pairs = [(q * PLANE + i, (q + way) * PLANE + i) for q in holders for i in range(PLANE)]
            run = lax.ppermute(value.astype(BF16), AXIS, pairs).astype(F32)
        total = total + run
    return total


def per_device(n, images, noise_draws, labels, step_index, valid_rows, counts, master, momentum, ema):
    direct = n == SHARDS
    index = lax.axis_index(AXIS)
    me = jnp.where(direct, lax.rem(index, PLANE), 0).astype(jnp.int32)[None]
    z = lax.div(index, PLANE)
    shards = [v.astype(BF16).reshape(-1, LINE) for v in (master, ema)]
    tables = tuple(jnp.asarray(v, BF16) for v in (group_table(), *spread_tables(), expand_table(), patch_table()))
    live = (jnp.arange(MB_DEV) < counts[0]).astype(jnp.int32)
    local_rows = jnp.sum(live * jnp.clip(valid_rows, 0, RES)).astype(F32)

    def early(after):
        clean, noise = gate([images, noise_draws], after) if after else (images, noise_draws)
        clean, noise = pixels(jnp.stack([clean, noise]))
        per_row = lambda v: jnp.repeat(v, PIX)[:, None]

        def inputs_of(sigma):
            noisy = clean + per_row(sigma) * noise
            skip, out_scale, in_scale = preconditioning_factors(sigma)
            x_in = jnp.pad((per_row(in_scale) * noisy).astype(BF16), ((0, 0), (0, LINE - 12)))
            return per_row(skip) * noisy, x_in, noise_features(sigma), per_row(out_scale)

        mask = pixel_live(counts, valid_rows)
        return inputs_of(karras(step_index)), inputs_of(karras(step_index + 1)), mask

    total = total_of(jnp.broadcast_to(local_rows, (8, LINE)), n)
    pixel_total = 3.0 * RES * total[0, 0]
    if direct:
        rooms = [jnp.pad(v, ((0, ROOM - SHARD), (0, 0))) for v in shards]
        (in_lo, in_hi, mask), pieces, before, second = gather_both(rooms[0], rooms[1], z, early)
        moves, flip = gather_moves(), (False,) * 4 + (True,) + (False,) * 4 + (True,)
        online = (pieces, moves, flip)
        (x_in,) = gate([in_hi[1]], [*before, in_lo[0], in_lo[1], in_lo[2], in_hi[0], in_hi[2], total])
        in_hi = (in_hi[0], x_in, *in_hi[2:])
    else:
        online, target = gather_plain(shards[0]), gather_plain(shards[1])
        in_lo, in_hi, mask = early(())
    model_o, saved = per_part(me, labels, online, in_hi, True, tables)
    if direct:
        target = (second(model_o), moves, flip)
    model_t, _ = per_part(me, labels, target, in_lo, False, tables)
    online_out = in_hi[0] + in_hi[3] * model_o[:, :12]
    target_out = in_lo[0] + in_lo[3] * model_t[:, :12]
    phi, out_scale = in_hi[2], in_hi[3]
    gap = online_out - target_out
    local_loss = jnp.sum(mask * jnp.square(gap))
    grad_model = out_scale * 2.0 * mask * gap / pixel_total
    bias_out = jnp.sum(grad_model.reshape(ROWS, 4, 3), axis=(0, 1))
    (h0s, h1, u1, h2, qkv, mixed, h3, u2, h4, vec, mod, emb, pre, wz, xp) = saved[:15]
    s_time, s_emb1, s_emb2, s_down, s11, s12, s_attn, s21, s22 = saved[15:]
    gm = tables[0]
    df = jnp.pad(grad_model, ((0, 0), (0, LINE - 12)))
    keep_top, send_top, rest, dh, du, dm, extra, dse = back_two_call(
        (me, df, wz, *tables[:5], vec, mod, emb, h4, u2, h3, qkv, mixed, h2, u1, s22, s21, s_attn, s12, s_emb2)
    )
    keep_low, send_low = back_one_call(
        (me, labels, dh, du, dm, extra, dse, gm, vec, emb, pre, phi, h1, h0s, xp, s11, s_down, s_emb1, s_time, rest)
    )
    small = jnp.concatenate([local_loss[None], bias_out])
    small = total_of(jnp.broadcast_to(small, (8, 4)), n)[0]
    if direct:
        part = jnp.concatenate([reduce_planes(keep_low, send_low), reduce_planes(keep_top, send_top)])
        reduced = reduce_column(part, z)[:SHARD].reshape(-1)
    else:
        both = [jnp.stack([k, s.astype(F32)], 2) for k, s in ((keep_low, send_low), (keep_top, send_top))]
        lines = jnp.concatenate(both).reshape(SHARDS, ROOM, LINE)[:, :SHARD].reshape(n, -1)
        reduced = lax.psum_scatter(lines, AXIS, scatter_dimension=0, tiled=True).reshape(-1)
    new_momentum = MOMENTUM * momentum + reduced
    new_master = master - LEARN_RATE * (reduced + MOMENTUM * new_momentum)
    new_ema = EMA_DECAY * ema + (1.0 - EMA_DECAY) * new_master
    return (small[0] / pixel_total, new_momentum, new_master, new_ema, small[1:])


def solution(mesh):
    n = mesh.shape[AXIS]

    def step(*args):
        return per_device(n, *args)

    return jax.shard_map(
        step,
        mesh=mesh,
        in_specs=(P(AXIS, None, None, None),) * 2 + (P(AXIS),) * 7,
        out_specs=(P(), P(AXIS), P(AXIS), P(AXIS), P()),
        check_vma=False,
    )
```

```python
import math

import jax
import jax.numpy as jnp
import numpy as np
from jax import lax
from jax.experimental import pallas as pl
from jax.experimental.pallas import tpu as pltpu
from jax.sharding import PartitionSpec as P

CH_BASE = 192
CH_MID = 384
EMB_DIM = 768
HEADS = 6
HEAD_DIM = 64
CLASSES = 1000
GROUPS = 32
RES = 32
MB_DEV = 2
DISCRETE = 40

EPSILON = 1e-05
SIGMA_DATA = 0.5
SIGMA_LOW = 0.002
SIGMA_HIGH = 80.0
RHO_POWER = 7.0
MOMENTUM = 0.9
EMA_DECAY = 0.9
LEARN_RATE = 2000.0

F32 = jnp.float32
BF16 = jnp.bfloat16
LINE = 128
HALF = RES // 2
PIX = HALF * HALF
ROWS = MB_DEV * PIX
GROUP_SIZE = PIX * (CH_MID // GROUPS)
CHUNK = 64
PADDED = 16 + MB_DEV * (PIX + 16)
NN = (((1,), (0,)), ((), ()))
NT = (((1,), (1,)), ((), ()))
TN = (((0,), (0,)), ((), ()))


class Place:
    pass


class Cut:
    def __init__(self):
        self.offset = 0

    def take(self, *shape):
        at = self.offset
        self.offset += math.prod(shape)
        return at // LINE


def block_place(cut):
    at = Place()
    at.gains = cut.take(4, CH_MID)
    at.conv_one = cut.take(9 * CH_MID, CH_MID)
    at.bias_one = cut.take(CH_MID)
    at.embed = cut.take(EMB_DIM, 2 * CH_MID)
    at.embed_bias = cut.take(2 * CH_MID)
    at.conv_two = cut.take(9 * CH_MID, CH_MID)
    at.bias_two = cut.take(CH_MID)
    return at


def places():
    cut, at = Cut(), Place()
    at.conv_in = cut.take(27, CH_BASE)
    at.bias_in = cut.take(CH_BASE)
    at.conv_down = cut.take(9 * CH_BASE, CH_MID)
    at.bias_down = cut.take(CH_MID)
    at.time_one = cut.take(CH_BASE, EMB_DIM)
    at.time_bias_one = cut.take(EMB_DIM)
    at.time_two = cut.take(EMB_DIM, EMB_DIM)
    at.time_bias_two = cut.take(EMB_DIM)
    at.class_table = cut.take(CLASSES, EMB_DIM)
    at.first = block_place(cut)
    at.second = block_place(cut)
    at.attn_gains = cut.take(2, CH_MID)
    at.attn_qkv = cut.take(CH_MID, 3 * CH_MID)
    at.attn_out = cut.take(CH_MID, CH_MID)
    at.attn_bias = cut.take(CH_MID)
    at.final_gains = cut.take(2, CH_MID)
    at.conv_out = cut.take(9 * CH_MID, 3)
    at.bias_out = cut.take(3)
    return at


AT = places()
TAIL = AT.conv_out
SHARDS, PLANE = 32, 8
SHARD = 2264
ROOM = 2272
ALL_LINES = SHARDS * SHARD
PLANES = [p * PLANE * SHARD for p in range(SHARDS // PLANE)]
BASE_ONE = AT.second.gains // 16 * 16
BASE_TWO = AT.first.conv_two // 16 * 16
BASE_THREE = AT.first.gains // 16 * 16

V_DOWN, V_G1, V_B11, V_B12, V_AG, V_AB, V_FG, V_G2, V_B21, V_B22 = 0, 1, 5, 6, 7, 9, 10, 12, 16, 17
VEC_ROWS = 24


def group_table():
    at = np.arange(CH_MID) // (CH_MID // GROUPS)
    return (at[:, None] == at[None, :]).astype(np.float32)


TAPS = 16


def spread_tables():
    select = np.zeros((LINE, LINE), np.float32)
    gather = np.zeros((LINE, LINE), np.float32)
    tile = np.zeros((LINE, LINE), np.float32)
    for ky in range(3):
        for kx in range(3):
            for a in range(2):
                for b in range(2):
                    dy, dx = (a + ky - 1) // 2, (b + kx - 1) // 2
                    shift = (dy + 1) * 3 + dx + 1
                    for c in range(3):
                        out = (a * 2 + b) * 3 + c
                        select[c * TAPS + ky * 3 + kx, shift * 12 + out] = 1.0
                        gather[out::12, out][:9] = 1.0
                        tile[c, out] = 1.0
    return select, gather, tile


def patch_table():
    pick = np.zeros((4, LINE, 32), np.float32)
    for a in range(2):
        for b in range(2):
            for ky in range(3):
                for kx in range(3):
                    (dy, ya), (dx, xb) = divmod(a + ky - 1, 2), divmod(b + kx - 1, 2)
                    shift = (dy + 1) * 3 + dx + 1
                    for c in range(3):
                        k = (ky * 3 + kx) * 3 + c
                        pick[a * 2 + b, shift * 12 + (ya * 2 + xb) * 3 + c, k // 2 + 16 * (k % 2)] = 1.0
    return pick


def expand_table():
    return (np.arange(3 * CH_MID)[None, :] // 3 == np.arange(CH_MID)[:, None]).astype(np.float32)


def colour(c):
    lane = lax.broadcasted_iota(jnp.int32, (1, 3 * CH_MID), 1)
    return lax.rem(lane, 3) == c


def first_lanes():
    return lax.broadcasted_iota(jnp.int32, (1, LINE), 1) < LINE // 2


def split3(v):
    hi = v.astype(BF16)
    rest = v - hi.astype(F32)
    mid = rest.astype(BF16)
    low = (rest - mid.astype(F32)).astype(BF16)
    return hi, mid, low


def dot(a, b, dims=NN):
    return lax.dot_general(a, b, dims, preferred_element_type=F32)


def dot3(a, b, dims=NN):
    rows = a.shape[0]
    hi, mid, low = split3(a)
    if rows % 16:
        out = dot(jnp.concatenate([p.astype(F32) for p in (hi, mid, low)], 0).astype(BF16), b, dims)
    else:
        out = dot(jnp.concatenate([hi, mid, low], 0), b, dims)
    return out[:rows] + out[rows : 2 * rows] + out[2 * rows :]


def outer(a, b):
    pa, pb = split3(a), split3(b)
    pairs = [(0, 0), (0, 1), (1, 0), (1, 1), (0, 2), (2, 0)]
    left = jnp.concatenate([pa[i].astype(F32) for i, _ in pairs], 0).astype(BF16)
    right = jnp.concatenate([pb[j].astype(F32) for _, j in pairs], 0).astype(BF16)
    return dot(left, right, TN)


def sigmoid(z):
    return 1.0 / (1.0 + jnp.exp(-z))


def silu(z):
    return z * sigmoid(z)


def silu_slope(z):
    s = sigmoid(z)
    return s * (1.0 + z * (1.0 - s))


def colsum(ref, base, count=PIX):
    def body(c, acc):
        return acc + jnp.sum(ref[pl.ds(pl.multiple_of(base + c * CHUNK, 8), CHUNK), :], 0, keepdims=True)

    return lax.fori_loop(0, count // CHUNK, body, jnp.zeros((1, ref.shape[1]), F32))


def eight(v):
    return jnp.broadcast_to(v, (8, v.shape[1]))


def group_mean(v, gm_ref):
    return dot3(eight(v), gm_ref[...])[:1] * (1.0 / GROUP_SIZE)


def group_stats(x_ref, img, gm_ref):
    mean = group_mean(colsum(x_ref, img * PIX), gm_ref)

    def body(c, acc):
        gap = x_ref[pl.ds(pl.multiple_of(img * PIX + c * CHUNK, 8), CHUNK), :] - mean
        return acc + jnp.sum(gap * gap, 0, keepdims=True)

    square = lax.fori_loop(0, PIX // CHUNK, body, jnp.zeros((1, CH_MID), F32))
    return mean, lax.rsqrt(group_mean(square, gm_ref) + EPSILON)


def norm_to(pbuf, x_ref, stats, scales, act):
    for img in range(MB_DEV):
        (mean, rstd), (k, o) = stats[img], scales[img]

        def body(c, carry):
            r = pl.multiple_of(img * PIX + c * CHUNK, 8)
            z = (x_ref[pl.ds(r, CHUNK), :] - mean) * rstd * k + o
            pbuf[pl.ds(r + 8, CHUNK), :] = silu(z) if act else z
            return carry

        lax.fori_loop(0, PIX // CHUNK, body, 0)


def norm_back(x_ref, d_ref, stats, scales, act, gm_ref, emit):
    sums = []
    for img in range(MB_DEV):
        (mean, rstd), (k, o) = stats[img], scales[img]

        def one(c, carry):
            r = pl.multiple_of(img * PIX + c * CHUNK, 8)
            xhat = (x_ref[pl.ds(r, CHUNK), :] - mean) * rstd
            dz = d_ref[pl.ds(r, CHUNK), :]
            if act:
                dz = dz * silu_slope(xhat * k + o)
                d_ref[pl.ds(r, CHUNK), :] = dz
            return (carry[0] + jnp.sum(dz, 0, keepdims=True), carry[1] + jnp.sum(dz * xhat, 0, keepdims=True))

        zero = jnp.zeros((1, CH_MID), F32)
        a, b = lax.fori_loop(0, PIX // CHUNK, one, (zero, zero))
        m1, m2 = group_mean(a * k, gm_ref), group_mean(b * k, gm_ref)

        def two(c, carry):
            r = pl.multiple_of(img * PIX + c * CHUNK, 8)
            xhat = (x_ref[pl.ds(r, CHUNK), :] - mean) * rstd
            emit(r, rstd * (d_ref[pl.ds(r, CHUNK), :] * k - m1 - xhat * m2))
            return carry

        lax.fori_loop(0, PIX // CHUNK, two, 0)
        sums.append((a, b))
    return sums


def clear_pads(sbuf):
    for k in range(3):
        for r in range(0, PADDED, PIX + 16):
            sbuf[k, pl.ds(r, 16), :] = jnp.zeros((16, sbuf.shape[2]), BF16)


def shift_to(sbuf, pbuf):
    column = lax.rem(lax.broadcasted_iota(jnp.int32, (CHUNK, CH_MID), 0), HALF)
    for r in range(0, ROWS, CHUNK):
        for k in range(3):
            v = pbuf[r + 7 + k : r + 7 + k + CHUNK, :]
            if k == 0:
                v = jnp.where(column == 0, 0.0, v)
            if k == 2:
                v = jnp.where(column == HALF - 1, 0.0, v)
            start = r + 16 * (r // PIX + 1)
            sbuf[k, start : start + CHUNK, :] = v.astype(BF16)


def shifted(sbuf, k, row):
    first = sbuf[k, pl.ds(pl.multiple_of(row, 16), PIX), :]
    second = sbuf[k, pl.ds(pl.multiple_of(row + PIX + 16, 16), PIX), :]
    return jnp.concatenate([first, second], 0)


def conv_forward(sbuf, w_ref, out_ref):
    def body(t, carry):
        lhs = shifted(sbuf, lax.rem(t, 3), lax.div(t, 3) * 16)
        out_ref[...] += dot(lhs, w_ref[pl.ds(pl.multiple_of(t * CH_MID, CH_MID), CH_MID), :])
        return carry

    lax.fori_loop(0, 9, body, 0)


def put_lines(g_ref, at, value, step, more=None):
    n = value.shape[0]
    low = at // 8 * 8
    start = low if more is None else pl.multiple_of(low + more, 8)
    view = g_ref.at[pl.ds(start, min(n * step + 8, g_ref.shape[0] - low)), :] if more is None else g_ref.at[pl.ds(start, n * step + 8), :]
    for j in range(step):
        view[pl.ds(at - low + j, n, stride=step), :] = value[:, j * LINE : (j + 1) * LINE]


def put_row(g_ref, at, row):
    for j in range(row.shape[1] // LINE):
        g_ref[pl.ds(at + j, 1), :] = row[:, j * LINE : (j + 1) * LINE]


def conv_back(sbuf, at_ref, w_ref, dx_ref, g_ref, at):
    dx_ref[...] = jnp.zeros_like(dx_ref)

    def body(s, carry):
        t = 8 - s
        d = shifted(sbuf, lax.rem(s, 3), lax.div(s, 3) * 16)
        w = w_ref[pl.ds(pl.multiple_of(t * CH_MID, CH_MID), CH_MID), :]
        dx_ref[...] += dot(d, w, NT)
        put_lines(g_ref, at, dot(at_ref[...], d), 3, t * (3 * CH_MID))
        return carry

    lax.fori_loop(0, 9, body, 0)


def transpose_to(at_ref, pbuf):
    for c in range(ROWS // LINE):
        at_ref[:, c * LINE : (c + 1) * LINE] = pbuf[8 + c * LINE : 8 + (c + 1) * LINE, :].T.astype(BF16)


class Lines:
    def __init__(self, held, wide):
        self.held, self.wide = held, wide

    def take(self, span):
        l0, l1 = span
        first = l0 // SHARD
        self.low = first * SHARD + (l0 - first * SHARD) // 16 * 16
        for s in range(first, (l1 - 1) // SHARD + 1):
            start = max(l0 - s * SHARD, 0) // 16 * 16
            count = -(-min(l1 - s * SHARD, SHARD) // 16) * 16 - start
            to = s * SHARD + start - self.low
            block = self.held.at[s // PLANE, s % PLANE]
            whole, rest = divmod(count, 256)

            def body(c, carry):
                self.wide[pl.ds(pl.multiple_of(to + c * 256, 8), 256), :] = block[
                    pl.ds(pl.multiple_of(start + c * 256, 16), 256), :
                ].astype(F32)
                return carry

            lax.fori_loop(0, whole, body, 0)
            if rest:
                done = whole * 256
                self.wide[to + done : to + count, :] = block[start + done : start + count, :].astype(F32)

    def line(self, at, scratch):
        shard = lax.div(at, SHARD)
        row = at - shard * SHARD
        low = pl.multiple_of(lax.div(row, 16) * 16, 16)
        scratch[...] = self.held[lax.div(shard, PLANE), lax.rem(shard, PLANE), pl.ds(low, 16), :].astype(F32)
        return scratch[pl.ds(row - low, 1), :]

    def matrix(self, w_ref, at, rows, step):
        block = 128 if rows % 192 else 192
        base = at - self.low
        low = base // 8 * 8

        def body(c, carry):
            r = pl.multiple_of(c * block, block)
            view = self.wide.at[pl.ds(pl.multiple_of(low + r * step, 8), block * step + 8), :]
            for j in range(step):
                v = view[pl.ds(base - low + j, block, stride=step), :]
                w_ref[pl.ds(r, block), j * LINE : (j + 1) * LINE] = v.astype(BF16)
            return carry

        lax.fori_loop(0, rows // block, body, 0)

    def row(self, at, step):
        base = at - self.low
        return jnp.concatenate([self.wide[pl.ds(base + j, 1), :] for j in range(step)], 1)


def attention_pair(qkv_ref, img, pair):
    rows = pl.ds(pl.multiple_of(img * PIX, PIX), PIX)
    return [qkv_ref[rows, part * CH_MID + pair * LINE : part * CH_MID + (pair + 1) * LINE] for part in range(3)]


def lane_half():
    return lax.broadcasted_iota(jnp.int32, (1, LINE), 1) < HEAD_DIM


def keep_half(v, half, side):
    mine = half if side == 0 else jnp.logical_not(half)
    return jnp.where(mine, v.astype(F32), 0.0).astype(BF16)


SPAN_TIME = (AT.time_one, AT.class_table)
SPAN_EMB1 = (AT.first.embed, AT.first.conv_two)
SPAN_EMB2 = (AT.second.embed, AT.second.conv_two)
SPAN_DOWN = (AT.conv_in, AT.time_one)
SPAN_ONE1 = (AT.first.gains, AT.first.embed)
SPAN_TWO1 = (AT.first.conv_two, AT.second.gains)
SPAN_ATTN = (AT.attn_gains, ALL_LINES)
SPAN_ONE2 = (AT.second.gains, AT.second.embed)
SPAN_TWO2 = (AT.second.conv_two, AT.attn_gains)


def block_scales(vec, row, mod_ref=None, mod_row=0):
    gain, shift = vec[row : row + 1, :], vec[row + 1 : row + 2, :]
    if mod_ref is None:
        return [(gain, shift)] * MB_DEV
    out = []
    for img in range(MB_DEV):
        scale = 1.0 + mod_ref[mod_row + img : mod_row + img + 1, :CH_MID]
        out.append((gain * scale, shift * scale + mod_ref[mod_row + img : mod_row + img + 1, CH_MID:]))
    return out


def upsample_masks(shift):
    dy, dx = shift // 3 - 1, shift % 3 - 1
    p = lax.broadcasted_iota(jnp.int32, (ROWS, 1), 0)
    i, j = lax.rem(lax.div(p, HALF), HALF), lax.rem(p, HALF)
    inside = (i + dy >= 0) & (i + dy < HALF) & (j + dx >= 0) & (j + dx < HALF)
    lane = lax.broadcasted_iota(jnp.int32, (1, LINE), 1)
    return inside & (lane >= shift * 12) & (lane < shift * 12 + 12), dy * HALF + dx


def forward_kernel(save, moves, flip, *refs):
    me, labels, x_in, phi, gm, sel, gat, tile, expand, pick = refs[:10]
    sources = max(move[0] for move in moves) + 1
    pieces, refs = refs[10 : 10 + sources], refs[10 + sources :]
    f_out = refs[0]
    (h0s, h1, u1, h2, qkv, mixed, h3, u2, h4, vec, mod, emb, pre, wz, xp) = refs[1:16]
    if save:
        sw_time, sw_emb1, sw_emb2, sw_down, sw_11, sw_12, sw_attn, sw_21, sw_22 = refs[16:25]
    held, wide, w_ref, w_sq, sbuf, pbuf, h0p, table, w_in, b_out, sems, save_sem = refs[25 if save else 16 :]
    src = Lines(held, wide)
    arriving = []
    for plane in range(SHARDS // PLANE):
        copies = []
        for n, lead, r, row, rows in moves:
            target = held.at[plane, r ^ me[0], pl.ds(row, rows), :]
            source = pieces[n].at[plane, lead] if flip[n] else pieces[n].at[lead, plane]
            copies.append(pltpu.make_async_copy(source, target, sems.at[plane]))
        for copy in copies:
            copy.start()
        arriving.append(copies)

    def arrive(plane):
        for copy in arriving[plane]:
            copy.wait()

    pending = []

    def keep(source, target):
        if save:
            cp = pltpu.make_async_copy(source, target, save_sem)
            cp.start()
            pending.append(cp)

    def free():
        while pending:
            pending.pop().wait()

    clear_pads(sbuf)
    pbuf[0:8, :] = jnp.zeros((8, CH_MID), F32)
    pbuf[ROWS + 8 : ROWS + 16, :] = jnp.zeros((8, CH_MID), F32)
    arrive(0)
    src.take(SPAN_TIME)
    src.matrix(w_sq.at[0], AT.time_one, CH_BASE, 6)
    src.matrix(w_sq.at[1], AT.time_two, EMB_DIM, 6)
    pre[...] = dot3(phi[...], w_sq[0, :CH_BASE, :]) + src.row(AT.time_bias_one, 6)
    emb[...] = dot3(silu(pre[...]), w_sq[1]) + src.row(AT.time_bias_two, 6)
    for n in range(MB_DEV):
        for j in range(6):
            cols = slice(j * LINE, (j + 1) * LINE)
            emb[n : n + 1, cols] += src.line(AT.class_table + labels[n] * 6 + j, table)
    keep(w_sq.at[1], sw_time if save else None)
    se = silu(emb[...])
    arrive(1)
    src.take(SPAN_EMB1)
    src.matrix(w_sq.at[0], AT.first.embed, EMB_DIM, 6)
    m1 = dot3(se, w_sq[0]) + src.row(AT.first.embed_bias, 6)
    free()
    keep(w_sq.at[0], sw_emb1 if save else None)
    mod[0:2, :] = m1[0:2]
    mod[4:8, :] = jnp.zeros((4, EMB_DIM), F32)

    src.take(SPAN_DOWN)
    trio = [wide[pl.ds(j, 16, stride=3), :] for j in range(3)]
    turned = [pltpu.roll(v, LINE // 2, 1) for v in trio[1:]]
    w_in[0:16, 0:LINE] = trio[0]
    w_in[0:16, LINE : 2 * LINE] = trio[1]
    w_in[16:32, 0:LINE] = jnp.where(first_lanes(), turned[0], turned[1])
    w_in[16:32, LINE : 2 * LINE] = turned[1]
    w_low = w_in[...].astype(BF16)
    spread = dot(x_in[...], gat[...], NT)
    around = jnp.zeros((ROWS, LINE), F32)
    for shift in range(9):
        inside, by = upsample_masks(shift)
        around = around + jnp.where(inside, spread if by == 0 else pltpu.roll(spread, (-by) % ROWS, 0), 0.0)
    around = around.astype(BF16)
    one = (lax.broadcasted_iota(jnp.int32, (1, 32), 1) == 29).astype(F32)
    for ph in range(4):
        patch = (dot(around, pick[ph]) + one).astype(BF16)
        xp[ph * ROWS : (ph + 1) * ROWS, :] = patch
        h0s[ph * ROWS : (ph + 1) * ROWS, :] = dot(patch, w_low).astype(BF16)
    for j in range(3):
        vec[V_DOWN : V_DOWN + 1, j * LINE : (j + 1) * LINE] = src.row(AT.bias_down + j, 1)
    src.matrix(w_ref, AT.conv_down, 9 * CH_BASE, 3)
    free()
    keep(w_ref.at[pl.ds(0, 9 * CH_BASE), :], sw_down if save else None)
    h1[...] = jnp.broadcast_to(vec[V_DOWN : V_DOWN + 1, :], (ROWS, CH_MID))
    p = lax.broadcasted_iota(jnp.int32, (ROWS, 1), 0)
    has_left, has_up = lax.rem(p, HALF) > 0, lax.rem(lax.div(p, HALF), HALF) > 0
    for ph in range(4):
        h0p[0:32, :] = jnp.zeros((32, h0p.shape[1]), F32)
        h0p[32 : 32 + ROWS, :] = h0s[ph * ROWS : (ph + 1) * ROWS, :].astype(F32)
        for ky in ((0, 2) if ph // 2 else (1,)):
            for kx in ((0, 2) if ph % 2 else (1,)):
                back = (16 if ky == 0 else 0) + (1 if kx == 0 else 0)
                v = h0p[32 - back : 32 - back + ROWS, :]
                if ky == 0:
                    v = jnp.where(has_up, v, 0.0)
                if kx == 0:
                    v = jnp.where(has_left, v, 0.0)
                t = 3 * ky + kx
                h1[...] += dot(v[:, :CH_BASE].astype(BF16), w_ref[t * CH_BASE : (t + 1) * CH_BASE, :])

    def vectors(row, at, count):
        for n in range(count):
            for j in range(3):
                vec[row + n : row + n + 1, j * LINE : (j + 1) * LINE] = src.row(at + 3 * n + j, 1)

    def half_block(x_ref, scales, bias_row, add_ref, out_ref, at, target):
        src.matrix(w_ref, at, 9 * CH_MID, 3)
        keep(w_ref, target)
        stats = [group_stats(x_ref, img, gm) for img in range(MB_DEV)]
        norm_to(pbuf, x_ref, stats, scales, True)
        shift_to(sbuf, pbuf)
        bias = jnp.broadcast_to(vec[bias_row : bias_row + 1, :], (ROWS, CH_MID))
        out_ref[...] = bias if add_ref is None else add_ref[...] + bias
        conv_forward(sbuf, w_ref, out_ref)

    def block(h_in, u, h_out, prefix, g_row, b1_row, b2_row, mod_row, spans, targets):
        src.take(spans[0])
        free()
        vectors(g_row, prefix.gains, 4)
        vectors(b1_row, prefix.bias_one, 1)
        half_block(h_in, block_scales(vec, g_row), b1_row, None, u, prefix.conv_one, targets[0])
        src.take(spans[1])
        free()
        vectors(b2_row, prefix.bias_two, 1)
        half_block(u, block_scales(vec, g_row + 2, mod, mod_row), b2_row, h_in, h_out, prefix.conv_two, targets[1])

    saved = (sw_11, sw_12, sw_21, sw_22) if save else (None,) * 4
    arrive(2)
    block(h1, u1, h2, AT.first, V_G1, V_B11, V_B12, 0, (SPAN_ONE1, SPAN_TWO1), saved[:2])

    arrive(3)
    src.take(SPAN_ATTN)
    free()
    vectors(V_AG, AT.attn_gains, 2)
    vectors(V_AB, AT.attn_bias, 1)
    vectors(V_FG, AT.final_gains, 2)
    base = AT.conv_out - src.low
    tap_row = lax.broadcasted_iota(jnp.int32, (TAPS, 1), 0) < 9
    taps = [jnp.where(tap_row, wide[pl.ds(base + j, TAPS, stride=9), :], 0.0) for j in range(9)]
    taps = jnp.concatenate(taps, 1)
    rows_out = jnp.concatenate([jnp.where(colour(c), taps, 0.0) for c in range(3)], 0).astype(BF16)
    wz[...] = jnp.zeros_like(wz)
    wz[0 : 3 * TAPS, :] = dot(rows_out, expand[...], NT).astype(BF16)
    last = AT.bias_out - src.low
    b_out[...] = dot(eight(wide[last : last + 1, :]).astype(BF16), tile[...])
    for part in range(3):
        base = AT.attn_qkv - src.low
        for j in range(3):
            v = wide[pl.ds(base + part * 3 + j, CH_MID, stride=9), :]
            w_ref[part * CH_MID : (part + 1) * CH_MID, j * LINE : (j + 1) * LINE] = v.astype(BF16)
    src.matrix(w_ref.at[pl.ds(3 * CH_MID, CH_MID), :], AT.attn_out, CH_MID, 3)
    keep(w_ref.at[pl.ds(0, 4 * CH_MID), :], sw_attn if save else None)
    stats = [group_stats(h2, img, gm) for img in range(MB_DEV)]
    norm_to(pbuf, h2, stats, block_scales(vec, V_AG), False)
    n_low = pbuf[8 : 8 + ROWS, :].astype(BF16)
    for part in range(3):
        v = dot(n_low, w_ref[part * CH_MID : (part + 1) * CH_MID, :])
        qkv[:, part * CH_MID : (part + 1) * CH_MID] = v.astype(BF16)
    half = lane_half()

    def heads(img, carry):
        for pair in range(HEADS // 2):
            q, k, v = attention_pair(qkv, img, pair)
            outs = []
            for side in range(2):
                s = dot(keep_half(q, half, side), k, NT) * HEAD_DIM ** (-0.5)
                e = jnp.exp(s - jnp.max(s, 1, keepdims=True))
                prob = (e / jnp.sum(e, 1, keepdims=True)).astype(BF16)
                outs.append(dot(prob, v))
            mixed[pl.ds(pl.multiple_of(img * PIX, PIX), PIX), pair * LINE : (pair + 1) * LINE] = jnp.where(
                half, outs[0], outs[1]
            ).astype(BF16)
        return carry

    lax.fori_loop(0, MB_DEV, heads, 0)
    h3[...] = h2[...] + dot(mixed[...], w_ref[3 * CH_MID : 4 * CH_MID, :]) + vec[V_AB : V_AB + 1, :]

    src.take(SPAN_EMB2)
    src.matrix(w_sq.at[1], AT.second.embed, EMB_DIM, 6)
    m2 = dot3(silu(emb[...]), w_sq[1]) + src.row(AT.second.embed_bias, 6)
    mod[2:4, :] = m2[0:2]
    free()
    keep(w_sq.at[1], sw_emb2 if save else None)
    block(h3, u2, h4, AT.second, V_G2, V_B21, V_B22, 2, (SPAN_ONE2, SPAN_TWO2), saved[2:])

    stats = [group_stats(h4, img, gm) for img in range(MB_DEV)]
    norm_to(pbuf, h4, stats, block_scales(vec, V_FG), True)
    z = dot(pbuf[8 : 8 + ROWS, :].astype(BF16), wz[...], NT)
    t_all = dot3(z, sel[...])
    u_all = jnp.zeros((ROWS, LINE), F32)
    for shift in range(9):
        inside, by = upsample_masks(shift)
        moved = t_all if by == 0 else pltpu.roll(t_all, (-by) % ROWS, 0)
        u_all = u_all + jnp.where(inside, moved, 0.0)
    f_out[...] = dot3(u_all, gat[...]) + b_out[0:1, :]
    free()


def vmem(*shape_dtype):
    return pltpu.VMEM(*shape_dtype)


VM = pl.BlockSpec(memory_space=pltpu.VMEM)
HB = pl.BlockSpec(memory_space=pl.ANY)
SM = pl.BlockSpec(memory_space=pltpu.SMEM)


def state_shapes():
    act = ((ROWS, CH_MID), F32)
    return [
        ((4 * ROWS, 256), BF16),
        act, act, act,
        ((ROWS, 3 * CH_MID), BF16),
        ((ROWS, CH_MID), BF16),
        act, act, act,
        ((VEC_ROWS, CH_MID), F32),
        ((8, EMB_DIM), F32),
        ((8, EMB_DIM), F32),
        ((8, EMB_DIM), F32),
        ((LINE, CH_MID), BF16),
        ((4 * ROWS, 32), BF16),
    ]


def weight_shapes():
    sq = ((EMB_DIM, EMB_DIM), BF16)
    conv = ((9 * CH_MID, CH_MID), BF16)
    return [sq, sq, sq, ((9 * CH_BASE, CH_MID), BF16), conv, conv, ((4 * CH_MID, CH_MID), BF16), conv, conv]


def forward_call(save, me, labels, lines, x_in, phi, tables):
    pieces, moves, flip = lines
    sds = lambda s: jax.ShapeDtypeStruct(*s)
    outs = [sds(((ROWS, LINE), F32))]
    out_specs = [VM]
    state = state_shapes()
    scratch = []
    if save:
        outs += [sds(s) for s in state] + [sds(s) for s in weight_shapes()]
        out_specs += [VM] * len(state) + [HB] * len(weight_shapes())
    else:
        scratch += [vmem(*s) for s in state]
    scratch += [
        vmem((SHARDS // PLANE, PLANE, ROOM, LINE), BF16),
        vmem((10432, LINE), F32),
        vmem((9 * CH_MID, CH_MID), BF16),
        vmem((2, EMB_DIM, EMB_DIM), BF16),
        vmem((3, PADDED, CH_MID), BF16),
        vmem((ROWS + 16, CH_MID), F32),
        vmem((ROWS + 48, 256), F32),
        vmem((16, LINE), F32),
        vmem((32, 2 * LINE), F32),
        vmem((8, LINE), F32),
        pltpu.SemaphoreType.DMA((SHARDS // PLANE,)),
        pltpu.SemaphoreType.DMA,
    ]

    def body(*refs):
        forward_kernel(save, moves, flip, *refs)

    return pl.pallas_call(
        body,
        out_shape=outs,
        in_specs=[SM] * 2 + [VM] * 8 + [HB] * len(pieces),
        out_specs=out_specs,
        scratch_shapes=scratch,
        name="forward_save" if save else "forward_plain",
        **kernel_params(),
    )(me, labels, x_in, phi, *tables, *pieces)


def column_sum(pbuf):
    def body(c, acc):
        return acc + jnp.sum(pbuf[pl.ds(pl.multiple_of(c * CHUNK + 8, 8), CHUNK), :], 0, keepdims=True)

    return lax.fori_loop(0, ROWS // CHUNK, body, jnp.zeros((1, CH_MID), F32))


def refill(pbuf, source):
    for c in range(0, ROWS, CHUNK):
        pbuf[8 + c : 8 + c + CHUNK, :] = source[c : c + CHUNK, :]


def block_back_two(dh, u_ref, at, base, rows, vec, mod, mod_row, weights, tools, g, dm):
    g_row, b1_row, b2_row = rows
    sbuf, pbuf, dx, at_ref, gm = tools
    put_row(g, at.bias_two - base, colsum(dh, 0, ROWS))
    u_stats = [group_stats(u_ref, img, gm) for img in range(MB_DEV)]
    scales = block_scales(vec, g_row + 2, mod, mod_row)
    norm_to(pbuf, u_ref, u_stats, scales, True)
    transpose_to(at_ref, pbuf)
    refill(pbuf, dh)
    shift_to(sbuf, pbuf)
    conv_back(sbuf, at_ref, weights.take(), dx, g, at.conv_two - base)
    weights.begin()

    def emit_inner(r, v):
        pbuf[pl.ds(r + 8, CHUNK), :] = v

    sums = norm_back(u_ref, dx, u_stats, scales, True, gm, emit_inner)
    gain, shift = vec[g_row + 2 : g_row + 3, :], vec[g_row + 3 : g_row + 4, :]
    d_gain = d_shift = 0.0
    dm[...] = jnp.zeros_like(dm)
    for img, (a, b) in enumerate(sums):
        scale = 1.0 + mod[mod_row + img : mod_row + img + 1, :CH_MID]
        d_gain, d_shift = d_gain + scale * b, d_shift + scale * a
        dm[img : img + 1, :CH_MID] = gain * b + shift * a
        dm[img : img + 1, CH_MID:] = a
    return d_gain, d_shift


def block_back_one(dh, x_ref, at, base, rows, vec, weights, tools, g):
    g_row, b1_row, b2_row = rows
    sbuf, pbuf, dx, at_ref, gm = tools
    put_row(g, at.bias_one - base, column_sum(pbuf))
    shift_to(sbuf, pbuf)
    stats = [group_stats(x_ref, img, gm) for img in range(MB_DEV)]
    scales = block_scales(vec, g_row)
    norm_to(pbuf, x_ref, stats, scales, True)
    transpose_to(at_ref, pbuf)
    conv_back(sbuf, at_ref, weights.take(), dx, g, at.conv_one - base)
    weights.begin()

    def emit_outer(r, v):
        dh[pl.ds(r, CHUNK), :] += v

    sums = norm_back(x_ref, dx, stats, scales, True, gm, emit_outer)
    put_row(g, at.gains - base, sums[0][1] + sums[1][1])
    put_row(g, at.gains + 3 - base, sums[0][0] + sums[1][0])


def rowsum(v):
    return jnp.sum(v, 0, keepdims=True)


def put_outer(g, at, left, right):
    for c in range(-(-left.shape[1] // LINE)):
        piece = outer(left[:, c * LINE : (c + 1) * LINE], right)
        put_lines(g, at + c * LINE * (EMB_DIM // LINE), piece, EMB_DIM // LINE)


class Weights:
    def __init__(self, sources, slots, sems):
        self.copies = []
        for n, source in enumerate(sources):
            target = slots.at[n % 2, pl.ds(0, source.shape[0]), :]
            self.copies.append((pltpu.make_async_copy(source, target, sems.at[n % 2]), target))
        self.begun = self.done = 0

    def begin(self):
        if self.begun < len(self.copies):
            self.copies[self.begun][0].start()
            self.begun += 1

    def take(self):
        copy, target = self.copies[self.done]
        copy.wait()
        self.done += 1
        return target


class Leave:
    def __init__(self, me, g, base, keep, send, stage, sems):
        self.core, self.place = lax.rem(me[0], 2), lax.div(me[0], 2)
        self.g, self.base, self.outs, self.stage, self.sems = g, base, (keep, send), stage, sems
        self.copies = []

    def plane(self, plane):
        for q in range(PLANE // 2):
            at = q ^ self.place
            first = PLANES[plane] + 2 * q * SHARD - self.base
            for side in range(2):
                core = 1 - self.core if side else self.core
                start = first + core * SHARD
                stage = self.stage.at[2 * q + side]
                whole, rest = divmod(ROOM, 288)

                def body(c, carry):
                    lines = self.g[pl.ds(pl.multiple_of(start + c * 288, 8), 288), :]
                    stage[pl.ds(pl.multiple_of(c * 288, 16), 288), :] = lines.astype(BF16)
                    return carry

                lax.fori_loop(0, whole, body, 0)
                lines = self.g[pl.ds(pl.multiple_of(start + whole * 288, 8), rest), :]
                stage[whole * 288 :, :] = lines.astype(BF16)
                copy = pltpu.make_async_copy(stage, self.outs[side].at[at], self.sems.at[side])
                copy.start()
                self.copies.append(copy)

    def below(self, count, rest):
        copy = pltpu.make_async_copy(self.g.at[pl.ds(0, count), :], rest, self.sems.at[2])
        copy.start()
        self.copies.append(copy)

    def wait(self):
        for copy in self.copies:
            copy.wait()


def clear_lines(g, first, count):
    if count:
        g[first : first + count, :] = jnp.zeros((count, LINE), F32)


def prepare(sbuf, pbuf):
    clear_pads(sbuf)
    pbuf[0:8, :] = jnp.zeros((8, CH_MID), F32)
    pbuf[ROWS + 8 : ROWS + 16, :] = jnp.zeros((8, CH_MID), F32)


def back_top_kernel(*refs):
    me, df, wz, gm, sel, gat, tile, expand, vec, mod, emb, h4, u2, h3, qkv, mixed, h2, s22, s21, s_attn, s_emb = refs[:21]
    keep, send, rest, dh, dse = refs[21:26]
    g, slots, sbuf, pbuf, dx, at_ref, stage, sems, out_sems, w_sq, dqkv, dm, sq_sem = refs[26:]
    base = BASE_ONE
    weights = Weights([s22, s21, s_attn], slots, sems)
    weights.begin()
    weights.begin()
    sq_copy = pltpu.make_async_copy(s_emb, w_sq, sq_sem)
    sq_copy.start()
    prepare(sbuf, pbuf)
    clear_lines(g, TAIL - base, g.shape[0] - (TAIL - base))
    tools = (sbuf, pbuf, dx, at_ref, gm)

    stats = [group_stats(h4, img, gm) for img in range(MB_DEV)]
    scales = block_scales(vec, V_FG)
    norm_to(pbuf, h4, stats, scales, True)
    transpose_to(at_ref, pbuf)
    spread = dot(df[...].astype(BF16), gat[...], NT)
    dt = jnp.zeros((ROWS, LINE), F32)
    for shift in range(9):
        inside, by = upsample_masks(shift)
        part = jnp.where(inside, spread, 0.0)
        dt = dt + (part if by == 0 else pltpu.roll(part, by % ROWS, 0))
    dz = dot(dt.astype(BF16), sel[...], NT)
    parts = split3(dz)
    dwz = dot(at_ref[...], parts[0]) + dot(at_ref[...], parts[1]) + dot(at_ref[...], parts[2])
    dx[...] = dot(parts[0], wz[...]) + dot(parts[1], wz[...]) + dot(parts[2], wz[...])
    d_rows = dot3(dwz.T[0 : 3 * TAPS, :], expand[...])
    d_taps = jnp.zeros((TAPS, 3 * CH_MID), F32)
    for c in range(3):
        d_taps = d_taps + jnp.where(colour(c), d_rows[c * TAPS : (c + 1) * TAPS, :], 0.0)
    for j in range(9):
        g[pl.ds(TAIL - base + j, 9, stride=9), :] = d_taps[0:9, j * LINE : (j + 1) * LINE]
    b_row = AT.bias_out - base
    g[b_row : b_row + 1, :] = dot3(eight(colsum(df, 0, ROWS)), tile[...], NT)[0:1]

    def emit_first(r, v):
        dh[pl.ds(r, CHUNK), :] = v

    sums = norm_back(h4, dx, stats, scales, True, gm, emit_first)
    put_row(g, AT.final_gains - base, sums[0][1] + sums[1][1])
    put_row(g, AT.final_gains + 3 - base, sums[0][0] + sums[1][0])

    rows = (V_G2, V_B21, V_B22)
    d_gain, d_shift = block_back_two(dh, u2, AT.second, base, rows, vec, mod, 2, weights, tools, g, dm)
    put_row(g, AT.second.gains + 6 - base, d_gain)
    put_row(g, AT.second.gains + 9 - base, d_shift)
    block_back_one(dh, h3, AT.second, base, rows, vec, weights, tools, g)
    se = silu(emb[...])
    put_outer(g, AT.second.embed - base, se, dm[...])
    put_row(g, AT.second.embed_bias - base, rowsum(dm[...]))
    sq_copy.wait()
    dse[...] = dot3(dm[...], w_sq[...], NT)

    put_row(g, AT.attn_bias - base, colsum(dh, 0, ROWS))
    w = weights.take()
    d_low = dh[...].astype(BF16)
    for c in range(ROWS // LINE):
        at_ref[:, c * LINE : (c + 1) * LINE] = mixed[c * LINE : (c + 1) * LINE, :].astype(F32).T.astype(BF16)
    put_lines(g, AT.attn_out - base, dot(at_ref[...], d_low), 3)
    pbuf[8 : 8 + ROWS, :] = dot(d_low, w[3 * CH_MID : 4 * CH_MID, :], NT)
    half = lane_half()
    scale = HEAD_DIM ** (-0.5)

    def heads(img, carry):
        rows = pl.ds(pl.multiple_of(img * PIX, PIX), PIX)
        for pair in range(HEADS // 2):
            q, k, v = attention_pair(qkv, img, pair)
            cols = slice(pair * LINE, (pair + 1) * LINE)
            do = pbuf[pl.ds(pl.multiple_of(img * PIX + 8, 8), PIX), cols].astype(BF16)
            dqs, dks, dvs = [], [], []
            for side in range(2):
                s = dot(keep_half(k, half, side), q, NT) * scale
                e = jnp.exp(s - jnp.max(s, 0, keepdims=True))
                prob = e / jnp.sum(e, 0, keepdims=True)
                dvs.append(dot(prob.astype(BF16), do))
                dp = dot(keep_half(v, half, side), do, NT)
                ds = prob * (dp - jnp.sum(dp * prob, 0, keepdims=True))
                dks.append(dot(ds.astype(BF16), q))
                dqs.append(dot(ds.T.astype(BF16), k))
            for part, pieces in enumerate((dqs, dks, dvs)):
                value = jnp.where(half, pieces[0], pieces[1])
                if part < 2:
                    value = value * scale
                dqkv[rows, part * CH_MID + pair * LINE : part * CH_MID + (pair + 1) * LINE] = value.astype(BF16)
        return carry

    lax.fori_loop(0, MB_DEV, heads, 0)
    stats = [group_stats(h2, img, gm) for img in range(MB_DEV)]
    scales = block_scales(vec, V_AG)
    norm_to(pbuf, h2, stats, scales, False)
    transpose_to(at_ref, pbuf)
    dx[...] = jnp.zeros_like(dx)
    for part in range(3):
        d = dqkv[:, part * CH_MID : (part + 1) * CH_MID]
        dw = dot(at_ref[...], d)
        for j in range(3):
            g[pl.ds(AT.attn_qkv - base + part * 3 + j, CH_MID, stride=9), :] = dw[:, j * LINE : (j + 1) * LINE]
        dx[...] += dot(d, w[part * CH_MID : (part + 1) * CH_MID, :], NT)
    weights.begin()

    def emit(r, v):
        dh[pl.ds(r, CHUNK), :] += v

    sums = norm_back(h2, dx, stats, scales, False, gm, emit)
    put_row(g, AT.attn_gains - base, sums[0][1] + sums[1][1])
    put_row(g, AT.attn_gains + 3 - base, sums[0][0] + sums[1][0])

    leave = Leave(me, g, base, keep, send, stage, out_sems)
    leave.plane(3)
    leave.below(PLANES[3] - base, rest)
    leave.wait()


def back_second_half_kernel(*refs):
    me, dh, gm, vec, mod, u1, s12, rest_in = refs[:8]
    keep, send, rest, du, dm, extra = refs[8:14]
    g, slots, sbuf, pbuf, dx, at_ref, stage, sems, out_sems, in_sem = refs[14:]
    base = BASE_TWO
    weights = Weights([s12], slots, sems)
    weights.begin()
    above = pltpu.make_async_copy(rest_in, g.at[pl.ds(BASE_ONE - base, PLANES[3] - BASE_ONE), :], in_sem)
    above.start()
    prepare(sbuf, pbuf)
    clear_lines(g, PLANES[3] - base, g.shape[0] - (PLANES[3] - base))
    above.wait()
    rows = (V_G1, V_B11, V_B12)
    tools = (sbuf, pbuf, dx, at_ref, gm)
    d_gain, d_shift = block_back_two(dh, u1, AT.first, base, rows, vec, mod, 0, weights, tools, g, dm)
    extra[...] = jnp.zeros_like(extra)
    extra[0:1, :] = d_gain
    extra[1:2, :] = d_shift
    for c in range(0, ROWS, CHUNK):
        du[c : c + CHUNK, :] = pbuf[8 + c : 8 + c + CHUNK, :]
    leave = Leave(me, g, base, keep, send, stage, out_sems)
    leave.plane(2)
    leave.below(PLANES[2] - base, rest)
    leave.wait()


def back_first_half_kernel(*refs):
    me, dh_in, du, dm, extra, dse_in, gm, vec, emb, h1, s11, s_emb, rest_in = refs[:13]
    keep, send, rest, dh, dse = refs[13:18]
    g, slots, sbuf, pbuf, dx, at_ref, stage, sems, out_sems, w_sq, in_sem, sq_sem = refs[18:]
    base = BASE_THREE
    weights = Weights([s11], slots, sems)
    weights.begin()
    sq_copy = pltpu.make_async_copy(s_emb, w_sq, sq_sem)
    sq_copy.start()
    above = pltpu.make_async_copy(rest_in, g.at[pl.ds(BASE_TWO - base, PLANES[2] - BASE_TWO), :], in_sem)
    above.start()
    prepare(sbuf, pbuf)
    clear_lines(g, PLANES[2] - base, g.shape[0] - (PLANES[2] - base))
    refill(pbuf, du)
    for c in range(0, ROWS, CHUNK):
        dh[c : c + CHUNK, :] = dh_in[c : c + CHUNK, :]
    above.wait()
    tools = (sbuf, pbuf, dx, at_ref, gm)
    put_outer(g, AT.first.embed - base, silu(emb[...]), dm[...])
    put_row(g, AT.first.embed_bias - base, rowsum(dm[...]))
    block_back_one(dh, h1, AT.first, base, (V_G1, V_B11, V_B12), vec, weights, tools, g)
    put_row(g, AT.first.gains + 6 - base, extra[0:1, :])
    put_row(g, AT.first.gains + 9 - base, extra[1:2, :])
    leave = Leave(me, g, base, keep, send, stage, out_sems)
    leave.plane(1)
    leave.below(PLANES[1] - base, rest)
    sq_copy.wait()
    dse[...] = dse_in[...] + dot3(dm[...], w_sq[...], NT)
    leave.wait()


def back_low_kernel(*refs):
    me, labels, dh, dse, emb, pre, phi, h0s, xp, s_down, s_time, rest_in = refs[:12]
    keep, send = refs[12:14]
    g, slots, sbuf, pbuf, h0t, stage, sems, out_sems, w_sq, demb_ref, dwin, dbin, in_sem, sq_sem = refs[14:]
    weights = Weights([s_down], slots, sems)
    weights.begin()
    sq_copy = pltpu.make_async_copy(s_time, w_sq, sq_sem)
    sq_copy.start()
    above = pltpu.make_async_copy(rest_in, g.at[pl.ds(BASE_THREE, PLANES[1] - BASE_THREE), :], in_sem)
    above.start()
    prepare(sbuf, pbuf)
    clear_lines(g, PLANES[1], g.shape[0] - PLANES[1])
    above.wait()
    demb = dse[...] * silu_slope(emb[...])
    put_row(g, AT.time_bias_two, rowsum(demb))
    put_outer(g, AT.time_two, silu(pre[...]), demb)
    sq_copy.wait()
    dpre = dot3(demb, w_sq[...], NT) * silu_slope(pre[...])
    put_row(g, AT.time_bias_one, rowsum(dpre))
    put_outer(g, AT.time_one, phi[...], dpre)
    clear = 240
    first, lines = AT.class_table, CLASSES * (EMB_DIM // LINE)

    def wipe(c, carry):
        g[pl.ds(first + c * clear, clear), :] = jnp.zeros((clear, LINE), F32)
        return carry

    lax.fori_loop(0, lines // clear, wipe, 0)
    demb_ref[...] = demb
    for n in range(MB_DEV):
        for j in range(EMB_DIM // LINE):
            at = first + labels[n] * (EMB_DIM // LINE) + j
            g[pl.ds(at, 1), :] += demb_ref[n : n + 1, j * LINE : (j + 1) * LINE]

    put_row(g, AT.bias_down, colsum(dh, 0, ROWS))
    refill(pbuf, dh)
    shift_to(sbuf, pbuf)
    w = weights.take()
    dwin[...] = jnp.zeros_like(dwin)
    dbin[...] = jnp.zeros_like(dbin)
    for ph in range(4):
        for c in range(ROWS // LINE):
            rows = slice(ph * ROWS + c * LINE, ph * ROWS + (c + 1) * LINE)
            h0t[:, c * LINE : (c + 1) * LINE] = h0s[rows, :].astype(F32).T.astype(BF16)
        d0 = jnp.zeros((ROWS, CH_BASE), F32)
        for ky in ((0, 2) if ph // 2 else (1,)):
            for kx in ((0, 2) if ph % 2 else (1,)):
                d = shifted(sbuf, 2 if kx == 0 else 1, 32 if ky == 0 else 16)
                t = 3 * ky + kx
                d0 = d0 + dot(d, w[t * CH_BASE : (t + 1) * CH_BASE, :], NT)
                put_lines(g, AT.conv_down + t * CH_BASE * 3, dot(h0t[0:CH_BASE, :], d), 3)
        dbin[0:1, :CH_BASE] += rowsum(d0)
        dwin[:, :CH_BASE] += dot(xp[ph * ROWS : (ph + 1) * ROWS, :], d0.astype(BF16), TN)
    dwin[29:30, :] = dbin[0:1, :]
    even, odd = dwin[0:16, :], dwin[16:32, :]
    turned = pltpu.roll(odd[:, :LINE], LINE // 2, 1), pltpu.roll(odd[:, LINE:], LINE // 2, 1)
    g[pl.ds(0, 14, stride=3), :] = even[0:14, :LINE]
    g[pl.ds(1, 14, stride=3), :] = jnp.where(first_lanes(), even[:, LINE:], turned[0])[0:14]
    g[pl.ds(2, 14, stride=3), :] = jnp.where(first_lanes(), turned[0], turned[1])[0:14]
    leave = Leave(me, g, 0, keep, send, stage, out_sems)
    leave.plane(0)
    leave.wait()


def kernel_params():
    return dict(
        compiler_params=pltpu.CompilerParams(vmem_limit_bytes=60 * 1024 * 1024),
        cost_estimate=pl.CostEstimate(flops=8 * 10**9, bytes_accessed=4 * 10**7, transcendentals=10**6),
    )


def back_call(kernel, name, lines, slots, args, smem, hbm, rest, outs, scratch, norms=True):
    sds = lambda *s: jax.ShapeDtypeStruct(*s)
    plane = sds((PLANE // 2, ROOM, LINE), BF16)
    rest = [sds((rest, LINE), F32)] if rest else []
    common = [
        vmem((lines + 8, LINE), F32),
        vmem((slots, 9 * CH_MID, CH_MID), BF16),
        vmem((3, PADDED, CH_MID), BF16),
        vmem((ROWS + 16, CH_MID), F32),
    ]
    if norms:
        common += [vmem((ROWS, CH_MID), F32), vmem((CH_MID, ROWS), BF16)]
    else:
        common += [vmem((256, ROWS), BF16)]
    common += [
        vmem((PLANE, ROOM, LINE), BF16),
        pltpu.SemaphoreType.DMA((2,)),
        pltpu.SemaphoreType.DMA((3,)),
    ]
    return pl.pallas_call(
        kernel,
        out_shape=[plane, plane, *rest, *(sds(*o) for o in outs)],
        in_specs=[SM] * smem + [VM] * (len(args) - smem - hbm) + [HB] * hbm,
        out_specs=[HB] * (2 + len(rest)) + [VM] * len(outs),
        scratch_shapes=common + scratch,
        name=name,
        **kernel_params(),
    )(*args)


ACT = ((ROWS, CH_MID), F32)
WIDE_ROW = ((8, EMB_DIM), F32)
DMA = pltpu.SemaphoreType.DMA


def back_top(args):
    scratch = [vmem((EMB_DIM, EMB_DIM), BF16), vmem((ROWS, 3 * CH_MID), BF16), vmem(*WIDE_ROW), DMA]
    lines = ALL_LINES - BASE_ONE
    return back_call(
        back_top_kernel, "back_top", lines, 2, args, 1, 4, PLANES[3] - BASE_ONE, [ACT, WIDE_ROW], scratch
    )


def back_second_half(args):
    outs = [ACT, WIDE_ROW, ((8, CH_MID), F32)]
    lines = PLANES[3] - BASE_TWO
    return back_call(back_second_half_kernel, "back_b", lines, 1, args, 1, 2, PLANES[2] - BASE_TWO, outs, [DMA])


def back_first_half(args):
    scratch = [vmem((EMB_DIM, EMB_DIM), BF16), DMA, DMA]
    lines = PLANES[2] - BASE_THREE
    return back_call(
        back_first_half_kernel, "back_c", lines, 1, args, 1, 3, PLANES[1] - BASE_THREE, [ACT, WIDE_ROW], scratch
    )


def back_low(args):
    scratch = [
        vmem((EMB_DIM, EMB_DIM), BF16),
        vmem(*WIDE_ROW),
        vmem((32, 2 * LINE), F32),
        vmem((8, 2 * LINE), F32),
        DMA,
        DMA,
    ]
    return back_call(back_low_kernel, "back_low", PLANES[1], 1, args, 2, 3, 0, [], scratch, False)


def karras(index):
    ramp_frac = index.astype(F32) / (DISCRETE - 1)
    low_root = SIGMA_LOW ** (1.0 / RHO_POWER)
    high_root = SIGMA_HIGH ** (1.0 / RHO_POWER)
    return (low_root + ramp_frac * (high_root - low_root)) ** RHO_POWER


def preconditioning_factors(sigma):
    variance_sum = sigma * sigma + SIGMA_DATA**2
    skip = SIGMA_DATA**2 / ((sigma - SIGMA_LOW) ** 2 + SIGMA_DATA**2)
    out = (sigma - SIGMA_LOW) * SIGMA_DATA * lax.rsqrt(variance_sum)
    return (skip, out, lax.rsqrt(variance_sum))


def noise_features(sigma):
    half_width = CH_BASE // 2
    frequency = jnp.exp(-math.log(10000.0) * jnp.arange(half_width, dtype=F32) / half_width)
    phases = 250.0 * jnp.log(sigma)[:, None] * frequency
    return jnp.pad(jnp.concatenate([jnp.cos(phases), jnp.sin(phases)], 1), ((0, 8 - MB_DEV), (0, 0)))


def pixels(images):
    lead = images.shape[0]
    split = images.reshape(lead, MB_DEV, HALF, 2, HALF, 2, 3)
    return split.transpose(0, 1, 2, 4, 3, 5, 6).reshape(lead, ROWS, 12)


def pixel_live(counts, valid_rows):
    row = lax.broadcasted_iota(jnp.int32, (ROWS, 12), 0)
    lane = lax.broadcasted_iota(jnp.int32, (ROWS, 12), 1)
    slot = row // PIX
    line = 2 * ((row // HALF) % HALF) + lane // 6
    top = jnp.where(slot == 0, valid_rows[0], valid_rows[1])
    return ((slot < counts[0]) & (line < top)).astype(F32)


def per_part(me, labels, lines, inputs, save, tables):
    _, x_in, phi, _ = inputs
    results = forward_call(save, me, labels, lines, x_in, phi, tables)
    return results[0], results[1:]


AXIS = "fsdp"
CORE, EAST, SOUTH, UP = 1, 2, 4, 8
CUT_ROWS = ROOM // 2


def swap(values, hop):
    return lax.ppermute(values, AXIS, [(i, i ^ hop) for i in range(SHARDS)])


def total_of(values, n):
    hop = 1
    while hop < n:
        values = values + lax.ppermute(values, AXIS, [(i, i ^ hop) for i in range(n)])
        hop *= 2
    return values


CUTS = (0, 880, 1760, ROOM)
TALL = SHARDS // PLANE


def gate(values, after):
    count = len(values)

    def body(*refs):
        pass

    return pl.pallas_call(
        body,
        out_shape=[jax.ShapeDtypeStruct(v.shape, v.dtype) for v in values],
        in_specs=[HB] * (count + len(after)),
        out_specs=[HB] * count,
        input_output_aliases={i: i for i in range(count)},
        name="gate",
    )(*values, *after)


def climb(values, way, far, first=0):
    planes = range(first, TALL - far) if way == 1 else range(TALL - 1 - first, far - 1, -1)
    pairs = [(q * PLANE + i, (q + way * far) * PLANE + i) for q in planes for i in range(PLANE)]
    return lax.ppermute(values, AXIS, pairs)


def column_window(slots, z):
    rows = []
    for p in range(TALL):
        value = slots[TALL - 1 + p]
        for q in range(1, TALL):
            value = jnp.where(z == q, slots[TALL - 1 - q + p], value)
        rows.append(value)
    return jnp.stack(rows)


def column_gather(own, z):
    below, above = [climb(own, 1, 1)], [climb(own, -1, 1)]
    for step in range(1, TALL - 1):
        below.append(climb(below[-1], 1, 1, step))
        above.append(climb(above[-1], -1, 1, step))
    return column_window([*below[::-1], own, *above], z), [below[0], above[0]], [below[-1], above[-1]]


def gather_lines(shard, z, early):
    ab, c = shard[: CUTS[2]], shard[CUTS[2] :]
    c_two = jnp.stack([c, swap(c, SOUTH)])
    c_four = jnp.concatenate([c_two, swap(c_two, EAST)])
    column, step, last = column_gather(ab, z)
    za, zb = column[:, : CUTS[1]], column[:, CUTS[1] :]
    done, ready = early(step)
    a_two, b_two = jnp.stack([za, swap(za, EAST)]), jnp.stack([zb, swap(zb, SOUTH)])
    a_far, b_far = swap(a_two, SOUTH), swap(b_two, EAST)
    (c_four,) = gate([c_four], [*last, *ready])
    c_all, _, _ = column_gather(c_four, z)
    pieces = [a_two, a_far, b_two, b_far, c_all]
    return done, pieces + [swap(v, CORE) for v in pieces]


def gather_moves():
    places = [(0, 1), (2, 3), (0, 2), (1, 3), (0, 2, 1, 3)]
    part = (0, 0, 1, 1, 2)
    moves = []
    for core in range(2):
        for n in range(5):
            row, end = CUTS[part[n]], CUTS[part[n] + 1]
            for lead, place in enumerate(places[n]):
                moves.append((core * 5 + n, lead, 2 * place + core, row, end - row))
    return moves


def gather_plain(shard):
    rows = shard.shape[0]
    lines = lax.all_gather(shard, AXIS, axis=0, tiled=True)
    if rows != ROOM:
        lines = jnp.pad(lines.reshape(SHARDS, SHARD, LINE), ((0, 0), (0, ROOM - SHARD), (0, 0)))
    lines = lines.reshape(TALL, PLANE, ROOM, LINE)
    return [lines], [(0, r, r, 0, ROOM) for r in range(PLANE)], (True,)


def low(v):
    return v.astype(BF16)


def wide(v):
    return v.astype(F32)


class PlaneSum:
    def __init__(self, keep, send):
        self.keep, self.got = keep, swap(send, CORE)
        self.a, self.b = slice(0, CUT_ROWS), slice(CUT_ROWS, ROOM)

    def quarter(self, i, rows):
        return wide(self.keep[i, rows]) + wide(self.got[i, rows])

    def first(self):
        a = low(jnp.stack([self.quarter(1, self.a), self.quarter(3, self.a)]))
        b = low(jnp.stack([self.quarter(2, self.b), self.quarter(3, self.b)]))
        return a, b

    def send_first(self, a, b):
        self.got_a, self.got_b = swap(a, EAST), swap(b, SOUTH)

    def last(self):
        return low(self.quarter(2, self.a) + wide(self.got_a[1])), low(self.quarter(1, self.b) + wide(self.got_b[1]))

    def send_last(self, a, b):
        self.end_a, self.end_b = swap(a, SOUTH), swap(b, EAST)

    def total(self):
        a = self.quarter(0, self.a) + wide(self.got_a[0]) + wide(self.end_a)
        b = self.quarter(0, self.b) + wide(self.got_b[0]) + wide(self.end_b)
        return jnp.concatenate([a, b])


def column_sums(parts, first, z):
    pick = lambda p: jnp.where(p == first, parts[0], parts[1])
    total = 0.0
    for way in (1, -1):
        run = None
        for far in range(TALL - 1, 0, -1):
            holders = [q for q in range(TALL) if q + way * far in (first, first + 1)]
            if not holders:
                continue
            value = pick(z + way * far)
            if run is not None:
                value = value + run
            pairs = [(q * PLANE + i, (q + way) * PLANE + i) for q in holders for i in range(PLANE)]
            run = wide(lax.ppermute(low(value), AXIS, pairs))
        total = total + run
    return total


def per_device(n, images, noise_draws, labels, step_index, valid_rows, counts, master, momentum, ema):
    direct = n == SHARDS
    index = lax.axis_index(AXIS)
    me = jnp.where(direct, lax.rem(index, PLANE), 0).astype(jnp.int32)[None]
    z = lax.div(index, PLANE)
    shards = [v.astype(BF16).reshape(-1, LINE) for v in (master, ema)]
    tables = tuple(jnp.asarray(v, BF16) for v in (group_table(), *spread_tables(), expand_table(), patch_table()))
    live = (jnp.arange(MB_DEV) < counts[0]).astype(jnp.int32)
    local_rows = jnp.sum(live * jnp.clip(valid_rows, 0, RES)).astype(F32)

    total = total_of(jnp.broadcast_to(local_rows, (8, LINE)), n)
    pixel_total = 3.0 * RES * total[0, 0]

    def early(after):
        clean, noise = gate([images, noise_draws], after) if after else (images, noise_draws)
        clean, noise = pixels(jnp.stack([clean, noise]))
        per_row = lambda v: jnp.repeat(v, PIX)[:, None]

        def inputs_of(sigma):
            noisy = clean + per_row(sigma) * noise
            skip, out_scale, in_scale = preconditioning_factors(sigma)
            x_in = jnp.pad((per_row(in_scale) * noisy).astype(BF16), ((0, 0), (0, LINE - 12)))
            return per_row(skip) * noisy, x_in, noise_features(sigma), per_row(out_scale)

        mask = pixel_live(counts, valid_rows)
        both = inputs_of(karras(step_index)), inputs_of(karras(step_index + 1))
        return (*both, mask), [v for part in both for v in part[:3]] + [mask, total]

    if direct:
        rooms = [jnp.pad(v, ((0, ROOM - SHARD), (0, 0))) for v in shards]
        target = gather_plain(rooms[1])
        (in_lo, in_hi, mask), pieces = gather_lines(rooms[0], z, early)
        online = (pieces, gather_moves(), (False,) * 4 + (True,) + (False,) * 4 + (True,))
    else:
        online, target = gather_plain(shards[0]), gather_plain(shards[1])
        in_lo, in_hi, mask = early(())[0]
    model_o, saved = per_part(me, labels, online, in_hi, True, tables)
    model_t, _ = per_part(jnp.zeros_like(me), labels, target, in_lo, False, tables)
    online_out = in_hi[0] + in_hi[3] * model_o[:, :12]
    target_out = in_lo[0] + in_lo[3] * model_t[:, :12]
    phi, out_scale = in_hi[2], in_hi[3]
    gap = online_out - target_out
    local_loss = jnp.sum(mask * jnp.square(gap))
    grad_model = out_scale * 2.0 * mask * gap / pixel_total
    bias_out = jnp.sum(grad_model.reshape(ROWS, 4, 3), axis=(0, 1))
    (h0s, h1, u1, h2, qkv, mixed, h3, u2, h4, vec, mod, emb, pre, wz, xp) = saved[:15]
    s_time, s_emb1, s_emb2, s_down, s11, s12, s_attn, s21, s22 = saved[15:]
    gm = tables[0]
    df = jnp.pad(grad_model, ((0, 0), (0, LINE - 12)))
    small = jnp.concatenate([local_loss[None], bias_out])
    small = jnp.broadcast_to(small, (8, 4))
    keep3, send3, rest, dh, dse = back_top(
        (me, df, wz, *tables[:5], vec, mod, emb, h4, u2, h3, qkv, mixed, h2, s22, s21, s_attn, s_emb2)
    )
    if direct:
        three = PlaneSum(keep3, send3)
    keep2, send2, rest, du, dm, extra = back_second_half((me, dh, gm, vec, mod, u1, s12, rest))
    if direct:
        first3 = three.first()
        (du,) = gate([du], first3)
        three.send_first(*first3)
        two = PlaneSum(keep2, send2)
    keep1, send1, rest, dh, dse = back_first_half((me, dh, du, dm, extra, dse, gm, vec, emb, h1, s11, s_emb1, rest))
    if direct:
        last3, first2 = three.last(), two.first()
        (dh,) = gate([dh], [*last3, *first2])
        three.send_last(*last3)
        two.send_first(*first2)
        one = PlaneSum(keep1, send1)
    keep0, send0 = back_low((me, labels, dh, dse, emb, pre, phi, h0s, xp, s_down, s_time, rest))
    if direct:
        zero = PlaneSum(keep0, send0)
        one.send_first(*one.first())
        two.send_last(*two.last())
        first0 = zero.first()
        zero.send_first(*first0)
        (small,) = gate([small], first0)
        small = total_of(small, n)
        top = [two.total(), three.total()]
        high = column_sums(top, 2, z)
        one.send_last(*one.last())
        zero.send_last(*zero.last())
        bottom = gate([zero.total(), one.total()], [small])
        reduced = column_sums(bottom, 0, z) + high
        own = jnp.where(z < 2, jnp.where(z == 0, bottom[0], bottom[1]), jnp.where(z == 2, top[0], top[1]))
        reduced = (reduced + own)[:SHARD].reshape(-1)
    else:
        small = total_of(small, n)
        both = [jnp.stack([wide(k), wide(s)], 1) for k, s in ((keep0, send0), (keep1, send1), (keep2, send2), (keep3, send3))]
        lines = jnp.stack(both).reshape(SHARDS, ROOM, LINE)[:, :SHARD].reshape(n, -1)
        reduced = lax.psum_scatter(lines, AXIS, scatter_dimension=0, tiled=True).reshape(-1)
    new_momentum = MOMENTUM * momentum + reduced
    new_master = master - LEARN_RATE * (reduced + MOMENTUM * new_momentum)
    new_ema = EMA_DECAY * ema + (1.0 - EMA_DECAY) * new_master
    return (small[0, 0] / pixel_total, new_momentum, new_master, new_ema, small[0, 1:])


def solution(mesh):
    n = mesh.shape[AXIS]

    def step(*args):
        return per_device(n, *args)

    return jax.shard_map(
        step,
        mesh=mesh,
        in_specs=(P(AXIS, None, None, None),) * 2 + (P(AXIS),) * 7,
        out_specs=(P(), P(AXIS), P(AXIS), P(AXIS), P()),
        check_vma=False,
    )
```

```python
import math

import jax
import jax.numpy as jnp
import numpy as np
from jax import lax
from jax.experimental import pallas as pl
from jax.experimental.pallas import tpu as pltpu
from jax.sharding import PartitionSpec as P

CH_BASE = 192
CH_MID = 384
EMB_DIM = 768
HEADS = 6
HEAD_DIM = 64
CLASSES = 1000
GROUPS = 32
RES = 32
MB_DEV = 2
DISCRETE = 40

EPSILON = 1e-05
SIGMA_DATA = 0.5
SIGMA_LOW = 0.002
SIGMA_HIGH = 80.0
RHO_POWER = 7.0
MOMENTUM = 0.9
EMA_DECAY = 0.9
LEARN_RATE = 2000.0

F32 = jnp.float32
BF16 = jnp.bfloat16
LINE = 128
HALF = RES // 2
PIX = HALF * HALF
ROWS = MB_DEV * PIX
GROUP_SIZE = PIX * (CH_MID // GROUPS)
CHUNK = 128
PADDED = 16 + MB_DEV * (PIX + 16)
NN = (((1,), (0,)), ((), ()))
NT = (((1,), (1,)), ((), ()))
TN = (((0,), (0,)), ((), ()))


class Place:
    pass


class Cut:
    def __init__(self):
        self.offset = 0

    def take(self, *shape):
        at = self.offset
        self.offset += math.prod(shape)
        return at // LINE


def block_place(cut):
    at = Place()
    at.gains = cut.take(4, CH_MID)
    at.conv_one = cut.take(9 * CH_MID, CH_MID)
    at.bias_one = cut.take(CH_MID)
    at.embed = cut.take(EMB_DIM, 2 * CH_MID)
    at.embed_bias = cut.take(2 * CH_MID)
    at.conv_two = cut.take(9 * CH_MID, CH_MID)
    at.bias_two = cut.take(CH_MID)
    return at


def places():
    cut, at = Cut(), Place()
    at.conv_in = cut.take(27, CH_BASE)
    at.bias_in = cut.take(CH_BASE)
    at.conv_down = cut.take(9 * CH_BASE, CH_MID)
    at.bias_down = cut.take(CH_MID)
    at.time_one = cut.take(CH_BASE, EMB_DIM)
    at.time_bias_one = cut.take(EMB_DIM)
    at.time_two = cut.take(EMB_DIM, EMB_DIM)
    at.time_bias_two = cut.take(EMB_DIM)
    at.class_table = cut.take(CLASSES, EMB_DIM)
    at.first = block_place(cut)
    at.second = block_place(cut)
    at.attn_gains = cut.take(2, CH_MID)
    at.attn_qkv = cut.take(CH_MID, 3 * CH_MID)
    at.attn_out = cut.take(CH_MID, CH_MID)
    at.attn_bias = cut.take(CH_MID)
    at.final_gains = cut.take(2, CH_MID)
    at.conv_out = cut.take(9 * CH_MID, 3)
    at.bias_out = cut.take(3)
    return at


AT = places()
TAIL = AT.conv_out
SHARDS, PLANE = 32, 8
SHARD = 2264
ROOM = 2272
ALL_LINES = SHARDS * SHARD
PLANES = [p * PLANE * SHARD for p in range(SHARDS // PLANE)]
BASE_ONE = AT.second.gains // 16 * 16
BASE_TWO = AT.first.conv_two // 16 * 16
BASE_THREE = AT.first.gains // 16 * 16

V_DOWN, V_G1, V_B11, V_B12, V_AG, V_AB, V_FG, V_G2, V_B21, V_B22 = 0, 1, 5, 6, 7, 9, 10, 12, 16, 17
VEC_ROWS = 24


def group_table():
    at = np.arange(CH_MID) // (CH_MID // GROUPS)
    return (at[:, None] == at[None, :]).astype(np.float32)


TAPS = 16


def spread_tables():
    select = np.zeros((LINE, LINE), np.float32)
    gather = np.zeros((LINE, LINE), np.float32)
    tile = np.zeros((LINE, LINE), np.float32)
    for ky in range(3):
        for kx in range(3):
            for a in range(2):
                for b in range(2):
                    dy, dx = (a + ky - 1) // 2, (b + kx - 1) // 2
                    shift = (dy + 1) * 3 + dx + 1
                    for c in range(3):
                        out = (a * 2 + b) * 3 + c
                        select[c * TAPS + ky * 3 + kx, shift * 12 + out] = 1.0
                        gather[out::12, out][:9] = 1.0
                        tile[c, out] = 1.0
    return select, gather, tile


def patch_table():
    pick = np.zeros((4, LINE, 32), np.float32)
    for a in range(2):
        for b in range(2):
            for ky in range(3):
                for kx in range(3):
                    (dy, ya), (dx, xb) = divmod(a + ky - 1, 2), divmod(b + kx - 1, 2)
                    shift = (dy + 1) * 3 + dx + 1
                    for c in range(3):
                        k = (ky * 3 + kx) * 3 + c
                        pick[a * 2 + b, shift * 12 + (ya * 2 + xb) * 3 + c, k // 2 + 16 * (k % 2)] = 1.0
    return pick


def expand_table():
    return (np.arange(3 * CH_MID)[None, :] // 3 == np.arange(CH_MID)[:, None]).astype(np.float32)


def colour(c):
    lane = lax.broadcasted_iota(jnp.int32, (1, 3 * CH_MID), 1)
    return lax.rem(lane, 3) == c


def first_lanes():
    return lax.broadcasted_iota(jnp.int32, (1, LINE), 1) < LINE // 2


def split3(v):
    hi = v.astype(BF16)
    rest = v - hi.astype(F32)
    mid = rest.astype(BF16)
    low = (rest - mid.astype(F32)).astype(BF16)
    return hi, mid, low


def dot(a, b, dims=NN):
    return lax.dot_general(a, b, dims, preferred_element_type=F32)


def dot3(a, b, dims=NN):
    rows = a.shape[0]
    hi, mid, low = split3(a)
    if rows % 16:
        out = dot(jnp.concatenate([p.astype(F32) for p in (hi, mid, low)], 0).astype(BF16), b, dims)
    else:
        out = dot(jnp.concatenate([hi, mid, low], 0), b, dims)
    return out[:rows] + out[rows : 2 * rows] + out[2 * rows :]


def outer(a, b):
    pa, pb = split3(a), split3(b)
    pairs = [(0, 0), (0, 1), (1, 0), (1, 1), (0, 2), (2, 0)]
    left = jnp.concatenate([pa[i].astype(F32) for i, _ in pairs], 0).astype(BF16)
    right = jnp.concatenate([pb[j].astype(F32) for _, j in pairs], 0).astype(BF16)
    return dot(left, right, TN)


def sigmoid(z):
    return 1.0 / (1.0 + jnp.exp(-z))


def silu(z):
    return z * sigmoid(z)


def silu_slope(z):
    s = sigmoid(z)
    return s * (1.0 + z * (1.0 - s))


def colsum(ref, base, count=PIX):
    def body(c, acc):
        return acc + jnp.sum(ref[pl.ds(pl.multiple_of(base + c * CHUNK, 8), CHUNK), :], 0, keepdims=True)

    return lax.fori_loop(0, count // CHUNK, body, jnp.zeros((1, ref.shape[1]), F32))


def eight(v):
    return jnp.broadcast_to(v, (8, v.shape[1]))


def group_means(rows, gm_ref):
    rows = rows + [jnp.zeros((8 - len(rows), CH_MID), F32)]
    means = dot3(jnp.concatenate(rows, 0), gm_ref[...]) * (1.0 / GROUP_SIZE)
    return [means[n : n + 1] for n in range(len(rows) - 1)]


def all_stats(x_ref, gm_ref):
    def total(c, acc):
        at = lambda img: pl.ds(pl.multiple_of(img * PIX + c * CHUNK, 8), CHUNK)
        return tuple(acc[img] + jnp.sum(x_ref[at(img), :], 0, keepdims=True) for img in range(MB_DEV))

    zero = (jnp.zeros((1, CH_MID), F32),) * MB_DEV
    means = group_means(list(lax.fori_loop(0, PIX // CHUNK, total, zero, unroll=2)), gm_ref)

    def square(c, acc):
        out = []
        for img in range(MB_DEV):
            gap = x_ref[pl.ds(pl.multiple_of(img * PIX + c * CHUNK, 8), CHUNK), :] - means[img]
            out.append(acc[img] + jnp.sum(gap * gap, 0, keepdims=True))
        return tuple(out)

    spreads = group_means(list(lax.fori_loop(0, PIX // CHUNK, square, zero, unroll=2)), gm_ref)
    return [(mean, lax.rsqrt(spread + EPSILON)) for mean, spread in zip(means, spreads)]


def norm_to(pbuf, x_ref, stats, scales, act):
    for img in range(MB_DEV):
        (mean, rstd), (k, o) = stats[img], scales[img]

        def body(c, carry):
            r = pl.multiple_of(img * PIX + c * CHUNK, 8)
            z = (x_ref[pl.ds(r, CHUNK), :] - mean) * rstd * k + o
            pbuf[pl.ds(r + 8, CHUNK), :] = silu(z) if act else z
            return carry

        lax.fori_loop(0, PIX // CHUNK, body, 0, unroll=2)


def norm_back(x_ref, d_ref, stats, scales, act, gm_ref, emit):
    def one(c, carry):
        out = []
        for img in range(MB_DEV):
            (mean, rstd), (k, o) = stats[img], scales[img]
            r = pl.multiple_of(img * PIX + c * CHUNK, 8)
            xhat = (x_ref[pl.ds(r, CHUNK), :] - mean) * rstd
            dz = d_ref[pl.ds(r, CHUNK), :]
            if act:
                dz = dz * silu_slope(xhat * k + o)
                d_ref[pl.ds(r, CHUNK), :] = dz
            out.append(carry[2 * img] + jnp.sum(dz, 0, keepdims=True))
            out.append(carry[2 * img + 1] + jnp.sum(dz * xhat, 0, keepdims=True))
        return tuple(out)

    sums = lax.fori_loop(0, PIX // CHUNK, one, (jnp.zeros((1, CH_MID), F32),) * (2 * MB_DEV), unroll=2)
    means = group_means([v * scales[n // 2][0] for n, v in enumerate(sums)], gm_ref)
    for img in range(MB_DEV):
        (mean, rstd), (k, o) = stats[img], scales[img]
        m1, m2 = means[2 * img], means[2 * img + 1]

        def two(c, carry):
            r = pl.multiple_of(img * PIX + c * CHUNK, 8)
            xhat = (x_ref[pl.ds(r, CHUNK), :] - mean) * rstd
            emit(r, rstd * (d_ref[pl.ds(r, CHUNK), :] * k - m1 - xhat * m2))
            return carry

        lax.fori_loop(0, PIX // CHUNK, two, 0, unroll=2)
    return [(sums[2 * img], sums[2 * img + 1]) for img in range(MB_DEV)]


def clear_pads(sbuf):
    for r in range(0, PADDED, PIX + 16):
        sbuf[r : r + 16, :] = jnp.zeros((16, sbuf.shape[1]), BF16)


def shift_to(sbuf, pbuf):
    column = lax.rem(lax.broadcasted_iota(jnp.int32, (CHUNK, CH_MID), 0), HALF)
    for r in range(0, ROWS, CHUNK):
        for k in range(3):
            v = pbuf[r + 7 + k : r + 7 + k + CHUNK, :]
            if k == 0:
                v = jnp.where(column == 0, 0.0, v)
            if k == 2:
                v = jnp.where(column == HALF - 1, 0.0, v)
            start = r + 16 * (r // PIX + 1)
            sbuf[start : start + CHUNK, k * CH_MID : (k + 1) * CH_MID] = v.astype(BF16)


def shifted(sbuf, row, cols=slice(None)):
    first = sbuf[pl.ds(pl.multiple_of(row, 16), PIX), cols]
    second = sbuf[pl.ds(pl.multiple_of(row + PIX + 16, 16), PIX), cols]
    return jnp.concatenate([first, second], 0)


def conv_forward(sbuf, w_ref, out_ref):
    depth = 3 * CH_MID

    def body(ky, carry):
        w = w_ref[pl.ds(pl.multiple_of(ky * depth, depth), depth), :]
        out_ref[...] += dot(shifted(sbuf, ky * 16), w)
        return carry

    lax.fori_loop(0, 3, body, 0, unroll=3)


def put_lines(g_ref, at, value, step, more=None):
    n = value.shape[0]
    low = at // 8 * 8
    start = low if more is None else pl.multiple_of(low + more, 8)
    view = g_ref.at[pl.ds(start, min(n * step + 8, g_ref.shape[0] - low)), :] if more is None else g_ref.at[pl.ds(start, n * step + 8), :]
    for j in range(step):
        view[pl.ds(at - low + j, n, stride=step), :] = value[:, j * LINE : (j + 1) * LINE]


def put_row(g_ref, at, row):
    for j in range(row.shape[1] // LINE):
        g_ref[pl.ds(at + j, 1), :] = row[:, j * LINE : (j + 1) * LINE]


def conv_back(sbuf, at_ref, w_ref, dx_ref, g_ref, at):
    dx_ref[...] = jnp.zeros_like(dx_ref)
    depth = 3 * CH_MID

    def body(s, carry):
        d = shifted(sbuf, s * 16)
        dw = dot(at_ref[...], d)
        dx = dx_ref[...]
        for k in range(3):
            part = slice(k * CH_MID, (k + 1) * CH_MID)
            tap = (2 - s) * depth + (2 - k) * CH_MID
            dx = dx + dot(d[:, part], w_ref[pl.ds(pl.multiple_of(tap, CH_MID), CH_MID), :], NT)
            put_lines(g_ref, at, dw[:, part], 3, 3 * tap)
        dx_ref[...] = dx
        return carry

    lax.fori_loop(0, 3, body, 0, unroll=3)


def transpose_to(at_ref, pbuf):
    for c in range(ROWS // LINE):
        at_ref[:, c * LINE : (c + 1) * LINE] = pbuf[8 + c * LINE : 8 + (c + 1) * LINE, :].T.astype(BF16)


class Lines:
    def __init__(self, held, wide):
        self.held, self.wide = held, wide

    def take(self, span):
        l0, l1 = span
        first = l0 // SHARD
        self.low = first * SHARD + (l0 - first * SHARD) // 16 * 16
        for s in range(first, (l1 - 1) // SHARD + 1):
            start = max(l0 - s * SHARD, 0) // 16 * 16
            count = -(-min(l1 - s * SHARD, SHARD) // 16) * 16 - start
            to = s * SHARD + start - self.low
            block = self.held.at[s // PLANE, s % PLANE]
            whole, rest = divmod(count, 256)

            def body(c, carry):
                self.wide[pl.ds(pl.multiple_of(to + c * 256, 8), 256), :] = block[
                    pl.ds(pl.multiple_of(start + c * 256, 16), 256), :
                ].astype(F32)
                return carry

            lax.fori_loop(0, whole, body, 0, unroll=2)
            if rest:
                done = whole * 256
                self.wide[to + done : to + count, :] = block[start + done : start + count, :].astype(F32)

    def line(self, at, scratch):
        shard = lax.div(at, SHARD)
        row = at - shard * SHARD
        low = pl.multiple_of(lax.div(row, 16) * 16, 16)
        scratch[...] = self.held[lax.div(shard, PLANE), lax.rem(shard, PLANE), pl.ds(low, 16), :].astype(F32)
        return scratch[pl.ds(row - low, 1), :]

    def matrix(self, w_ref, at, rows, step):
        block = 128 if rows % 192 else 192
        base = at - self.low
        low = base // 8 * 8

        def body(c, carry):
            r = pl.multiple_of(c * block, block)
            view = self.wide.at[pl.ds(pl.multiple_of(low + r * step, 8), block * step + 8), :]
            for j in range(step):
                v = view[pl.ds(base - low + j, block, stride=step), :]
                w_ref[pl.ds(r, block), j * LINE : (j + 1) * LINE] = v.astype(BF16)
            return carry

        lax.fori_loop(0, rows // block, body, 0, unroll=3 if (rows // block) % 3 == 0 else 2)

    def row(self, at, step):
        base = at - self.low
        return jnp.concatenate([self.wide[pl.ds(base + j, 1), :] for j in range(step)], 1)


def attention_pair(qkv_ref, img, pair):
    rows = pl.ds(pl.multiple_of(img * PIX, PIX), PIX)
    return [qkv_ref[rows, part * CH_MID + pair * LINE : part * CH_MID + (pair + 1) * LINE] for part in range(3)]


def lane_half():
    return lax.broadcasted_iota(jnp.int32, (1, LINE), 1) < HEAD_DIM


def keep_half(v, half, side):
    mine = half if side == 0 else jnp.logical_not(half)
    return jnp.where(mine, v.astype(F32), 0.0).astype(BF16)


SPAN_TIME = (AT.time_one, AT.class_table)
SPAN_EMB1 = (AT.first.embed, AT.first.conv_two)
SPAN_EMB2 = (AT.second.embed, AT.second.conv_two)
SPAN_DOWN = (AT.conv_in, AT.time_one)
SPAN_ONE1 = (AT.first.gains, AT.first.embed)
SPAN_TWO1 = (AT.first.conv_two, AT.second.gains)
SPAN_ATTN = (AT.attn_gains, ALL_LINES)
SPAN_ONE2 = (AT.second.gains, AT.second.embed)
SPAN_TWO2 = (AT.second.conv_two, AT.attn_gains)


def block_scales(vec, row, mod_ref=None, mod_row=0):
    gain, shift = vec[row : row + 1, :], vec[row + 1 : row + 2, :]
    if mod_ref is None:
        return [(gain, shift)] * MB_DEV
    out = []
    for img in range(MB_DEV):
        scale = 1.0 + mod_ref[mod_row + img : mod_row + img + 1, :CH_MID]
        out.append((gain * scale, shift * scale + mod_ref[mod_row + img : mod_row + img + 1, CH_MID:]))
    return out


def upsample_masks(shift):
    dy, dx = shift // 3 - 1, shift % 3 - 1
    p = lax.broadcasted_iota(jnp.int32, (ROWS, 1), 0)
    i, j = lax.rem(lax.div(p, HALF), HALF), lax.rem(p, HALF)
    inside = (i + dy >= 0) & (i + dy < HALF) & (j + dx >= 0) & (j + dx < HALF)
    lane = lax.broadcasted_iota(jnp.int32, (1, LINE), 1)
    return inside & (lane >= shift * 12) & (lane < shift * 12 + 12), dy * HALF + dx


def forward_kernel(save, moves, flip, *refs):
    me, labels, x_in, phi, gm, sel, gat, tile, expand, pick = refs[:10]
    sources = max(move[0] for move in moves) + 1
    pieces, refs = refs[10 : 10 + sources], refs[10 + sources :]
    f_out = refs[0]
    (h0s, h1, u1, h2, qkv, mixed, h3, u2, h4, vec, mod, emb, pre, wz, xp) = refs[1:16]
    if save:
        sw_time, sw_emb1, sw_emb2, sw_down, sw_11, sw_12, sw_attn, sw_21, sw_22 = refs[16:25]
    held, wide, w_ref, w_sq, sbuf, pbuf, h0p, table, w_in, b_out, sems, save_sem = refs[25 if save else 16 :]
    src = Lines(held, wide)
    arriving = []
    for plane in range(SHARDS // PLANE):
        copies = []
        for n, lead, r, row, rows in moves:
            target = held.at[plane, r ^ me[0], pl.ds(row, rows), :]
            source = pieces[n].at[plane, lead] if flip[n] else pieces[n].at[lead, plane]
            copies.append(pltpu.make_async_copy(source, target, sems.at[plane]))
        for copy in copies:
            copy.start()
        arriving.append(copies)

    def arrive(plane):
        for copy in arriving[plane]:
            copy.wait()

    pending = []

    def keep(source, target):
        if save:
            cp = pltpu.make_async_copy(source, target, save_sem)
            cp.start()
            pending.append(cp)

    def free():
        while pending:
            pending.pop().wait()

    clear_pads(sbuf)
    pbuf[0:8, :] = jnp.zeros((8, CH_MID), F32)
    pbuf[ROWS + 8 : ROWS + 16, :] = jnp.zeros((8, CH_MID), F32)
    arrive(0)
    src.take(SPAN_TIME)
    src.matrix(w_sq.at[0], AT.time_one, CH_BASE, 6)
    src.matrix(w_sq.at[1], AT.time_two, EMB_DIM, 6)
    pre[...] = dot3(phi[...], w_sq[0, :CH_BASE, :]) + src.row(AT.time_bias_one, 6)
    emb[...] = dot3(silu(pre[...]), w_sq[1]) + src.row(AT.time_bias_two, 6)
    for n in range(MB_DEV):
        for j in range(6):
            cols = slice(j * LINE, (j + 1) * LINE)
            emb[n : n + 1, cols] += src.line(AT.class_table + labels[n] * 6 + j, table)
    keep(w_sq.at[1], sw_time if save else None)
    se = silu(emb[...])
    arrive(1)
    src.take(SPAN_EMB1)
    src.matrix(w_sq.at[0], AT.first.embed, EMB_DIM, 6)
    m1 = dot3(se, w_sq[0]) + src.row(AT.first.embed_bias, 6)
    free()
    keep(w_sq.at[0], sw_emb1 if save else None)
    mod[0:2, :] = m1[0:2]
    mod[4:8, :] = jnp.zeros((4, EMB_DIM), F32)

    src.take(SPAN_DOWN)
    trio = [wide[pl.ds(j, 16, stride=3), :] for j in range(3)]
    turned = [pltpu.roll(v, LINE // 2, 1) for v in trio[1:]]
    w_in[0:16, 0:LINE] = trio[0]
    w_in[0:16, LINE : 2 * LINE] = trio[1]
    w_in[16:32, 0:LINE] = jnp.where(first_lanes(), turned[0], turned[1])
    w_in[16:32, LINE : 2 * LINE] = turned[1]
    w_low = w_in[...].astype(BF16)
    spread = dot(x_in[...], gat[...], NT)
    around = jnp.zeros((ROWS, LINE), F32)
    for shift in range(9):
        inside, by = upsample_masks(shift)
        around = around + jnp.where(inside, spread if by == 0 else pltpu.roll(spread, (-by) % ROWS, 0), 0.0)
    around = around.astype(BF16)
    one = (lax.broadcasted_iota(jnp.int32, (1, 32), 1) == 29).astype(F32)
    for ph in range(4):
        patch = (dot(around, pick[ph]) + one).astype(BF16)
        xp[ph * ROWS : (ph + 1) * ROWS, :] = patch
        h0s[ph * ROWS : (ph + 1) * ROWS, :] = dot(patch, w_low).astype(BF16)
    for j in range(3):
        vec[V_DOWN : V_DOWN + 1, j * LINE : (j + 1) * LINE] = src.row(AT.bias_down + j, 1)
    src.matrix(w_ref, AT.conv_down, 9 * CH_BASE, 3)
    free()
    keep(w_ref.at[pl.ds(0, 9 * CH_BASE), :], sw_down if save else None)
    h1[...] = jnp.broadcast_to(vec[V_DOWN : V_DOWN + 1, :], (ROWS, CH_MID))
    p = lax.broadcasted_iota(jnp.int32, (ROWS, 1), 0)
    has_left, has_up = lax.rem(p, HALF) > 0, lax.rem(lax.div(p, HALF), HALF) > 0
    for ph in range(4):
        h0p[0:32, :] = jnp.zeros((32, h0p.shape[1]), F32)
        h0p[32 : 32 + ROWS, :] = h0s[ph * ROWS : (ph + 1) * ROWS, :].astype(F32)
        for ky in ((0, 2) if ph // 2 else (1,)):
            for kx in ((0, 2) if ph % 2 else (1,)):
                back = (16 if ky == 0 else 0) + (1 if kx == 0 else 0)
                v = h0p[32 - back : 32 - back + ROWS, :]
                if ky == 0:
                    v = jnp.where(has_up, v, 0.0)
                if kx == 0:
                    v = jnp.where(has_left, v, 0.0)
                t = 3 * ky + kx
                h1[...] += dot(v[:, :CH_BASE].astype(BF16), w_ref[t * CH_BASE : (t + 1) * CH_BASE, :])

    def vectors(row, at, count):
        for n in range(count):
            for j in range(3):
                vec[row + n : row + n + 1, j * LINE : (j + 1) * LINE] = src.row(at + 3 * n + j, 1)

    def half_block(x_ref, scales, bias_row, add_ref, out_ref, at, target):
        src.matrix(w_ref, at, 9 * CH_MID, 3)
        keep(w_ref, target)
        stats = all_stats(x_ref, gm)
        norm_to(pbuf, x_ref, stats, scales, True)
        shift_to(sbuf, pbuf)
        bias = jnp.broadcast_to(vec[bias_row : bias_row + 1, :], (ROWS, CH_MID))
        out_ref[...] = bias if add_ref is None else add_ref[...] + bias
        conv_forward(sbuf, w_ref, out_ref)

    def block(h_in, u, h_out, prefix, g_row, b1_row, b2_row, mod_row, spans, targets):
        src.take(spans[0])
        free()
        vectors(g_row, prefix.gains, 4)
        vectors(b1_row, prefix.bias_one, 1)
        half_block(h_in, block_scales(vec, g_row), b1_row, None, u, prefix.conv_one, targets[0])
        src.take(spans[1])
        free()
        vectors(b2_row, prefix.bias_two, 1)
        half_block(u, block_scales(vec, g_row + 2, mod, mod_row), b2_row, h_in, h_out, prefix.conv_two, targets[1])

    saved = (sw_11, sw_12, sw_21, sw_22) if save else (None,) * 4
    arrive(2)
    block(h1, u1, h2, AT.first, V_G1, V_B11, V_B12, 0, (SPAN_ONE1, SPAN_TWO1), saved[:2])

    arrive(3)
    src.take(SPAN_ATTN)
    free()
    vectors(V_AG, AT.attn_gains, 2)
    vectors(V_AB, AT.attn_bias, 1)
    vectors(V_FG, AT.final_gains, 2)
    base = AT.conv_out - src.low
    tap_row = lax.broadcasted_iota(jnp.int32, (TAPS, 1), 0) < 9
    taps = [jnp.where(tap_row, wide[pl.ds(base + j, TAPS, stride=9), :], 0.0) for j in range(9)]
    taps = jnp.concatenate(taps, 1)
    rows_out = jnp.concatenate([jnp.where(colour(c), taps, 0.0) for c in range(3)], 0).astype(BF16)
    wz[...] = jnp.zeros_like(wz)
    wz[0 : 3 * TAPS, :] = dot(rows_out, expand[...], NT).astype(BF16)
    last = AT.bias_out - src.low
    b_out[...] = dot(eight(wide[last : last + 1, :]).astype(BF16), tile[...])
    for part in range(3):
        base = AT.attn_qkv - src.low
        for j in range(3):
            v = wide[pl.ds(base + part * 3 + j, CH_MID, stride=9), :]
            w_ref[part * CH_MID : (part + 1) * CH_MID, j * LINE : (j + 1) * LINE] = v.astype(BF16)
    src.matrix(w_ref.at[pl.ds(3 * CH_MID, CH_MID), :], AT.attn_out, CH_MID, 3)
    keep(w_ref.at[pl.ds(0, 4 * CH_MID), :], sw_attn if save else None)
    stats = all_stats(h2, gm)
    norm_to(pbuf, h2, stats, block_scales(vec, V_AG), False)
    n_low = pbuf[8 : 8 + ROWS, :].astype(BF16)
    for part in range(3):
        v = dot(n_low, w_ref[part * CH_MID : (part + 1) * CH_MID, :])
        qkv[:, part * CH_MID : (part + 1) * CH_MID] = v.astype(BF16)
    half = lane_half()

    def heads(img, carry):
        for pair in range(HEADS // 2):
            q, k, v = attention_pair(qkv, img, pair)
            outs = []
            for side in range(2):
                s = dot(keep_half(q, half, side), k, NT) * HEAD_DIM ** (-0.5)
                e = jnp.exp(s - jnp.max(s, 1, keepdims=True))
                prob = (e / jnp.sum(e, 1, keepdims=True)).astype(BF16)
                outs.append(dot(prob, v))
            mixed[pl.ds(pl.multiple_of(img * PIX, PIX), PIX), pair * LINE : (pair + 1) * LINE] = jnp.where(
                half, outs[0], outs[1]
            ).astype(BF16)
        return carry

    lax.fori_loop(0, MB_DEV, heads, 0, unroll=2)
    h3[...] = h2[...] + dot(mixed[...], w_ref[3 * CH_MID : 4 * CH_MID, :]) + vec[V_AB : V_AB + 1, :]

    src.take(SPAN_EMB2)
    src.matrix(w_sq.at[1], AT.second.embed, EMB_DIM, 6)
    m2 = dot3(silu(emb[...]), w_sq[1]) + src.row(AT.second.embed_bias, 6)
    mod[2:4, :] = m2[0:2]
    free()
    keep(w_sq.at[1], sw_emb2 if save else None)
    block(h3, u2, h4, AT.second, V_G2, V_B21, V_B22, 2, (SPAN_ONE2, SPAN_TWO2), saved[2:])

    stats = all_stats(h4, gm)
    norm_to(pbuf, h4, stats, block_scales(vec, V_FG), True)
    z = dot(pbuf[8 : 8 + ROWS, :].astype(BF16), wz[...], NT)
    t_all = dot3(z, sel[...])
    u_all = jnp.zeros((ROWS, LINE), F32)
    for shift in range(9):
        inside, by = upsample_masks(shift)
        moved = t_all if by == 0 else pltpu.roll(t_all, (-by) % ROWS, 0)
        u_all = u_all + jnp.where(inside, moved, 0.0)
    f_out[...] = dot3(u_all, gat[...]) + b_out[0:1, :]
    free()


def vmem(*shape_dtype):
    return pltpu.VMEM(*shape_dtype)


VM = pl.BlockSpec(memory_space=pltpu.VMEM)
HB = pl.BlockSpec(memory_space=pl.ANY)
SM = pl.BlockSpec(memory_space=pltpu.SMEM)


def state_shapes():
    act = ((ROWS, CH_MID), F32)
    return [
        ((4 * ROWS, 256), BF16),
        act, act, act,
        ((ROWS, 3 * CH_MID), BF16),
        ((ROWS, CH_MID), BF16),
        act, act, act,
        ((VEC_ROWS, CH_MID), F32),
        ((8, EMB_DIM), F32),
        ((8, EMB_DIM), F32),
        ((8, EMB_DIM), F32),
        ((LINE, CH_MID), BF16),
        ((4 * ROWS, 32), BF16),
    ]


def weight_shapes():
    sq = ((EMB_DIM, EMB_DIM), BF16)
    conv = ((9 * CH_MID, CH_MID), BF16)
    return [sq, sq, sq, ((9 * CH_BASE, CH_MID), BF16), conv, conv, ((4 * CH_MID, CH_MID), BF16), conv, conv]


def forward_call(save, me, labels, lines, x_in, phi, tables):
    pieces, moves, flip = lines
    sds = lambda s: jax.ShapeDtypeStruct(*s)
    outs = [sds(((ROWS, LINE), F32))]
    out_specs = [VM]
    state = state_shapes()
    scratch = []
    if save:
        outs += [sds(s) for s in state] + [sds(s) for s in weight_shapes()]
        out_specs += [VM] * len(state) + [HB] * len(weight_shapes())
    else:
        scratch += [vmem(*s) for s in state]
    scratch += [
        vmem((SHARDS // PLANE, PLANE, ROOM, LINE), BF16),
        vmem((10432, LINE), F32),
        vmem((9 * CH_MID, CH_MID), BF16),
        vmem((2, EMB_DIM, EMB_DIM), BF16),
        vmem((PADDED, 3 * CH_MID), BF16),
        vmem((ROWS + 16, CH_MID), F32),
        vmem((ROWS + 48, 256), F32),
        vmem((16, LINE), F32),
        vmem((32, 2 * LINE), F32),
        vmem((8, LINE), F32),
        pltpu.SemaphoreType.DMA((SHARDS // PLANE,)),
        pltpu.SemaphoreType.DMA,
    ]

    def body(*refs):
        forward_kernel(save, moves, flip, *refs)

    return pl.pallas_call(
        body,
        out_shape=outs,
        in_specs=[SM] * 2 + [VM] * 8 + [HB] * len(pieces),
        out_specs=out_specs,
        scratch_shapes=scratch,
        name="forward_save" if save else "forward_plain",
        **kernel_params(),
    )(me, labels, x_in, phi, *tables, *pieces)


def column_sum(pbuf):
    def body(c, acc):
        return acc + jnp.sum(pbuf[pl.ds(pl.multiple_of(c * CHUNK + 8, 8), CHUNK), :], 0, keepdims=True)

    return lax.fori_loop(0, ROWS // CHUNK, body, jnp.zeros((1, CH_MID), F32))


def refill(pbuf, source):
    for c in range(0, ROWS, CHUNK):
        pbuf[8 + c : 8 + c + CHUNK, :] = source[c : c + CHUNK, :]


def block_back_two(dh, u_ref, at, base, rows, vec, mod, mod_row, weights, tools, g, dm):
    g_row, b1_row, b2_row = rows
    sbuf, pbuf, dx, at_ref, gm = tools
    put_row(g, at.bias_two - base, colsum(dh, 0, ROWS))
    u_stats = all_stats(u_ref, gm)
    scales = block_scales(vec, g_row + 2, mod, mod_row)
    norm_to(pbuf, u_ref, u_stats, scales, True)
    transpose_to(at_ref, pbuf)
    refill(pbuf, dh)
    shift_to(sbuf, pbuf)
    conv_back(sbuf, at_ref, weights.take(), dx, g, at.conv_two - base)
    weights.begin()

    def emit_inner(r, v):
        pbuf[pl.ds(r + 8, CHUNK), :] = v

    sums = norm_back(u_ref, dx, u_stats, scales, True, gm, emit_inner)
    gain, shift = vec[g_row + 2 : g_row + 3, :], vec[g_row + 3 : g_row + 4, :]
    d_gain = d_shift = 0.0
    dm[...] = jnp.zeros_like(dm)
    for img, (a, b) in enumerate(sums):
        scale = 1.0 + mod[mod_row + img : mod_row + img + 1, :CH_MID]
        d_gain, d_shift = d_gain + scale * b, d_shift + scale * a
        dm[img : img + 1, :CH_MID] = gain * b + shift * a
        dm[img : img + 1, CH_MID:] = a
    return d_gain, d_shift


def block_back_one(dh, x_ref, at, base, rows, vec, weights, tools, g):
    g_row, b1_row, b2_row = rows
    sbuf, pbuf, dx, at_ref, gm = tools
    put_row(g, at.bias_one - base, column_sum(pbuf))
    shift_to(sbuf, pbuf)
    stats = all_stats(x_ref, gm)
    scales = block_scales(vec, g_row)
    norm_to(pbuf, x_ref, stats, scales, True)
    transpose_to(at_ref, pbuf)
    conv_back(sbuf, at_ref, weights.take(), dx, g, at.conv_one - base)
    weights.begin()

    def emit_outer(r, v):
        dh[pl.ds(r, CHUNK), :] += v

    sums = norm_back(x_ref, dx, stats, scales, True, gm, emit_outer)
    put_row(g, at.gains - base, sums[0][1] + sums[1][1])
    put_row(g, at.gains + 3 - base, sums[0][0] + sums[1][0])


def rowsum(v):
    return jnp.sum(v, 0, keepdims=True)


def put_outer(g, at, left, right):
    for c in range(-(-left.shape[1] // LINE)):
        piece = outer(left[:, c * LINE : (c + 1) * LINE], right)
        put_lines(g, at + c * LINE * (EMB_DIM // LINE), piece, EMB_DIM // LINE)


class Weights:
    def __init__(self, sources, slots, sems):
        self.copies = []
        for n, source in enumerate(sources):
            target = slots.at[n % 2, pl.ds(0, source.shape[0]), :]
            self.copies.append((pltpu.make_async_copy(source, target, sems.at[n % 2]), target))
        self.begun = self.done = 0

    def begin(self):
        if self.begun < len(self.copies):
            self.copies[self.begun][0].start()
            self.begun += 1

    def take(self):
        copy, target = self.copies[self.done]
        copy.wait()
        self.done += 1
        return target


class Leave:
    def __init__(self, me, g, base, keep, send, stage, sems):
        self.core, self.place = lax.rem(me[0], 2), lax.div(me[0], 2)
        self.g, self.base, self.outs, self.stage, self.sems = g, base, (keep, send), stage, sems
        self.copies = []

    def plane(self, plane):
        for q in range(PLANE // 2):
            at = q ^ self.place
            first = PLANES[plane] + 2 * q * SHARD - self.base
            for side in range(2):
                core = 1 - self.core if side else self.core
                start = first + core * SHARD
                stage = self.stage.at[2 * q + side]
                whole, rest = divmod(ROOM, 288)

                def body(c, carry):
                    lines = self.g[pl.ds(pl.multiple_of(start + c * 288, 8), 288), :]
                    stage[pl.ds(pl.multiple_of(c * 288, 16), 288), :] = lines.astype(BF16)
                    return carry

                lax.fori_loop(0, whole, body, 0)
                lines = self.g[pl.ds(pl.multiple_of(start + whole * 288, 8), rest), :]
                stage[whole * 288 :, :] = lines.astype(BF16)
                copy = pltpu.make_async_copy(stage, self.outs[side].at[at], self.sems.at[side])
                copy.start()
                self.copies.append(copy)

    def below(self, count, rest):
        copy = pltpu.make_async_copy(self.g.at[pl.ds(0, count), :], rest, self.sems.at[2])
        copy.start()
        self.copies.append(copy)

    def wait(self):
        for copy in self.copies:
            copy.wait()


def clear_lines(g, first, count):
    if count:
        g[first : first + count, :] = jnp.zeros((count, LINE), F32)


def prepare(sbuf, pbuf):
    clear_pads(sbuf)
    pbuf[0:8, :] = jnp.zeros((8, CH_MID), F32)
    pbuf[ROWS + 8 : ROWS + 16, :] = jnp.zeros((8, CH_MID), F32)


def back_top_kernel(*refs):
    me, df, wz, gm, sel, gat, tile, expand, vec, mod, emb, h4, u2, h3, qkv, mixed, h2, s22, s21, s_attn, s_emb = refs[:21]
    keep, send, rest, dh, dse = refs[21:26]
    g, slots, sbuf, pbuf, dx, at_ref, stage, sems, out_sems, w_sq, dqkv, dm, sq_sem = refs[26:]
    base = BASE_ONE
    weights = Weights([s22, s21, s_attn], slots, sems)
    weights.begin()
    weights.begin()
    sq_copy = pltpu.make_async_copy(s_emb, w_sq, sq_sem)
    sq_copy.start()
    prepare(sbuf, pbuf)
    clear_lines(g, TAIL - base, g.shape[0] - (TAIL - base))
    tools = (sbuf, pbuf, dx, at_ref, gm)

    stats = all_stats(h4, gm)
    scales = block_scales(vec, V_FG)
    norm_to(pbuf, h4, stats, scales, True)
    transpose_to(at_ref, pbuf)
    spread = dot(df[...].astype(BF16), gat[...], NT)
    dt = jnp.zeros((ROWS, LINE), F32)
    for shift in range(9):
        inside, by = upsample_masks(shift)
        part = jnp.where(inside, spread, 0.0)
        dt = dt + (part if by == 0 else pltpu.roll(part, by % ROWS, 0))
    dz = dot(dt.astype(BF16), sel[...], NT)
    parts = split3(dz)
    dwz = dot(at_ref[...], parts[0]) + dot(at_ref[...], parts[1]) + dot(at_ref[...], parts[2])
    dx[...] = dot(parts[0], wz[...]) + dot(parts[1], wz[...]) + dot(parts[2], wz[...])
    d_rows = dot3(dwz.T[0 : 3 * TAPS, :], expand[...])
    d_taps = jnp.zeros((TAPS, 3 * CH_MID), F32)
    for c in range(3):
        d_taps = d_taps + jnp.where(colour(c), d_rows[c * TAPS : (c + 1) * TAPS, :], 0.0)
    for j in range(9):
        g[pl.ds(TAIL - base + j, 9, stride=9), :] = d_taps[0:9, j * LINE : (j + 1) * LINE]
    b_row = AT.bias_out - base
    g[b_row : b_row + 1, :] = dot3(eight(colsum(df, 0, ROWS)), tile[...], NT)[0:1]

    def emit_first(r, v):
        dh[pl.ds(r, CHUNK), :] = v

    sums = norm_back(h4, dx, stats, scales, True, gm, emit_first)
    put_row(g, AT.final_gains - base, sums[0][1] + sums[1][1])
    put_row(g, AT.final_gains + 3 - base, sums[0][0] + sums[1][0])

    rows = (V_G2, V_B21, V_B22)
    d_gain, d_shift = block_back_two(dh, u2, AT.second, base, rows, vec, mod, 2, weights, tools, g, dm)
    put_row(g, AT.second.gains + 6 - base, d_gain)
    put_row(g, AT.second.gains + 9 - base, d_shift)
    block_back_one(dh, h3, AT.second, base, rows, vec, weights, tools, g)
    se = silu(emb[...])
    put_outer(g, AT.second.embed - base, se, dm[...])
    put_row(g, AT.second.embed_bias - base, rowsum(dm[...]))
    sq_copy.wait()
    dse[...] = dot3(dm[...], w_sq[...], NT)

    put_row(g, AT.attn_bias - base, colsum(dh, 0, ROWS))
    w = weights.take()
    d_low = dh[...].astype(BF16)
    for c in range(ROWS // LINE):
        at_ref[:, c * LINE : (c + 1) * LINE] = mixed[c * LINE : (c + 1) * LINE, :].astype(F32).T.astype(BF16)
    put_lines(g, AT.attn_out - base, dot(at_ref[...], d_low), 3)
    pbuf[8 : 8 + ROWS, :] = dot(d_low, w[3 * CH_MID : 4 * CH_MID, :], NT)
    half = lane_half()
    scale = HEAD_DIM ** (-0.5)

    def heads(img, carry):
        rows = pl.ds(pl.multiple_of(img * PIX, PIX), PIX)
        for pair in range(HEADS // 2):
            q, k, v = attention_pair(qkv, img, pair)
            cols = slice(pair * LINE, (pair + 1) * LINE)
            do = pbuf[pl.ds(pl.multiple_of(img * PIX + 8, 8), PIX), cols].astype(BF16)
            dqs, dks, dvs = [], [], []
            for side in range(2):
                s = dot(keep_half(k, half, side), q, NT) * scale
                e = jnp.exp(s - jnp.max(s, 0, keepdims=True))
                prob = e / jnp.sum(e, 0, keepdims=True)
                dvs.append(dot(prob.astype(BF16), do))
                dp = dot(keep_half(v, half, side), do, NT)
                ds = prob * (dp - jnp.sum(dp * prob, 0, keepdims=True))
                dks.append(dot(ds.astype(BF16), q))
                dqs.append(dot(ds.T.astype(BF16), k))
            for part, pieces in enumerate((dqs, dks, dvs)):
                value = jnp.where(half, pieces[0], pieces[1])
                if part < 2:
                    value = value * scale
                dqkv[rows, part * CH_MID + pair * LINE : part * CH_MID + (pair + 1) * LINE] = value.astype(BF16)
        return carry

    lax.fori_loop(0, MB_DEV, heads, 0, unroll=2)
    stats = all_stats(h2, gm)
    scales = block_scales(vec, V_AG)
    norm_to(pbuf, h2, stats, scales, False)
    transpose_to(at_ref, pbuf)
    dx[...] = jnp.zeros_like(dx)
    for part in range(3):
        d = dqkv[:, part * CH_MID : (part + 1) * CH_MID]
        dw = dot(at_ref[...], d)
        for j in range(3):
            g[pl.ds(AT.attn_qkv - base + part * 3 + j, CH_MID, stride=9), :] = dw[:, j * LINE : (j + 1) * LINE]
        dx[...] += dot(d, w[part * CH_MID : (part + 1) * CH_MID, :], NT)
    weights.begin()

    def emit(r, v):
        dh[pl.ds(r, CHUNK), :] += v

    sums = norm_back(h2, dx, stats, scales, False, gm, emit)
    put_row(g, AT.attn_gains - base, sums[0][1] + sums[1][1])
    put_row(g, AT.attn_gains + 3 - base, sums[0][0] + sums[1][0])

    leave = Leave(me, g, base, keep, send, stage, out_sems)
    leave.plane(3)
    leave.below(PLANES[3] - base, rest)
    leave.wait()


def back_second_half_kernel(*refs):
    me, dh, gm, vec, mod, u1, s12, rest_in = refs[:8]
    keep, send, rest, du, dm, extra = refs[8:14]
    g, slots, sbuf, pbuf, dx, at_ref, stage, sems, out_sems, in_sem = refs[14:]
    base = BASE_TWO
    weights = Weights([s12], slots, sems)
    weights.begin()
    above = pltpu.make_async_copy(rest_in, g.at[pl.ds(BASE_ONE - base, PLANES[3] - BASE_ONE), :], in_sem)
    above.start()
    prepare(sbuf, pbuf)
    clear_lines(g, PLANES[3] - base, g.shape[0] - (PLANES[3] - base))
    above.wait()
    rows = (V_G1, V_B11, V_B12)
    tools = (sbuf, pbuf, dx, at_ref, gm)
    d_gain, d_shift = block_back_two(dh, u1, AT.first, base, rows, vec, mod, 0, weights, tools, g, dm)
    extra[...] = jnp.zeros_like(extra)
    extra[0:1, :] = d_gain
    extra[1:2, :] = d_shift
    for c in range(0, ROWS, CHUNK):
        du[c : c + CHUNK, :] = pbuf[8 + c : 8 + c + CHUNK, :]
    leave = Leave(me, g, base, keep, send, stage, out_sems)
    leave.plane(2)
    leave.below(PLANES[2] - base, rest)
    leave.wait()


def back_first_half_kernel(*refs):
    me, dh_in, du, dm, extra, dse_in, gm, vec, emb, h1, s11, s_emb, rest_in = refs[:13]
    keep, send, rest, dh, dse = refs[13:18]
    g, slots, sbuf, pbuf, dx, at_ref, stage, sems, out_sems, w_sq, in_sem, sq_sem = refs[18:]
    base = BASE_THREE
    weights = Weights([s11], slots, sems)
    weights.begin()
    sq_copy = pltpu.make_async_copy(s_emb, w_sq, sq_sem)
    sq_copy.start()
    above = pltpu.make_async_copy(rest_in, g.at[pl.ds(BASE_TWO - base, PLANES[2] - BASE_TWO), :], in_sem)
    above.start()
    prepare(sbuf, pbuf)
    clear_lines(g, PLANES[2] - base, g.shape[0] - (PLANES[2] - base))
    refill(pbuf, du)
    for c in range(0, ROWS, CHUNK):
        dh[c : c + CHUNK, :] = dh_in[c : c + CHUNK, :]
    above.wait()
    tools = (sbuf, pbuf, dx, at_ref, gm)
    put_outer(g, AT.first.embed - base, silu(emb[...]), dm[...])
    put_row(g, AT.first.embed_bias - base, rowsum(dm[...]))
    block_back_one(dh, h1, AT.first, base, (V_G1, V_B11, V_B12), vec, weights, tools, g)
    put_row(g, AT.first.gains + 6 - base, extra[0:1, :])
    put_row(g, AT.first.gains + 9 - base, extra[1:2, :])
    leave = Leave(me, g, base, keep, send, stage, out_sems)
    leave.plane(1)
    leave.below(PLANES[1] - base, rest)
    sq_copy.wait()
    dse[...] = dse_in[...] + dot3(dm[...], w_sq[...], NT)
    leave.wait()


def back_low_kernel(*refs):
    me, labels, dh, dse, emb, pre, phi, h0s, xp, s_down, s_time, rest_in = refs[:12]
    keep, send = refs[12:14]
    g, slots, sbuf, pbuf, h0t, stage, sems, out_sems, w_sq, demb_ref, dwin, dbin, in_sem, sq_sem = refs[14:]
    weights = Weights([s_down], slots, sems)
    weights.begin()
    sq_copy = pltpu.make_async_copy(s_time, w_sq, sq_sem)
    sq_copy.start()
    above = pltpu.make_async_copy(rest_in, g.at[pl.ds(BASE_THREE, PLANES[1] - BASE_THREE), :], in_sem)
    above.start()
    prepare(sbuf, pbuf)
    clear_lines(g, PLANES[1], g.shape[0] - PLANES[1])
    above.wait()
    demb = dse[...] * silu_slope(emb[...])
    put_row(g, AT.time_bias_two, rowsum(demb))
    put_outer(g, AT.time_two, silu(pre[...]), demb)
    sq_copy.wait()
    dpre = dot3(demb, w_sq[...], NT) * silu_slope(pre[...])
    put_row(g, AT.time_bias_one, rowsum(dpre))
    put_outer(g, AT.time_one, phi[...], dpre)
    clear = 240
    first, lines = AT.class_table, CLASSES * (EMB_DIM // LINE)

    def wipe(c, carry):
        g[pl.ds(first + c * clear, clear), :] = jnp.zeros((clear, LINE), F32)
        return carry

    lax.fori_loop(0, lines // clear, wipe, 0)
    demb_ref[...] = demb
    for n in range(MB_DEV):
        for j in range(EMB_DIM // LINE):
            at = first + labels[n] * (EMB_DIM // LINE) + j
            g[pl.ds(at, 1), :] += demb_ref[n : n + 1, j * LINE : (j + 1) * LINE]

    put_row(g, AT.bias_down, colsum(dh, 0, ROWS))
    refill(pbuf, dh)
    shift_to(sbuf, pbuf)
    w = weights.take()
    dwin[...] = jnp.zeros_like(dwin)
    dbin[...] = jnp.zeros_like(dbin)
    for ph in range(4):
        for c in range(ROWS // LINE):
            rows = slice(ph * ROWS + c * LINE, ph * ROWS + (c + 1) * LINE)
            h0t[:, c * LINE : (c + 1) * LINE] = h0s[rows, :].astype(F32).T.astype(BF16)
        d0 = jnp.zeros((ROWS, CH_BASE), F32)
        for ky in ((0, 2) if ph // 2 else (1,)):
            for kx in ((0, 2) if ph % 2 else (1,)):
                side = 2 if kx == 0 else 1
                d = shifted(sbuf, 32 if ky == 0 else 16, slice(side * CH_MID, (side + 1) * CH_MID))
                t = 3 * ky + kx
                d0 = d0 + dot(d, w[t * CH_BASE : (t + 1) * CH_BASE, :], NT)
                put_lines(g, AT.conv_down + t * CH_BASE * 3, dot(h0t[0:CH_BASE, :], d), 3)
        dbin[0:1, :CH_BASE] += rowsum(d0)
        dwin[:, :CH_BASE] += dot(xp[ph * ROWS : (ph + 1) * ROWS, :], d0.astype(BF16), TN)
    dwin[29:30, :] = dbin[0:1, :]
    even, odd = dwin[0:16, :], dwin[16:32, :]
    turned = pltpu.roll(odd[:, :LINE], LINE // 2, 1), pltpu.roll(odd[:, LINE:], LINE // 2, 1)
    g[pl.ds(0, 14, stride=3), :] = even[0:14, :LINE]
    g[pl.ds(1, 14, stride=3), :] = jnp.where(first_lanes(), even[:, LINE:], turned[0])[0:14]
    g[pl.ds(2, 14, stride=3), :] = jnp.where(first_lanes(), turned[0], turned[1])[0:14]
    leave = Leave(me, g, 0, keep, send, stage, out_sems)
    leave.plane(0)
    leave.wait()


def kernel_params():
    return dict(
        compiler_params=pltpu.CompilerParams(vmem_limit_bytes=60 * 1024 * 1024),
        cost_estimate=pl.CostEstimate(flops=8 * 10**9, bytes_accessed=4 * 10**7, transcendentals=10**6),
    )


def back_call(kernel, name, lines, slots, args, smem, hbm, rest, outs, scratch, norms=True):
    sds = lambda *s: jax.ShapeDtypeStruct(*s)
    plane = sds((PLANE // 2, ROOM, LINE), BF16)
    rest = [sds((rest, LINE), F32)] if rest else []
    common = [
        vmem((lines + 8, LINE), F32),
        vmem((slots, 9 * CH_MID, CH_MID), BF16),
        vmem((PADDED, 3 * CH_MID), BF16),
        vmem((ROWS + 16, CH_MID), F32),
    ]
    if norms:
        common += [vmem((ROWS, CH_MID), F32), vmem((CH_MID, ROWS), BF16)]
    else:
        common += [vmem((256, ROWS), BF16)]
    common += [
        vmem((PLANE, ROOM, LINE), BF16),
        pltpu.SemaphoreType.DMA((2,)),
        pltpu.SemaphoreType.DMA((3,)),
    ]
    return pl.pallas_call(
        kernel,
        out_shape=[plane, plane, *rest, *(sds(*o) for o in outs)],
        in_specs=[SM] * smem + [VM] * (len(args) - smem - hbm) + [HB] * hbm,
        out_specs=[HB] * (2 + len(rest)) + [VM] * len(outs),
        scratch_shapes=common + scratch,
        name=name,
        **kernel_params(),
    )(*args)


ACT = ((ROWS, CH_MID), F32)
WIDE_ROW = ((8, EMB_DIM), F32)
DMA = pltpu.SemaphoreType.DMA


def back_top(args):
    scratch = [vmem((EMB_DIM, EMB_DIM), BF16), vmem((ROWS, 3 * CH_MID), BF16), vmem(*WIDE_ROW), DMA]
    lines = ALL_LINES - BASE_ONE
    return back_call(
        back_top_kernel, "back_top", lines, 2, args, 1, 4, PLANES[3] - BASE_ONE, [ACT, WIDE_ROW], scratch
    )


def back_second_half(args):
    outs = [ACT, WIDE_ROW, ((8, CH_MID), F32)]
    lines = PLANES[3] - BASE_TWO
    return back_call(back_second_half_kernel, "back_b", lines, 1, args, 1, 2, PLANES[2] - BASE_TWO, outs, [DMA])


def back_first_half(args):
    scratch = [vmem((EMB_DIM, EMB_DIM), BF16), DMA, DMA]
    lines = PLANES[2] - BASE_THREE
    return back_call(
        back_first_half_kernel, "back_c", lines, 1, args, 1, 3, PLANES[1] - BASE_THREE, [ACT, WIDE_ROW], scratch
    )


def back_low(args):
    scratch = [
        vmem((EMB_DIM, EMB_DIM), BF16),
        vmem(*WIDE_ROW),
        vmem((32, 2 * LINE), F32),
        vmem((8, 2 * LINE), F32),
        DMA,
        DMA,
    ]
    return back_call(back_low_kernel, "back_low", PLANES[1], 1, args, 2, 3, 0, [], scratch, False)


def karras(index):
    ramp_frac = index.astype(F32) / (DISCRETE - 1)
    low_root = SIGMA_LOW ** (1.0 / RHO_POWER)
    high_root = SIGMA_HIGH ** (1.0 / RHO_POWER)
    return (low_root + ramp_frac * (high_root - low_root)) ** RHO_POWER


def preconditioning_factors(sigma):
    variance_sum = sigma * sigma + SIGMA_DATA**2
    skip = SIGMA_DATA**2 / ((sigma - SIGMA_LOW) ** 2 + SIGMA_DATA**2)
    out = (sigma - SIGMA_LOW) * SIGMA_DATA * lax.rsqrt(variance_sum)
    return (skip, out, lax.rsqrt(variance_sum))


def noise_features(sigma):
    half_width = CH_BASE // 2
    frequency = jnp.exp(-math.log(10000.0) * jnp.arange(half_width, dtype=F32) / half_width)
    phases = 250.0 * jnp.log(sigma)[:, None] * frequency
    return jnp.pad(jnp.concatenate([jnp.cos(phases), jnp.sin(phases)], 1), ((0, 8 - MB_DEV), (0, 0)))


def pixels(images):
    lead = images.shape[0]
    split = images.reshape(lead, MB_DEV, HALF, 2, HALF, 2, 3)
    return split.transpose(0, 1, 2, 4, 3, 5, 6).reshape(lead, ROWS, 12)


def pixel_live(counts, valid_rows):
    row = lax.broadcasted_iota(jnp.int32, (ROWS, 12), 0)
    lane = lax.broadcasted_iota(jnp.int32, (ROWS, 12), 1)
    slot = row // PIX
    line = 2 * ((row // HALF) % HALF) + lane // 6
    top = jnp.where(slot == 0, valid_rows[0], valid_rows[1])
    return ((slot < counts[0]) & (line < top)).astype(F32)


def per_part(me, labels, lines, inputs, save, tables):
    _, x_in, phi, _ = inputs
    results = forward_call(save, me, labels, lines, x_in, phi, tables)
    return results[0], results[1:]


AXIS = "fsdp"
CORE, EAST, SOUTH, UP = 1, 2, 4, 8
CUT_ROWS = ROOM // 2


def swap(values, hop):
    return lax.ppermute(values, AXIS, [(i, i ^ hop) for i in range(SHARDS)])


def total_of(values, n):
    hop = 1
    while hop < n:
        values = values + lax.ppermute(values, AXIS, [(i, i ^ hop) for i in range(n)])
        hop *= 2
    return values


CUTS = (0, 880, 1760, ROOM)
TALL = SHARDS // PLANE


def gate(values, after):
    count = len(values)

    def body(*refs):
        pass

    return pl.pallas_call(
        body,
        out_shape=[jax.ShapeDtypeStruct(v.shape, v.dtype) for v in values],
        in_specs=[HB] * (count + len(after)),
        out_specs=[HB] * count,
        input_output_aliases={i: i for i in range(count)},
        name="gate",
    )(*values, *after)


def climb(values, way, far, first=0):
    planes = range(first, TALL - far) if way == 1 else range(TALL - 1 - first, far - 1, -1)
    pairs = [(q * PLANE + i, (q + way * far) * PLANE + i) for q in planes for i in range(PLANE)]
    return lax.ppermute(values, AXIS, pairs)


def column_window(slots, z):
    rows = []
    for p in range(TALL):
        value = slots[TALL - 1 + p]
        for q in range(1, TALL):
            value = jnp.where(z == q, slots[TALL - 1 - q + p], value)
        rows.append(value)
    return jnp.stack(rows)


def column_gather(own, z):
    below, above = [climb(own, 1, 1)], [climb(own, -1, 1)]
    for step in range(1, TALL - 1):
        below.append(climb(below[-1], 1, 1, step))
        above.append(climb(above[-1], -1, 1, step))
    return column_window([*below[::-1], own, *above], z), [below[0], above[0]], [below[-1], above[-1]]


def gather_lines(shard, z, early):
    ab, c = shard[: CUTS[2]], shard[CUTS[2] :]
    c_two = jnp.stack([c, swap(c, SOUTH)])
    c_four = jnp.concatenate([c_two, swap(c_two, EAST)])
    column, step, last = column_gather(ab, z)
    za, zb = column[:, : CUTS[1]], column[:, CUTS[1] :]
    done, ready = early(step)
    a_two, b_two = jnp.stack([za, swap(za, EAST)]), jnp.stack([zb, swap(zb, SOUTH)])
    a_far, b_far = swap(a_two, SOUTH), swap(b_two, EAST)
    (c_four,) = gate([c_four], [*last, *ready])
    c_all, _, _ = column_gather(c_four, z)
    pieces = [a_two, a_far, b_two, b_far, c_all]
    return done, pieces + [swap(v, CORE) for v in pieces]


def gather_moves():
    places = [(0, 1), (2, 3), (0, 2), (1, 3), (0, 2, 1, 3)]
    part = (0, 0, 1, 1, 2)
    moves = []
    for core in range(2):
        for n in range(5):
            row, end = CUTS[part[n]], CUTS[part[n] + 1]
            for lead, place in enumerate(places[n]):
                moves.append((core * 5 + n, lead, 2 * place + core, row, end - row))
    return moves


def gather_plain(shard):
    rows = shard.shape[0]
    lines = lax.all_gather(shard, AXIS, axis=0, tiled=True)
    if rows != ROOM:
        lines = jnp.pad(lines.reshape(SHARDS, SHARD, LINE), ((0, 0), (0, ROOM - SHARD), (0, 0)))
    lines = lines.reshape(TALL, PLANE, ROOM, LINE)
    return [lines], [(0, r, r, 0, ROOM) for r in range(PLANE)], (True,)


def low(v):
    return v.astype(BF16)


def wide(v):
    return v.astype(F32)


class PlaneSum:
    def __init__(self, keep, send):
        self.keep, self.got = keep, swap(send, CORE)
        self.a, self.b = slice(0, CUT_ROWS), slice(CUT_ROWS, ROOM)

    def quarter(self, i, rows):
        return wide(self.keep[i, rows]) + wide(self.got[i, rows])

    def first(self):
        a = low(jnp.stack([self.quarter(1, self.a), self.quarter(3, self.a)]))
        b = low(jnp.stack([self.quarter(2, self.b), self.quarter(3, self.b)]))
        return a, b

    def send_first(self, a, b):
        self.got_a, self.got_b = swap(a, EAST), swap(b, SOUTH)

    def last(self):
        return low(self.quarter(2, self.a) + wide(self.got_a[1])), low(self.quarter(1, self.b) + wide(self.got_b[1]))

    def send_last(self, a, b):
        self.end_a, self.end_b = swap(a, SOUTH), swap(b, EAST)

    def total(self):
        a = self.quarter(0, self.a) + wide(self.got_a[0]) + wide(self.end_a)
        b = self.quarter(0, self.b) + wide(self.got_b[0]) + wide(self.end_b)
        return jnp.concatenate([a, b])


def column_sums(parts, first, z):
    pick = lambda p: jnp.where(p == first, parts[0], parts[1])
    total = 0.0
    for way in (1, -1):
        run = None
        for far in range(TALL - 1, 0, -1):
            holders = [q for q in range(TALL) if q + way * far in (first, first + 1)]
            if not holders:
                continue
            value = pick(z + way * far)
            if run is not None:
                value = value + run
            pairs = [(q * PLANE + i, (q + way) * PLANE + i) for q in holders for i in range(PLANE)]
            run = wide(lax.ppermute(low(value), AXIS, pairs))
        total = total + run
    return total


def per_device(n, images, noise_draws, labels, step_index, valid_rows, counts, master, momentum, ema):
    direct = n == SHARDS
    index = lax.axis_index(AXIS)
    me = jnp.where(direct, lax.rem(index, PLANE), 0).astype(jnp.int32)[None]
    z = lax.div(index, PLANE)
    shards = [v.astype(BF16).reshape(-1, LINE) for v in (master, ema)]
    tables = tuple(jnp.asarray(v, BF16) for v in (group_table(), *spread_tables(), expand_table(), patch_table()))
    live = (jnp.arange(MB_DEV) < counts[0]).astype(jnp.int32)
    local_rows = jnp.sum(live * jnp.clip(valid_rows, 0, RES)).astype(F32)

    total = total_of(jnp.broadcast_to(local_rows, (8, LINE)), n)
    pixel_total = 3.0 * RES * total[0, 0]

    def early(after):
        clean, noise = gate([images, noise_draws], after) if after else (images, noise_draws)
        clean, noise = pixels(jnp.stack([clean, noise]))
        per_row = lambda v: jnp.repeat(v, PIX)[:, None]

        def inputs_of(sigma):
            noisy = clean + per_row(sigma) * noise
            skip, out_scale, in_scale = preconditioning_factors(sigma)
            x_in = jnp.pad((per_row(in_scale) * noisy).astype(BF16), ((0, 0), (0, LINE - 12)))
            return per_row(skip) * noisy, x_in, noise_features(sigma), per_row(out_scale)

        mask = pixel_live(counts, valid_rows)
        both = inputs_of(karras(step_index)), inputs_of(karras(step_index + 1))
        return (*both, mask), [v for part in both for v in part[:3]] + [mask, total]

    if direct:
        rooms = [jnp.pad(v, ((0, ROOM - SHARD), (0, 0))) for v in shards]
        target = gather_plain(rooms[1])
        (in_lo, in_hi, mask), pieces = gather_lines(rooms[0], z, early)
        online = (pieces, gather_moves(), (False,) * 4 + (True,) + (False,) * 4 + (True,))
    else:
        online, target = gather_plain(shards[0]), gather_plain(shards[1])
        in_lo, in_hi, mask = early(())[0]
    model_o, saved = per_part(me, labels, online, in_hi, True, tables)
    model_t, _ = per_part(jnp.zeros_like(me), labels, target, in_lo, False, tables)
    online_out = in_hi[0] + in_hi[3] * model_o[:, :12]
    target_out = in_lo[0] + in_lo[3] * model_t[:, :12]
    phi, out_scale = in_hi[2], in_hi[3]
    gap = online_out - target_out
    local_loss = jnp.sum(mask * jnp.square(gap))
    grad_model = out_scale * 2.0 * mask * gap / pixel_total
    bias_out = jnp.sum(grad_model.reshape(ROWS, 4, 3), axis=(0, 1))
    (h0s, h1, u1, h2, qkv, mixed, h3, u2, h4, vec, mod, emb, pre, wz, xp) = saved[:15]
    s_time, s_emb1, s_emb2, s_down, s11, s12, s_attn, s21, s22 = saved[15:]
    gm = tables[0]
    df = jnp.pad(grad_model, ((0, 0), (0, LINE - 12)))
    small = jnp.concatenate([local_loss[None], bias_out])
    small = jnp.broadcast_to(small, (8, 4))
    keep3, send3, rest, dh, dse = back_top(
        (me, df, wz, *tables[:5], vec, mod, emb, h4, u2, h3, qkv, mixed, h2, s22, s21, s_attn, s_emb2)
    )
    if direct:
        three = PlaneSum(keep3, send3)
    keep2, send2, rest, du, dm, extra = back_second_half((me, dh, gm, vec, mod, u1, s12, rest))
    if direct:
        first3 = three.first()
        (du,) = gate([du], first3)
        three.send_first(*first3)
        two = PlaneSum(keep2, send2)
    keep1, send1, rest, dh, dse = back_first_half((me, dh, du, dm, extra, dse, gm, vec, emb, h1, s11, s_emb1, rest))
    if direct:
        last3, first2 = three.last(), two.first()
        (dh,) = gate([dh], [*last3, *first2])
        three.send_last(*last3)
        two.send_first(*first2)
        one = PlaneSum(keep1, send1)
    keep0, send0 = back_low((me, labels, dh, dse, emb, pre, phi, h0s, xp, s_down, s_time, rest))
    if direct:
        zero = PlaneSum(keep0, send0)
        one.send_first(*one.first())
        two.send_last(*two.last())
        first0 = zero.first()
        zero.send_first(*first0)
        (small,) = gate([small], first0)
        small = total_of(small, n)
        top = [two.total(), three.total()]
        high = column_sums(top, 2, z)
        one.send_last(*one.last())
        zero.send_last(*zero.last())
        bottom = gate([zero.total(), one.total()], [small])
        reduced = column_sums(bottom, 0, z) + high
        own = jnp.where(z < 2, jnp.where(z == 0, bottom[0], bottom[1]), jnp.where(z == 2, top[0], top[1]))
        reduced = (reduced + own)[:SHARD].reshape(-1)
    else:
        small = total_of(small, n)
        both = [jnp.stack([wide(k), wide(s)], 1) for k, s in ((keep0, send0), (keep1, send1), (keep2, send2), (keep3, send3))]
        lines = jnp.stack(both).reshape(SHARDS, ROOM, LINE)[:, :SHARD].reshape(n, -1)
        reduced = lax.psum_scatter(lines, AXIS, scatter_dimension=0, tiled=True).reshape(-1)
    new_momentum = MOMENTUM * momentum + reduced
    new_master = master - LEARN_RATE * (reduced + MOMENTUM * new_momentum)
    new_ema = EMA_DECAY * ema + (1.0 - EMA_DECAY) * new_master
    return (small[0, 0] / pixel_total, new_momentum, new_master, new_ema, small[0, 1:])


def solution(mesh):
    n = mesh.shape[AXIS]

    def step(*args):
        return per_device(n, *args)

    return jax.shard_map(
        step,
        mesh=mesh,
        in_specs=(P(AXIS, None, None, None),) * 2 + (P(AXIS),) * 7,
        out_specs=(P(), P(AXIS), P(AXIS), P(AXIS), P()),
        check_vma=False,
    )
```

```python
import math

import jax
import jax.numpy as jnp
import numpy as np
from jax import lax
from jax.experimental import pallas as pl
from jax.experimental.pallas import tpu as pltpu
from jax.sharding import PartitionSpec as P

CH_BASE = 192
CH_MID = 384
EMB_DIM = 768
HEADS = 6
HEAD_DIM = 64
CLASSES = 1000
GROUPS = 32
RES = 32
MB_DEV = 2
DISCRETE = 40

EPSILON = 1e-05
SIGMA_DATA = 0.5
SIGMA_LOW = 0.002
SIGMA_HIGH = 80.0
RHO_POWER = 7.0
MOMENTUM = 0.9
EMA_DECAY = 0.9
LEARN_RATE = 2000.0

F32 = jnp.float32
BF16 = jnp.bfloat16
LINE = 128
HALF = RES // 2
PIX = HALF * HALF
ROWS = MB_DEV * PIX
GROUP_SIZE = PIX * (CH_MID // GROUPS)
CHUNK = 128
PADDED = 16 + MB_DEV * (PIX + 16)
NN = (((1,), (0,)), ((), ()))
NT = (((1,), (1,)), ((), ()))
TN = (((0,), (0,)), ((), ()))


class Place:
    pass


class Cut:
    def __init__(self):
        self.offset = 0

    def take(self, *shape):
        at = self.offset
        self.offset += math.prod(shape)
        return at // LINE


def block_place(cut):
    at = Place()
    at.gains = cut.take(4, CH_MID)
    at.conv_one = cut.take(9 * CH_MID, CH_MID)
    at.bias_one = cut.take(CH_MID)
    at.embed = cut.take(EMB_DIM, 2 * CH_MID)
    at.embed_bias = cut.take(2 * CH_MID)
    at.conv_two = cut.take(9 * CH_MID, CH_MID)
    at.bias_two = cut.take(CH_MID)
    return at


def places():
    cut, at = Cut(), Place()
    at.conv_in = cut.take(27, CH_BASE)
    at.bias_in = cut.take(CH_BASE)
    at.conv_down = cut.take(9 * CH_BASE, CH_MID)
    at.bias_down = cut.take(CH_MID)
    at.time_one = cut.take(CH_BASE, EMB_DIM)
    at.time_bias_one = cut.take(EMB_DIM)
    at.time_two = cut.take(EMB_DIM, EMB_DIM)
    at.time_bias_two = cut.take(EMB_DIM)
    at.class_table = cut.take(CLASSES, EMB_DIM)
    at.first = block_place(cut)
    at.second = block_place(cut)
    at.attn_gains = cut.take(2, CH_MID)
    at.attn_qkv = cut.take(CH_MID, 3 * CH_MID)
    at.attn_out = cut.take(CH_MID, CH_MID)
    at.attn_bias = cut.take(CH_MID)
    at.final_gains = cut.take(2, CH_MID)
    at.conv_out = cut.take(9 * CH_MID, 3)
    at.bias_out = cut.take(3)
    return at


AT = places()
TAIL = AT.conv_out
SHARDS, PLANE = 32, 8
SHARD = 2264
ROOM = 2272
ALL_LINES = SHARDS * SHARD
PLANES = [p * PLANE * SHARD for p in range(SHARDS // PLANE)]
BASE_ONE = AT.second.gains // 16 * 16
BASE_TWO = AT.first.conv_two // 16 * 16
BASE_THREE = AT.first.gains // 16 * 16

V_DOWN, V_G1, V_B11, V_B12, V_AG, V_AB, V_FG, V_G2, V_B21, V_B22 = 0, 1, 5, 6, 7, 9, 10, 12, 16, 17
VEC_ROWS = 24


def group_table():
    at = np.arange(CH_MID) // (CH_MID // GROUPS)
    return (at[:, None] == at[None, :]).astype(np.float32)


TAPS = 16


def spread_tables():
    select = np.zeros((LINE, LINE), np.float32)
    gather = np.zeros((LINE, LINE), np.float32)
    tile = np.zeros((LINE, LINE), np.float32)
    for ky in range(3):
        for kx in range(3):
            for a in range(2):
                for b in range(2):
                    dy, dx = (a + ky - 1) // 2, (b + kx - 1) // 2
                    shift = (dy + 1) * 3 + dx + 1
                    for c in range(3):
                        out = (a * 2 + b) * 3 + c
                        select[c * TAPS + ky * 3 + kx, shift * 12 + out] = 1.0
                        gather[out::12, out][:9] = 1.0
                        tile[c, out] = 1.0
    return select, gather, tile


def patch_table():
    pick = np.zeros((4, LINE, 32), np.float32)
    for a in range(2):
        for b in range(2):
            for ky in range(3):
                for kx in range(3):
                    (dy, ya), (dx, xb) = divmod(a + ky - 1, 2), divmod(b + kx - 1, 2)
                    shift = (dy + 1) * 3 + dx + 1
                    for c in range(3):
                        k = (ky * 3 + kx) * 3 + c
                        pick[a * 2 + b, shift * 12 + (ya * 2 + xb) * 3 + c, k // 2 + 16 * (k % 2)] = 1.0
    return pick


def expand_table():
    return (np.arange(3 * CH_MID)[None, :] // 3 == np.arange(CH_MID)[:, None]).astype(np.float32)


def colour(c):
    lane = lax.broadcasted_iota(jnp.int32, (1, 3 * CH_MID), 1)
    return lax.rem(lane, 3) == c


def first_lanes():
    return lax.broadcasted_iota(jnp.int32, (1, LINE), 1) < LINE // 2


def split3(v):
    hi = v.astype(BF16)
    rest = v - hi.astype(F32)
    mid = rest.astype(BF16)
    low = (rest - mid.astype(F32)).astype(BF16)
    return hi, mid, low


def dot(a, b, dims=NN):
    return lax.dot_general(a, b, dims, preferred_element_type=F32)


def dot3(a, b, dims=NN):
    rows = a.shape[0]
    hi, mid, low = split3(a)
    if rows % 16:
        out = dot(jnp.concatenate([p.astype(F32) for p in (hi, mid, low)], 0).astype(BF16), b, dims)
    else:
        out = dot(jnp.concatenate([hi, mid, low], 0), b, dims)
    return out[:rows] + out[rows : 2 * rows] + out[2 * rows :]


def outer(a, b):
    pa, pb = split3(a), split3(b)
    pairs = [(0, 0), (0, 1), (1, 0), (1, 1), (0, 2), (2, 0)]
    left = jnp.concatenate([pa[i].astype(F32) for i, _ in pairs], 0).astype(BF16)
    right = jnp.concatenate([pb[j].astype(F32) for _, j in pairs], 0).astype(BF16)
    return dot(left, right, TN)


def sigmoid(z):
    return 1.0 / (1.0 + jnp.exp(-z))


def silu(z):
    return z * sigmoid(z)


def silu_slope(z):
    s = sigmoid(z)
    return s * (1.0 + z * (1.0 - s))


def colsum(ref, base, count=PIX):
    def body(c, acc):
        return acc + jnp.sum(ref[pl.ds(pl.multiple_of(base + c * CHUNK, 8), CHUNK), :], 0, keepdims=True)

    return lax.fori_loop(0, count // CHUNK, body, jnp.zeros((1, ref.shape[1]), F32))


def eight(v):
    return jnp.broadcast_to(v, (8, v.shape[1]))


def group_means(rows, gm_ref):
    rows = rows + [jnp.zeros((8 - len(rows), CH_MID), F32)]
    means = dot3(jnp.concatenate(rows, 0), gm_ref[...]) * (1.0 / GROUP_SIZE)
    return [means[n : n + 1] for n in range(len(rows) - 1)]


def all_stats(x_ref, gm_ref):
    def total(c, acc):
        at = lambda img: pl.ds(pl.multiple_of(img * PIX + c * CHUNK, 8), CHUNK)
        return tuple(acc[img] + jnp.sum(x_ref[at(img), :], 0, keepdims=True) for img in range(MB_DEV))

    zero = (jnp.zeros((1, CH_MID), F32),) * MB_DEV
    means = group_means(list(lax.fori_loop(0, PIX // CHUNK, total, zero, unroll=2)), gm_ref)

    def square(c, acc):
        out = []
        for img in range(MB_DEV):
            gap = x_ref[pl.ds(pl.multiple_of(img * PIX + c * CHUNK, 8), CHUNK), :] - means[img]
            out.append(acc[img] + jnp.sum(gap * gap, 0, keepdims=True))
        return tuple(out)

    spreads = group_means(list(lax.fori_loop(0, PIX // CHUNK, square, zero, unroll=2)), gm_ref)
    return [(mean, lax.rsqrt(spread + EPSILON)) for mean, spread in zip(means, spreads)]


def norm_to(pbuf, x_ref, stats, scales, act):
    for img in range(MB_DEV):
        (mean, rstd), (k, o) = stats[img], scales[img]

        def body(c, carry):
            r = pl.multiple_of(img * PIX + c * CHUNK, 8)
            z = (x_ref[pl.ds(r, CHUNK), :] - mean) * rstd * k + o
            pbuf[pl.ds(r + 8, CHUNK), :] = silu(z) if act else z
            return carry

        lax.fori_loop(0, PIX // CHUNK, body, 0, unroll=2)


def norm_back(x_ref, d_ref, stats, scales, act, gm_ref, emit):
    def one(c, carry):
        out = []
        for img in range(MB_DEV):
            (mean, rstd), (k, o) = stats[img], scales[img]
            r = pl.multiple_of(img * PIX + c * CHUNK, 8)
            xhat = (x_ref[pl.ds(r, CHUNK), :] - mean) * rstd
            dz = d_ref[pl.ds(r, CHUNK), :]
            if act:
                dz = dz * silu_slope(xhat * k + o)
                d_ref[pl.ds(r, CHUNK), :] = dz
            out.append(carry[2 * img] + jnp.sum(dz, 0, keepdims=True))
            out.append(carry[2 * img + 1] + jnp.sum(dz * xhat, 0, keepdims=True))
        return tuple(out)

    sums = lax.fori_loop(0, PIX // CHUNK, one, (jnp.zeros((1, CH_MID), F32),) * (2 * MB_DEV), unroll=2)
    means = group_means([v * scales[n // 2][0] for n, v in enumerate(sums)], gm_ref)
    for img in range(MB_DEV):
        (mean, rstd), (k, o) = stats[img], scales[img]
        m1, m2 = means[2 * img], means[2 * img + 1]

        def two(c, carry):
            r = pl.multiple_of(img * PIX + c * CHUNK, 8)
            xhat = (x_ref[pl.ds(r, CHUNK), :] - mean) * rstd
            emit(r, rstd * (d_ref[pl.ds(r, CHUNK), :] * k - m1 - xhat * m2))
            return carry

        lax.fori_loop(0, PIX // CHUNK, two, 0, unroll=2)
    return [(sums[2 * img], sums[2 * img + 1]) for img in range(MB_DEV)]


def clear_pads(sbuf):
    for r in range(0, PADDED, PIX + 16):
        sbuf[r : r + 16, :] = jnp.zeros((16, sbuf.shape[1]), BF16)


def shift_to(sbuf, pbuf):
    column = lax.rem(lax.broadcasted_iota(jnp.int32, (CHUNK, CH_MID), 0), HALF)
    for r in range(0, ROWS, CHUNK):
        for k in range(3):
            v = pbuf[r + 7 + k : r + 7 + k + CHUNK, :]
            if k == 0:
                v = jnp.where(column == 0, 0.0, v)
            if k == 2:
                v = jnp.where(column == HALF - 1, 0.0, v)
            start = r + 16 * (r // PIX + 1)
            sbuf[start : start + CHUNK, k * CH_MID : (k + 1) * CH_MID] = v.astype(BF16)


def shifted(sbuf, row, cols=slice(None)):
    first = sbuf[pl.ds(pl.multiple_of(row, 16), PIX), cols]
    second = sbuf[pl.ds(pl.multiple_of(row + PIX + 16, 16), PIX), cols]
    return jnp.concatenate([first, second], 0)


def conv_forward(sbuf, w_ref, out_ref):
    depth = 3 * CH_MID

    def body(ky, carry):
        w = w_ref[pl.ds(pl.multiple_of(ky * depth, depth), depth), :]
        out_ref[...] += dot(shifted(sbuf, ky * 16), w)
        return carry

    lax.fori_loop(0, 3, body, 0, unroll=3)


def put_lines(g_ref, at, value, step, more=None):
    n = value.shape[0]
    low = at // 8 * 8
    start = low if more is None else pl.multiple_of(low + more, 8)
    view = g_ref.at[pl.ds(start, min(n * step + 8, g_ref.shape[0] - low)), :] if more is None else g_ref.at[pl.ds(start, n * step + 8), :]
    for j in range(step):
        view[pl.ds(at - low + j, n, stride=step), :] = value[:, j * LINE : (j + 1) * LINE]


def put_row(g_ref, at, row):
    for j in range(row.shape[1] // LINE):
        g_ref[pl.ds(at + j, 1), :] = row[:, j * LINE : (j + 1) * LINE]


def conv_back(sbuf, at_ref, w_ref, dx_ref, g_ref, at):
    dx_ref[...] = jnp.zeros_like(dx_ref)
    depth = 3 * CH_MID

    def body(s, carry):
        d = shifted(sbuf, s * 16)
        dw = dot(at_ref[...], d)
        dx = dx_ref[...]
        for k in range(3):
            part = slice(k * CH_MID, (k + 1) * CH_MID)
            tap = (2 - s) * depth + (2 - k) * CH_MID
            dx = dx + dot(d[:, part], w_ref[pl.ds(pl.multiple_of(tap, CH_MID), CH_MID), :], NT)
            put_lines(g_ref, at, dw[:, part], 3, 3 * tap)
        dx_ref[...] = dx
        return carry

    lax.fori_loop(0, 3, body, 0, unroll=3)


def transpose_to(at_ref, pbuf):
    for c in range(ROWS // LINE):
        at_ref[:, c * LINE : (c + 1) * LINE] = pbuf[8 + c * LINE : 8 + (c + 1) * LINE, :].T.astype(BF16)


class Lines:
    def __init__(self, held, wide):
        self.held, self.wide = held, wide

    def take(self, span):
        l0, l1 = span
        first = l0 // SHARD
        self.low = first * SHARD + (l0 - first * SHARD) // 16 * 16
        for s in range(first, (l1 - 1) // SHARD + 1):
            start = max(l0 - s * SHARD, 0) // 16 * 16
            count = -(-min(l1 - s * SHARD, SHARD) // 16) * 16 - start
            to = s * SHARD + start - self.low
            block = self.held.at[s // PLANE, s % PLANE]
            whole, rest = divmod(count, 256)

            def body(c, carry):
                self.wide[pl.ds(pl.multiple_of(to + c * 256, 8), 256), :] = block[
                    pl.ds(pl.multiple_of(start + c * 256, 16), 256), :
                ].astype(F32)
                return carry

            lax.fori_loop(0, whole, body, 0, unroll=2)
            if rest:
                done = whole * 256
                self.wide[to + done : to + count, :] = block[start + done : start + count, :].astype(F32)

    def line(self, at, scratch):
        shard = lax.div(at, SHARD)
        row = at - shard * SHARD
        low = pl.multiple_of(lax.div(row, 16) * 16, 16)
        scratch[...] = self.held[lax.div(shard, PLANE), lax.rem(shard, PLANE), pl.ds(low, 16), :].astype(F32)
        return scratch[pl.ds(row - low, 1), :]

    def matrix(self, w_ref, at, rows, step):
        block = 128 if rows % 192 else 192
        base = at - self.low
        low = base // 8 * 8

        def body(c, carry):
            r = pl.multiple_of(c * block, block)
            view = self.wide.at[pl.ds(pl.multiple_of(low + r * step, 8), block * step + 8), :]
            for j in range(step):
                v = view[pl.ds(base - low + j, block, stride=step), :]
                w_ref[pl.ds(r, block), j * LINE : (j + 1) * LINE] = v.astype(BF16)
            return carry

        lax.fori_loop(0, rows // block, body, 0, unroll=3 if (rows // block) % 3 == 0 else 2)

    def row(self, at, step):
        base = at - self.low
        return jnp.concatenate([self.wide[pl.ds(base + j, 1), :] for j in range(step)], 1)


def attention_pair(qkv_ref, img, pair):
    rows = pl.ds(pl.multiple_of(img * PIX, PIX), PIX)
    return [qkv_ref[rows, part * CH_MID + pair * LINE : part * CH_MID + (pair + 1) * LINE] for part in range(3)]


def lane_half():
    return lax.broadcasted_iota(jnp.int32, (1, LINE), 1) < HEAD_DIM


def keep_half(v, half, side):
    mine = half if side == 0 else jnp.logical_not(half)
    return jnp.where(mine, v.astype(F32), 0.0).astype(BF16)


SPAN_TIME = (AT.time_one, AT.class_table)
SPAN_EMB1 = (AT.first.embed, AT.first.conv_two)
SPAN_EMB2 = (AT.second.embed, AT.second.conv_two)
SPAN_DOWN = (AT.conv_in, AT.time_one)
SPAN_ONE1 = (AT.first.gains, AT.first.embed)
SPAN_TWO1 = (AT.first.conv_two, AT.second.gains)
SPAN_ATTN = (AT.attn_gains, ALL_LINES)
SPAN_ONE2 = (AT.second.gains, AT.second.embed)
SPAN_TWO2 = (AT.second.conv_two, AT.attn_gains)


def block_scales(vec, row, mod_ref=None, mod_row=0):
    gain, shift = vec[row : row + 1, :], vec[row + 1 : row + 2, :]
    if mod_ref is None:
        return [(gain, shift)] * MB_DEV
    out = []
    for img in range(MB_DEV):
        scale = 1.0 + mod_ref[mod_row + img : mod_row + img + 1, :CH_MID]
        out.append((gain * scale, shift * scale + mod_ref[mod_row + img : mod_row + img + 1, CH_MID:]))
    return out


def upsample_masks(shift):
    dy, dx = shift // 3 - 1, shift % 3 - 1
    p = lax.broadcasted_iota(jnp.int32, (ROWS, 1), 0)
    i, j = lax.rem(lax.div(p, HALF), HALF), lax.rem(p, HALF)
    inside = (i + dy >= 0) & (i + dy < HALF) & (j + dx >= 0) & (j + dx < HALF)
    lane = lax.broadcasted_iota(jnp.int32, (1, LINE), 1)
    return inside & (lane >= shift * 12) & (lane < shift * 12 + 12), dy * HALF + dx


def forward_kernel(save, moves, flip, *refs):
    me, labels, x_in, phi, gm, sel, gat, tile, expand, pick = refs[:10]
    sources = max(move[0] for move in moves) + 1
    pieces, refs = refs[10 : 10 + sources], refs[10 + sources :]
    f_out = refs[0]
    (h0s, h1, u1, h2, qkv, mixed, h3, u2, h4, vec, mod, emb, pre, wz, xp) = refs[1:16]
    if save:
        sw_time, sw_emb1, sw_emb2, sw_down, sw_11, sw_12, sw_attn, sw_21, sw_22 = refs[16:25]
    held, wide, w_ref, w_sq, sbuf, pbuf, h0p, table, w_in, b_out, sems, save_sem = refs[25 if save else 16 :]
    src = Lines(held, wide)
    arriving = []
    for plane in range(SHARDS // PLANE):
        copies = []
        for n, lead, r, row, rows in moves:
            target = held.at[plane, r ^ me[0], pl.ds(row, rows), :]
            source = pieces[n].at[plane, lead] if flip[n] else pieces[n].at[lead, plane]
            copies.append(pltpu.make_async_copy(source, target, sems.at[plane]))
        for copy in copies:
            copy.start()
        arriving.append(copies)

    def arrive(plane):
        for copy in arriving[plane]:
            copy.wait()

    pending = []

    def keep(source, target):
        if save:
            cp = pltpu.make_async_copy(source, target, save_sem)
            cp.start()
            pending.append(cp)

    def free():
        while pending:
            pending.pop().wait()

    clear_pads(sbuf)
    pbuf[0:8, :] = jnp.zeros((8, CH_MID), F32)
    pbuf[ROWS + 8 : ROWS + 16, :] = jnp.zeros((8, CH_MID), F32)
    arrive(0)
    src.take(SPAN_TIME)
    src.matrix(w_sq.at[0], AT.time_one, CH_BASE, 6)
    src.matrix(w_sq.at[1], AT.time_two, EMB_DIM, 6)
    pre[...] = dot3(phi[...], w_sq[0, :CH_BASE, :]) + src.row(AT.time_bias_one, 6)
    emb[...] = dot3(silu(pre[...]), w_sq[1]) + src.row(AT.time_bias_two, 6)
    for n in range(MB_DEV):
        for j in range(6):
            cols = slice(j * LINE, (j + 1) * LINE)
            emb[n : n + 1, cols] += src.line(AT.class_table + labels[n] * 6 + j, table)
    keep(w_sq.at[1], sw_time if save else None)
    se = silu(emb[...])
    arrive(1)
    src.take(SPAN_EMB1)
    src.matrix(w_sq.at[0], AT.first.embed, EMB_DIM, 6)
    m1 = dot3(se, w_sq[0]) + src.row(AT.first.embed_bias, 6)
    free()
    keep(w_sq.at[0], sw_emb1 if save else None)
    mod[0:2, :] = m1[0:2]
    mod[4:8, :] = jnp.zeros((4, EMB_DIM), F32)

    src.take(SPAN_DOWN)
    trio = [wide[pl.ds(j, 16, stride=3), :] for j in range(3)]
    turned = [pltpu.roll(v, LINE // 2, 1) for v in trio[1:]]
    w_in[0:16, 0:LINE] = trio[0]
    w_in[0:16, LINE : 2 * LINE] = trio[1]
    w_in[16:32, 0:LINE] = jnp.where(first_lanes(), turned[0], turned[1])
    w_in[16:32, LINE : 2 * LINE] = turned[1]
    w_low = w_in[...].astype(BF16)
    spread = dot(x_in[...], gat[...], NT)
    around = jnp.zeros((ROWS, LINE), F32)
    for shift in range(9):
        inside, by = upsample_masks(shift)
        around = around + jnp.where(inside, spread if by == 0 else pltpu.roll(spread, (-by) % ROWS, 0), 0.0)
    around = around.astype(BF16)
    one = (lax.broadcasted_iota(jnp.int32, (1, 32), 1) == 29).astype(F32)
    for ph in range(4):
        patch = (dot(around, pick[ph]) + one).astype(BF16)
        xp[ph * ROWS : (ph + 1) * ROWS, :] = patch
        h0s[ph * ROWS : (ph + 1) * ROWS, :] = dot(patch, w_low).astype(BF16)
    for j in range(3):
        vec[V_DOWN : V_DOWN + 1, j * LINE : (j + 1) * LINE] = src.row(AT.bias_down + j, 1)
    src.matrix(w_ref, AT.conv_down, 9 * CH_BASE, 3)
    free()
    keep(w_ref.at[pl.ds(0, 9 * CH_BASE), :], sw_down if save else None)
    h1[...] = jnp.broadcast_to(vec[V_DOWN : V_DOWN + 1, :], (ROWS, CH_MID))
    p = lax.broadcasted_iota(jnp.int32, (ROWS, 1), 0)
    has_left, has_up = lax.rem(p, HALF) > 0, lax.rem(lax.div(p, HALF), HALF) > 0
    for ph in range(4):
        h0p[0:32, :] = jnp.zeros((32, h0p.shape[1]), F32)
        h0p[32 : 32 + ROWS, :] = h0s[ph * ROWS : (ph + 1) * ROWS, :].astype(F32)
        for ky in ((0, 2) if ph // 2 else (1,)):
            for kx in ((0, 2) if ph % 2 else (1,)):
                back = (16 if ky == 0 else 0) + (1 if kx == 0 else 0)
                v = h0p[32 - back : 32 - back + ROWS, :]
                if ky == 0:
                    v = jnp.where(has_up, v, 0.0)
                if kx == 0:
                    v = jnp.where(has_left, v, 0.0)
                t = 3 * ky + kx
                h1[...] += dot(v[:, :CH_BASE].astype(BF16), w_ref[t * CH_BASE : (t + 1) * CH_BASE, :])

    def vectors(row, at, count):
        for n in range(count):
            for j in range(3):
                vec[row + n : row + n + 1, j * LINE : (j + 1) * LINE] = src.row(at + 3 * n + j, 1)

    def half_block(x_ref, scales, bias_row, add_ref, out_ref, at, target):
        src.matrix(w_ref, at, 9 * CH_MID, 3)
        keep(w_ref, target)
        stats = all_stats(x_ref, gm)
        norm_to(pbuf, x_ref, stats, scales, True)
        shift_to(sbuf, pbuf)
        bias = jnp.broadcast_to(vec[bias_row : bias_row + 1, :], (ROWS, CH_MID))
        out_ref[...] = bias if add_ref is None else add_ref[...] + bias
        conv_forward(sbuf, w_ref, out_ref)

    def block(h_in, u, h_out, prefix, g_row, b1_row, b2_row, mod_row, spans, targets):
        src.take(spans[0])
        free()
        vectors(g_row, prefix.gains, 4)
        vectors(b1_row, prefix.bias_one, 1)
        half_block(h_in, block_scales(vec, g_row), b1_row, None, u, prefix.conv_one, targets[0])
        src.take(spans[1])
        free()
        vectors(b2_row, prefix.bias_two, 1)
        half_block(u, block_scales(vec, g_row + 2, mod, mod_row), b2_row, h_in, h_out, prefix.conv_two, targets[1])

    saved = (sw_11, sw_12, sw_21, sw_22) if save else (None,) * 4
    arrive(2)
    block(h1, u1, h2, AT.first, V_G1, V_B11, V_B12, 0, (SPAN_ONE1, SPAN_TWO1), saved[:2])

    arrive(3)
    src.take(SPAN_ATTN)
    free()
    vectors(V_AG, AT.attn_gains, 2)
    vectors(V_AB, AT.attn_bias, 1)
    vectors(V_FG, AT.final_gains, 2)
    base = AT.conv_out - src.low
    tap_row = lax.broadcasted_iota(jnp.int32, (TAPS, 1), 0) < 9
    taps = [jnp.where(tap_row, wide[pl.ds(base + j, TAPS, stride=9), :], 0.0) for j in range(9)]
    taps = jnp.concatenate(taps, 1)
    rows_out = jnp.concatenate([jnp.where(colour(c), taps, 0.0) for c in range(3)], 0).astype(BF16)
    wz[...] = jnp.zeros_like(wz)
    wz[0 : 3 * TAPS, :] = dot(rows_out, expand[...], NT).astype(BF16)
    last = AT.bias_out - src.low
    b_out[...] = dot(eight(wide[last : last + 1, :]).astype(BF16), tile[...])
    for part in range(3):
        base = AT.attn_qkv - src.low
        for j in range(3):
            v = wide[pl.ds(base + part * 3 + j, CH_MID, stride=9), :]
            w_ref[part * CH_MID : (part + 1) * CH_MID, j * LINE : (j + 1) * LINE] = v.astype(BF16)
    src.matrix(w_ref.at[pl.ds(3 * CH_MID, CH_MID), :], AT.attn_out, CH_MID, 3)
    keep(w_ref.at[pl.ds(0, 4 * CH_MID), :], sw_attn if save else None)
    stats = all_stats(h2, gm)
    norm_to(pbuf, h2, stats, block_scales(vec, V_AG), False)
    n_low = pbuf[8 : 8 + ROWS, :].astype(BF16)
    for part in range(3):
        v = dot(n_low, w_ref[part * CH_MID : (part + 1) * CH_MID, :])
        qkv[:, part * CH_MID : (part + 1) * CH_MID] = v.astype(BF16)
    half = lane_half()

    def heads(img, carry):
        for pair in range(HEADS // 2):
            q, k, v = attention_pair(qkv, img, pair)
            outs = []
            for side in range(2):
                s = dot(keep_half(q, half, side), k, NT) * HEAD_DIM ** (-0.5)
                e = jnp.exp(s - jnp.max(s, 1, keepdims=True))
                prob = (e / jnp.sum(e, 1, keepdims=True)).astype(BF16)
                outs.append(dot(prob, v))
            mixed[pl.ds(pl.multiple_of(img * PIX, PIX), PIX), pair * LINE : (pair + 1) * LINE] = jnp.where(
                half, outs[0], outs[1]
            ).astype(BF16)
        return carry

    lax.fori_loop(0, MB_DEV, heads, 0, unroll=2)
    h3[...] = h2[...] + dot(mixed[...], w_ref[3 * CH_MID : 4 * CH_MID, :]) + vec[V_AB : V_AB + 1, :]

    src.take(SPAN_EMB2)
    src.matrix(w_sq.at[1], AT.second.embed, EMB_DIM, 6)
    m2 = dot3(silu(emb[...]), w_sq[1]) + src.row(AT.second.embed_bias, 6)
    mod[2:4, :] = m2[0:2]
    free()
    keep(w_sq.at[1], sw_emb2 if save else None)
    block(h3, u2, h4, AT.second, V_G2, V_B21, V_B22, 2, (SPAN_ONE2, SPAN_TWO2), saved[2:])

    stats = all_stats(h4, gm)
    norm_to(pbuf, h4, stats, block_scales(vec, V_FG), True)
    z = dot(pbuf[8 : 8 + ROWS, :].astype(BF16), wz[...], NT)
    t_all = dot3(z, sel[...])
    u_all = jnp.zeros((ROWS, LINE), F32)
    for shift in range(9):
        inside, by = upsample_masks(shift)
        moved = t_all if by == 0 else pltpu.roll(t_all, (-by) % ROWS, 0)
        u_all = u_all + jnp.where(inside, moved, 0.0)
    f_out[...] = dot3(u_all, gat[...]) + b_out[0:1, :]
    free()


def vmem(*shape_dtype):
    return pltpu.VMEM(*shape_dtype)


VM = pl.BlockSpec(memory_space=pltpu.VMEM)
HB = pl.BlockSpec(memory_space=pl.ANY)
SM = pl.BlockSpec(memory_space=pltpu.SMEM)


def state_shapes():
    act = ((ROWS, CH_MID), F32)
    return [
        ((4 * ROWS, 256), BF16),
        act, act, act,
        ((ROWS, 3 * CH_MID), BF16),
        ((ROWS, CH_MID), BF16),
        act, act, act,
        ((VEC_ROWS, CH_MID), F32),
        ((8, EMB_DIM), F32),
        ((8, EMB_DIM), F32),
        ((8, EMB_DIM), F32),
        ((LINE, CH_MID), BF16),
        ((4 * ROWS, 32), BF16),
    ]


def weight_shapes():
    sq = ((EMB_DIM, EMB_DIM), BF16)
    conv = ((9 * CH_MID, CH_MID), BF16)
    return [sq, sq, sq, ((9 * CH_BASE, CH_MID), BF16), conv, conv, ((4 * CH_MID, CH_MID), BF16), conv, conv]


def forward_call(save, me, labels, lines, x_in, phi, tables):
    pieces, moves, flip = lines
    sds = lambda s: jax.ShapeDtypeStruct(*s)
    outs = [sds(((ROWS, LINE), F32))]
    out_specs = [VM]
    state = state_shapes()
    scratch = []
    if save:
        outs += [sds(s) for s in state] + [sds(s) for s in weight_shapes()]
        out_specs += [VM] * len(state) + [HB] * len(weight_shapes())
    else:
        scratch += [vmem(*s) for s in state]
    scratch += [
        vmem((SHARDS // PLANE, PLANE, ROOM, LINE), BF16),
        vmem((10432, LINE), F32),
        vmem((9 * CH_MID, CH_MID), BF16),
        vmem((2, EMB_DIM, EMB_DIM), BF16),
        vmem((PADDED, 3 * CH_MID), BF16),
        vmem((ROWS + 16, CH_MID), F32),
        vmem((ROWS + 48, 256), F32),
        vmem((16, LINE), F32),
        vmem((32, 2 * LINE), F32),
        vmem((8, LINE), F32),
        pltpu.SemaphoreType.DMA((SHARDS // PLANE,)),
        pltpu.SemaphoreType.DMA,
    ]

    def body(*refs):
        forward_kernel(save, moves, flip, *refs)

    return pl.pallas_call(
        body,
        out_shape=outs,
        in_specs=[SM] * 2 + [VM] * 8 + [HB] * len(pieces),
        out_specs=out_specs,
        scratch_shapes=scratch,
        name="forward_save" if save else "forward_plain",
        **kernel_params(),
    )(me, labels, x_in, phi, *tables, *pieces)


def column_sum(pbuf):
    def body(c, acc):
        return acc + jnp.sum(pbuf[pl.ds(pl.multiple_of(c * CHUNK + 8, 8), CHUNK), :], 0, keepdims=True)

    return lax.fori_loop(0, ROWS // CHUNK, body, jnp.zeros((1, CH_MID), F32))


def refill(pbuf, source):
    for c in range(0, ROWS, CHUNK):
        pbuf[8 + c : 8 + c + CHUNK, :] = source[c : c + CHUNK, :]


def block_back_two(dh, u_ref, at, base, rows, vec, mod, mod_row, weights, tools, g, dm):
    g_row, b1_row, b2_row = rows
    sbuf, pbuf, dx, at_ref, gm = tools
    put_row(g, at.bias_two - base, colsum(dh, 0, ROWS))
    u_stats = all_stats(u_ref, gm)
    scales = block_scales(vec, g_row + 2, mod, mod_row)
    norm_to(pbuf, u_ref, u_stats, scales, True)
    transpose_to(at_ref, pbuf)
    refill(pbuf, dh)
    shift_to(sbuf, pbuf)
    conv_back(sbuf, at_ref, weights.take(), dx, g, at.conv_two - base)
    weights.begin()

    def emit_inner(r, v):
        pbuf[pl.ds(r + 8, CHUNK), :] = v

    sums = norm_back(u_ref, dx, u_stats, scales, True, gm, emit_inner)
    gain, shift = vec[g_row + 2 : g_row + 3, :], vec[g_row + 3 : g_row + 4, :]
    d_gain = d_shift = 0.0
    dm[...] = jnp.zeros_like(dm)
    for img, (a, b) in enumerate(sums):
        scale = 1.0 + mod[mod_row + img : mod_row + img + 1, :CH_MID]
        d_gain, d_shift = d_gain + scale * b, d_shift + scale * a
        dm[img : img + 1, :CH_MID] = gain * b + shift * a
        dm[img : img + 1, CH_MID:] = a
    return d_gain, d_shift


def block_back_one(dh, x_ref, at, base, rows, vec, weights, tools, g):
    g_row, b1_row, b2_row = rows
    sbuf, pbuf, dx, at_ref, gm = tools
    put_row(g, at.bias_one - base, column_sum(pbuf))
    shift_to(sbuf, pbuf)
    stats = all_stats(x_ref, gm)
    scales = block_scales(vec, g_row)
    norm_to(pbuf, x_ref, stats, scales, True)
    transpose_to(at_ref, pbuf)
    conv_back(sbuf, at_ref, weights.take(), dx, g, at.conv_one - base)
    weights.begin()

    def emit_outer(r, v):
        dh[pl.ds(r, CHUNK), :] += v

    sums = norm_back(x_ref, dx, stats, scales, True, gm, emit_outer)
    put_row(g, at.gains - base, sums[0][1] + sums[1][1])
    put_row(g, at.gains + 3 - base, sums[0][0] + sums[1][0])


def rowsum(v):
    return jnp.sum(v, 0, keepdims=True)


def put_outer(g, at, left, right):
    for c in range(-(-left.shape[1] // LINE)):
        piece = outer(left[:, c * LINE : (c + 1) * LINE], right)
        put_lines(g, at + c * LINE * (EMB_DIM // LINE), piece, EMB_DIM // LINE)


class Weights:
    def __init__(self, sources, slots, sems):
        self.copies = []
        for n, source in enumerate(sources):
            target = slots.at[n % 2, pl.ds(0, source.shape[0]), :]
            self.copies.append((pltpu.make_async_copy(source, target, sems.at[n % 2]), target))
        self.begun = self.done = 0

    def begin(self):
        if self.begun < len(self.copies):
            self.copies[self.begun][0].start()
            self.begun += 1

    def take(self):
        copy, target = self.copies[self.done]
        copy.wait()
        self.done += 1
        return target


class Leave:
    def __init__(self, me, g, base, keep, send, stage, sems, pad):
        self.pad = pad
        self.core, self.place = lax.rem(me[0], 2), lax.div(me[0], 2)
        self.g, self.base, self.outs, self.stage, self.sems = g, base, (keep, send), stage, sems
        self.copies = []

    def plane(self, plane):
        for q in range(PLANE // 2):
            at = q ^ self.place
            first = PLANES[plane] + 2 * q * SHARD - self.base
            for side in range(2):
                core = 1 - self.core if side else self.core
                start = first + core * SHARD
                stage = self.stage.at[2 * q + side]
                whole, rest = divmod(ROOM, 288)

                def body(c, carry):
                    lines = self.g[pl.ds(pl.multiple_of(start + c * 288, 8), 288), :]
                    stage[pl.ds(pl.multiple_of(c * 288, 16), 288), :] = lines.astype(BF16)
                    return carry

                lax.fori_loop(0, whole, body, 0)
                lines = self.g[pl.ds(pl.multiple_of(start + whole * 288, 8), rest - 8), :]
                stage[whole * 288 :, :] = jnp.concatenate([lines, self.pad[...]], 0).astype(BF16)
                copy = pltpu.make_async_copy(stage, self.outs[side].at[at], self.sems.at[side])
                copy.start()
                self.copies.append(copy)

    def below(self, count, rest):
        copy = pltpu.make_async_copy(self.g.at[pl.ds(0, count), :], rest, self.sems.at[2])
        copy.start()
        self.copies.append(copy)

    def wait(self):
        for copy in self.copies:
            copy.wait()


def clear_lines(g, first, count):
    if count:
        g[first : first + count, :] = jnp.zeros((count, LINE), F32)


def prepare(sbuf, pbuf):
    clear_pads(sbuf)
    pbuf[0:8, :] = jnp.zeros((8, CH_MID), F32)
    pbuf[ROWS + 8 : ROWS + 16, :] = jnp.zeros((8, CH_MID), F32)


def back_top_kernel(*refs):
    me, pad, df, wz, gm, sel, gat, tile, expand, vec, mod, emb, h4, u2, h3, qkv, mixed, h2, s22, s21, s_attn, s_emb = refs[:22]
    keep, send, rest, dh, dse = refs[22:27]
    g, slots, sbuf, pbuf, dx, at_ref, stage, sems, out_sems, w_sq, dqkv, dm, sq_sem = refs[27:]
    base = BASE_ONE
    weights = Weights([s22, s21, s_attn], slots, sems)
    weights.begin()
    weights.begin()
    sq_copy = pltpu.make_async_copy(s_emb, w_sq, sq_sem)
    sq_copy.start()
    prepare(sbuf, pbuf)
    clear_lines(g, TAIL - base, g.shape[0] - (TAIL - base))
    tools = (sbuf, pbuf, dx, at_ref, gm)

    stats = all_stats(h4, gm)
    scales = block_scales(vec, V_FG)
    norm_to(pbuf, h4, stats, scales, True)
    transpose_to(at_ref, pbuf)
    spread = dot(df[...].astype(BF16), gat[...], NT)
    dt = jnp.zeros((ROWS, LINE), F32)
    for shift in range(9):
        inside, by = upsample_masks(shift)
        part = jnp.where(inside, spread, 0.0)
        dt = dt + (part if by == 0 else pltpu.roll(part, by % ROWS, 0))
    dz = dot(dt.astype(BF16), sel[...], NT)
    parts = split3(dz)
    dwz = dot(at_ref[...], parts[0]) + dot(at_ref[...], parts[1]) + dot(at_ref[...], parts[2])
    dx[...] = dot(parts[0], wz[...]) + dot(parts[1], wz[...]) + dot(parts[2], wz[...])
    d_rows = dot3(dwz.T[0 : 3 * TAPS, :], expand[...])
    d_taps = jnp.zeros((TAPS, 3 * CH_MID), F32)
    for c in range(3):
        d_taps = d_taps + jnp.where(colour(c), d_rows[c * TAPS : (c + 1) * TAPS, :], 0.0)
    for j in range(9):
        g[pl.ds(TAIL - base + j, 9, stride=9), :] = d_taps[0:9, j * LINE : (j + 1) * LINE]
    b_row = AT.bias_out - base
    g[b_row : b_row + 1, :] = dot3(eight(colsum(df, 0, ROWS)), tile[...], NT)[0:1]

    def emit_first(r, v):
        dh[pl.ds(r, CHUNK), :] = v

    sums = norm_back(h4, dx, stats, scales, True, gm, emit_first)
    put_row(g, AT.final_gains - base, sums[0][1] + sums[1][1])
    put_row(g, AT.final_gains + 3 - base, sums[0][0] + sums[1][0])

    rows = (V_G2, V_B21, V_B22)
    d_gain, d_shift = block_back_two(dh, u2, AT.second, base, rows, vec, mod, 2, weights, tools, g, dm)
    put_row(g, AT.second.gains + 6 - base, d_gain)
    put_row(g, AT.second.gains + 9 - base, d_shift)
    block_back_one(dh, h3, AT.second, base, rows, vec, weights, tools, g)
    se = silu(emb[...])
    put_outer(g, AT.second.embed - base, se, dm[...])
    put_row(g, AT.second.embed_bias - base, rowsum(dm[...]))
    sq_copy.wait()
    dse[...] = dot3(dm[...], w_sq[...], NT)

    put_row(g, AT.attn_bias - base, colsum(dh, 0, ROWS))
    w = weights.take()
    d_low = dh[...].astype(BF16)
    for c in range(ROWS // LINE):
        at_ref[:, c * LINE : (c + 1) * LINE] = mixed[c * LINE : (c + 1) * LINE, :].astype(F32).T.astype(BF16)
    put_lines(g, AT.attn_out - base, dot(at_ref[...], d_low), 3)
    pbuf[8 : 8 + ROWS, :] = dot(d_low, w[3 * CH_MID : 4 * CH_MID, :], NT)
    half = lane_half()
    scale = HEAD_DIM ** (-0.5)

    def heads(img, carry):
        rows = pl.ds(pl.multiple_of(img * PIX, PIX), PIX)
        for pair in range(HEADS // 2):
            q, k, v = attention_pair(qkv, img, pair)
            cols = slice(pair * LINE, (pair + 1) * LINE)
            do = pbuf[pl.ds(pl.multiple_of(img * PIX + 8, 8), PIX), cols].astype(BF16)
            dqs, dks, dvs = [], [], []
            for side in range(2):
                s = dot(keep_half(k, half, side), q, NT) * scale
                e = jnp.exp(s - jnp.max(s, 0, keepdims=True))
                prob = e / jnp.sum(e, 0, keepdims=True)
                dvs.append(dot(prob.astype(BF16), do))
                dp = dot(keep_half(v, half, side), do, NT)
                ds = prob * (dp - jnp.sum(dp * prob, 0, keepdims=True))
                dks.append(dot(ds.astype(BF16), q))
                dqs.append(dot(ds.T.astype(BF16), k))
            for part, pieces in enumerate((dqs, dks, dvs)):
                value = jnp.where(half, pieces[0], pieces[1])
                if part < 2:
                    value = value * scale
                dqkv[rows, part * CH_MID + pair * LINE : part * CH_MID + (pair + 1) * LINE] = value.astype(BF16)
        return carry

    lax.fori_loop(0, MB_DEV, heads, 0, unroll=2)
    stats = all_stats(h2, gm)
    scales = block_scales(vec, V_AG)
    norm_to(pbuf, h2, stats, scales, False)
    transpose_to(at_ref, pbuf)
    dx[...] = jnp.zeros_like(dx)
    for part in range(3):
        d = dqkv[:, part * CH_MID : (part + 1) * CH_MID]
        dw = dot(at_ref[...], d)
        for j in range(3):
            g[pl.ds(AT.attn_qkv - base + part * 3 + j, CH_MID, stride=9), :] = dw[:, j * LINE : (j + 1) * LINE]
        dx[...] += dot(d, w[part * CH_MID : (part + 1) * CH_MID, :], NT)
    weights.begin()

    def emit(r, v):
        dh[pl.ds(r, CHUNK), :] += v

    sums = norm_back(h2, dx, stats, scales, False, gm, emit)
    put_row(g, AT.attn_gains - base, sums[0][1] + sums[1][1])
    put_row(g, AT.attn_gains + 3 - base, sums[0][0] + sums[1][0])

    leave = Leave(me, g, base, keep, send, stage, out_sems, pad)
    leave.plane(3)
    leave.below(PLANES[3] - base, rest)
    leave.wait()


def back_second_half_kernel(*refs):
    me, pad, dh, gm, vec, mod, u1, s12, rest_in = refs[:9]
    keep, send, rest, du, dm, extra = refs[9:15]
    g, slots, sbuf, pbuf, dx, at_ref, stage, sems, out_sems, in_sem = refs[15:]
    base = BASE_TWO
    weights = Weights([s12], slots, sems)
    weights.begin()
    above = pltpu.make_async_copy(rest_in, g.at[pl.ds(BASE_ONE - base, PLANES[3] - BASE_ONE), :], in_sem)
    above.start()
    prepare(sbuf, pbuf)
    clear_lines(g, PLANES[3] - base, g.shape[0] - (PLANES[3] - base))
    above.wait()
    rows = (V_G1, V_B11, V_B12)
    tools = (sbuf, pbuf, dx, at_ref, gm)
    d_gain, d_shift = block_back_two(dh, u1, AT.first, base, rows, vec, mod, 0, weights, tools, g, dm)
    extra[...] = jnp.zeros_like(extra)
    extra[0:1, :] = d_gain
    extra[1:2, :] = d_shift
    for c in range(0, ROWS, CHUNK):
        du[c : c + CHUNK, :] = pbuf[8 + c : 8 + c + CHUNK, :]
    leave = Leave(me, g, base, keep, send, stage, out_sems, pad)
    leave.plane(2)
    leave.below(PLANES[2] - base, rest)
    leave.wait()


def back_first_half_kernel(*refs):
    me, pad, dh_in, du, dm, extra, dse_in, gm, vec, emb, h1, s11, s_emb, rest_in = refs[:14]
    keep, send, rest, dh, dse = refs[14:19]
    g, slots, sbuf, pbuf, dx, at_ref, stage, sems, out_sems, w_sq, in_sem, sq_sem = refs[19:]
    base = BASE_THREE
    weights = Weights([s11], slots, sems)
    weights.begin()
    sq_copy = pltpu.make_async_copy(s_emb, w_sq, sq_sem)
    sq_copy.start()
    above = pltpu.make_async_copy(rest_in, g.at[pl.ds(BASE_TWO - base, PLANES[2] - BASE_TWO), :], in_sem)
    above.start()
    prepare(sbuf, pbuf)
    clear_lines(g, PLANES[2] - base, g.shape[0] - (PLANES[2] - base))
    refill(pbuf, du)
    for c in range(0, ROWS, CHUNK):
        dh[c : c + CHUNK, :] = dh_in[c : c + CHUNK, :]
    above.wait()
    tools = (sbuf, pbuf, dx, at_ref, gm)
    put_outer(g, AT.first.embed - base, silu(emb[...]), dm[...])
    put_row(g, AT.first.embed_bias - base, rowsum(dm[...]))
    block_back_one(dh, h1, AT.first, base, (V_G1, V_B11, V_B12), vec, weights, tools, g)
    put_row(g, AT.first.gains + 6 - base, extra[0:1, :])
    put_row(g, AT.first.gains + 9 - base, extra[1:2, :])
    leave = Leave(me, g, base, keep, send, stage, out_sems, pad)
    leave.plane(1)
    leave.below(PLANES[1] - base, rest)
    sq_copy.wait()
    dse[...] = dse_in[...] + dot3(dm[...], w_sq[...], NT)
    leave.wait()


def back_low_kernel(*refs):
    me, labels, pad, dh, dse, emb, pre, phi, h0s, xp, s_down, s_time, rest_in = refs[:13]
    keep, send = refs[13:15]
    g, slots, sbuf, pbuf, h0t, stage, sems, out_sems, w_sq, demb_ref, dwin, dbin, in_sem, sq_sem = refs[15:]
    weights = Weights([s_down], slots, sems)
    weights.begin()
    sq_copy = pltpu.make_async_copy(s_time, w_sq, sq_sem)
    sq_copy.start()
    above = pltpu.make_async_copy(rest_in, g.at[pl.ds(BASE_THREE, PLANES[1] - BASE_THREE), :], in_sem)
    above.start()
    prepare(sbuf, pbuf)
    clear_lines(g, PLANES[1], g.shape[0] - PLANES[1])
    above.wait()
    demb = dse[...] * silu_slope(emb[...])
    put_row(g, AT.time_bias_two, rowsum(demb))
    put_outer(g, AT.time_two, silu(pre[...]), demb)
    sq_copy.wait()
    dpre = dot3(demb, w_sq[...], NT) * silu_slope(pre[...])
    put_row(g, AT.time_bias_one, rowsum(dpre))
    put_outer(g, AT.time_one, phi[...], dpre)
    clear = 240
    first, lines = AT.class_table, CLASSES * (EMB_DIM // LINE)

    def wipe(c, carry):
        g[pl.ds(first + c * clear, clear), :] = jnp.zeros((clear, LINE), F32)
        return carry

    lax.fori_loop(0, lines // clear, wipe, 0)
    demb_ref[...] = demb
    for n in range(MB_DEV):
        for j in range(EMB_DIM // LINE):
            at = first + labels[n] * (EMB_DIM // LINE) + j
            g[pl.ds(at, 1), :] += demb_ref[n : n + 1, j * LINE : (j + 1) * LINE]

    put_row(g, AT.bias_down, colsum(dh, 0, ROWS))
    refill(pbuf, dh)
    shift_to(sbuf, pbuf)
    w = weights.take()
    dwin[...] = jnp.zeros_like(dwin)
    dbin[...] = jnp.zeros_like(dbin)
    for ph in range(4):
        for c in range(ROWS // LINE):
            rows = slice(ph * ROWS + c * LINE, ph * ROWS + (c + 1) * LINE)
            h0t[:, c * LINE : (c + 1) * LINE] = h0s[rows, :].astype(F32).T.astype(BF16)
        d0 = jnp.zeros((ROWS, CH_BASE), F32)
        for ky in ((0, 2) if ph // 2 else (1,)):
            for kx in ((0, 2) if ph % 2 else (1,)):
                side = 2 if kx == 0 else 1
                d = shifted(sbuf, 32 if ky == 0 else 16, slice(side * CH_MID, (side + 1) * CH_MID))
                t = 3 * ky + kx
                d0 = d0 + dot(d, w[t * CH_BASE : (t + 1) * CH_BASE, :], NT)
                put_lines(g, AT.conv_down + t * CH_BASE * 3, dot(h0t[0:CH_BASE, :], d), 3)
        dbin[0:1, :CH_BASE] += rowsum(d0)
        dwin[:, :CH_BASE] += dot(xp[ph * ROWS : (ph + 1) * ROWS, :], d0.astype(BF16), TN)
    dwin[29:30, :] = dbin[0:1, :]
    even, odd = dwin[0:16, :], dwin[16:32, :]
    turned = pltpu.roll(odd[:, :LINE], LINE // 2, 1), pltpu.roll(odd[:, LINE:], LINE // 2, 1)
    g[pl.ds(0, 14, stride=3), :] = even[0:14, :LINE]
    g[pl.ds(1, 14, stride=3), :] = jnp.where(first_lanes(), even[:, LINE:], turned[0])[0:14]
    g[pl.ds(2, 14, stride=3), :] = jnp.where(first_lanes(), turned[0], turned[1])[0:14]
    leave = Leave(me, g, 0, keep, send, stage, out_sems, pad)
    leave.plane(0)
    leave.wait()


def kernel_params():
    return dict(
        compiler_params=pltpu.CompilerParams(vmem_limit_bytes=60 * 1024 * 1024),
        cost_estimate=pl.CostEstimate(flops=8 * 10**9, bytes_accessed=4 * 10**7, transcendentals=10**6),
    )


def back_call(kernel, name, lines, slots, args, smem, hbm, rest, outs, scratch, norms=True):
    sds = lambda *s: jax.ShapeDtypeStruct(*s)
    plane = sds((PLANE // 2, ROOM, LINE), BF16)
    rest = [sds((rest, LINE), F32)] if rest else []
    common = [
        vmem((lines + 8, LINE), F32),
        vmem((slots, 9 * CH_MID, CH_MID), BF16),
        vmem((PADDED, 3 * CH_MID), BF16),
        vmem((ROWS + 16, CH_MID), F32),
    ]
    if norms:
        common += [vmem((ROWS, CH_MID), F32), vmem((CH_MID, ROWS), BF16)]
    else:
        common += [vmem((256, ROWS), BF16)]
    common += [
        vmem((PLANE, ROOM, LINE), BF16),
        pltpu.SemaphoreType.DMA((2,)),
        pltpu.SemaphoreType.DMA((3,)),
    ]
    return pl.pallas_call(
        kernel,
        out_shape=[plane, plane, *rest, *(sds(*o) for o in outs)],
        in_specs=[SM] * smem + [VM] * (len(args) - smem - hbm) + [HB] * hbm,
        out_specs=[HB] * (2 + len(rest)) + [VM] * len(outs),
        scratch_shapes=common + scratch,
        name=name,
        **kernel_params(),
    )(*args)


ACT = ((ROWS, CH_MID), F32)
WIDE_ROW = ((8, EMB_DIM), F32)
DMA = pltpu.SemaphoreType.DMA


def back_top(args):
    scratch = [vmem((EMB_DIM, EMB_DIM), BF16), vmem((ROWS, 3 * CH_MID), BF16), vmem(*WIDE_ROW), DMA]
    lines = ALL_LINES - BASE_ONE
    return back_call(
        back_top_kernel, "back_top", lines, 2, args, 1, 4, PLANES[3] - BASE_ONE, [ACT, WIDE_ROW], scratch
    )


def back_second_half(args):
    outs = [ACT, WIDE_ROW, ((8, CH_MID), F32)]
    lines = PLANES[3] - BASE_TWO
    return back_call(back_second_half_kernel, "back_b", lines, 1, args, 1, 2, PLANES[2] - BASE_TWO, outs, [DMA])


def back_first_half(args):
    scratch = [vmem((EMB_DIM, EMB_DIM), BF16), DMA, DMA]
    lines = PLANES[2] - BASE_THREE
    return back_call(
        back_first_half_kernel, "back_c", lines, 1, args, 1, 3, PLANES[1] - BASE_THREE, [ACT, WIDE_ROW], scratch
    )


def back_low(args):
    scratch = [
        vmem((EMB_DIM, EMB_DIM), BF16),
        vmem(*WIDE_ROW),
        vmem((32, 2 * LINE), F32),
        vmem((8, 2 * LINE), F32),
        DMA,
        DMA,
    ]
    return back_call(back_low_kernel, "back_low", PLANES[1], 1, args, 2, 3, 0, [], scratch, False)


def karras(index):
    ramp_frac = index.astype(F32) / (DISCRETE - 1)
    low_root = SIGMA_LOW ** (1.0 / RHO_POWER)
    high_root = SIGMA_HIGH ** (1.0 / RHO_POWER)
    return (low_root + ramp_frac * (high_root - low_root)) ** RHO_POWER


def preconditioning_factors(sigma):
    variance_sum = sigma * sigma + SIGMA_DATA**2
    skip = SIGMA_DATA**2 / ((sigma - SIGMA_LOW) ** 2 + SIGMA_DATA**2)
    out = (sigma - SIGMA_LOW) * SIGMA_DATA * lax.rsqrt(variance_sum)
    return (skip, out, lax.rsqrt(variance_sum))


def noise_features(sigma):
    half_width = CH_BASE // 2
    frequency = jnp.exp(-math.log(10000.0) * jnp.arange(half_width, dtype=F32) / half_width)
    phases = 250.0 * jnp.log(sigma)[:, None] * frequency
    return jnp.pad(jnp.concatenate([jnp.cos(phases), jnp.sin(phases)], 1), ((0, 8 - MB_DEV), (0, 0)))


def pixels(images):
    lead = images.shape[0]
    split = images.reshape(lead, MB_DEV, HALF, 2, HALF, 2, 3)
    return split.transpose(0, 1, 2, 4, 3, 5, 6).reshape(lead, ROWS, 12)


def pixel_live(counts, valid_rows):
    row = lax.broadcasted_iota(jnp.int32, (ROWS, 12), 0)
    lane = lax.broadcasted_iota(jnp.int32, (ROWS, 12), 1)
    slot = row // PIX
    line = 2 * ((row // HALF) % HALF) + lane // 6
    top = jnp.where(slot == 0, valid_rows[0], valid_rows[1])
    return ((slot < counts[0]) & (line < top)).astype(F32)


def per_part(me, labels, lines, inputs, save, tables):
    _, x_in, phi, _ = inputs
    results = forward_call(save, me, labels, lines, x_in, phi, tables)
    return results[0], results[1:]


AXIS = "fsdp"
CORE, EAST, SOUTH, UP = 1, 2, 4, 8
CUT_ROWS = ROOM // 2


def swap(values, hop):
    return lax.ppermute(values, AXIS, [(i, i ^ hop) for i in range(SHARDS)])


def total_of(values, n):
    hop = 1
    while hop < n:
        values = values + lax.ppermute(values, AXIS, [(i, i ^ hop) for i in range(n)])
        hop *= 2
    return values


CUTS = (0, 880, 1760, ROOM)
TALL = SHARDS // PLANE


def gate(values, after):
    count = len(values)

    def body(*refs):
        pass

    return pl.pallas_call(
        body,
        out_shape=[jax.ShapeDtypeStruct(v.shape, v.dtype) for v in values],
        in_specs=[HB] * (count + len(after)),
        out_specs=[HB] * count,
        input_output_aliases={i: i for i in range(count)},
        name="gate",
    )(*values, *after)


def climb(values, way, far, first=0):
    planes = range(first, TALL - far) if way == 1 else range(TALL - 1 - first, far - 1, -1)
    pairs = [(q * PLANE + i, (q + way * far) * PLANE + i) for q in planes for i in range(PLANE)]
    return lax.ppermute(values, AXIS, pairs)


def column_window(slots, z):
    rows = []
    for p in range(TALL):
        value = slots[TALL - 1 + p]
        for q in range(1, TALL):
            value = jnp.where(z == q, slots[TALL - 1 - q + p], value)
        rows.append(value)
    return jnp.stack(rows)


def column_gather(own, z):
    below, above = [climb(own, 1, 1)], [climb(own, -1, 1)]
    for step in range(1, TALL - 1):
        below.append(climb(below[-1], 1, 1, step))
        above.append(climb(above[-1], -1, 1, step))
    return column_window([*below[::-1], own, *above], z), [below[0], above[0]], [below[-1], above[-1]]


def gather_lines(shard, z, early):
    ab, c = shard[: CUTS[2]], shard[CUTS[2] :]
    c_two = jnp.stack([c, swap(c, SOUTH)])
    c_four = jnp.concatenate([c_two, swap(c_two, EAST)])
    column, step, last = column_gather(ab, z)
    za, zb = column[:, : CUTS[1]], column[:, CUTS[1] :]
    done, ready = early(step)
    a_two, b_two = jnp.stack([za, swap(za, EAST)]), jnp.stack([zb, swap(zb, SOUTH)])
    a_far, b_far = swap(a_two, SOUTH), swap(b_two, EAST)
    (c_four,) = gate([c_four], [*last, *ready])
    c_all, _, _ = column_gather(c_four, z)
    pieces = [a_two, a_far, b_two, b_far, c_all]
    return done, pieces + [swap(v, CORE) for v in pieces]


def gather_moves():
    places = [(0, 1), (2, 3), (0, 2), (1, 3), (0, 2, 1, 3)]
    part = (0, 0, 1, 1, 2)
    moves = []
    for core in range(2):
        for n in range(5):
            row, end = CUTS[part[n]], CUTS[part[n] + 1]
            for lead, place in enumerate(places[n]):
                moves.append((core * 5 + n, lead, 2 * place + core, row, end - row))
    return moves


def gather_plain(shard):
    rows = shard.shape[0]
    lines = lax.all_gather(shard, AXIS, axis=0, tiled=True)
    if rows != ROOM:
        lines = jnp.pad(lines.reshape(SHARDS, SHARD, LINE), ((0, 0), (0, ROOM - SHARD), (0, 0)))
    lines = lines.reshape(TALL, PLANE, ROOM, LINE)
    return [lines], [(0, r, r, 0, ROOM) for r in range(PLANE)], (True,)


def digit_weights():
    return np.array([8.0 ** (k - 40) if k < 82 else 0.0 for k in range(LINE)], np.float32)[None]


def to_digits(values):
    weights = digit_weights()
    inverse = np.where(weights > 0, 1.0 / np.where(weights > 0, weights, 1.0), 0.0).astype(np.float32)
    size = jnp.abs(values)[:, None] * inverse
    digit = jnp.floor(size) - 8.0 * jnp.floor(size * 0.125)
    digit = jnp.where(size < 2.0**27, digit, 0.0)
    return jnp.where(values[:, None] < 0, -digit, digit)


def from_digits(rows):
    return jnp.sum(rows * digit_weights(), 1)


def low(v):
    return v.astype(BF16)


def wide(v):
    return v.astype(F32)


class PlaneSum:
    def __init__(self, keep, send):
        self.keep, self.got = keep, swap(send, CORE)
        self.a, self.b = slice(0, CUT_ROWS), slice(CUT_ROWS, ROOM)

    def quarter(self, i, rows):
        return wide(self.keep[i, rows]) + wide(self.got[i, rows])

    def first(self):
        a = low(jnp.stack([self.quarter(1, self.a), self.quarter(3, self.a)]))
        b = low(jnp.stack([self.quarter(2, self.b), self.quarter(3, self.b)]))
        return a, b

    def send_first(self, a, b):
        self.got_a, self.got_b = swap(a, EAST), swap(b, SOUTH)

    def last(self):
        return low(self.quarter(2, self.a) + wide(self.got_a[1])), low(self.quarter(1, self.b) + wide(self.got_b[1]))

    def send_last(self, a, b):
        self.end_a, self.end_b = swap(a, SOUTH), swap(b, EAST)

    def total(self):
        a = self.quarter(0, self.a) + wide(self.got_a[0]) + wide(self.end_a)
        b = self.quarter(0, self.b) + wide(self.got_b[0]) + wide(self.end_b)
        return jnp.concatenate([a, b])


def column_sums(parts, first, z):
    pick = lambda p: jnp.where(p == first, parts[0], parts[1])
    total = 0.0
    for way in (1, -1):
        run = None
        for far in range(TALL - 1, 0, -1):
            holders = [q for q in range(TALL) if q + way * far in (first, first + 1)]
            if not holders:
                continue
            value = pick(z + way * far)
            if run is not None:
                value = value + run
            pairs = [(q * PLANE + i, (q + way) * PLANE + i) for q in holders for i in range(PLANE)]
            run = wide(lax.ppermute(low(value), AXIS, pairs))
        total = total + run
    return total


def per_device(n, images, noise_draws, labels, step_index, valid_rows, counts, master, momentum, ema):
    direct = n == SHARDS
    index = lax.axis_index(AXIS)
    me = jnp.where(direct, lax.rem(index, PLANE), 0).astype(jnp.int32)[None]
    z = lax.div(index, PLANE)
    shards = [v.astype(BF16).reshape(-1, LINE) for v in (master, ema)]
    tables = tuple(jnp.asarray(v, BF16) for v in (group_table(), *spread_tables(), expand_table(), patch_table()))
    live = (jnp.arange(MB_DEV) < counts[0]).astype(jnp.int32)
    local_rows = jnp.sum(live * jnp.clip(valid_rows, 0, RES)).astype(F32)

    total = total_of(jnp.broadcast_to(local_rows, (8, LINE)), n)
    pixel_total = 3.0 * RES * total[0, 0]

    def early(after):
        clean, noise = gate([images, noise_draws], after) if after else (images, noise_draws)
        clean, noise = pixels(jnp.stack([clean, noise]))
        per_row = lambda v: jnp.repeat(v, PIX)[:, None]

        def inputs_of(sigma):
            noisy = clean + per_row(sigma) * noise
            skip, out_scale, in_scale = preconditioning_factors(sigma)
            x_in = jnp.pad((per_row(in_scale) * noisy).astype(BF16), ((0, 0), (0, LINE - 12)))
            return per_row(skip) * noisy, x_in, noise_features(sigma), per_row(out_scale)

        mask = pixel_live(counts, valid_rows)
        both = inputs_of(karras(step_index)), inputs_of(karras(step_index + 1))
        return (*both, mask), [v for part in both for v in part[:3]] + [mask, total]

    if direct:
        rooms = [jnp.pad(v, ((0, ROOM - SHARD), (0, 0))) for v in shards]
        target = gather_plain(rooms[1])
        (in_lo, in_hi, mask), pieces = gather_lines(rooms[0], z, early)
        online = (pieces, gather_moves(), (False,) * 4 + (True,) + (False,) * 4 + (True,))
    else:
        online, target = gather_plain(shards[0]), gather_plain(shards[1])
        in_lo, in_hi, mask = early(())[0]
    model_t, _ = per_part(jnp.zeros_like(me), labels, target, in_lo, False, tables)
    if direct:
        (x_in,) = gate([in_hi[1]], [model_t])
        in_hi = (in_hi[0], x_in, *in_hi[2:])
    model_o, saved = per_part(me, labels, online, in_hi, True, tables)
    online_out = in_hi[0] + in_hi[3] * model_o[:, :12]
    target_out = in_lo[0] + in_lo[3] * model_t[:, :12]
    phi, out_scale = in_hi[2], in_hi[3]
    gap = online_out - target_out
    local_loss = jnp.sum(mask * jnp.square(gap))
    grad_model = out_scale * 2.0 * mask * gap / pixel_total
    bias_out = jnp.sum(grad_model.reshape(ROWS, 4, 3), axis=(0, 1))
    (h0s, h1, u1, h2, qkv, mixed, h3, u2, h4, vec, mod, emb, pre, wz, xp) = saved[:15]
    s_time, s_emb1, s_emb2, s_down, s11, s12, s_attn, s21, s22 = saved[15:]
    gm = tables[0]
    df = jnp.pad(grad_model, ((0, 0), (0, LINE - 12)))
    small = jnp.concatenate([local_loss[None], bias_out])
    pad = jnp.pad(to_digits(small), ((0, 4), (0, 0)))
    keep3, send3, rest, dh, dse = back_top(
        (me, pad, df, wz, *tables[:5], vec, mod, emb, h4, u2, h3, qkv, mixed, h2, s22, s21, s_attn, s_emb2)
    )
    if direct:
        three = PlaneSum(keep3, send3)
    keep2, send2, rest, du, dm, extra = back_second_half((me, pad, dh, gm, vec, mod, u1, s12, rest))
    if direct:
        first3 = three.first()
        (du,) = gate([du], first3)
        three.send_first(*first3)
        two = PlaneSum(keep2, send2)
    keep1, send1, rest, dh, dse = back_first_half((me, pad, dh, du, dm, extra, dse, gm, vec, emb, h1, s11, s_emb1, rest))
    if direct:
        last3, first2 = three.last(), two.first()
        (dh,) = gate([dh], [*last3, *first2])
        three.send_last(*last3)
        two.send_first(*first2)
        one = PlaneSum(keep1, send1)
    keep0, send0 = back_low((me, labels, pad, dh, dse, emb, pre, phi, h0s, xp, s_down, s_time, rest))
    if direct:
        zero = PlaneSum(keep0, send0)
        one.send_first(*one.first())
        two.send_last(*two.last())
        zero.send_first(*zero.first())
        top = [two.total(), three.total()]
        high = column_sums(top, 2, z)
        one.send_last(*one.last())
        zero.send_last(*zero.last())
        bottom = [zero.total(), one.total()]
        reduced = column_sums(bottom, 0, z) + high
        own = jnp.where(z < 2, jnp.where(z == 0, bottom[0], bottom[1]), jnp.where(z == 2, top[0], top[1]))
        reduced = reduced + own
        small = from_digits(reduced[SHARD : SHARD + 4])
        reduced = reduced[:SHARD].reshape(-1)
    else:
        small = total_of(jnp.broadcast_to(small, (8, 4)), n)[0]
        both = [jnp.stack([wide(k), wide(s)], 1) for k, s in ((keep0, send0), (keep1, send1), (keep2, send2), (keep3, send3))]
        lines = jnp.stack(both).reshape(SHARDS, ROOM, LINE)[:, :SHARD].reshape(n, -1)
        reduced = lax.psum_scatter(lines, AXIS, scatter_dimension=0, tiled=True).reshape(-1)
    new_momentum = MOMENTUM * momentum + reduced
    new_master = master - LEARN_RATE * (reduced + MOMENTUM * new_momentum)
    new_ema = EMA_DECAY * ema + (1.0 - EMA_DECAY) * new_master
    return (small[0] / pixel_total, new_momentum, new_master, new_ema, small[1:])


def solution(mesh):
    n = mesh.shape[AXIS]

    def step(*args):
        return per_device(n, *args)

    return jax.shard_map(
        step,
        mesh=mesh,
        in_specs=(P(AXIS, None, None, None),) * 2 + (P(AXIS),) * 7,
        out_specs=(P(), P(AXIS), P(AXIS), P(AXIS), P()),
        check_vma=False,
    )
```

```python
import math

import jax
import jax.numpy as jnp
import numpy as np
from jax import lax
from jax.experimental import pallas as pl
from jax.experimental.pallas import tpu as pltpu
from jax.sharding import PartitionSpec as P

CH_BASE = 192
CH_MID = 384
EMB_DIM = 768
HEADS = 6
HEAD_DIM = 64
CLASSES = 1000
GROUPS = 32
RES = 32
MB_DEV = 2
DISCRETE = 40

EPSILON = 1e-05
SIGMA_DATA = 0.5
SIGMA_LOW = 0.002
SIGMA_HIGH = 80.0
RHO_POWER = 7.0
MOMENTUM = 0.9
EMA_DECAY = 0.9
LEARN_RATE = 2000.0

F32 = jnp.float32
BF16 = jnp.bfloat16
LINE = 128
HALF = RES // 2
PIX = HALF * HALF
ROWS = MB_DEV * PIX
GROUP_SIZE = PIX * (CH_MID // GROUPS)
CHUNK = 128
PADDED = 16 + MB_DEV * (PIX + 16)
NN = (((1,), (0,)), ((), ()))
NT = (((1,), (1,)), ((), ()))
TN = (((0,), (0,)), ((), ()))


class Place:
    pass


class Cut:
    def __init__(self):
        self.offset = 0

    def take(self, *shape):
        at = self.offset
        self.offset += math.prod(shape)
        return at // LINE


def block_place(cut):
    at = Place()
    at.gains = cut.take(4, CH_MID)
    at.conv_one = cut.take(9 * CH_MID, CH_MID)
    at.bias_one = cut.take(CH_MID)
    at.embed = cut.take(EMB_DIM, 2 * CH_MID)
    at.embed_bias = cut.take(2 * CH_MID)
    at.conv_two = cut.take(9 * CH_MID, CH_MID)
    at.bias_two = cut.take(CH_MID)
    return at


def places():
    cut, at = Cut(), Place()
    at.conv_in = cut.take(27, CH_BASE)
    at.bias_in = cut.take(CH_BASE)
    at.conv_down = cut.take(9 * CH_BASE, CH_MID)
    at.bias_down = cut.take(CH_MID)
    at.time_one = cut.take(CH_BASE, EMB_DIM)
    at.time_bias_one = cut.take(EMB_DIM)
    at.time_two = cut.take(EMB_DIM, EMB_DIM)
    at.time_bias_two = cut.take(EMB_DIM)
    at.class_table = cut.take(CLASSES, EMB_DIM)
    at.first = block_place(cut)
    at.second = block_place(cut)
    at.attn_gains = cut.take(2, CH_MID)
    at.attn_qkv = cut.take(CH_MID, 3 * CH_MID)
    at.attn_out = cut.take(CH_MID, CH_MID)
    at.attn_bias = cut.take(CH_MID)
    at.final_gains = cut.take(2, CH_MID)
    at.conv_out = cut.take(9 * CH_MID, 3)
    at.bias_out = cut.take(3)
    return at


AT = places()
TAIL = AT.conv_out
SHARDS, PLANE = 32, 8
SHARD = 2264
ROOM = 2272
ALL_LINES = SHARDS * SHARD
PLANES = [p * PLANE * SHARD for p in range(SHARDS // PLANE)]
BASE_ONE = AT.second.gains // 16 * 16
BASE_TWO = AT.first.conv_two // 16 * 16
BASE_THREE = AT.first.gains // 16 * 16

V_DOWN, V_G1, V_B11, V_B12, V_AG, V_AB, V_FG, V_G2, V_B21, V_B22 = 0, 1, 5, 6, 7, 9, 10, 12, 16, 17
VEC_ROWS = 24


def group_table():
    at = np.arange(CH_MID) // (CH_MID // GROUPS)
    return (at[:, None] == at[None, :]).astype(np.float32)


TAPS = 16


def spread_tables():
    select = np.zeros((LINE, LINE), np.float32)
    gather = np.zeros((LINE, LINE), np.float32)
    tile = np.zeros((LINE, LINE), np.float32)
    for ky in range(3):
        for kx in range(3):
            for a in range(2):
                for b in range(2):
                    dy, dx = (a + ky - 1) // 2, (b + kx - 1) // 2
                    shift = (dy + 1) * 3 + dx + 1
                    for c in range(3):
                        out = (a * 2 + b) * 3 + c
                        select[c * TAPS + ky * 3 + kx, shift * 12 + out] = 1.0
                        gather[out::12, out][:9] = 1.0
                        tile[c, out] = 1.0
    return select, gather, tile


def patch_table():
    pick = np.zeros((4, LINE, 32), np.float32)
    for a in range(2):
        for b in range(2):
            for ky in range(3):
                for kx in range(3):
                    (dy, ya), (dx, xb) = divmod(a + ky - 1, 2), divmod(b + kx - 1, 2)
                    shift = (dy + 1) * 3 + dx + 1
                    for c in range(3):
                        k = (ky * 3 + kx) * 3 + c
                        pick[a * 2 + b, shift * 12 + (ya * 2 + xb) * 3 + c, k // 2 + 16 * (k % 2)] = 1.0
    return pick


def expand_table():
    return (np.arange(3 * CH_MID)[None, :] // 3 == np.arange(CH_MID)[:, None]).astype(np.float32)


def colour(c):
    lane = lax.broadcasted_iota(jnp.int32, (1, 3 * CH_MID), 1)
    return lax.rem(lane, 3) == c


def first_lanes():
    return lax.broadcasted_iota(jnp.int32, (1, LINE), 1) < LINE // 2


def split3(v):
    hi = v.astype(BF16)
    rest = v - hi.astype(F32)
    mid = rest.astype(BF16)
    low = (rest - mid.astype(F32)).astype(BF16)
    return hi, mid, low


def dot(a, b, dims=NN):
    return lax.dot_general(a, b, dims, preferred_element_type=F32)


def dot3(a, b, dims=NN):
    rows = a.shape[0]
    hi, mid, low = split3(a)
    if rows % 16:
        out = dot(jnp.concatenate([p.astype(F32) for p in (hi, mid, low)], 0).astype(BF16), b, dims)
    else:
        out = dot(jnp.concatenate([hi, mid, low], 0), b, dims)
    return out[:rows] + out[rows : 2 * rows] + out[2 * rows :]


def outer(a, b):
    pa, pb = split3(a), split3(b)
    pairs = [(0, 0), (0, 1), (1, 0), (1, 1), (0, 2), (2, 0)]
    left = jnp.concatenate([pa[i].astype(F32) for i, _ in pairs], 0).astype(BF16)
    right = jnp.concatenate([pb[j].astype(F32) for _, j in pairs], 0).astype(BF16)
    return dot(left, right, TN)


def sigmoid(z):
    return 1.0 / (1.0 + jnp.exp(-z))


def silu(z):
    return z * sigmoid(z)


def silu_slope(z):
    s = sigmoid(z)
    return s * (1.0 + z * (1.0 - s))


def colsum(ref, base, count=PIX):
    def body(c, acc):
        return acc + jnp.sum(ref[pl.ds(pl.multiple_of(base + c * CHUNK, 8), CHUNK), :], 0, keepdims=True)

    return lax.fori_loop(0, count // CHUNK, body, jnp.zeros((1, ref.shape[1]), F32))


def eight(v):
    return jnp.broadcast_to(v, (8, v.shape[1]))


def group_means(rows, gm_ref):
    rows = rows + [jnp.zeros((8 - len(rows), CH_MID), F32)]
    means = dot3(jnp.concatenate(rows, 0), gm_ref[...]) * (1.0 / GROUP_SIZE)
    return [means[n : n + 1] for n in range(len(rows) - 1)]


def all_stats(x_ref, gm_ref):
    def total(c, acc):
        at = lambda img: pl.ds(pl.multiple_of(img * PIX + c * CHUNK, 8), CHUNK)
        return tuple(acc[img] + jnp.sum(x_ref[at(img), :], 0, keepdims=True) for img in range(MB_DEV))

    zero = (jnp.zeros((1, CH_MID), F32),) * MB_DEV
    means = group_means(list(lax.fori_loop(0, PIX // CHUNK, total, zero, unroll=2)), gm_ref)

    def square(c, acc):
        out = []
        for img in range(MB_DEV):
            gap = x_ref[pl.ds(pl.multiple_of(img * PIX + c * CHUNK, 8), CHUNK), :] - means[img]
            out.append(acc[img] + jnp.sum(gap * gap, 0, keepdims=True))
        return tuple(out)

    spreads = group_means(list(lax.fori_loop(0, PIX // CHUNK, square, zero, unroll=2)), gm_ref)
    return [(mean, lax.rsqrt(spread + EPSILON)) for mean, spread in zip(means, spreads)]


def norm_to(pbuf, x_ref, stats, scales, act):
    for img in range(MB_DEV):
        (mean, rstd), (k, o) = stats[img], scales[img]

        def body(c, carry):
            r = pl.multiple_of(img * PIX + c * CHUNK, 8)
            z = (x_ref[pl.ds(r, CHUNK), :] - mean) * rstd * k + o
            pbuf[pl.ds(r + 8, CHUNK), :] = silu(z) if act else z
            return carry

        lax.fori_loop(0, PIX // CHUNK, body, 0, unroll=2)


def norm_back(x_ref, d_ref, stats, scales, act, gm_ref, emit):
    def one(c, carry):
        out = []
        for img in range(MB_DEV):
            (mean, rstd), (k, o) = stats[img], scales[img]
            r = pl.multiple_of(img * PIX + c * CHUNK, 8)
            xhat = (x_ref[pl.ds(r, CHUNK), :] - mean) * rstd
            dz = d_ref[pl.ds(r, CHUNK), :]
            if act:
                dz = dz * silu_slope(xhat * k + o)
                d_ref[pl.ds(r, CHUNK), :] = dz
            out.append(carry[2 * img] + jnp.sum(dz, 0, keepdims=True))
            out.append(carry[2 * img + 1] + jnp.sum(dz * xhat, 0, keepdims=True))
        return tuple(out)

    sums = lax.fori_loop(0, PIX // CHUNK, one, (jnp.zeros((1, CH_MID), F32),) * (2 * MB_DEV), unroll=2)
    means = group_means([v * scales[n // 2][0] for n, v in enumerate(sums)], gm_ref)
    for img in range(MB_DEV):
        (mean, rstd), (k, o) = stats[img], scales[img]
        m1, m2 = means[2 * img], means[2 * img + 1]

        def two(c, carry):
            r = pl.multiple_of(img * PIX + c * CHUNK, 8)
            xhat = (x_ref[pl.ds(r, CHUNK), :] - mean) * rstd
            emit(r, rstd * (d_ref[pl.ds(r, CHUNK), :] * k - m1 - xhat * m2))
            return carry

        lax.fori_loop(0, PIX // CHUNK, two, 0, unroll=2)
    return [(sums[2 * img], sums[2 * img + 1]) for img in range(MB_DEV)]


def clear_pads(sbuf):
    for r in range(0, PADDED, PIX + 16):
        sbuf[r : r + 16, :] = jnp.zeros((16, sbuf.shape[1]), BF16)


def shift_to(sbuf, pbuf):
    column = lax.rem(lax.broadcasted_iota(jnp.int32, (CHUNK, CH_MID), 0), HALF)
    for r in range(0, ROWS, CHUNK):
        for k in range(3):
            v = pbuf[r + 7 + k : r + 7 + k + CHUNK, :]
            if k == 0:
                v = jnp.where(column == 0, 0.0, v)
            if k == 2:
                v = jnp.where(column == HALF - 1, 0.0, v)
            start = r + 16 * (r // PIX + 1)
            sbuf[start : start + CHUNK, k * CH_MID : (k + 1) * CH_MID] = v.astype(BF16)


def shifted(sbuf, row, cols=slice(None)):
    first = sbuf[pl.ds(pl.multiple_of(row, 16), PIX), cols]
    second = sbuf[pl.ds(pl.multiple_of(row + PIX + 16, 16), PIX), cols]
    return jnp.concatenate([first, second], 0)


def conv_forward(sbuf, w_ref, out_ref):
    depth = 3 * CH_MID

    def body(ky, carry):
        w = w_ref[pl.ds(pl.multiple_of(ky * depth, depth), depth), :]
        out_ref[...] += dot(shifted(sbuf, ky * 16), w)
        return carry

    lax.fori_loop(0, 3, body, 0, unroll=3)


def put_lines(g_ref, at, value, step, more=None):
    n = value.shape[0]
    low = at // 8 * 8
    start = low if more is None else pl.multiple_of(low + more, 8)
    view = g_ref.at[pl.ds(start, min(n * step + 8, g_ref.shape[0] - low)), :] if more is None else g_ref.at[pl.ds(start, n * step + 8), :]
    for j in range(step):
        view[pl.ds(at - low + j, n, stride=step), :] = value[:, j * LINE : (j + 1) * LINE]


def put_row(g_ref, at, row):
    for j in range(row.shape[1] // LINE):
        g_ref[pl.ds(at + j, 1), :] = row[:, j * LINE : (j + 1) * LINE]


def conv_back(sbuf, at_ref, w_ref, dx_ref, g_ref, at):
    dx_ref[...] = jnp.zeros_like(dx_ref)
    depth = 3 * CH_MID

    def body(s, carry):
        d = shifted(sbuf, s * 16)
        dw = dot(at_ref[...], d)
        dx = dx_ref[...]
        for k in range(3):
            part = slice(k * CH_MID, (k + 1) * CH_MID)
            tap = (2 - s) * depth + (2 - k) * CH_MID
            dx = dx + dot(d[:, part], w_ref[pl.ds(pl.multiple_of(tap, CH_MID), CH_MID), :], NT)
            put_lines(g_ref, at, dw[:, part], 3, 3 * tap)
        dx_ref[...] = dx
        return carry

    lax.fori_loop(0, 3, body, 0, unroll=3)


def transpose_to(at_ref, pbuf):
    for c in range(ROWS // LINE):
        at_ref[:, c * LINE : (c + 1) * LINE] = pbuf[8 + c * LINE : 8 + (c + 1) * LINE, :].T.astype(BF16)


class Lines:
    def __init__(self, held, wide):
        self.held, self.wide = held, wide

    def take(self, span):
        l0, l1 = span
        first = l0 // SHARD
        self.low = first * SHARD + (l0 - first * SHARD) // 16 * 16
        for s in range(first, (l1 - 1) // SHARD + 1):
            start = max(l0 - s * SHARD, 0) // 16 * 16
            count = -(-min(l1 - s * SHARD, SHARD) // 16) * 16 - start
            to = s * SHARD + start - self.low
            block = self.held.at[s // PLANE, s % PLANE]
            whole, rest = divmod(count, 256)

            def body(c, carry):
                self.wide[pl.ds(pl.multiple_of(to + c * 256, 8), 256), :] = block[
                    pl.ds(pl.multiple_of(start + c * 256, 16), 256), :
                ].astype(F32)
                return carry

            lax.fori_loop(0, whole, body, 0, unroll=2)
            if rest:
                done = whole * 256
                self.wide[to + done : to + count, :] = block[start + done : start + count, :].astype(F32)

    def line(self, at, scratch):
        shard = lax.div(at, SHARD)
        row = at - shard * SHARD
        low = pl.multiple_of(lax.div(row, 16) * 16, 16)
        scratch[...] = self.held[lax.div(shard, PLANE), lax.rem(shard, PLANE), pl.ds(low, 16), :].astype(F32)
        return scratch[pl.ds(row - low, 1), :]

    def matrix(self, w_ref, at, rows, step):
        block = 128 if rows % 192 else 192
        base = at - self.low
        low = base // 8 * 8

        def body(c, carry):
            r = pl.multiple_of(c * block, block)
            view = self.wide.at[pl.ds(pl.multiple_of(low + r * step, 8), block * step + 8), :]
            for j in range(step):
                v = view[pl.ds(base - low + j, block, stride=step), :]
                w_ref[pl.ds(r, block), j * LINE : (j + 1) * LINE] = v.astype(BF16)
            return carry

        lax.fori_loop(0, rows // block, body, 0, unroll=3 if (rows // block) % 3 == 0 else 2)

    def row(self, at, step):
        base = at - self.low
        return jnp.concatenate([self.wide[pl.ds(base + j, 1), :] for j in range(step)], 1)


def attention_pair(qkv_ref, img, pair):
    rows = pl.ds(pl.multiple_of(img * PIX, PIX), PIX)
    return [qkv_ref[rows, part * CH_MID + pair * LINE : part * CH_MID + (pair + 1) * LINE] for part in range(3)]


def lane_half():
    return lax.broadcasted_iota(jnp.int32, (1, LINE), 1) < HEAD_DIM


def keep_half(v, half, side):
    mine = half if side == 0 else jnp.logical_not(half)
    return jnp.where(mine, v.astype(F32), 0.0).astype(BF16)


SPAN_TIME = (AT.time_one, AT.class_table)
SPAN_EMB1 = (AT.first.embed, AT.first.conv_two)
SPAN_EMB2 = (AT.second.embed, AT.second.conv_two)
SPAN_DOWN = (AT.conv_in, AT.time_one)
SPAN_ONE1 = (AT.first.gains, AT.first.embed)
SPAN_TWO1 = (AT.first.conv_two, AT.second.gains)
SPAN_ATTN = (AT.attn_gains, ALL_LINES)
SPAN_ONE2 = (AT.second.gains, AT.second.embed)
SPAN_TWO2 = (AT.second.conv_two, AT.attn_gains)


def block_scales(vec, row, mod_ref=None, mod_row=0):
    gain, shift = vec[row : row + 1, :], vec[row + 1 : row + 2, :]
    if mod_ref is None:
        return [(gain, shift)] * MB_DEV
    out = []
    for img in range(MB_DEV):
        scale = 1.0 + mod_ref[mod_row + img : mod_row + img + 1, :CH_MID]
        out.append((gain * scale, shift * scale + mod_ref[mod_row + img : mod_row + img + 1, CH_MID:]))
    return out


def upsample_masks(shift):
    dy, dx = shift // 3 - 1, shift % 3 - 1
    p = lax.broadcasted_iota(jnp.int32, (ROWS, 1), 0)
    i, j = lax.rem(lax.div(p, HALF), HALF), lax.rem(p, HALF)
    inside = (i + dy >= 0) & (i + dy < HALF) & (j + dx >= 0) & (j + dx < HALF)
    lane = lax.broadcasted_iota(jnp.int32, (1, LINE), 1)
    return inside & (lane >= shift * 12) & (lane < shift * 12 + 12), dy * HALF + dx


def forward_kernel(save, moves, flip, *refs):
    me, labels, x_in, phi, gm, sel, gat, tile, expand, pick = refs[:10]
    sources = max(move[0] for move in moves) + 1
    pieces, refs = refs[10 : 10 + sources], refs[10 + sources :]
    f_out = refs[0]
    (h0s, h1, u1, h2, qkv, mixed, h3, u2, h4, vec, mod, emb, pre, wz, xp) = refs[1:16]
    if save:
        sw_time, sw_emb1, sw_emb2, sw_down, sw_11, sw_12, sw_attn, sw_21, sw_22 = refs[16:25]
    held, wide, w_ref, w_sq, sbuf, pbuf, h0p, table, w_in, b_out, sems, save_sem = refs[25 if save else 16 :]
    src = Lines(held, wide)
    arriving = []
    for plane in range(TALL):
        copies = []
        for n, lead, r, row, rows in moves:
            target = held.at[plane, r ^ me[0], pl.ds(row, rows), :]
            source = pieces[n].at[plane, lead] if flip[n] else pieces[n].at[lead, plane]
            copies.append(pltpu.make_async_copy(source, target, sems.at[plane]))
        arriving.append(copies)

    def arrive(plane):
        for copy in arriving[plane]:
            copy.wait()

    for plane in range(TALL):
        for copy in arriving[plane]:
            copy.start()
    pending = []

    def keep(source, target):
        if save:
            cp = pltpu.make_async_copy(source, target, save_sem)
            cp.start()
            pending.append(cp)

    def free():
        while pending:
            pending.pop().wait()

    clear_pads(sbuf)
    pbuf[0:8, :] = jnp.zeros((8, CH_MID), F32)
    pbuf[ROWS + 8 : ROWS + 16, :] = jnp.zeros((8, CH_MID), F32)
    arrive(0)
    src.take(SPAN_TIME)
    src.matrix(w_sq.at[0], AT.time_one, CH_BASE, 6)
    src.matrix(w_sq.at[1], AT.time_two, EMB_DIM, 6)
    pre[...] = dot3(phi[...], w_sq[0, :CH_BASE, :]) + src.row(AT.time_bias_one, 6)
    emb[...] = dot3(silu(pre[...]), w_sq[1]) + src.row(AT.time_bias_two, 6)
    for n in range(MB_DEV):
        for j in range(6):
            cols = slice(j * LINE, (j + 1) * LINE)
            emb[n : n + 1, cols] += src.line(AT.class_table + labels[n] * 6 + j, table)
    keep(w_sq.at[1], sw_time if save else None)
    se = silu(emb[...])
    arrive(1)
    src.take(SPAN_EMB1)
    src.matrix(w_sq.at[0], AT.first.embed, EMB_DIM, 6)
    m1 = dot3(se, w_sq[0]) + src.row(AT.first.embed_bias, 6)
    free()
    keep(w_sq.at[0], sw_emb1 if save else None)
    mod[0:2, :] = m1[0:2]
    mod[4:8, :] = jnp.zeros((4, EMB_DIM), F32)

    src.take(SPAN_DOWN)
    trio = [wide[pl.ds(j, 16, stride=3), :] for j in range(3)]
    turned = [pltpu.roll(v, LINE // 2, 1) for v in trio[1:]]
    w_in[0:16, 0:LINE] = trio[0]
    w_in[0:16, LINE : 2 * LINE] = trio[1]
    w_in[16:32, 0:LINE] = jnp.where(first_lanes(), turned[0], turned[1])
    w_in[16:32, LINE : 2 * LINE] = turned[1]
    w_low = w_in[...].astype(BF16)
    spread = dot(x_in[...], gat[...], NT)
    around = jnp.zeros((ROWS, LINE), F32)
    for shift in range(9):
        inside, by = upsample_masks(shift)
        around = around + jnp.where(inside, spread if by == 0 else pltpu.roll(spread, (-by) % ROWS, 0), 0.0)
    around = around.astype(BF16)
    one = (lax.broadcasted_iota(jnp.int32, (1, 32), 1) == 29).astype(F32)
    for ph in range(4):
        patch = (dot(around, pick[ph]) + one).astype(BF16)
        xp[ph * ROWS : (ph + 1) * ROWS, :] = patch
        h0s[ph * ROWS : (ph + 1) * ROWS, :] = dot(patch, w_low).astype(BF16)
    for j in range(3):
        vec[V_DOWN : V_DOWN + 1, j * LINE : (j + 1) * LINE] = src.row(AT.bias_down + j, 1)
    src.matrix(w_ref, AT.conv_down, 9 * CH_BASE, 3)
    free()
    keep(w_ref.at[pl.ds(0, 9 * CH_BASE), :], sw_down if save else None)
    h1[...] = jnp.broadcast_to(vec[V_DOWN : V_DOWN + 1, :], (ROWS, CH_MID))
    p = lax.broadcasted_iota(jnp.int32, (ROWS, 1), 0)
    has_left, has_up = lax.rem(p, HALF) > 0, lax.rem(lax.div(p, HALF), HALF) > 0
    for ph in range(4):
        h0p[0:32, :] = jnp.zeros((32, h0p.shape[1]), F32)
        h0p[32 : 32 + ROWS, :] = h0s[ph * ROWS : (ph + 1) * ROWS, :].astype(F32)
        for ky in ((0, 2) if ph // 2 else (1,)):
            for kx in ((0, 2) if ph % 2 else (1,)):
                back = (16 if ky == 0 else 0) + (1 if kx == 0 else 0)
                v = h0p[32 - back : 32 - back + ROWS, :]
                if ky == 0:
                    v = jnp.where(has_up, v, 0.0)
                if kx == 0:
                    v = jnp.where(has_left, v, 0.0)
                t = 3 * ky + kx
                h1[...] += dot(v[:, :CH_BASE].astype(BF16), w_ref[t * CH_BASE : (t + 1) * CH_BASE, :])

    def vectors(row, at, count):
        for n in range(count):
            for j in range(3):
                vec[row + n : row + n + 1, j * LINE : (j + 1) * LINE] = src.row(at + 3 * n + j, 1)

    def half_block(x_ref, scales, bias_row, add_ref, out_ref, at, target):
        src.matrix(w_ref, at, 9 * CH_MID, 3)
        keep(w_ref, target)
        stats = all_stats(x_ref, gm)
        norm_to(pbuf, x_ref, stats, scales, True)
        shift_to(sbuf, pbuf)
        bias = jnp.broadcast_to(vec[bias_row : bias_row + 1, :], (ROWS, CH_MID))
        out_ref[...] = bias if add_ref is None else add_ref[...] + bias
        conv_forward(sbuf, w_ref, out_ref)

    def block(h_in, u, h_out, prefix, g_row, b1_row, b2_row, mod_row, spans, targets):
        src.take(spans[0])
        free()
        vectors(g_row, prefix.gains, 4)
        vectors(b1_row, prefix.bias_one, 1)
        half_block(h_in, block_scales(vec, g_row), b1_row, None, u, prefix.conv_one, targets[0])
        src.take(spans[1])
        free()
        vectors(b2_row, prefix.bias_two, 1)
        half_block(u, block_scales(vec, g_row + 2, mod, mod_row), b2_row, h_in, h_out, prefix.conv_two, targets[1])

    saved = (sw_11, sw_12, sw_21, sw_22) if save else (None,) * 4
    arrive(2)
    block(h1, u1, h2, AT.first, V_G1, V_B11, V_B12, 0, (SPAN_ONE1, SPAN_TWO1), saved[:2])

    arrive(3)
    src.take(SPAN_ATTN)
    free()
    vectors(V_AG, AT.attn_gains, 2)
    vectors(V_AB, AT.attn_bias, 1)
    vectors(V_FG, AT.final_gains, 2)
    base = AT.conv_out - src.low
    tap_row = lax.broadcasted_iota(jnp.int32, (TAPS, 1), 0) < 9
    taps = [jnp.where(tap_row, wide[pl.ds(base + j, TAPS, stride=9), :], 0.0) for j in range(9)]
    taps = jnp.concatenate(taps, 1)
    rows_out = jnp.concatenate([jnp.where(colour(c), taps, 0.0) for c in range(3)], 0).astype(BF16)
    wz[...] = jnp.zeros_like(wz)
    wz[0 : 3 * TAPS, :] = dot(rows_out, expand[...], NT).astype(BF16)
    last = AT.bias_out - src.low
    b_out[...] = dot(eight(wide[last : last + 1, :]).astype(BF16), tile[...])
    for part in range(3):
        base = AT.attn_qkv - src.low
        for j in range(3):
            v = wide[pl.ds(base + part * 3 + j, CH_MID, stride=9), :]
            w_ref[part * CH_MID : (part + 1) * CH_MID, j * LINE : (j + 1) * LINE] = v.astype(BF16)
    src.matrix(w_ref.at[pl.ds(3 * CH_MID, CH_MID), :], AT.attn_out, CH_MID, 3)
    keep(w_ref.at[pl.ds(0, 4 * CH_MID), :], sw_attn if save else None)
    stats = all_stats(h2, gm)
    norm_to(pbuf, h2, stats, block_scales(vec, V_AG), False)
    n_low = pbuf[8 : 8 + ROWS, :].astype(BF16)
    for part in range(3):
        v = dot(n_low, w_ref[part * CH_MID : (part + 1) * CH_MID, :])
        qkv[:, part * CH_MID : (part + 1) * CH_MID] = v.astype(BF16)
    half = lane_half()

    def heads(img, carry):
        for pair in range(HEADS // 2):
            q, k, v = attention_pair(qkv, img, pair)
            outs = []
            for side in range(2):
                s = dot(keep_half(q, half, side), k, NT) * HEAD_DIM ** (-0.5)
                e = jnp.exp(s - jnp.max(s, 1, keepdims=True))
                prob = (e / jnp.sum(e, 1, keepdims=True)).astype(BF16)
                outs.append(dot(prob, v))
            mixed[pl.ds(pl.multiple_of(img * PIX, PIX), PIX), pair * LINE : (pair + 1) * LINE] = jnp.where(
                half, outs[0], outs[1]
            ).astype(BF16)
        return carry

    lax.fori_loop(0, MB_DEV, heads, 0, unroll=2)
    h3[...] = h2[...] + dot(mixed[...], w_ref[3 * CH_MID : 4 * CH_MID, :]) + vec[V_AB : V_AB + 1, :]

    src.take(SPAN_EMB2)
    src.matrix(w_sq.at[1], AT.second.embed, EMB_DIM, 6)
    m2 = dot3(silu(emb[...]), w_sq[1]) + src.row(AT.second.embed_bias, 6)
    mod[2:4, :] = m2[0:2]
    free()
    keep(w_sq.at[1], sw_emb2 if save else None)
    block(h3, u2, h4, AT.second, V_G2, V_B21, V_B22, 2, (SPAN_ONE2, SPAN_TWO2), saved[2:])

    stats = all_stats(h4, gm)
    norm_to(pbuf, h4, stats, block_scales(vec, V_FG), True)
    z = dot(pbuf[8 : 8 + ROWS, :].astype(BF16), wz[...], NT)
    t_all = dot3(z, sel[...])
    u_all = jnp.zeros((ROWS, LINE), F32)
    for shift in range(9):
        inside, by = upsample_masks(shift)
        moved = t_all if by == 0 else pltpu.roll(t_all, (-by) % ROWS, 0)
        u_all = u_all + jnp.where(inside, moved, 0.0)
    f_out[...] = dot3(u_all, gat[...]) + b_out[0:1, :]
    free()


def vmem(*shape_dtype):
    return pltpu.VMEM(*shape_dtype)


VM = pl.BlockSpec(memory_space=pltpu.VMEM)
HB = pl.BlockSpec(memory_space=pl.ANY)
SM = pl.BlockSpec(memory_space=pltpu.SMEM)


def state_shapes():
    act = ((ROWS, CH_MID), F32)
    return [
        ((4 * ROWS, 256), BF16),
        act, act, act,
        ((ROWS, 3 * CH_MID), BF16),
        ((ROWS, CH_MID), BF16),
        act, act, act,
        ((VEC_ROWS, CH_MID), F32),
        ((8, EMB_DIM), F32),
        ((8, EMB_DIM), F32),
        ((8, EMB_DIM), F32),
        ((LINE, CH_MID), BF16),
        ((4 * ROWS, 32), BF16),
    ]


def weight_shapes():
    sq = ((EMB_DIM, EMB_DIM), BF16)
    conv = ((9 * CH_MID, CH_MID), BF16)
    return [sq, sq, sq, ((9 * CH_BASE, CH_MID), BF16), conv, conv, ((4 * CH_MID, CH_MID), BF16), conv, conv]


def forward_call(save, me, labels, lines, x_in, phi, tables):
    pieces, moves, flip = lines
    sds = lambda s: jax.ShapeDtypeStruct(*s)
    outs = [sds(((ROWS, LINE), F32))]
    out_specs = [VM]
    state = state_shapes()
    scratch = []
    if save:
        outs += [sds(s) for s in state] + [sds(s) for s in weight_shapes()]
        out_specs += [VM] * len(state) + [HB] * len(weight_shapes())
    else:
        scratch += [vmem(*s) for s in state]
    scratch += [
        vmem((SHARDS // PLANE, PLANE, ROOM, LINE), BF16),
        vmem((10432, LINE), F32),
        vmem((9 * CH_MID, CH_MID), BF16),
        vmem((2, EMB_DIM, EMB_DIM), BF16),
        vmem((PADDED, 3 * CH_MID), BF16),
        vmem((ROWS + 16, CH_MID), F32),
        vmem((ROWS + 48, 256), F32),
        vmem((16, LINE), F32),
        vmem((32, 2 * LINE), F32),
        vmem((8, LINE), F32),
        pltpu.SemaphoreType.DMA((SHARDS // PLANE,)),
        pltpu.SemaphoreType.DMA,
    ]

    def body(*refs):
        forward_kernel(save, moves, flip, *refs)

    return pl.pallas_call(
        body,
        out_shape=outs,
        in_specs=[SM] * 2 + [VM] * 8 + [HB] * len(pieces),
        out_specs=out_specs,
        scratch_shapes=scratch,
        name="forward_save" if save else "forward_plain",
        **kernel_params(),
    )(me, labels, x_in, phi, *tables, *pieces)


def column_sum(pbuf):
    def body(c, acc):
        return acc + jnp.sum(pbuf[pl.ds(pl.multiple_of(c * CHUNK + 8, 8), CHUNK), :], 0, keepdims=True)

    return lax.fori_loop(0, ROWS // CHUNK, body, jnp.zeros((1, CH_MID), F32))


def refill(pbuf, source):
    for c in range(0, ROWS, CHUNK):
        pbuf[8 + c : 8 + c + CHUNK, :] = source[c : c + CHUNK, :]


def block_back_two(dh, u_ref, at, base, rows, vec, mod, mod_row, weights, tools, g, dm):
    g_row, b1_row, b2_row = rows
    sbuf, pbuf, dx, at_ref, gm = tools
    put_row(g, at.bias_two - base, colsum(dh, 0, ROWS))
    u_stats = all_stats(u_ref, gm)
    scales = block_scales(vec, g_row + 2, mod, mod_row)
    norm_to(pbuf, u_ref, u_stats, scales, True)
    transpose_to(at_ref, pbuf)
    refill(pbuf, dh)
    shift_to(sbuf, pbuf)
    conv_back(sbuf, at_ref, weights.take(), dx, g, at.conv_two - base)
    weights.begin()

    def emit_inner(r, v):
        pbuf[pl.ds(r + 8, CHUNK), :] = v

    sums = norm_back(u_ref, dx, u_stats, scales, True, gm, emit_inner)
    gain, shift = vec[g_row + 2 : g_row + 3, :], vec[g_row + 3 : g_row + 4, :]
    d_gain = d_shift = 0.0
    dm[...] = jnp.zeros_like(dm)
    for img, (a, b) in enumerate(sums):
        scale = 1.0 + mod[mod_row + img : mod_row + img + 1, :CH_MID]
        d_gain, d_shift = d_gain + scale * b, d_shift + scale * a
        dm[img : img + 1, :CH_MID] = gain * b + shift * a
        dm[img : img + 1, CH_MID:] = a
    return d_gain, d_shift


def block_back_one(dh, x_ref, at, base, rows, vec, weights, tools, g):
    g_row, b1_row, b2_row = rows
    sbuf, pbuf, dx, at_ref, gm = tools
    put_row(g, at.bias_one - base, column_sum(pbuf))
    shift_to(sbuf, pbuf)
    stats = all_stats(x_ref, gm)
    scales = block_scales(vec, g_row)
    norm_to(pbuf, x_ref, stats, scales, True)
    transpose_to(at_ref, pbuf)
    conv_back(sbuf, at_ref, weights.take(), dx, g, at.conv_one - base)
    weights.begin()

    def emit_outer(r, v):
        dh[pl.ds(r, CHUNK), :] += v

    sums = norm_back(x_ref, dx, stats, scales, True, gm, emit_outer)
    put_row(g, at.gains - base, sums[0][1] + sums[1][1])
    put_row(g, at.gains + 3 - base, sums[0][0] + sums[1][0])


def rowsum(v):
    return jnp.sum(v, 0, keepdims=True)


def put_outer(g, at, left, right):
    for c in range(-(-left.shape[1] // LINE)):
        piece = outer(left[:, c * LINE : (c + 1) * LINE], right)
        put_lines(g, at + c * LINE * (EMB_DIM // LINE), piece, EMB_DIM // LINE)


class Weights:
    def __init__(self, sources, slots, sems):
        self.copies = []
        for n, source in enumerate(sources):
            target = slots.at[n % 2, pl.ds(0, source.shape[0]), :]
            self.copies.append((pltpu.make_async_copy(source, target, sems.at[n % 2]), target))
        self.begun = self.done = 0

    def begin(self):
        if self.begun < len(self.copies):
            self.copies[self.begun][0].start()
            self.begun += 1

    def take(self):
        copy, target = self.copies[self.done]
        copy.wait()
        self.done += 1
        return target


class Leave:
    def __init__(self, me, g, base, keep, send, stage, sems, pad):
        self.pad = pad
        self.core, self.place = lax.rem(me[0], 2), lax.div(me[0], 2)
        self.g, self.base, self.outs, self.stage, self.sems = g, base, (keep, send), stage, sems
        self.copies = []

    def plane(self, plane):
        for q in range(PLANE // 2):
            at = q ^ self.place
            first = PLANES[plane] + 2 * q * SHARD - self.base
            for side in range(2):
                core = 1 - self.core if side else self.core
                start = first + core * SHARD
                stage = self.stage.at[2 * q + side]
                whole, rest = divmod(ROOM, 288)

                def body(c, carry):
                    lines = self.g[pl.ds(pl.multiple_of(start + c * 288, 8), 288), :]
                    stage[pl.ds(pl.multiple_of(c * 288, 16), 288), :] = lines.astype(BF16)
                    return carry

                lax.fori_loop(0, whole, body, 0)
                lines = self.g[pl.ds(pl.multiple_of(start + whole * 288, 8), rest - 8), :]
                stage[whole * 288 :, :] = jnp.concatenate([lines, self.pad[...]], 0).astype(BF16)
                copy = pltpu.make_async_copy(stage, self.outs[side].at[at], self.sems.at[side])
                copy.start()
                self.copies.append(copy)

    def below(self, count, rest):
        copy = pltpu.make_async_copy(self.g.at[pl.ds(0, count), :], rest, self.sems.at[2])
        copy.start()
        self.copies.append(copy)

    def wait(self):
        for copy in self.copies:
            copy.wait()


def clear_lines(g, first, count):
    if count:
        g[first : first + count, :] = jnp.zeros((count, LINE), F32)


def prepare(sbuf, pbuf):
    clear_pads(sbuf)
    pbuf[0:8, :] = jnp.zeros((8, CH_MID), F32)
    pbuf[ROWS + 8 : ROWS + 16, :] = jnp.zeros((8, CH_MID), F32)


def back_top_kernel(*refs):
    me, total, f_o, f_t, base_o, base_t, out_o, out_t, mask, inverse, wz, gm, sel, gat, tile, expand, vec, mod, emb, h4, u2, h3, qkv, mixed, h2, s22, s21, s_attn, s_emb = refs[:29]
    keep, send, rest, dh, dse, pad = refs[29:35]
    g, slots, sbuf, pbuf, dx, at_ref, stage, sems, out_sems, w_sq, dqkv, dm, sq_sem = refs[35:]
    base = BASE_ONE
    weights = Weights([s22, s21, s_attn], slots, sems)
    weights.begin()
    weights.begin()
    sq_copy = pltpu.make_async_copy(s_emb, w_sq, sq_sem)
    sq_copy.start()
    prepare(sbuf, pbuf)
    clear_lines(g, TAIL - base, g.shape[0] - (TAIL - base))
    tools = (sbuf, pbuf, dx, at_ref, gm)

    stats = all_stats(h4, gm)
    scales = block_scales(vec, V_FG)
    norm_to(pbuf, h4, stats, scales, True)
    transpose_to(at_ref, pbuf)
    gap = (base_o[...] + out_o[...] * f_o[:, :12]) - (base_t[...] + out_t[...] * f_t[:, :12])
    loss = jnp.sum(mask[...] * (gap * gap))
    df = jnp.pad(out_o[...] * 2.0 * mask[...] * gap / total[0], ((0, 0), (0, LINE - 12)))
    spread = dot(df.astype(BF16), gat[...], NT)
    dt = jnp.zeros((ROWS, LINE), F32)
    for shift in range(9):
        inside, by = upsample_masks(shift)
        part = jnp.where(inside, spread, 0.0)
        dt = dt + (part if by == 0 else pltpu.roll(part, by % ROWS, 0))
    dz = dot(dt.astype(BF16), sel[...], NT)
    parts = split3(dz)
    dwz = dot(at_ref[...], parts[0]) + dot(at_ref[...], parts[1]) + dot(at_ref[...], parts[2])
    dx[...] = dot(parts[0], wz[...]) + dot(parts[1], wz[...]) + dot(parts[2], wz[...])
    d_rows = dot3(dwz.T[0 : 3 * TAPS, :], expand[...])
    d_taps = jnp.zeros((TAPS, 3 * CH_MID), F32)
    for c in range(3):
        d_taps = d_taps + jnp.where(colour(c), d_rows[c * TAPS : (c + 1) * TAPS, :], 0.0)
    for j in range(9):
        g[pl.ds(TAIL - base + j, 9, stride=9), :] = d_taps[0:9, j * LINE : (j + 1) * LINE]
    b_row = AT.bias_out - base
    bias = dot3(eight(rowsum(df)), tile[...], NT)[0:1]
    g[b_row : b_row + 1, :] = bias
    row = lax.broadcasted_iota(jnp.int32, (8, 1), 0)
    lane = lax.broadcasted_iota(jnp.int32, (1, LINE), 1)
    values = jnp.where(row == 0, loss, 0.0)
    for c in range(3):
        values = values + jnp.where(row == c + 1, jnp.sum(jnp.where(lane == c, bias, 0.0)), 0.0)
    pad[...] = to_digits(values, inverse[...])

    def emit_first(r, v):
        dh[pl.ds(r, CHUNK), :] = v

    sums = norm_back(h4, dx, stats, scales, True, gm, emit_first)
    put_row(g, AT.final_gains - base, sums[0][1] + sums[1][1])
    put_row(g, AT.final_gains + 3 - base, sums[0][0] + sums[1][0])

    rows = (V_G2, V_B21, V_B22)
    d_gain, d_shift = block_back_two(dh, u2, AT.second, base, rows, vec, mod, 2, weights, tools, g, dm)
    put_row(g, AT.second.gains + 6 - base, d_gain)
    put_row(g, AT.second.gains + 9 - base, d_shift)
    block_back_one(dh, h3, AT.second, base, rows, vec, weights, tools, g)
    se = silu(emb[...])
    put_outer(g, AT.second.embed - base, se, dm[...])
    put_row(g, AT.second.embed_bias - base, rowsum(dm[...]))
    sq_copy.wait()
    dse[...] = dot3(dm[...], w_sq[...], NT)

    put_row(g, AT.attn_bias - base, colsum(dh, 0, ROWS))
    w = weights.take()
    d_low = dh[...].astype(BF16)
    for c in range(ROWS // LINE):
        at_ref[:, c * LINE : (c + 1) * LINE] = mixed[c * LINE : (c + 1) * LINE, :].astype(F32).T.astype(BF16)
    put_lines(g, AT.attn_out - base, dot(at_ref[...], d_low), 3)
    pbuf[8 : 8 + ROWS, :] = dot(d_low, w[3 * CH_MID : 4 * CH_MID, :], NT)
    half = lane_half()
    scale = HEAD_DIM ** (-0.5)

    def heads(img, carry):
        rows = pl.ds(pl.multiple_of(img * PIX, PIX), PIX)
        for pair in range(HEADS // 2):
            q, k, v = attention_pair(qkv, img, pair)
            cols = slice(pair * LINE, (pair + 1) * LINE)
            do = pbuf[pl.ds(pl.multiple_of(img * PIX + 8, 8), PIX), cols].astype(BF16)
            dqs, dks, dvs = [], [], []
            for side in range(2):
                s = dot(keep_half(k, half, side), q, NT) * scale
                e = jnp.exp(s - jnp.max(s, 0, keepdims=True))
                prob = e / jnp.sum(e, 0, keepdims=True)
                dvs.append(dot(prob.astype(BF16), do))
                dp = dot(keep_half(v, half, side), do, NT)
                ds = prob * (dp - jnp.sum(dp * prob, 0, keepdims=True))
                dks.append(dot(ds.astype(BF16), q))
                dqs.append(dot(ds.T.astype(BF16), k))
            for part, pieces in enumerate((dqs, dks, dvs)):
                value = jnp.where(half, pieces[0], pieces[1])
                if part < 2:
                    value = value * scale
                dqkv[rows, part * CH_MID + pair * LINE : part * CH_MID + (pair + 1) * LINE] = value.astype(BF16)
        return carry

    lax.fori_loop(0, MB_DEV, heads, 0, unroll=2)
    stats = all_stats(h2, gm)
    scales = block_scales(vec, V_AG)
    norm_to(pbuf, h2, stats, scales, False)
    transpose_to(at_ref, pbuf)
    dx[...] = jnp.zeros_like(dx)
    for part in range(3):
        d = dqkv[:, part * CH_MID : (part + 1) * CH_MID]
        dw = dot(at_ref[...], d)
        for j in range(3):
            g[pl.ds(AT.attn_qkv - base + part * 3 + j, CH_MID, stride=9), :] = dw[:, j * LINE : (j + 1) * LINE]
        dx[...] += dot(d, w[part * CH_MID : (part + 1) * CH_MID, :], NT)
    weights.begin()

    def emit(r, v):
        dh[pl.ds(r, CHUNK), :] += v

    sums = norm_back(h2, dx, stats, scales, False, gm, emit)
    put_row(g, AT.attn_gains - base, sums[0][1] + sums[1][1])
    put_row(g, AT.attn_gains + 3 - base, sums[0][0] + sums[1][0])

    leave = Leave(me, g, base, keep, send, stage, out_sems, pad)
    leave.plane(3)
    leave.below(PLANES[3] - base, rest)
    leave.wait()


def back_second_half_kernel(*refs):
    me, pad, dh, gm, vec, mod, u1, s12, rest_in = refs[:9]
    keep, send, rest, du, dm, extra = refs[9:15]
    g, slots, sbuf, pbuf, dx, at_ref, stage, sems, out_sems, in_sem = refs[15:]
    base = BASE_TWO
    weights = Weights([s12], slots, sems)
    weights.begin()
    above = pltpu.make_async_copy(rest_in, g.at[pl.ds(BASE_ONE - base, PLANES[3] - BASE_ONE), :], in_sem)
    above.start()
    prepare(sbuf, pbuf)
    clear_lines(g, PLANES[3] - base, g.shape[0] - (PLANES[3] - base))
    above.wait()
    rows = (V_G1, V_B11, V_B12)
    tools = (sbuf, pbuf, dx, at_ref, gm)
    d_gain, d_shift = block_back_two(dh, u1, AT.first, base, rows, vec, mod, 0, weights, tools, g, dm)
    extra[...] = jnp.zeros_like(extra)
    extra[0:1, :] = d_gain
    extra[1:2, :] = d_shift
    for c in range(0, ROWS, CHUNK):
        du[c : c + CHUNK, :] = pbuf[8 + c : 8 + c + CHUNK, :]
    leave = Leave(me, g, base, keep, send, stage, out_sems, pad)
    leave.plane(2)
    leave.below(PLANES[2] - base, rest)
    leave.wait()


def back_first_half_kernel(*refs):
    me, pad, dh_in, du, dm, extra, dse_in, gm, vec, emb, h1, s11, s_emb, rest_in = refs[:14]
    keep, send, rest, dh, dse = refs[14:19]
    g, slots, sbuf, pbuf, dx, at_ref, stage, sems, out_sems, w_sq, in_sem, sq_sem = refs[19:]
    base = BASE_THREE
    weights = Weights([s11], slots, sems)
    weights.begin()
    sq_copy = pltpu.make_async_copy(s_emb, w_sq, sq_sem)
    sq_copy.start()
    above = pltpu.make_async_copy(rest_in, g.at[pl.ds(BASE_TWO - base, PLANES[2] - BASE_TWO), :], in_sem)
    above.start()
    prepare(sbuf, pbuf)
    clear_lines(g, PLANES[2] - base, g.shape[0] - (PLANES[2] - base))
    refill(pbuf, du)
    for c in range(0, ROWS, CHUNK):
        dh[c : c + CHUNK, :] = dh_in[c : c + CHUNK, :]
    above.wait()
    tools = (sbuf, pbuf, dx, at_ref, gm)
    put_outer(g, AT.first.embed - base, silu(emb[...]), dm[...])
    put_row(g, AT.first.embed_bias - base, rowsum(dm[...]))
    block_back_one(dh, h1, AT.first, base, (V_G1, V_B11, V_B12), vec, weights, tools, g)
    put_row(g, AT.first.gains + 6 - base, extra[0:1, :])
    put_row(g, AT.first.gains + 9 - base, extra[1:2, :])
    leave = Leave(me, g, base, keep, send, stage, out_sems, pad)
    leave.plane(1)
    leave.below(PLANES[1] - base, rest)
    sq_copy.wait()
    dse[...] = dse_in[...] + dot3(dm[...], w_sq[...], NT)
    leave.wait()


def back_low_kernel(*refs):
    me, labels, pad, dh, dse, emb, pre, phi, h0s, xp, s_down, s_time, rest_in = refs[:13]
    keep, send = refs[13:15]
    g, slots, sbuf, pbuf, h0t, stage, sems, out_sems, w_sq, demb_ref, dwin, dbin, in_sem, sq_sem = refs[15:]
    weights = Weights([s_down], slots, sems)
    weights.begin()
    sq_copy = pltpu.make_async_copy(s_time, w_sq, sq_sem)
    sq_copy.start()
    above = pltpu.make_async_copy(rest_in, g.at[pl.ds(BASE_THREE, PLANES[1] - BASE_THREE), :], in_sem)
    above.start()
    prepare(sbuf, pbuf)
    clear_lines(g, PLANES[1], g.shape[0] - PLANES[1])
    above.wait()
    demb = dse[...] * silu_slope(emb[...])
    put_row(g, AT.time_bias_two, rowsum(demb))
    put_outer(g, AT.time_two, silu(pre[...]), demb)
    sq_copy.wait()
    dpre = dot3(demb, w_sq[...], NT) * silu_slope(pre[...])
    put_row(g, AT.time_bias_one, rowsum(dpre))
    put_outer(g, AT.time_one, phi[...], dpre)
    clear = 240
    first, lines = AT.class_table, CLASSES * (EMB_DIM // LINE)

    def wipe(c, carry):
        g[pl.ds(first + c * clear, clear), :] = jnp.zeros((clear, LINE), F32)
        return carry

    lax.fori_loop(0, lines // clear, wipe, 0)
    demb_ref[...] = demb
    for n in range(MB_DEV):
        for j in range(EMB_DIM // LINE):
            at = first + labels[n] * (EMB_DIM // LINE) + j
            g[pl.ds(at, 1), :] += demb_ref[n : n + 1, j * LINE : (j + 1) * LINE]

    put_row(g, AT.bias_down, colsum(dh, 0, ROWS))
    refill(pbuf, dh)
    shift_to(sbuf, pbuf)
    w = weights.take()
    dwin[...] = jnp.zeros_like(dwin)
    dbin[...] = jnp.zeros_like(dbin)
    for ph in range(4):
        for c in range(ROWS // LINE):
            rows = slice(ph * ROWS + c * LINE, ph * ROWS + (c + 1) * LINE)
            h0t[:, c * LINE : (c + 1) * LINE] = h0s[rows, :].astype(F32).T.astype(BF16)
        d0 = jnp.zeros((ROWS, CH_BASE), F32)
        for ky in ((0, 2) if ph // 2 else (1,)):
            for kx in ((0, 2) if ph % 2 else (1,)):
                side = 2 if kx == 0 else 1
                d = shifted(sbuf, 32 if ky == 0 else 16, slice(side * CH_MID, (side + 1) * CH_MID))
                t = 3 * ky + kx
                d0 = d0 + dot(d, w[t * CH_BASE : (t + 1) * CH_BASE, :], NT)
                put_lines(g, AT.conv_down + t * CH_BASE * 3, dot(h0t[0:CH_BASE, :], d), 3)
        dbin[0:1, :CH_BASE] += rowsum(d0)
        dwin[:, :CH_BASE] += dot(xp[ph * ROWS : (ph + 1) * ROWS, :], d0.astype(BF16), TN)
    dwin[29:30, :] = dbin[0:1, :]
    even, odd = dwin[0:16, :], dwin[16:32, :]
    turned = pltpu.roll(odd[:, :LINE], LINE // 2, 1), pltpu.roll(odd[:, LINE:], LINE // 2, 1)
    g[pl.ds(0, 14, stride=3), :] = even[0:14, :LINE]
    g[pl.ds(1, 14, stride=3), :] = jnp.where(first_lanes(), even[:, LINE:], turned[0])[0:14]
    g[pl.ds(2, 14, stride=3), :] = jnp.where(first_lanes(), turned[0], turned[1])[0:14]
    leave = Leave(me, g, 0, keep, send, stage, out_sems, pad)
    leave.plane(0)
    leave.wait()


def kernel_params():
    return dict(
        compiler_params=pltpu.CompilerParams(vmem_limit_bytes=60 * 1024 * 1024),
        cost_estimate=pl.CostEstimate(flops=8 * 10**9, bytes_accessed=4 * 10**7, transcendentals=10**6),
    )


def back_call(kernel, name, lines, slots, args, smem, hbm, rest, outs, scratch, norms=True):
    sds = lambda *s: jax.ShapeDtypeStruct(*s)
    plane = sds((PLANE // 2, ROOM, LINE), BF16)
    rest = [sds((rest, LINE), F32)] if rest else []
    common = [
        vmem((lines + 8, LINE), F32),
        vmem((slots, 9 * CH_MID, CH_MID), BF16),
        vmem((PADDED, 3 * CH_MID), BF16),
        vmem((ROWS + 16, CH_MID), F32),
    ]
    if norms:
        common += [vmem((ROWS, CH_MID), F32), vmem((CH_MID, ROWS), BF16)]
    else:
        common += [vmem((256, ROWS), BF16)]
    common += [
        vmem((PLANE, ROOM, LINE), BF16),
        pltpu.SemaphoreType.DMA((2,)),
        pltpu.SemaphoreType.DMA((3,)),
    ]
    return pl.pallas_call(
        kernel,
        out_shape=[plane, plane, *rest, *(sds(*o) for o in outs)],
        in_specs=[SM] * smem + [VM] * (len(args) - smem - hbm) + [HB] * hbm,
        out_specs=[HB] * (2 + len(rest)) + [VM] * len(outs),
        scratch_shapes=common + scratch,
        name=name,
        **kernel_params(),
    )(*args)


ACT = ((ROWS, CH_MID), F32)
WIDE_ROW = ((8, EMB_DIM), F32)
DMA = pltpu.SemaphoreType.DMA


def back_top(args):
    scratch = [vmem((EMB_DIM, EMB_DIM), BF16), vmem((ROWS, 3 * CH_MID), BF16), vmem(*WIDE_ROW), DMA]
    lines = ALL_LINES - BASE_ONE
    return back_call(
        back_top_kernel, "back_top", lines, 2, args, 2, 4, PLANES[3] - BASE_ONE, [ACT, WIDE_ROW, ((8, LINE), F32)], scratch
    )


def back_second_half(args):
    outs = [ACT, WIDE_ROW, ((8, CH_MID), F32)]
    lines = PLANES[3] - BASE_TWO
    return back_call(back_second_half_kernel, "back_b", lines, 1, args, 1, 2, PLANES[2] - BASE_TWO, outs, [DMA])


def back_first_half(args):
    scratch = [vmem((EMB_DIM, EMB_DIM), BF16), DMA, DMA]
    lines = PLANES[2] - BASE_THREE
    return back_call(
        back_first_half_kernel, "back_c", lines, 1, args, 1, 3, PLANES[1] - BASE_THREE, [ACT, WIDE_ROW], scratch
    )


def back_low(args):
    scratch = [
        vmem((EMB_DIM, EMB_DIM), BF16),
        vmem(*WIDE_ROW),
        vmem((32, 2 * LINE), F32),
        vmem((8, 2 * LINE), F32),
        DMA,
        DMA,
    ]
    return back_call(back_low_kernel, "back_low", PLANES[1], 1, args, 2, 3, 0, [], scratch, False)


def karras(index):
    ramp_frac = index.astype(F32) / (DISCRETE - 1)
    low_root = SIGMA_LOW ** (1.0 / RHO_POWER)
    high_root = SIGMA_HIGH ** (1.0 / RHO_POWER)
    return (low_root + ramp_frac * (high_root - low_root)) ** RHO_POWER


def preconditioning_factors(sigma):
    variance_sum = sigma * sigma + SIGMA_DATA**2
    skip = SIGMA_DATA**2 / ((sigma - SIGMA_LOW) ** 2 + SIGMA_DATA**2)
    out = (sigma - SIGMA_LOW) * SIGMA_DATA * lax.rsqrt(variance_sum)
    return (skip, out, lax.rsqrt(variance_sum))


def noise_features(sigma):
    half_width = CH_BASE // 2
    frequency = jnp.exp(-math.log(10000.0) * jnp.arange(half_width, dtype=F32) / half_width)
    phases = 250.0 * jnp.log(sigma)[:, None] * frequency
    return jnp.pad(jnp.concatenate([jnp.cos(phases), jnp.sin(phases)], 1), ((0, 8 - MB_DEV), (0, 0)))


def pixels(images):
    lead = images.shape[0]
    split = images.reshape(lead, MB_DEV, HALF, 2, HALF, 2, 3)
    return split.transpose(0, 1, 2, 4, 3, 5, 6).reshape(lead, ROWS, 12)


def pixel_live(counts, valid_rows):
    row = lax.broadcasted_iota(jnp.int32, (ROWS, 12), 0)
    lane = lax.broadcasted_iota(jnp.int32, (ROWS, 12), 1)
    slot = row // PIX
    line = 2 * ((row // HALF) % HALF) + lane // 6
    top = jnp.where(slot == 0, valid_rows[0], valid_rows[1])
    return ((slot < counts[0]) & (line < top)).astype(F32)


def per_part(me, labels, lines, inputs, save, tables):
    _, x_in, phi, _ = inputs
    results = forward_call(save, me, labels, lines, x_in, phi, tables)
    return results[0], results[1:]


AXIS = "fsdp"
CORE, EAST, SOUTH, UP = 1, 2, 4, 8
CUT_ROWS = ROOM // 2


def swap(values, hop):
    return lax.ppermute(values, AXIS, [(i, i ^ hop) for i in range(SHARDS)])


def total_of(values, n):
    hop = 1
    while hop < n:
        values = values + lax.ppermute(values, AXIS, [(i, i ^ hop) for i in range(n)])
        hop *= 2
    return values


CUTS = (0, 880, 1760, ROOM)
TALL = SHARDS // PLANE


def gate(values, after):
    count = len(values)

    def body(*refs):
        pass

    return pl.pallas_call(
        body,
        out_shape=[jax.ShapeDtypeStruct(v.shape, v.dtype) for v in values],
        in_specs=[HB] * (count + len(after)),
        out_specs=[HB] * count,
        input_output_aliases={i: i for i in range(count)},
        name="gate",
    )(*values, *after)


def climb(values, way, far, first=0):
    planes = range(first, TALL - far) if way == 1 else range(TALL - 1 - first, far - 1, -1)
    pairs = [(q * PLANE + i, (q + way * far) * PLANE + i) for q in planes for i in range(PLANE)]
    return lax.ppermute(values, AXIS, pairs)


def column_window(slots, z):
    rows = []
    for p in range(TALL):
        value = slots[TALL - 1 + p]
        for q in range(1, TALL):
            value = jnp.where(z == q, slots[TALL - 1 - q + p], value)
        rows.append(value)
    return jnp.stack(rows)


def column_gather(own, z):
    below, above = [climb(own, 1, 1)], [climb(own, -1, 1)]
    for step in range(1, TALL - 1):
        below.append(climb(below[-1], 1, 1, step))
        above.append(climb(above[-1], -1, 1, step))
    return column_window([*below[::-1], own, *above], z), [below[0], above[0]], [below[-1], above[-1]]


def gather_lines(shard, z, early):
    ab, c = shard[: CUTS[2]], shard[CUTS[2] :]
    c_two = jnp.stack([c, swap(c, SOUTH)])
    c_four = jnp.concatenate([c_two, swap(c_two, EAST)])
    column, step, last = column_gather(ab, z)
    za, zb = column[:, : CUTS[1]], column[:, CUTS[1] :]
    done, ready = early(step)
    a_two, b_two = jnp.stack([za, swap(za, EAST)]), jnp.stack([zb, swap(zb, SOUTH)])
    a_far, b_far = swap(a_two, SOUTH), swap(b_two, EAST)
    (c_four,) = gate([c_four], [*last, *ready])
    c_all, _, _ = column_gather(c_four, z)
    pieces = [a_two, a_far, b_two, b_far, c_all]
    return done, pieces + [swap(v, CORE) for v in pieces]


def gather_moves():
    places = [(0, 1), (2, 3), (0, 2), (1, 3), (0, 2, 1, 3)]
    part = (0, 0, 1, 1, 2)
    moves = []
    for core in range(2):
        for n in range(5):
            row, end = CUTS[part[n]], CUTS[part[n] + 1]
            for lead, place in enumerate(places[n]):
                moves.append((core * 5 + n, lead, 2 * place + core, row, end - row))
    return moves


def gather_plain(shard):
    rows = shard.shape[0]
    lines = lax.all_gather(shard, AXIS, axis=0, tiled=True)
    if rows != ROOM:
        lines = jnp.pad(lines.reshape(SHARDS, SHARD, LINE), ((0, 0), (0, ROOM - SHARD), (0, 0)))
    lines = lines.reshape(TALL, PLANE, ROOM, LINE)
    return [lines], [(0, r, r, 0, ROOM) for r in range(PLANE)], (True,)


def digit_weights():
    return np.array([8.0 ** (k - 40) if k < 82 else 0.0 for k in range(LINE)], np.float32)[None]


def inverse_weights():
    weights = digit_weights()
    return np.where(weights > 0, 1.0 / np.where(weights > 0, weights, 1.0), 0.0).astype(np.float32)


def to_digits(values, inverse):
    size = jnp.abs(values) * inverse
    digit = jnp.floor(size) - 8.0 * jnp.floor(size * 0.125)
    digit = jnp.where(size < 2.0**27, digit, 0.0)
    return jnp.where(values < 0, -digit, digit)


def from_digits(rows):
    return jnp.sum(rows * digit_weights(), 1)


def low(v):
    return v.astype(BF16)


def wide(v):
    return v.astype(F32)


class PlaneSum:
    def __init__(self, keep, send):
        self.keep, self.got = keep, swap(send, CORE)
        self.a, self.b = slice(0, CUT_ROWS), slice(CUT_ROWS, ROOM)

    def quarter(self, i, rows):
        return wide(self.keep[i, rows]) + wide(self.got[i, rows])

    def first(self):
        a = low(jnp.stack([self.quarter(1, self.a), self.quarter(3, self.a)]))
        b = low(jnp.stack([self.quarter(2, self.b), self.quarter(3, self.b)]))
        return a, b

    def send_first(self, a, b):
        self.got_a, self.got_b = swap(a, EAST), swap(b, SOUTH)

    def last(self):
        return low(self.quarter(2, self.a) + wide(self.got_a[1])), low(self.quarter(1, self.b) + wide(self.got_b[1]))

    def send_last(self, a, b):
        self.end_a, self.end_b = swap(a, SOUTH), swap(b, EAST)

    def total(self):
        a = self.quarter(0, self.a) + wide(self.got_a[0]) + wide(self.end_a)
        b = self.quarter(0, self.b) + wide(self.got_b[0]) + wide(self.end_b)
        return jnp.concatenate([a, b])


def column_sums(parts, first, z):
    pick = lambda p: jnp.where(p == first, parts[0], parts[1])
    total = 0.0
    for way in (1, -1):
        run = None
        for far in range(TALL - 1, 0, -1):
            holders = [q for q in range(TALL) if q + way * far in (first, first + 1)]
            if not holders:
                continue
            value = pick(z + way * far)
            if run is not None:
                value = value + run
            pairs = [(q * PLANE + i, (q + way) * PLANE + i) for q in holders for i in range(PLANE)]
            run = wide(lax.ppermute(low(value), AXIS, pairs))
        total = total + run
    return total


def per_device(n, images, noise_draws, labels, step_index, valid_rows, counts, master, momentum, ema):
    direct = n == SHARDS
    index = lax.axis_index(AXIS)
    me = jnp.where(direct, lax.rem(index, PLANE), 0).astype(jnp.int32)[None]
    z = lax.div(index, PLANE)
    shards = [v.astype(BF16).reshape(-1, LINE) for v in (master, ema)]
    tables = tuple(jnp.asarray(v, BF16) for v in (group_table(), *spread_tables(), expand_table(), patch_table()))
    live = (jnp.arange(MB_DEV) < counts[0]).astype(jnp.int32)
    local_rows = jnp.sum(live * jnp.clip(valid_rows, 0, RES)).astype(F32)

    total = total_of(jnp.broadcast_to(local_rows, (8, LINE)), n)
    pixel_total = 3.0 * RES * total[0, 0]

    def early(after):
        clean, noise = gate([images, noise_draws], after) if after else (images, noise_draws)
        clean, noise = pixels(jnp.stack([clean, noise]))
        per_row = lambda v: jnp.repeat(v, PIX)[:, None]

        def inputs_of(sigma):
            noisy = clean + per_row(sigma) * noise
            skip, out_scale, in_scale = preconditioning_factors(sigma)
            x_in = jnp.pad((per_row(in_scale) * noisy).astype(BF16), ((0, 0), (0, LINE - 12)))
            return per_row(skip) * noisy, x_in, noise_features(sigma), per_row(out_scale)

        mask = pixel_live(counts, valid_rows)
        both = inputs_of(karras(step_index)), inputs_of(karras(step_index + 1))
        return (*both, mask), [v for part in both for v in part[:3]] + [mask, total]

    if direct:
        rooms = [jnp.pad(v, ((0, ROOM - SHARD), (0, 0))) for v in shards]
        target = gather_plain(rooms[1])
        (in_lo, in_hi, mask), pieces = gather_lines(rooms[0], z, early)
        online = (pieces, gather_moves(), (False,) * 4 + (True,) + (False,) * 4 + (True,))
    else:
        online, target = gather_plain(shards[0]), gather_plain(shards[1])
        in_lo, in_hi, mask = early(())[0]
    model_t, _ = per_part(jnp.zeros_like(me), labels, target, in_lo, False, tables)
    if direct:
        (x_in,) = gate([in_hi[1]], [model_t])
        in_hi = (in_hi[0], x_in, *in_hi[2:])
    model_o, saved = per_part(me, labels, online, in_hi, True, tables)
    phi = in_hi[2]
    (h0s, h1, u1, h2, qkv, mixed, h3, u2, h4, vec, mod, emb, pre, wz, xp) = saved[:15]
    s_time, s_emb1, s_emb2, s_down, s11, s12, s_attn, s21, s22 = saved[15:]
    gm = tables[0]
    inverse = jnp.asarray(inverse_weights())
    losses = (model_o, model_t, in_hi[0], in_lo[0], in_hi[3], in_lo[3], mask, inverse)
    keep3, send3, rest, dh, dse, pad = back_top(
        (me, pixel_total[None], *losses, wz, *tables[:5], vec, mod, emb, h4, u2, h3, qkv, mixed, h2, s22, s21, s_attn, s_emb2)
    )
    if direct:
        three = PlaneSum(keep3, send3)
    keep2, send2, rest, du, dm, extra = back_second_half((me, pad, dh, gm, vec, mod, u1, s12, rest))
    if direct:
        first3 = three.first()
        (du,) = gate([du], first3)
        three.send_first(*first3)
        two = PlaneSum(keep2, send2)
    keep1, send1, rest, dh, dse = back_first_half((me, pad, dh, du, dm, extra, dse, gm, vec, emb, h1, s11, s_emb1, rest))
    if direct:
        last3, first2 = three.last(), two.first()
        (dh,) = gate([dh], [*last3, *first2])
        three.send_last(*last3)
        two.send_first(*first2)
        one = PlaneSum(keep1, send1)
    keep0, send0 = back_low((me, labels, pad, dh, dse, emb, pre, phi, h0s, xp, s_down, s_time, rest))
    if direct:
        zero = PlaneSum(keep0, send0)
        one.send_first(*one.first())
        two.send_last(*two.last())
        zero.send_first(*zero.first())
        top = [two.total(), three.total()]
        high = column_sums(top, 2, z)
        one.send_last(*one.last())
        zero.send_last(*zero.last())
        bottom = [zero.total(), one.total()]
        reduced = column_sums(bottom, 0, z) + high
        own = jnp.where(z < 2, jnp.where(z == 0, bottom[0], bottom[1]), jnp.where(z == 2, top[0], top[1]))
        reduced = reduced + own
        small = from_digits(reduced[SHARD : SHARD + 4])
        reduced = reduced[:SHARD].reshape(-1)
    else:
        small = from_digits(total_of(pad, n)[:4])
        both = [jnp.stack([wide(k), wide(s)], 1) for k, s in ((keep0, send0), (keep1, send1), (keep2, send2), (keep3, send3))]
        lines = jnp.stack(both).reshape(SHARDS, ROOM, LINE)[:, :SHARD].reshape(n, -1)
        reduced = lax.psum_scatter(lines, AXIS, scatter_dimension=0, tiled=True).reshape(-1)
    new_momentum = MOMENTUM * momentum + reduced
    new_master = master - LEARN_RATE * (reduced + MOMENTUM * new_momentum)
    new_ema = EMA_DECAY * ema + (1.0 - EMA_DECAY) * new_master
    return (small[0] / pixel_total, new_momentum, new_master, new_ema, small[1:])


def solution(mesh):
    n = mesh.shape[AXIS]

    def step(*args):
        return per_device(n, *args)

    return jax.shard_map(
        step,
        mesh=mesh,
        in_specs=(P(AXIS, None, None, None),) * 2 + (P(AXIS),) * 7,
        out_specs=(P(), P(AXIS), P(AXIS), P(AXIS), P()),
        check_vma=False,
    )
```

```python
import math

import jax
import jax.numpy as jnp
import numpy as np
from jax import lax
from jax.experimental import pallas as pl
from jax.experimental.pallas import tpu as pltpu
from jax.sharding import PartitionSpec as P

CH_BASE = 192
CH_MID = 384
EMB_DIM = 768
HEADS = 6
HEAD_DIM = 64
CLASSES = 1000
GROUPS = 32
RES = 32
MB_DEV = 2
DISCRETE = 40

EPSILON = 1e-05
SIGMA_DATA = 0.5
SIGMA_LOW = 0.002
SIGMA_HIGH = 80.0
RHO_POWER = 7.0
MOMENTUM = 0.9
EMA_DECAY = 0.9
LEARN_RATE = 2000.0

F32 = jnp.float32
BF16 = jnp.bfloat16
LINE = 128
HALF = RES // 2
PIX = HALF * HALF
ROWS = MB_DEV * PIX
GROUP_SIZE = PIX * (CH_MID // GROUPS)
CHUNK = 128
PADDED = 16 + MB_DEV * (PIX + 16)
NN = (((1,), (0,)), ((), ()))
NT = (((1,), (1,)), ((), ()))
TN = (((0,), (0,)), ((), ()))


class Place:
    pass


class Cut:
    def __init__(self):
        self.offset = 0

    def take(self, *shape):
        at = self.offset
        self.offset += math.prod(shape)
        return at // LINE


def block_place(cut):
    at = Place()
    at.gains = cut.take(4, CH_MID)
    at.conv_one = cut.take(9 * CH_MID, CH_MID)
    at.bias_one = cut.take(CH_MID)
    at.embed = cut.take(EMB_DIM, 2 * CH_MID)
    at.embed_bias = cut.take(2 * CH_MID)
    at.conv_two = cut.take(9 * CH_MID, CH_MID)
    at.bias_two = cut.take(CH_MID)
    return at


def places():
    cut, at = Cut(), Place()
    at.conv_in = cut.take(27, CH_BASE)
    at.bias_in = cut.take(CH_BASE)
    at.conv_down = cut.take(9 * CH_BASE, CH_MID)
    at.bias_down = cut.take(CH_MID)
    at.time_one = cut.take(CH_BASE, EMB_DIM)
    at.time_bias_one = cut.take(EMB_DIM)
    at.time_two = cut.take(EMB_DIM, EMB_DIM)
    at.time_bias_two = cut.take(EMB_DIM)
    at.class_table = cut.take(CLASSES, EMB_DIM)
    at.first = block_place(cut)
    at.second = block_place(cut)
    at.attn_gains = cut.take(2, CH_MID)
    at.attn_qkv = cut.take(CH_MID, 3 * CH_MID)
    at.attn_out = cut.take(CH_MID, CH_MID)
    at.attn_bias = cut.take(CH_MID)
    at.final_gains = cut.take(2, CH_MID)
    at.conv_out = cut.take(9 * CH_MID, 3)
    at.bias_out = cut.take(3)
    return at


AT = places()
TAIL = AT.conv_out
SHARDS, PLANE = 32, 8
SHARD = 2264
ROOM = 2272
ALL_LINES = SHARDS * SHARD
PLANES = [p * PLANE * SHARD for p in range(SHARDS // PLANE)]
BASE_ONE = AT.second.gains // 16 * 16
BASE_TWO = AT.first.conv_two // 16 * 16
BASE_THREE = AT.first.gains // 16 * 16

V_DOWN, V_G1, V_B11, V_B12, V_AG, V_AB, V_FG, V_G2, V_B21, V_B22 = 0, 1, 5, 6, 7, 9, 10, 12, 16, 17
VEC_ROWS = 24


def group_table():
    at = np.arange(CH_MID) // (CH_MID // GROUPS)
    return (at[:, None] == at[None, :]).astype(np.float32)


TAPS = 16


def spread_tables():
    select = np.zeros((LINE, LINE), np.float32)
    gather = np.zeros((LINE, LINE), np.float32)
    tile = np.zeros((LINE, LINE), np.float32)
    for ky in range(3):
        for kx in range(3):
            for a in range(2):
                for b in range(2):
                    dy, dx = (a + ky - 1) // 2, (b + kx - 1) // 2
                    shift = (dy + 1) * 3 + dx + 1
                    for c in range(3):
                        out = (a * 2 + b) * 3 + c
                        select[c * TAPS + ky * 3 + kx, shift * 12 + out] = 1.0
                        gather[out::12, out][:9] = 1.0
                        tile[c, out] = 1.0
    return select, gather, tile


def patch_table():
    pick = np.zeros((4, LINE, 32), np.float32)
    for a in range(2):
        for b in range(2):
            for ky in range(3):
                for kx in range(3):
                    (dy, ya), (dx, xb) = divmod(a + ky - 1, 2), divmod(b + kx - 1, 2)
                    shift = (dy + 1) * 3 + dx + 1
                    for c in range(3):
                        k = (ky * 3 + kx) * 3 + c
                        pick[a * 2 + b, shift * 12 + (ya * 2 + xb) * 3 + c, k // 2 + 16 * (k % 2)] = 1.0
    return pick


def expand_table():
    return (np.arange(3 * CH_MID)[None, :] // 3 == np.arange(CH_MID)[:, None]).astype(np.float32)


def colour(c):
    lane = lax.broadcasted_iota(jnp.int32, (1, 3 * CH_MID), 1)
    return lax.rem(lane, 3) == c


def first_lanes():
    return lax.broadcasted_iota(jnp.int32, (1, LINE), 1) < LINE // 2


def split3(v):
    hi = v.astype(BF16)
    rest = v - hi.astype(F32)
    mid = rest.astype(BF16)
    low = (rest - mid.astype(F32)).astype(BF16)
    return hi, mid, low


def dot(a, b, dims=NN):
    return lax.dot_general(a, b, dims, preferred_element_type=F32)


def dot3(a, b, dims=NN):
    rows = a.shape[0]
    hi, mid, low = split3(a)
    if rows % 16:
        out = dot(jnp.concatenate([p.astype(F32) for p in (hi, mid, low)], 0).astype(BF16), b, dims)
    else:
        out = dot(jnp.concatenate([hi, mid, low], 0), b, dims)
    return out[:rows] + out[rows : 2 * rows] + out[2 * rows :]


def outer(a, b):
    pa, pb = split3(a), split3(b)
    pairs = [(0, 0), (0, 1), (1, 0), (1, 1), (0, 2), (2, 0)]
    left = jnp.concatenate([pa[i].astype(F32) for i, _ in pairs], 0).astype(BF16)
    right = jnp.concatenate([pb[j].astype(F32) for _, j in pairs], 0).astype(BF16)
    return dot(left, right, TN)


def sigmoid(z):
    return 1.0 / (1.0 + jnp.exp(-z))


def silu(z):
    return z * sigmoid(z)


def silu_slope(z):
    s = sigmoid(z)
    return s * (1.0 + z * (1.0 - s))


def colsum(ref, base, count=PIX):
    def body(c, acc):
        return acc + jnp.sum(ref[pl.ds(pl.multiple_of(base + c * CHUNK, 8), CHUNK), :], 0, keepdims=True)

    return lax.fori_loop(0, count // CHUNK, body, jnp.zeros((1, ref.shape[1]), F32))


def eight(v):
    return jnp.broadcast_to(v, (8, v.shape[1]))


def group_means(rows, gm_ref):
    rows = rows + [jnp.zeros((8 - len(rows), CH_MID), F32)]
    means = dot3(jnp.concatenate(rows, 0), gm_ref[...]) * (1.0 / GROUP_SIZE)
    return [means[n : n + 1] for n in range(len(rows) - 1)]


def all_stats(x_ref, gm_ref):
    def total(c, acc):
        at = lambda img: pl.ds(pl.multiple_of(img * PIX + c * CHUNK, 8), CHUNK)
        return tuple(acc[img] + jnp.sum(x_ref[at(img), :], 0, keepdims=True) for img in range(MB_DEV))

    zero = (jnp.zeros((1, CH_MID), F32),) * MB_DEV
    means = group_means(list(lax.fori_loop(0, PIX // CHUNK, total, zero, unroll=2)), gm_ref)

    def square(c, acc):
        out = []
        for img in range(MB_DEV):
            gap = x_ref[pl.ds(pl.multiple_of(img * PIX + c * CHUNK, 8), CHUNK), :] - means[img]
            out.append(acc[img] + jnp.sum(gap * gap, 0, keepdims=True))
        return tuple(out)

    spreads = group_means(list(lax.fori_loop(0, PIX // CHUNK, square, zero, unroll=2)), gm_ref)
    return [(mean, lax.rsqrt(spread + EPSILON)) for mean, spread in zip(means, spreads)]


def norm_to(pbuf, x_ref, stats, scales, act):
    for img in range(MB_DEV):
        (mean, rstd), (k, o) = stats[img], scales[img]

        def body(c, carry):
            r = pl.multiple_of(img * PIX + c * CHUNK, 8)
            z = (x_ref[pl.ds(r, CHUNK), :] - mean) * rstd * k + o
            pbuf[pl.ds(r + 8, CHUNK), :] = silu(z) if act else z
            return carry

        lax.fori_loop(0, PIX // CHUNK, body, 0, unroll=2)


def norm_back(x_ref, d_ref, stats, scales, act, gm_ref, emit):
    def one(c, carry):
        out = []
        for img in range(MB_DEV):
            (mean, rstd), (k, o) = stats[img], scales[img]
            r = pl.multiple_of(img * PIX + c * CHUNK, 8)
            xhat = (x_ref[pl.ds(r, CHUNK), :] - mean) * rstd
            dz = d_ref[pl.ds(r, CHUNK), :]
            if act:
                dz = dz * silu_slope(xhat * k + o)
                d_ref[pl.ds(r, CHUNK), :] = dz
            out.append(carry[2 * img] + jnp.sum(dz, 0, keepdims=True))
            out.append(carry[2 * img + 1] + jnp.sum(dz * xhat, 0, keepdims=True))
        return tuple(out)

    sums = lax.fori_loop(0, PIX // CHUNK, one, (jnp.zeros((1, CH_MID), F32),) * (2 * MB_DEV), unroll=2)
    means = group_means([v * scales[n // 2][0] for n, v in enumerate(sums)], gm_ref)
    for img in range(MB_DEV):
        (mean, rstd), (k, o) = stats[img], scales[img]
        m1, m2 = means[2 * img], means[2 * img + 1]

        def two(c, carry):
            r = pl.multiple_of(img * PIX + c * CHUNK, 8)
            xhat = (x_ref[pl.ds(r, CHUNK), :] - mean) * rstd
            emit(r, rstd * (d_ref[pl.ds(r, CHUNK), :] * k - m1 - xhat * m2))
            return carry

        lax.fori_loop(0, PIX // CHUNK, two, 0, unroll=2)
    return [(sums[2 * img], sums[2 * img + 1]) for img in range(MB_DEV)]


def clear_pads(sbuf):
    for r in range(0, PADDED, PIX + 16):
        sbuf[r : r + 16, :] = jnp.zeros((16, sbuf.shape[1]), BF16)


def shift_to(sbuf, pbuf):
    column = lax.rem(lax.broadcasted_iota(jnp.int32, (CHUNK, CH_MID), 0), HALF)
    for r in range(0, ROWS, CHUNK):
        for k in range(3):
            v = pbuf[r + 7 + k : r + 7 + k + CHUNK, :]
            if k == 0:
                v = jnp.where(column == 0, 0.0, v)
            if k == 2:
                v = jnp.where(column == HALF - 1, 0.0, v)
            start = r + 16 * (r // PIX + 1)
            sbuf[start : start + CHUNK, k * CH_MID : (k + 1) * CH_MID] = v.astype(BF16)


def shifted(sbuf, row, cols=slice(None)):
    first = sbuf[pl.ds(pl.multiple_of(row, 16), PIX), cols]
    second = sbuf[pl.ds(pl.multiple_of(row + PIX + 16, 16), PIX), cols]
    return jnp.concatenate([first, second], 0)


def conv_forward(sbuf, w_ref, out_ref):
    depth = 3 * CH_MID

    def body(ky, carry):
        w = w_ref[pl.ds(pl.multiple_of(ky * depth, depth), depth), :]
        out_ref[...] += dot(shifted(sbuf, ky * 16), w)
        return carry

    lax.fori_loop(0, 3, body, 0, unroll=3)


def put_lines(g_ref, at, value, step, more=None):
    n = value.shape[0]
    low = at // 8 * 8
    start = low if more is None else pl.multiple_of(low + more, 8)
    view = g_ref.at[pl.ds(start, min(n * step + 8, g_ref.shape[0] - low)), :] if more is None else g_ref.at[pl.ds(start, n * step + 8), :]
    for j in range(step):
        view[pl.ds(at - low + j, n, stride=step), :] = value[:, j * LINE : (j + 1) * LINE]


def put_row(g_ref, at, row):
    for j in range(row.shape[1] // LINE):
        g_ref[pl.ds(at + j, 1), :] = row[:, j * LINE : (j + 1) * LINE]


def conv_back(sbuf, at_ref, w_ref, dx_ref, g_ref, at):
    dx_ref[...] = jnp.zeros_like(dx_ref)
    depth = 3 * CH_MID

    def body(s, carry):
        d = shifted(sbuf, s * 16)
        dw = dot(at_ref[...], d)
        dx = dx_ref[...]
        for k in range(3):
            part = slice(k * CH_MID, (k + 1) * CH_MID)
            tap = (2 - s) * depth + (2 - k) * CH_MID
            dx = dx + dot(d[:, part], w_ref[pl.ds(pl.multiple_of(tap, CH_MID), CH_MID), :], NT)
            put_lines(g_ref, at, dw[:, part], 3, 3 * tap)
        dx_ref[...] = dx
        return carry

    lax.fori_loop(0, 3, body, 0, unroll=3)


def transpose_to(at_ref, pbuf):
    for c in range(ROWS // LINE):
        at_ref[:, c * LINE : (c + 1) * LINE] = pbuf[8 + c * LINE : 8 + (c + 1) * LINE, :].T.astype(BF16)


class Lines:
    def __init__(self, held, wide):
        self.held, self.wide = held, wide

    def take(self, span):
        l0, l1 = span
        first = l0 // SHARD
        self.low = first * SHARD + (l0 - first * SHARD) // 16 * 16
        for s in range(first, (l1 - 1) // SHARD + 1):
            start = max(l0 - s * SHARD, 0) // 16 * 16
            count = -(-min(l1 - s * SHARD, SHARD) // 16) * 16 - start
            to = s * SHARD + start - self.low
            block = self.held.at[s // PLANE, s % PLANE]
            whole, rest = divmod(count, 256)

            def body(c, carry):
                self.wide[pl.ds(pl.multiple_of(to + c * 256, 8), 256), :] = block[
                    pl.ds(pl.multiple_of(start + c * 256, 16), 256), :
                ].astype(F32)
                return carry

            lax.fori_loop(0, whole, body, 0, unroll=4)
            if rest:
                done = whole * 256
                self.wide[to + done : to + count, :] = block[start + done : start + count, :].astype(F32)

    def line(self, at, scratch):
        shard = lax.div(at, SHARD)
        row = at - shard * SHARD
        low = pl.multiple_of(lax.div(row, 16) * 16, 16)
        scratch[...] = self.held[lax.div(shard, PLANE), lax.rem(shard, PLANE), pl.ds(low, 16), :].astype(F32)
        return scratch[pl.ds(row - low, 1), :]

    def matrix(self, w_ref, at, rows, step):
        block = 128 if rows % 192 else 192
        base = at - self.low
        low = base // 8 * 8

        def body(c, carry):
            r = pl.multiple_of(c * block, block)
            view = self.wide.at[pl.ds(pl.multiple_of(low + r * step, 8), block * step + 8), :]
            for j in range(step):
                v = view[pl.ds(base - low + j, block, stride=step), :]
                w_ref[pl.ds(r, block), j * LINE : (j + 1) * LINE] = v.astype(BF16)
            return carry

        lax.fori_loop(0, rows // block, body, 0, unroll=6 if (rows // block) % 6 == 0 else 3 if (rows // block) % 3 == 0 else 2)

    def row(self, at, step):
        base = at - self.low
        return jnp.concatenate([self.wide[pl.ds(base + j, 1), :] for j in range(step)], 1)


def attention_pair(qkv_ref, img, pair):
    rows = pl.ds(pl.multiple_of(img * PIX, PIX), PIX)
    return [qkv_ref[rows, part * CH_MID + pair * LINE : part * CH_MID + (pair + 1) * LINE] for part in range(3)]


def lane_half():
    return lax.broadcasted_iota(jnp.int32, (1, LINE), 1) < HEAD_DIM


def keep_half(v, half, side):
    mine = half if side == 0 else jnp.logical_not(half)
    return jnp.where(mine, v.astype(F32), 0.0).astype(BF16)


SPAN_TIME = (AT.time_one, AT.class_table)
SPAN_EMB1 = (AT.first.embed, AT.first.conv_two)
SPAN_EMB2 = (AT.second.embed, AT.second.conv_two)
SPAN_DOWN = (AT.conv_in, AT.time_one)
SPAN_ONE1 = (AT.first.gains, AT.first.embed)
SPAN_TWO1 = (AT.first.conv_two, AT.second.gains)
SPAN_ATTN = (AT.attn_gains, ALL_LINES)
SPAN_ONE2 = (AT.second.gains, AT.second.embed)
SPAN_TWO2 = (AT.second.conv_two, AT.attn_gains)


def block_scales(vec, row, mod_ref=None, mod_row=0):
    gain, shift = vec[row : row + 1, :], vec[row + 1 : row + 2, :]
    if mod_ref is None:
        return [(gain, shift)] * MB_DEV
    out = []
    for img in range(MB_DEV):
        scale = 1.0 + mod_ref[mod_row + img : mod_row + img + 1, :CH_MID]
        out.append((gain * scale, shift * scale + mod_ref[mod_row + img : mod_row + img + 1, CH_MID:]))
    return out


def upsample_masks(shift):
    dy, dx = shift // 3 - 1, shift % 3 - 1
    p = lax.broadcasted_iota(jnp.int32, (ROWS, 1), 0)
    i, j = lax.rem(lax.div(p, HALF), HALF), lax.rem(p, HALF)
    inside = (i + dy >= 0) & (i + dy < HALF) & (j + dx >= 0) & (j + dx < HALF)
    lane = lax.broadcasted_iota(jnp.int32, (1, LINE), 1)
    return inside & (lane >= shift * 12) & (lane < shift * 12 + 12), dy * HALF + dx


def forward_kernel(save, moves, flip, *refs):
    me, labels, x_in, phi, gm, sel, gat, tile, expand, pick = refs[:10]
    sources = max(move[0] for move in moves) + 1
    pieces, refs = refs[10 : 10 + sources], refs[10 + sources :]
    f_out = refs[0]
    (h0s, h1, u1, h2, qkv, mixed, h3, u2, h4, vec, mod, emb, pre, wz, xp) = refs[1:16]
    if save:
        sw_time, sw_emb1, sw_emb2, sw_down, sw_11, sw_12, sw_attn, sw_21, sw_22 = refs[16:25]
    held, wide, w_ref, w_sq, sbuf, pbuf, h0p, table, w_in, b_out, sems, save_sem = refs[25 if save else 16 :]
    src = Lines(held, wide)
    arriving = []
    for plane in range(TALL):
        copies = []
        for n, lead, r, row, rows in moves:
            target = held.at[plane, r ^ me[0], pl.ds(row, rows), :]
            source = pieces[n].at[plane, lead] if flip[n] else pieces[n].at[lead, plane]
            copies.append(pltpu.make_async_copy(source, target, sems.at[plane]))
        arriving.append(copies)

    def arrive(plane):
        for copy in arriving[plane]:
            copy.wait()

    for plane in range(TALL):
        for copy in arriving[plane]:
            copy.start()
    pending = []

    def keep(source, target):
        if save:
            cp = pltpu.make_async_copy(source, target, save_sem)
            cp.start()
            pending.append(cp)

    def free():
        while pending:
            pending.pop().wait()

    clear_pads(sbuf)
    pbuf[0:8, :] = jnp.zeros((8, CH_MID), F32)
    pbuf[ROWS + 8 : ROWS + 16, :] = jnp.zeros((8, CH_MID), F32)
    arrive(0)
    src.take(SPAN_TIME)
    src.matrix(w_sq.at[0], AT.time_one, CH_BASE, 6)
    src.matrix(w_sq.at[1], AT.time_two, EMB_DIM, 6)
    pre[...] = dot3(phi[...], w_sq[0, :CH_BASE, :]) + src.row(AT.time_bias_one, 6)
    emb[...] = dot3(silu(pre[...]), w_sq[1]) + src.row(AT.time_bias_two, 6)
    for n in range(MB_DEV):
        for j in range(6):
            cols = slice(j * LINE, (j + 1) * LINE)
            emb[n : n + 1, cols] += src.line(AT.class_table + labels[n] * 6 + j, table)
    keep(w_sq.at[1], sw_time if save else None)
    se = silu(emb[...])
    arrive(1)
    src.take(SPAN_EMB1)
    src.matrix(w_sq.at[0], AT.first.embed, EMB_DIM, 6)
    m1 = dot3(se, w_sq[0]) + src.row(AT.first.embed_bias, 6)
    free()
    keep(w_sq.at[0], sw_emb1 if save else None)
    mod[0:2, :] = m1[0:2]
    mod[4:8, :] = jnp.zeros((4, EMB_DIM), F32)

    src.take(SPAN_DOWN)
    trio = [wide[pl.ds(j, 16, stride=3), :] for j in range(3)]
    turned = [pltpu.roll(v, LINE // 2, 1) for v in trio[1:]]
    w_in[0:16, 0:LINE] = trio[0]
    w_in[0:16, LINE : 2 * LINE] = trio[1]
    w_in[16:32, 0:LINE] = jnp.where(first_lanes(), turned[0], turned[1])
    w_in[16:32, LINE : 2 * LINE] = turned[1]
    w_low = w_in[...].astype(BF16)
    spread = dot(x_in[...], gat[...], NT)
    around = jnp.zeros((ROWS, LINE), F32)
    for shift in range(9):
        inside, by = upsample_masks(shift)
        around = around + jnp.where(inside, spread if by == 0 else pltpu.roll(spread, (-by) % ROWS, 0), 0.0)
    around = around.astype(BF16)
    one = (lax.broadcasted_iota(jnp.int32, (1, 32), 1) == 29).astype(F32)
    for ph in range(4):
        patch = (dot(around, pick[ph]) + one).astype(BF16)
        xp[ph * ROWS : (ph + 1) * ROWS, :] = patch
        h0s[ph * ROWS : (ph + 1) * ROWS, :] = dot(patch, w_low).astype(BF16)
    for j in range(3):
        vec[V_DOWN : V_DOWN + 1, j * LINE : (j + 1) * LINE] = src.row(AT.bias_down + j, 1)
    src.matrix(w_ref, AT.conv_down, 9 * CH_BASE, 3)
    free()
    keep(w_ref.at[pl.ds(0, 9 * CH_BASE), :], sw_down if save else None)
    h1[...] = jnp.broadcast_to(vec[V_DOWN : V_DOWN + 1, :], (ROWS, CH_MID))
    p = lax.broadcasted_iota(jnp.int32, (ROWS, 1), 0)
    has_left, has_up = lax.rem(p, HALF) > 0, lax.rem(lax.div(p, HALF), HALF) > 0
    for ph in range(4):
        h0p[0:32, :] = jnp.zeros((32, h0p.shape[1]), F32)
        h0p[32 : 32 + ROWS, :] = h0s[ph * ROWS : (ph + 1) * ROWS, :].astype(F32)
        for ky in ((0, 2) if ph // 2 else (1,)):
            for kx in ((0, 2) if ph % 2 else (1,)):
                back = (16 if ky == 0 else 0) + (1 if kx == 0 else 0)
                v = h0p[32 - back : 32 - back + ROWS, :]
                if ky == 0:
                    v = jnp.where(has_up, v, 0.0)
                if kx == 0:
                    v = jnp.where(has_left, v, 0.0)
                t = 3 * ky + kx
                h1[...] += dot(v[:, :CH_BASE].astype(BF16), w_ref[t * CH_BASE : (t + 1) * CH_BASE, :])

    def vectors(row, at, count):
        for n in range(count):
            for j in range(3):
                vec[row + n : row + n + 1, j * LINE : (j + 1) * LINE] = src.row(at + 3 * n + j, 1)

    def half_block(x_ref, scales, bias_row, add_ref, out_ref, at, target):
        src.matrix(w_ref, at, 9 * CH_MID, 3)
        keep(w_ref, target)
        stats = all_stats(x_ref, gm)
        norm_to(pbuf, x_ref, stats, scales, True)
        shift_to(sbuf, pbuf)
        bias = jnp.broadcast_to(vec[bias_row : bias_row + 1, :], (ROWS, CH_MID))
        out_ref[...] = bias if add_ref is None else add_ref[...] + bias
        conv_forward(sbuf, w_ref, out_ref)

    def block(h_in, u, h_out, prefix, g_row, b1_row, b2_row, mod_row, spans, targets):
        src.take(spans[0])
        free()
        vectors(g_row, prefix.gains, 4)
        vectors(b1_row, prefix.bias_one, 1)
        half_block(h_in, block_scales(vec, g_row), b1_row, None, u, prefix.conv_one, targets[0])
        src.take(spans[1])
        free()
        vectors(b2_row, prefix.bias_two, 1)
        half_block(u, block_scales(vec, g_row + 2, mod, mod_row), b2_row, h_in, h_out, prefix.conv_two, targets[1])

    saved = (sw_11, sw_12, sw_21, sw_22) if save else (None,) * 4
    arrive(2)
    block(h1, u1, h2, AT.first, V_G1, V_B11, V_B12, 0, (SPAN_ONE1, SPAN_TWO1), saved[:2])

    arrive(3)
    src.take(SPAN_ATTN)
    free()
    vectors(V_AG, AT.attn_gains, 2)
    vectors(V_AB, AT.attn_bias, 1)
    vectors(V_FG, AT.final_gains, 2)
    base = AT.conv_out - src.low
    tap_row = lax.broadcasted_iota(jnp.int32, (TAPS, 1), 0) < 9
    taps = [jnp.where(tap_row, wide[pl.ds(base + j, TAPS, stride=9), :], 0.0) for j in range(9)]
    taps = jnp.concatenate(taps, 1)
    rows_out = jnp.concatenate([jnp.where(colour(c), taps, 0.0) for c in range(3)], 0).astype(BF16)
    wz[...] = jnp.zeros_like(wz)
    wz[0 : 3 * TAPS, :] = dot(rows_out, expand[...], NT).astype(BF16)
    last = AT.bias_out - src.low
    b_out[...] = dot(eight(wide[last : last + 1, :]).astype(BF16), tile[...])
    for part in range(3):
        base = AT.attn_qkv - src.low
        for j in range(3):
            v = wide[pl.ds(base + part * 3 + j, CH_MID, stride=9), :]
            w_ref[part * CH_MID : (part + 1) * CH_MID, j * LINE : (j + 1) * LINE] = v.astype(BF16)
    src.matrix(w_ref.at[pl.ds(3 * CH_MID, CH_MID), :], AT.attn_out, CH_MID, 3)
    keep(w_ref.at[pl.ds(0, 4 * CH_MID), :], sw_attn if save else None)
    stats = all_stats(h2, gm)
    norm_to(pbuf, h2, stats, block_scales(vec, V_AG), False)
    n_low = pbuf[8 : 8 + ROWS, :].astype(BF16)
    for part in range(3):
        v = dot(n_low, w_ref[part * CH_MID : (part + 1) * CH_MID, :])
        qkv[:, part * CH_MID : (part + 1) * CH_MID] = v.astype(BF16)
    half = lane_half()

    def heads(img, carry):
        for pair in range(HEADS // 2):
            q, k, v = attention_pair(qkv, img, pair)
            outs = []
            for side in range(2):
                s = dot(keep_half(q, half, side), k, NT) * HEAD_DIM ** (-0.5)
                e = jnp.exp(s - jnp.max(s, 1, keepdims=True))
                prob = (e / jnp.sum(e, 1, keepdims=True)).astype(BF16)
                outs.append(dot(prob, v))
            mixed[pl.ds(pl.multiple_of(img * PIX, PIX), PIX), pair * LINE : (pair + 1) * LINE] = jnp.where(
                half, outs[0], outs[1]
            ).astype(BF16)
        return carry

    lax.fori_loop(0, MB_DEV, heads, 0, unroll=2)
    h3[...] = h2[...] + dot(mixed[...], w_ref[3 * CH_MID : 4 * CH_MID, :]) + vec[V_AB : V_AB + 1, :]

    src.take(SPAN_EMB2)
    src.matrix(w_sq.at[1], AT.second.embed, EMB_DIM, 6)
    m2 = dot3(silu(emb[...]), w_sq[1]) + src.row(AT.second.embed_bias, 6)
    mod[2:4, :] = m2[0:2]
    free()
    keep(w_sq.at[1], sw_emb2 if save else None)
    block(h3, u2, h4, AT.second, V_G2, V_B21, V_B22, 2, (SPAN_ONE2, SPAN_TWO2), saved[2:])

    stats = all_stats(h4, gm)
    norm_to(pbuf, h4, stats, block_scales(vec, V_FG), True)
    z = dot(pbuf[8 : 8 + ROWS, :].astype(BF16), wz[...], NT)
    t_all = dot3(z, sel[...])
    u_all = jnp.zeros((ROWS, LINE), F32)
    for shift in range(9):
        inside, by = upsample_masks(shift)
        moved = t_all if by == 0 else pltpu.roll(t_all, (-by) % ROWS, 0)
        u_all = u_all + jnp.where(inside, moved, 0.0)
    f_out[...] = dot3(u_all, gat[...]) + b_out[0:1, :]
    free()


def vmem(*shape_dtype):
    return pltpu.VMEM(*shape_dtype)


VM = pl.BlockSpec(memory_space=pltpu.VMEM)
HB = pl.BlockSpec(memory_space=pl.ANY)
SM = pl.BlockSpec(memory_space=pltpu.SMEM)


def state_shapes():
    act = ((ROWS, CH_MID), F32)
    return [
        ((4 * ROWS, 256), BF16),
        act, act, act,
        ((ROWS, 3 * CH_MID), BF16),
        ((ROWS, CH_MID), BF16),
        act, act, act,
        ((VEC_ROWS, CH_MID), F32),
        ((8, EMB_DIM), F32),
        ((8, EMB_DIM), F32),
        ((8, EMB_DIM), F32),
        ((LINE, CH_MID), BF16),
        ((4 * ROWS, 32), BF16),
    ]


def weight_shapes():
    sq = ((EMB_DIM, EMB_DIM), BF16)
    conv = ((9 * CH_MID, CH_MID), BF16)
    return [sq, sq, sq, ((9 * CH_BASE, CH_MID), BF16), conv, conv, ((4 * CH_MID, CH_MID), BF16), conv, conv]


def forward_call(save, me, labels, lines, x_in, phi, tables):
    pieces, moves, flip = lines
    sds = lambda s: jax.ShapeDtypeStruct(*s)
    outs = [sds(((ROWS, LINE), F32))]
    out_specs = [VM]
    state = state_shapes()
    scratch = []
    if save:
        outs += [sds(s) for s in state] + [sds(s) for s in weight_shapes()]
        out_specs += [VM] * len(state) + [HB] * len(weight_shapes())
    else:
        scratch += [vmem(*s) for s in state]
    scratch += [
        vmem((SHARDS // PLANE, PLANE, ROOM, LINE), BF16),
        vmem((10432, LINE), F32),
        vmem((9 * CH_MID, CH_MID), BF16),
        vmem((2, EMB_DIM, EMB_DIM), BF16),
        vmem((PADDED, 3 * CH_MID), BF16),
        vmem((ROWS + 16, CH_MID), F32),
        vmem((ROWS + 48, 256), F32),
        vmem((16, LINE), F32),
        vmem((32, 2 * LINE), F32),
        vmem((8, LINE), F32),
        pltpu.SemaphoreType.DMA((SHARDS // PLANE,)),
        pltpu.SemaphoreType.DMA,
    ]

    def body(*refs):
        forward_kernel(save, moves, flip, *refs)

    return pl.pallas_call(
        body,
        out_shape=outs,
        in_specs=[SM] * 2 + [VM] * 8 + [HB] * len(pieces),
        out_specs=out_specs,
        scratch_shapes=scratch,
        name="forward_save" if save else "forward_plain",
        **kernel_params(),
    )(me, labels, x_in, phi, *tables, *pieces)


def column_sum(pbuf):
    def body(c, acc):
        return acc + jnp.sum(pbuf[pl.ds(pl.multiple_of(c * CHUNK + 8, 8), CHUNK), :], 0, keepdims=True)

    return lax.fori_loop(0, ROWS // CHUNK, body, jnp.zeros((1, CH_MID), F32))


def refill(pbuf, source):
    for c in range(0, ROWS, CHUNK):
        pbuf[8 + c : 8 + c + CHUNK, :] = source[c : c + CHUNK, :]


def block_back_two(dh, u_ref, at, base, rows, vec, mod, mod_row, weights, tools, g, dm):
    g_row, b1_row, b2_row = rows
    sbuf, pbuf, dx, at_ref, gm = tools
    put_row(g, at.bias_two - base, colsum(dh, 0, ROWS))
    u_stats = all_stats(u_ref, gm)
    scales = block_scales(vec, g_row + 2, mod, mod_row)
    norm_to(pbuf, u_ref, u_stats, scales, True)
    transpose_to(at_ref, pbuf)
    refill(pbuf, dh)
    shift_to(sbuf, pbuf)
    conv_back(sbuf, at_ref, weights.take(), dx, g, at.conv_two - base)
    weights.begin()

    def emit_inner(r, v):
        pbuf[pl.ds(r + 8, CHUNK), :] = v

    sums = norm_back(u_ref, dx, u_stats, scales, True, gm, emit_inner)
    gain, shift = vec[g_row + 2 : g_row + 3, :], vec[g_row + 3 : g_row + 4, :]
    d_gain = d_shift = 0.0
    dm[...] = jnp.zeros_like(dm)
    for img, (a, b) in enumerate(sums):
        scale = 1.0 + mod[mod_row + img : mod_row + img + 1, :CH_MID]
        d_gain, d_shift = d_gain + scale * b, d_shift + scale * a
        dm[img : img + 1, :CH_MID] = gain * b + shift * a
        dm[img : img + 1, CH_MID:] = a
    return d_gain, d_shift


def block_back_one(dh, x_ref, at, base, rows, vec, weights, tools, g):
    g_row, b1_row, b2_row = rows
    sbuf, pbuf, dx, at_ref, gm = tools
    put_row(g, at.bias_one - base, column_sum(pbuf))
    shift_to(sbuf, pbuf)
    stats = all_stats(x_ref, gm)
    scales = block_scales(vec, g_row)
    norm_to(pbuf, x_ref, stats, scales, True)
    transpose_to(at_ref, pbuf)
    conv_back(sbuf, at_ref, weights.take(), dx, g, at.conv_one - base)
    weights.begin()

    def emit_outer(r, v):
        dh[pl.ds(r, CHUNK), :] += v

    sums = norm_back(x_ref, dx, stats, scales, True, gm, emit_outer)
    put_row(g, at.gains - base, sums[0][1] + sums[1][1])
    put_row(g, at.gains + 3 - base, sums[0][0] + sums[1][0])


def rowsum(v):
    return jnp.sum(v, 0, keepdims=True)


def put_outer(g, at, left, right):
    for c in range(-(-left.shape[1] // LINE)):
        piece = outer(left[:, c * LINE : (c + 1) * LINE], right)
        put_lines(g, at + c * LINE * (EMB_DIM // LINE), piece, EMB_DIM // LINE)


class Weights:
    def __init__(self, sources, slots, sems):
        self.copies = []
        for n, source in enumerate(sources):
            target = slots.at[n % 2, pl.ds(0, source.shape[0]), :]
            self.copies.append((pltpu.make_async_copy(source, target, sems.at[n % 2]), target))
        self.begun = self.done = 0

    def begin(self):
        if self.begun < len(self.copies):
            self.copies[self.begun][0].start()
            self.begun += 1

    def take(self):
        copy, target = self.copies[self.done]
        copy.wait()
        self.done += 1
        return target


class Leave:
    def __init__(self, me, g, base, keep, send, stage, sems, pad):
        self.pad = pad
        self.core, self.place = lax.rem(me[0], 2), lax.div(me[0], 2)
        self.g, self.base, self.outs, self.stage, self.sems = g, base, (keep, send), stage, sems
        self.copies = []

    def plane(self, plane):
        for q in range(PLANE // 2):
            at = q ^ self.place
            first = PLANES[plane] + 2 * q * SHARD - self.base
            for side in range(2):
                core = 1 - self.core if side else self.core
                start = first + core * SHARD
                stage = self.stage.at[2 * q + side]
                whole, rest = divmod(ROOM, 288)

                def body(c, carry):
                    lines = self.g[pl.ds(pl.multiple_of(start + c * 288, 8), 288), :]
                    stage[pl.ds(pl.multiple_of(c * 288, 16), 288), :] = lines.astype(BF16)
                    return carry

                lax.fori_loop(0, whole, body, 0, unroll=7)
                lines = self.g[pl.ds(pl.multiple_of(start + whole * 288, 8), rest - 8), :]
                stage[whole * 288 :, :] = jnp.concatenate([lines, self.pad[...]], 0).astype(BF16)
                copy = pltpu.make_async_copy(stage, self.outs[side].at[at], self.sems.at[side])
                copy.start()
                self.copies.append(copy)

    def below(self, count, rest):
        copy = pltpu.make_async_copy(self.g.at[pl.ds(0, count), :], rest, self.sems.at[2])
        copy.start()
        self.copies.append(copy)

    def wait(self):
        for copy in self.copies:
            copy.wait()


def clear_lines(g, first, count):
    if count:
        g[first : first + count, :] = jnp.zeros((count, LINE), F32)


def prepare(sbuf, pbuf):
    clear_pads(sbuf)
    pbuf[0:8, :] = jnp.zeros((8, CH_MID), F32)
    pbuf[ROWS + 8 : ROWS + 16, :] = jnp.zeros((8, CH_MID), F32)


def back_top_kernel(*refs):
    me, total, f_o, f_t, base_o, base_t, out_o, out_t, mask, inverse, wz, gm, sel, gat, tile, expand, vec, mod, emb, h4, u2, h3, qkv, mixed, h2, s22, s21, s_attn, s_emb = refs[:29]
    keep, send, rest, dh, dse, pad = refs[29:35]
    g, slots, sbuf, pbuf, dx, at_ref, stage, sems, out_sems, w_sq, dqkv, dm, sq_sem = refs[35:]
    base = BASE_ONE
    weights = Weights([s22, s21, s_attn], slots, sems)
    weights.begin()
    weights.begin()
    sq_copy = pltpu.make_async_copy(s_emb, w_sq, sq_sem)
    sq_copy.start()
    prepare(sbuf, pbuf)
    clear_lines(g, TAIL - base, g.shape[0] - (TAIL - base))
    tools = (sbuf, pbuf, dx, at_ref, gm)

    stats = all_stats(h4, gm)
    scales = block_scales(vec, V_FG)
    norm_to(pbuf, h4, stats, scales, True)
    transpose_to(at_ref, pbuf)
    gap = (base_o[...] + out_o[...] * f_o[:, :12]) - (base_t[...] + out_t[...] * f_t[:, :12])
    loss = jnp.sum(mask[...] * (gap * gap))
    df = jnp.pad(out_o[...] * 2.0 * mask[...] * gap / total[0], ((0, 0), (0, LINE - 12)))
    spread = dot(df.astype(BF16), gat[...], NT)
    dt = jnp.zeros((ROWS, LINE), F32)
    for shift in range(9):
        inside, by = upsample_masks(shift)
        part = jnp.where(inside, spread, 0.0)
        dt = dt + (part if by == 0 else pltpu.roll(part, by % ROWS, 0))
    dz = dot(dt.astype(BF16), sel[...], NT)
    parts = split3(dz)
    dwz = dot(at_ref[...], parts[0]) + dot(at_ref[...], parts[1]) + dot(at_ref[...], parts[2])
    dx[...] = dot(parts[0], wz[...]) + dot(parts[1], wz[...]) + dot(parts[2], wz[...])
    d_rows = dot3(dwz.T[0 : 3 * TAPS, :], expand[...])
    d_taps = jnp.zeros((TAPS, 3 * CH_MID), F32)
    for c in range(3):
        d_taps = d_taps + jnp.where(colour(c), d_rows[c * TAPS : (c + 1) * TAPS, :], 0.0)
    for j in range(9):
        g[pl.ds(TAIL - base + j, 9, stride=9), :] = d_taps[0:9, j * LINE : (j + 1) * LINE]
    b_row = AT.bias_out - base
    bias = dot3(eight(rowsum(df)), tile[...], NT)[0:1]
    g[b_row : b_row + 1, :] = bias
    row = lax.broadcasted_iota(jnp.int32, (8, 1), 0)
    lane = lax.broadcasted_iota(jnp.int32, (1, LINE), 1)
    values = jnp.where(row == 0, loss, 0.0)
    for c in range(3):
        values = values + jnp.where(row == c + 1, jnp.sum(jnp.where(lane == c, bias, 0.0)), 0.0)
    pad[...] = to_digits(values, inverse[...])

    def emit_first(r, v):
        dh[pl.ds(r, CHUNK), :] = v

    sums = norm_back(h4, dx, stats, scales, True, gm, emit_first)
    put_row(g, AT.final_gains - base, sums[0][1] + sums[1][1])
    put_row(g, AT.final_gains + 3 - base, sums[0][0] + sums[1][0])

    rows = (V_G2, V_B21, V_B22)
    d_gain, d_shift = block_back_two(dh, u2, AT.second, base, rows, vec, mod, 2, weights, tools, g, dm)
    put_row(g, AT.second.gains + 6 - base, d_gain)
    put_row(g, AT.second.gains + 9 - base, d_shift)
    block_back_one(dh, h3, AT.second, base, rows, vec, weights, tools, g)
    se = silu(emb[...])
    put_outer(g, AT.second.embed - base, se, dm[...])
    put_row(g, AT.second.embed_bias - base, rowsum(dm[...]))
    sq_copy.wait()
    dse[...] = dot3(dm[...], w_sq[...], NT)

    put_row(g, AT.attn_bias - base, colsum(dh, 0, ROWS))
    w = weights.take()
    d_low = dh[...].astype(BF16)
    for c in range(ROWS // LINE):
        at_ref[:, c * LINE : (c + 1) * LINE] = mixed[c * LINE : (c + 1) * LINE, :].astype(F32).T.astype(BF16)
    put_lines(g, AT.attn_out - base, dot(at_ref[...], d_low), 3)
    pbuf[8 : 8 + ROWS, :] = dot(d_low, w[3 * CH_MID : 4 * CH_MID, :], NT)
    half = lane_half()
    scale = HEAD_DIM ** (-0.5)

    def heads(img, carry):
        rows = pl.ds(pl.multiple_of(img * PIX, PIX), PIX)
        for pair in range(HEADS // 2):
            q, k, v = attention_pair(qkv, img, pair)
            cols = slice(pair * LINE, (pair + 1) * LINE)
            do = pbuf[pl.ds(pl.multiple_of(img * PIX + 8, 8), PIX), cols].astype(BF16)
            dqs, dks, dvs = [], [], []
            for side in range(2):
                s = dot(keep_half(k, half, side), q, NT) * scale
                e = jnp.exp(s - jnp.max(s, 0, keepdims=True))
                prob = e / jnp.sum(e, 0, keepdims=True)
                dvs.append(dot(prob.astype(BF16), do))
                dp = dot(keep_half(v, half, side), do, NT)
                ds = prob * (dp - jnp.sum(dp * prob, 0, keepdims=True))
                dks.append(dot(ds.astype(BF16), q))
                dqs.append(dot(ds.T.astype(BF16), k))
            for part, pieces in enumerate((dqs, dks, dvs)):
                value = jnp.where(half, pieces[0], pieces[1])
                if part < 2:
                    value = value * scale
                dqkv[rows, part * CH_MID + pair * LINE : part * CH_MID + (pair + 1) * LINE] = value.astype(BF16)
        return carry

    lax.fori_loop(0, MB_DEV, heads, 0, unroll=2)
    stats = all_stats(h2, gm)
    scales = block_scales(vec, V_AG)
    norm_to(pbuf, h2, stats, scales, False)
    transpose_to(at_ref, pbuf)
    dx[...] = jnp.zeros_like(dx)
    for part in range(3):
        d = dqkv[:, part * CH_MID : (part + 1) * CH_MID]
        dw = dot(at_ref[...], d)
        for j in range(3):
            g[pl.ds(AT.attn_qkv - base + part * 3 + j, CH_MID, stride=9), :] = dw[:, j * LINE : (j + 1) * LINE]
        dx[...] += dot(d, w[part * CH_MID : (part + 1) * CH_MID, :], NT)
    weights.begin()

    def emit(r, v):
        dh[pl.ds(r, CHUNK), :] += v

    sums = norm_back(h2, dx, stats, scales, False, gm, emit)
    put_row(g, AT.attn_gains - base, sums[0][1] + sums[1][1])
    put_row(g, AT.attn_gains + 3 - base, sums[0][0] + sums[1][0])

    leave = Leave(me, g, base, keep, send, stage, out_sems, pad)
    leave.plane(3)
    leave.below(PLANES[3] - base, rest)
    leave.wait()


def back_second_half_kernel(*refs):
    me, pad, dh, gm, vec, mod, u1, s12, rest_in = refs[:9]
    keep, send, rest, du, dm, extra = refs[9:15]
    g, slots, sbuf, pbuf, dx, at_ref, stage, sems, out_sems, in_sem = refs[15:]
    base = BASE_TWO
    weights = Weights([s12], slots, sems)
    weights.begin()
    above = pltpu.make_async_copy(rest_in, g.at[pl.ds(BASE_ONE - base, PLANES[3] - BASE_ONE), :], in_sem)
    above.start()
    prepare(sbuf, pbuf)
    clear_lines(g, PLANES[3] - base, g.shape[0] - (PLANES[3] - base))
    above.wait()
    rows = (V_G1, V_B11, V_B12)
    tools = (sbuf, pbuf, dx, at_ref, gm)
    d_gain, d_shift = block_back_two(dh, u1, AT.first, base, rows, vec, mod, 0, weights, tools, g, dm)
    extra[...] = jnp.zeros_like(extra)
    extra[0:1, :] = d_gain
    extra[1:2, :] = d_shift
    for c in range(0, ROWS, CHUNK):
        du[c : c + CHUNK, :] = pbuf[8 + c : 8 + c + CHUNK, :]
    leave = Leave(me, g, base, keep, send, stage, out_sems, pad)
    leave.plane(2)
    leave.below(PLANES[2] - base, rest)
    leave.wait()


def back_first_half_kernel(*refs):
    me, pad, dh_in, du, dm, extra, dse_in, gm, vec, emb, h1, s11, s_emb, rest_in = refs[:14]
    keep, send, rest, dh, dse = refs[14:19]
    g, slots, sbuf, pbuf, dx, at_ref, stage, sems, out_sems, w_sq, in_sem, sq_sem = refs[19:]
    base = BASE_THREE
    weights = Weights([s11], slots, sems)
    weights.begin()
    sq_copy = pltpu.make_async_copy(s_emb, w_sq, sq_sem)
    sq_copy.start()
    above = pltpu.make_async_copy(rest_in, g.at[pl.ds(BASE_TWO - base, PLANES[2] - BASE_TWO), :], in_sem)
    above.start()
    prepare(sbuf, pbuf)
    clear_lines(g, PLANES[2] - base, g.shape[0] - (PLANES[2] - base))
    refill(pbuf, du)
    for c in range(0, ROWS, CHUNK):
        dh[c : c + CHUNK, :] = dh_in[c : c + CHUNK, :]
    above.wait()
    tools = (sbuf, pbuf, dx, at_ref, gm)
    put_outer(g, AT.first.embed - base, silu(emb[...]), dm[...])
    put_row(g, AT.first.embed_bias - base, rowsum(dm[...]))
    block_back_one(dh, h1, AT.first, base, (V_G1, V_B11, V_B12), vec, weights, tools, g)
    put_row(g, AT.first.gains + 6 - base, extra[0:1, :])
    put_row(g, AT.first.gains + 9 - base, extra[1:2, :])
    leave = Leave(me, g, base, keep, send, stage, out_sems, pad)
    leave.plane(1)
    leave.below(PLANES[1] - base, rest)
    sq_copy.wait()
    dse[...] = dse_in[...] + dot3(dm[...], w_sq[...], NT)
    leave.wait()


def back_low_kernel(*refs):
    me, labels, pad, dh, dse, emb, pre, phi, h0s, xp, s_down, s_time, rest_in = refs[:13]
    keep, send = refs[13:15]
    g, slots, sbuf, pbuf, h0t, stage, sems, out_sems, w_sq, demb_ref, dwin, dbin, in_sem, sq_sem = refs[15:]
    weights = Weights([s_down], slots, sems)
    weights.begin()
    sq_copy = pltpu.make_async_copy(s_time, w_sq, sq_sem)
    sq_copy.start()
    above = pltpu.make_async_copy(rest_in, g.at[pl.ds(BASE_THREE, PLANES[1] - BASE_THREE), :], in_sem)
    above.start()
    prepare(sbuf, pbuf)
    clear_lines(g, PLANES[1], g.shape[0] - PLANES[1])
    above.wait()
    demb = dse[...] * silu_slope(emb[...])
    put_row(g, AT.time_bias_two, rowsum(demb))
    put_outer(g, AT.time_two, silu(pre[...]), demb)
    sq_copy.wait()
    dpre = dot3(demb, w_sq[...], NT) * silu_slope(pre[...])
    put_row(g, AT.time_bias_one, rowsum(dpre))
    put_outer(g, AT.time_one, phi[...], dpre)
    clear = 240
    first, lines = AT.class_table, CLASSES * (EMB_DIM // LINE)

    def wipe(c, carry):
        g[pl.ds(first + c * clear, clear), :] = jnp.zeros((clear, LINE), F32)
        return carry

    lax.fori_loop(0, lines // clear, wipe, 0)
    demb_ref[...] = demb
    for n in range(MB_DEV):
        for j in range(EMB_DIM // LINE):
            at = first + labels[n] * (EMB_DIM // LINE) + j
            g[pl.ds(at, 1), :] += demb_ref[n : n + 1, j * LINE : (j + 1) * LINE]

    put_row(g, AT.bias_down, colsum(dh, 0, ROWS))
    refill(pbuf, dh)
    shift_to(sbuf, pbuf)
    w = weights.take()
    dwin[...] = jnp.zeros_like(dwin)
    dbin[...] = jnp.zeros_like(dbin)
    for ph in range(4):
        for c in range(ROWS // LINE):
            rows = slice(ph * ROWS + c * LINE, ph * ROWS + (c + 1) * LINE)
            h0t[:, c * LINE : (c + 1) * LINE] = h0s[rows, :].astype(F32).T.astype(BF16)
        d0 = jnp.zeros((ROWS, CH_BASE), F32)
        for ky in ((0, 2) if ph // 2 else (1,)):
            for kx in ((0, 2) if ph % 2 else (1,)):
                side = 2 if kx == 0 else 1
                d = shifted(sbuf, 32 if ky == 0 else 16, slice(side * CH_MID, (side + 1) * CH_MID))
                t = 3 * ky + kx
                d0 = d0 + dot(d, w[t * CH_BASE : (t + 1) * CH_BASE, :], NT)
                put_lines(g, AT.conv_down + t * CH_BASE * 3, dot(h0t[0:CH_BASE, :], d), 3)
        dbin[0:1, :CH_BASE] += rowsum(d0)
        dwin[:, :CH_BASE] += dot(xp[ph * ROWS : (ph + 1) * ROWS, :], d0.astype(BF16), TN)
    dwin[29:30, :] = dbin[0:1, :]
    even, odd = dwin[0:16, :], dwin[16:32, :]
    turned = pltpu.roll(odd[:, :LINE], LINE // 2, 1), pltpu.roll(odd[:, LINE:], LINE // 2, 1)
    g[pl.ds(0, 14, stride=3), :] = even[0:14, :LINE]
    g[pl.ds(1, 14, stride=3), :] = jnp.where(first_lanes(), even[:, LINE:], turned[0])[0:14]
    g[pl.ds(2, 14, stride=3), :] = jnp.where(first_lanes(), turned[0], turned[1])[0:14]
    leave = Leave(me, g, 0, keep, send, stage, out_sems, pad)
    leave.plane(0)
    leave.wait()


def kernel_params():
    return dict(
        compiler_params=pltpu.CompilerParams(vmem_limit_bytes=60 * 1024 * 1024),
        cost_estimate=pl.CostEstimate(flops=8 * 10**9, bytes_accessed=4 * 10**7, transcendentals=10**6),
    )


def back_call(kernel, name, lines, slots, args, smem, hbm, rest, outs, scratch, norms=True):
    sds = lambda *s: jax.ShapeDtypeStruct(*s)
    plane = sds((PLANE // 2, ROOM, LINE), BF16)
    rest = [sds((rest, LINE), F32)] if rest else []
    common = [
        vmem((lines + 8, LINE), F32),
        vmem((slots, 9 * CH_MID, CH_MID), BF16),
        vmem((PADDED, 3 * CH_MID), BF16),
        vmem((ROWS + 16, CH_MID), F32),
    ]
    if norms:
        common += [vmem((ROWS, CH_MID), F32), vmem((CH_MID, ROWS), BF16)]
    else:
        common += [vmem((256, ROWS), BF16)]
    common += [
        vmem((PLANE, ROOM, LINE), BF16),
        pltpu.SemaphoreType.DMA((2,)),
        pltpu.SemaphoreType.DMA((3,)),
    ]
    return pl.pallas_call(
        kernel,
        out_shape=[plane, plane, *rest, *(sds(*o) for o in outs)],
        in_specs=[SM] * smem + [VM] * (len(args) - smem - hbm) + [HB] * hbm,
        out_specs=[HB] * (2 + len(rest)) + [VM] * len(outs),
        scratch_shapes=common + scratch,
        name=name,
        **kernel_params(),
    )(*args)


ACT = ((ROWS, CH_MID), F32)
WIDE_ROW = ((8, EMB_DIM), F32)
DMA = pltpu.SemaphoreType.DMA


def back_top(args):
    scratch = [vmem((EMB_DIM, EMB_DIM), BF16), vmem((ROWS, 3 * CH_MID), BF16), vmem(*WIDE_ROW), DMA]
    lines = ALL_LINES - BASE_ONE
    return back_call(
        back_top_kernel, "back_top", lines, 2, args, 2, 4, PLANES[3] - BASE_ONE, [ACT, WIDE_ROW, ((8, LINE), F32)], scratch
    )


def back_second_half(args):
    outs = [ACT, WIDE_ROW, ((8, CH_MID), F32)]
    lines = PLANES[3] - BASE_TWO
    return back_call(back_second_half_kernel, "back_b", lines, 1, args, 1, 2, PLANES[2] - BASE_TWO, outs, [DMA])


def back_first_half(args):
    scratch = [vmem((EMB_DIM, EMB_DIM), BF16), DMA, DMA]
    lines = PLANES[2] - BASE_THREE
    return back_call(
        back_first_half_kernel, "back_c", lines, 1, args, 1, 3, PLANES[1] - BASE_THREE, [ACT, WIDE_ROW], scratch
    )


def back_low(args):
    scratch = [
        vmem((EMB_DIM, EMB_DIM), BF16),
        vmem(*WIDE_ROW),
        vmem((32, 2 * LINE), F32),
        vmem((8, 2 * LINE), F32),
        DMA,
        DMA,
    ]
    return back_call(back_low_kernel, "back_low", PLANES[1], 1, args, 2, 3, 0, [], scratch, False)


def karras(index):
    ramp_frac = index.astype(F32) / (DISCRETE - 1)
    low_root = SIGMA_LOW ** (1.0 / RHO_POWER)
    high_root = SIGMA_HIGH ** (1.0 / RHO_POWER)
    return (low_root + ramp_frac * (high_root - low_root)) ** RHO_POWER


def preconditioning_factors(sigma):
    variance_sum = sigma * sigma + SIGMA_DATA**2
    skip = SIGMA_DATA**2 / ((sigma - SIGMA_LOW) ** 2 + SIGMA_DATA**2)
    out = (sigma - SIGMA_LOW) * SIGMA_DATA * lax.rsqrt(variance_sum)
    return (skip, out, lax.rsqrt(variance_sum))


def noise_features(sigma):
    half_width = CH_BASE // 2
    frequency = jnp.exp(-math.log(10000.0) * jnp.arange(half_width, dtype=F32) / half_width)
    phases = 250.0 * jnp.log(sigma)[:, None] * frequency
    return jnp.pad(jnp.concatenate([jnp.cos(phases), jnp.sin(phases)], 1), ((0, 8 - MB_DEV), (0, 0)))


def pixels(images):
    lead = images.shape[0]
    split = images.reshape(lead, MB_DEV, HALF, 2, HALF, 2, 3)
    return split.transpose(0, 1, 2, 4, 3, 5, 6).reshape(lead, ROWS, 12)


def pixel_live(counts, valid_rows):
    row = lax.broadcasted_iota(jnp.int32, (ROWS, 12), 0)
    lane = lax.broadcasted_iota(jnp.int32, (ROWS, 12), 1)
    slot = row // PIX
    line = 2 * ((row // HALF) % HALF) + lane // 6
    top = jnp.where(slot == 0, valid_rows[0], valid_rows[1])
    return ((slot < counts[0]) & (line < top)).astype(F32)


def per_part(me, labels, lines, inputs, save, tables):
    _, x_in, phi, _ = inputs
    results = forward_call(save, me, labels, lines, x_in, phi, tables)
    return results[0], results[1:]


AXIS = "fsdp"
CORE, EAST, SOUTH, UP = 1, 2, 4, 8
CUT_ROWS = ROOM // 2


def swap(values, hop):
    return lax.ppermute(values, AXIS, [(i, i ^ hop) for i in range(SHARDS)])


def total_of(values, n):
    hop = 1
    while hop < n:
        values = values + lax.ppermute(values, AXIS, [(i, i ^ hop) for i in range(n)])
        hop *= 2
    return values


CUTS = (0, 880, 1760, ROOM)
TALL = SHARDS // PLANE


def gate(values, after):
    count = len(values)

    def body(*refs):
        pass

    return pl.pallas_call(
        body,
        out_shape=[jax.ShapeDtypeStruct(v.shape, v.dtype) for v in values],
        in_specs=[HB] * (count + len(after)),
        out_specs=[HB] * count,
        input_output_aliases={i: i for i in range(count)},
        name="gate",
    )(*values, *after)


def climb(values, way, far, first=0):
    planes = range(first, TALL - far) if way == 1 else range(TALL - 1 - first, far - 1, -1)
    pairs = [(q * PLANE + i, (q + way * far) * PLANE + i) for q in planes for i in range(PLANE)]
    return lax.ppermute(values, AXIS, pairs)


def column_window(slots, z):
    rows = []
    for p in range(TALL):
        value = slots[TALL - 1 + p]
        for q in range(1, TALL):
            value = jnp.where(z == q, slots[TALL - 1 - q + p], value)
        rows.append(value)
    return jnp.stack(rows)


def column_gather(own, z):
    below, above = [climb(own, 1, 1)], [climb(own, -1, 1)]
    for step in range(1, TALL - 1):
        below.append(climb(below[-1], 1, 1, step))
        above.append(climb(above[-1], -1, 1, step))
    return column_window([*below[::-1], own, *above], z), [below[0], above[0]], [below[-1], above[-1]]


def gather_lines(shard, z, early):
    ab, c = shard[: CUTS[2]], shard[CUTS[2] :]
    c_two = jnp.stack([c, swap(c, SOUTH)])
    c_four = jnp.concatenate([c_two, swap(c_two, EAST)])
    column, step, last = column_gather(ab, z)
    za, zb = column[:, : CUTS[1]], column[:, CUTS[1] :]
    done, ready = early(step)
    a_two, b_two = jnp.stack([za, swap(za, EAST)]), jnp.stack([zb, swap(zb, SOUTH)])
    a_far, b_far = swap(a_two, SOUTH), swap(b_two, EAST)
    (c_four,) = gate([c_four], [*last, *ready])
    c_all, _, _ = column_gather(c_four, z)
    pieces = [a_two, a_far, b_two, b_far, c_all]
    return done, pieces + [swap(v, CORE) for v in pieces]


def gather_moves():
    places = [(0, 1), (2, 3), (0, 2), (1, 3), (0, 2, 1, 3)]
    part = (0, 0, 1, 1, 2)
    moves = []
    for core in range(2):
        for n in range(5):
            row, end = CUTS[part[n]], CUTS[part[n] + 1]
            for lead, place in enumerate(places[n]):
                moves.append((core * 5 + n, lead, 2 * place + core, row, end - row))
    return moves


def gather_plain(shard):
    rows = shard.shape[0]
    lines = lax.all_gather(shard, AXIS, axis=0, tiled=True)
    if rows != ROOM:
        lines = jnp.pad(lines.reshape(SHARDS, SHARD, LINE), ((0, 0), (0, ROOM - SHARD), (0, 0)))
    lines = lines.reshape(TALL, PLANE, ROOM, LINE)
    return [lines], [(0, r, r, 0, ROOM) for r in range(PLANE)], (True,)


def digit_weights():
    return np.array([8.0 ** (k - 40) if k < 82 else 0.0 for k in range(LINE)], np.float32)[None]


def inverse_weights():
    weights = digit_weights()
    return np.where(weights > 0, 1.0 / np.where(weights > 0, weights, 1.0), 0.0).astype(np.float32)


def to_digits(values, inverse):
    size = jnp.abs(values) * inverse
    digit = jnp.floor(size) - 8.0 * jnp.floor(size * 0.125)
    digit = jnp.where(size < 2.0**27, digit, 0.0)
    return jnp.where(values < 0, -digit, digit)


def from_digits(rows):
    return jnp.sum(rows * digit_weights(), 1)


def low(v):
    return v.astype(BF16)


def wide(v):
    return v.astype(F32)


class PlaneSum:
    def __init__(self, keep, send):
        self.keep, self.got = keep, swap(send, CORE)
        self.a, self.b = slice(0, CUT_ROWS), slice(CUT_ROWS, ROOM)

    def quarter(self, i, rows):
        return wide(self.keep[i, rows]) + wide(self.got[i, rows])

    def first(self):
        a = low(jnp.stack([self.quarter(1, self.a), self.quarter(3, self.a)]))
        b = low(jnp.stack([self.quarter(2, self.b), self.quarter(3, self.b)]))
        return a, b

    def send_first(self, a, b):
        self.got_a, self.got_b = swap(a, EAST), swap(b, SOUTH)

    def last(self):
        return low(self.quarter(2, self.a) + wide(self.got_a[1])), low(self.quarter(1, self.b) + wide(self.got_b[1]))

    def send_last(self, a, b):
        self.end_a, self.end_b = swap(a, SOUTH), swap(b, EAST)

    def total(self):
        a = self.quarter(0, self.a) + wide(self.got_a[0]) + wide(self.end_a)
        b = self.quarter(0, self.b) + wide(self.got_b[0]) + wide(self.end_b)
        return jnp.concatenate([a, b])


def column_sums(parts, first, z):
    pick = lambda p: jnp.where(p == first, parts[0], parts[1])
    total = 0.0
    for way in (1, -1):
        run = None
        for far in range(TALL - 1, 0, -1):
            holders = [q for q in range(TALL) if q + way * far in (first, first + 1)]
            if not holders:
                continue
            value = pick(z + way * far)
            if run is not None:
                value = value + run
            pairs = [(q * PLANE + i, (q + way) * PLANE + i) for q in holders for i in range(PLANE)]
            run = wide(lax.ppermute(low(value), AXIS, pairs))
        total = total + run
    return total


def per_device(n, images, noise_draws, labels, step_index, valid_rows, counts, master, momentum, ema):
    direct = n == SHARDS
    index = lax.axis_index(AXIS)
    me = jnp.where(direct, lax.rem(index, PLANE), 0).astype(jnp.int32)[None]
    z = lax.div(index, PLANE)
    shards = [v.astype(BF16).reshape(-1, LINE) for v in (master, ema)]
    tables = tuple(jnp.asarray(v, BF16) for v in (group_table(), *spread_tables(), expand_table(), patch_table()))
    live = (jnp.arange(MB_DEV) < counts[0]).astype(jnp.int32)
    local_rows = jnp.sum(live * jnp.clip(valid_rows, 0, RES)).astype(F32)

    total = total_of(jnp.broadcast_to(local_rows, (8, LINE)), n)
    pixel_total = 3.0 * RES * total[0, 0]

    def early(after):
        clean, noise = gate([images, noise_draws], after) if after else (images, noise_draws)
        clean, noise = pixels(jnp.stack([clean, noise]))
        per_row = lambda v: jnp.repeat(v, PIX)[:, None]

        def inputs_of(sigma):
            noisy = clean + per_row(sigma) * noise
            skip, out_scale, in_scale = preconditioning_factors(sigma)
            x_in = jnp.pad((per_row(in_scale) * noisy).astype(BF16), ((0, 0), (0, LINE - 12)))
            return per_row(skip) * noisy, x_in, noise_features(sigma), per_row(out_scale)

        mask = pixel_live(counts, valid_rows)
        both = inputs_of(karras(step_index)), inputs_of(karras(step_index + 1))
        return (*both, mask), [v for part in both for v in part[:3]] + [mask, total]

    if direct:
        rooms = [jnp.pad(v, ((0, ROOM - SHARD), (0, 0))) for v in shards]
        target = gather_plain(rooms[1])
        (in_lo, in_hi, mask), pieces = gather_lines(rooms[0], z, early)
        online = (pieces, gather_moves(), (False,) * 4 + (True,) + (False,) * 4 + (True,))
    else:
        online, target = gather_plain(shards[0]), gather_plain(shards[1])
        in_lo, in_hi, mask = early(())[0]
    model_t, _ = per_part(jnp.zeros_like(me), labels, target, in_lo, False, tables)
    if direct:
        (x_in,) = gate([in_hi[1]], [model_t])
        in_hi = (in_hi[0], x_in, *in_hi[2:])
    model_o, saved = per_part(me, labels, online, in_hi, True, tables)
    phi = in_hi[2]
    (h0s, h1, u1, h2, qkv, mixed, h3, u2, h4, vec, mod, emb, pre, wz, xp) = saved[:15]
    s_time, s_emb1, s_emb2, s_down, s11, s12, s_attn, s21, s22 = saved[15:]
    gm = tables[0]
    inverse = jnp.asarray(inverse_weights())
    losses = (model_o, model_t, in_hi[0], in_lo[0], in_hi[3], in_lo[3], mask, inverse)
    keep3, send3, rest, dh, dse, pad = back_top(
        (me, pixel_total[None], *losses, wz, *tables[:5], vec, mod, emb, h4, u2, h3, qkv, mixed, h2, s22, s21, s_attn, s_emb2)
    )
    if direct:
        three = PlaneSum(keep3, send3)
    keep2, send2, rest, du, dm, extra = back_second_half((me, pad, dh, gm, vec, mod, u1, s12, rest))
    if direct:
        first3 = three.first()
        (du,) = gate([du], first3)
        three.send_first(*first3)
        two = PlaneSum(keep2, send2)
    keep1, send1, rest, dh, dse = back_first_half((me, pad, dh, du, dm, extra, dse, gm, vec, emb, h1, s11, s_emb1, rest))
    if direct:
        last3, first2 = three.last(), two.first()
        (dh,) = gate([dh], [*last3, *first2])
        three.send_last(*last3)
        two.send_first(*first2)
        one = PlaneSum(keep1, send1)
    keep0, send0 = back_low((me, labels, pad, dh, dse, emb, pre, phi, h0s, xp, s_down, s_time, rest))
    if direct:
        zero = PlaneSum(keep0, send0)
        one.send_first(*one.first())
        two.send_last(*two.last())
        zero.send_first(*zero.first())
        top = [two.total(), three.total()]
        high = column_sums(top, 2, z)
        one.send_last(*one.last())
        zero.send_last(*zero.last())
        bottom = [zero.total(), one.total()]
        reduced = column_sums(bottom, 0, z) + high
        own = jnp.where(z < 2, jnp.where(z == 0, bottom[0], bottom[1]), jnp.where(z == 2, top[0], top[1]))
        reduced = reduced + own
        small = from_digits(reduced[SHARD : SHARD + 4])
        reduced = reduced[:SHARD].reshape(-1)
    else:
        small = from_digits(total_of(pad, n)[:4])
        both = [jnp.stack([wide(k), wide(s)], 1) for k, s in ((keep0, send0), (keep1, send1), (keep2, send2), (keep3, send3))]
        lines = jnp.stack(both).reshape(SHARDS, ROOM, LINE)[:, :SHARD].reshape(n, -1)
        reduced = lax.psum_scatter(lines, AXIS, scatter_dimension=0, tiled=True).reshape(-1)
    new_momentum = MOMENTUM * momentum + reduced
    new_master = master - LEARN_RATE * (reduced + MOMENTUM * new_momentum)
    new_ema = EMA_DECAY * ema + (1.0 - EMA_DECAY) * new_master
    return (small[0] / pixel_total, new_momentum, new_master, new_ema, small[1:])


def solution(mesh):
    n = mesh.shape[AXIS]

    def step(*args):
        return per_device(n, *args)

    return jax.shard_map(
        step,
        mesh=mesh,
        in_specs=(P(AXIS, None, None, None),) * 2 + (P(AXIS),) * 7,
        out_specs=(P(), P(AXIS), P(AXIS), P(AXIS), P()),
        check_vma=False,
    )
```
